32 devices in a mesh: section: 2 (over y), group: 4 (over x, core), replica: 4 (over z).
Axes of the slice: x: 2, y: 2, z: 4, core: 2. Of those that a mesh axis runs over, the one named last changes fastest.
Arguments:
- images: bfloat16 [2, 32, 197, 1024], P(None, ('group', 'replica')), may hold values from -6 to 6
- cotangent: bfloat16 [2, 32, 197, 1024], P(None, ('group', 'replica')), may hold values from -6 to 6
- counts: int32 [2, 16], P(None, ('group', 'replica')), may hold values from 1 to 2, as said below
- qkv_weight: bfloat16 [2, 1024, 3072], P('section', 'group'), may hold values from -0.1875 to 0.1875
- out_weight: bfloat16 [2, 1024, 1024], P('section', 'group'), may hold values from -0.75 to 0.75
- expand_weight: bfloat16 [2, 1024, 4096], P('section', 'group'), may hold values from -0.1875 to 0.1875
- reduce_weight: bfloat16 [2, 4096, 1024], P('section', 'group'), may hold values from -0.09375 to 0.09375
- norm_gains: bfloat16 [2, 2, 1024], P('section', None, 'group'), may hold values from 0.5 to 1.5
- biases: bfloat16 [2, 6, 1024], P('section', None, 'group'), may hold values from -3 to 3
- expand_bias: bfloat16 [2, 4096], P('section', 'group'), may hold values from -3 to 3
Outputs:
- section_outputs: bfloat16 [2, 2, 32, 197, 1024], P('section', None, ('group', 'replica'))
- input_grads: bfloat16 [2, 2, 32, 197, 1024], P('section', None, ('group', 'replica'))
- query_key_value_gradient: float32 [2, 1024, 3072], P('section', 'group')
- projection_gradient: float32 [2, 1024, 1024], P('section', 'group')
- expand_grad: float32 [2, 1024, 4096], P('section', 'group')
- reduce_grad: float32 [2, 4096, 1024], P('section', 'group')
- gain_grad: float32 [2, 2, 1024], P('section', None, 'group')
- bias_grad: float32 [2, 6, 1024], P('section', None, 'group')
- expand_bias_grad: float32 [2, 4096], P('section', 'group')
The draws below stay inside these ranges and needn't reach their ends.
Inputs may be any that keep to these rules, and one draw needn't show every extreme that they name: counts[m, j] is how many of device j's 2 image slots in micro-batch m hold an image (the lowest ones); in every micro-batch some device has 2 and some 1.
All inputs are finite; a program needn't handle non-finite values.
Results may differ from the reference program's by a relative error of at most 0.015.
Values may be sent and summed in bfloat16 or wider, within the bound.
No kernel may reach another device: no remote copies, remote signals or barrier semaphores. Data moves between devices by JAX's collectives and lax.ppermute only.
A program may use at most 320 MiB of HBM per device.

```python
import jax
import jax.numpy as jnp
from jax import lax

D = 1024
HEADS = 16
FF = 4096
SEQ = 197
MICRO = 2
SLOTS = 2
DEVS = 16
IMAGES = 32


def draw_counts(key, part):
    key = jax.random.fold_in(key, 11)
    first_key, second_key = jax.random.split(key)
    filled = SLOTS - jax.random.randint(first_key, (MICRO, DEVS), 0, 2)
    chosen = jax.random.permutation(second_key, DEVS)
    filled = filled.at[:, chosen[0]].set(SLOTS).at[:, chosen[1]].set(SLOTS - 1)
    return filled.astype(jnp.int32)


def raised(drawn, key, source, target, parts, factor):
    def block_of(dim):
        return (jnp.arange(drawn.shape[dim]) // (drawn.shape[dim] // parts)).reshape((-1,) + (1,) * (drawn.ndim - 1 - dim))

    first = jax.random.permutation(key, parts)[block_of(target)]
    other_side = (block_of(target) + parts // 2) % parts
    return jnp.where((block_of(source) == first) | (block_of(source) == other_side), factor * drawn, drawn)


def block_scale(stream_key, extent, cuts, least, high):
    def one(axis_at, shards_of):
        draws = jax.random.uniform(jax.random.fold_in(jax.random.fold_in(stream_key, 6), axis_at), (shards_of,), jnp.float32, least / len(cuts), high / len(cuts))
        return jnp.repeat(jnp.exp(draws), extent[axis_at] // shards_of).reshape((-1,) + (1,) * (len(extent) - axis_at - 1))

    factor_of = one(*cuts[0])
    for cut in cuts[1:]:
        factor_of = factor_of * one(*cut)
    return factor_of


def scatter_about(rng, extent, scale, most, cuts=(), kind=jnp.bfloat16):
    level = block_scale(rng, extent, cuts, -0.22, 0.18) if cuts else 1.0
    array = jax.random.normal(rng, extent, jnp.float32) * scale * level
    return jnp.minimum(jnp.maximum(array, -most), most).astype(kind)


def noise_with(stream_key, shape, scale, bound, pieces, heavy, dtype=jnp.bfloat16):
    drawn = scale * jax.random.normal(stream_key, shape, jnp.float32)
    if pieces:
        drawn = drawn * block_scale(stream_key, shape, pieces, -0.22, 0.18)
    return jnp.clip(raised(drawn, jax.random.fold_in(stream_key, 3), *heavy), -bound, bound).astype(dtype)


def setup_inputs(seed: int = 0) -> dict:
    seeds = jax.random.split(jax.random.key(seed), 11)
    images = noise_with(seeds[0], (MICRO, IMAGES, SEQ, D), 1.0, 6.0, ((1, 16),), (1, 3, 16, 2.0))
    cotangent = noise_with(seeds[1], (MICRO, IMAGES, SEQ, D), 1.0, 6.0, ((1, 16),), (1, 3, 16, 2.0))
    counts = draw_counts(jax.random.fold_in(seeds[10], 71), 0)
    qkv_weight = scatter_about(seeds[3], (2, D, 3 * D), D ** -0.5, 0.1875, ((0, 2), (1, 4)))
    out_weight = scatter_about(seeds[4], (2, D, D), (D // 16) ** -0.5, 0.75, ((0, 2), (1, 4)))
    expand_weight = scatter_about(seeds[5], (2, D, FF), D ** -0.5, 0.1875, ((0, 2), (1, 4)))
    reduce_weight = scatter_about(seeds[6], (2, FF, D), FF ** -0.5, 0.09375, ((0, 2), (1, 4)))
    norm_gains = jnp.clip(1.0 + 0.1 * jax.random.normal(seeds[7], (2, 2, D), jnp.float32), 0.5, 1.5).astype(jnp.bfloat16)
    biases = scatter_about(seeds[8], (2, 6, D), 0.5, 3.0, ((0, 2), (2, 4)))
    expand_bias = scatter_about(seeds[9], (2, FF), 0.5, 3.0, ((0, 2), (1, 4)))
    return dict(images=images, cotangent=cotangent, counts=counts, qkv_weight=qkv_weight, out_weight=out_weight, expand_weight=expand_weight, reduce_weight=reduce_weight, norm_gains=norm_gains, biases=biases, expand_bias=expand_bias)


@jax.custom_vjp
def low(v):
    return lax.optimization_barrier(v.astype(jnp.bfloat16)).astype(jnp.float32)

@jax.custom_vjp
def low_back(v):
    return v

def low_keep(v):
    return (low(v), None)

def low_pass(kept, grad):
    return (grad,)

def back_keep(v):
    return (v, None)

def back_low(kept, grad):
    return (low(grad),)
low.defvjp(low_keep, low_pass)
low_back.defvjp(back_keep, back_low)
EPSILON = 1e-06

def normalize(values, gain, shift):
    center = values - lax.optimization_barrier(jnp.mean(values, axis=-1, keepdims=True))
    spread = lax.optimization_barrier(jnp.mean(center * center, axis=-1, keepdims=True))
    return center * lax.rsqrt(spread + EPSILON) * gain + shift

def block_layer(inputs, alive, params):
    query_key_value_weight, projection_weight, expansion_weight, contraction_weight, gain_rows, bias_broadcast, exp_b = params
    highest = lax.Precision.HIGHEST
    count, length, width = inputs.shape
    head_size = width // HEADS
    scale = head_size ** (-0.5)
    normalized_input = low(normalize(inputs, gain_rows[0], bias_broadcast[0]))
    query_key_value_bias = jnp.concatenate([bias_broadcast[2], jnp.zeros_like(bias_broadcast[2]), bias_broadcast[3]])
    packed = jnp.einsum('bld,de->ble', normalized_input, query_key_value_weight, precision=highest) + query_key_value_bias
    packed = low_back(low(packed)).reshape(count, length, 3, HEADS, head_size)
    queries, key_rows, value_rows = (packed[:, :, 0], packed[:, :, 1], packed[:, :, 2])
    scores = low_back(jnp.einsum('bqhe,bkhe->bhqk', queries, key_rows, precision=highest) * scale)
    attend = low(jax.nn.softmax(scores, axis=-1))
    attended_output = jnp.einsum('bhqk,bkhe->bqhe', attend, value_rows, precision=highest).reshape(count, length, width)
    attended_output = low_back(low(attended_output))
    branch = low_back(jnp.einsum('bld,de->ble', attended_output, projection_weight, precision=highest) + bias_broadcast[4])
    middle = inputs + branch
    second_residual = low(normalize(middle, gain_rows[1], bias_broadcast[1]))
    hidden = low_back(jnp.einsum('bld,df->blf', second_residual, expansion_weight, precision=highest) + exp_b)
    activated_hidden = low(jax.nn.gelu(hidden, approximate=False))
    feed = low_back(jnp.einsum('blf,fd->bld', activated_hidden, contraction_weight, precision=highest) + bias_broadcast[5])
    return (middle + feed) * alive[:, None, None]

def run_layer(inputs, alive, params):
    total, length, width = inputs.shape
    grouped = 4 * SLOTS
    blocks = inputs.reshape(total // grouped, grouped, length, width)
    alive_blocks = alive.reshape(total // grouped, grouped)

    def one_block(pair):
        return block_layer(pair[0], pair[1], params)
    result = lax.map(jax.checkpoint(one_block), (blocks, alive_blocks))
    return result.reshape(total, length, width)

def reference(images, cotangent, counts, qkv_weight, out_weight, expand_weight, reduce_weight, norm_gains, biases, expand_bias):
    positions = jnp.arange(IMAGES).astype(jnp.int32)
    slot_index = positions % SLOTS
    owner = positions // SLOTS
    alive = (slot_index[None, :] < counts[:, owner]).astype(jnp.float32).reshape(MICRO * IMAGES)
    inputs = images.astype(jnp.float32).reshape(MICRO * IMAGES, SEQ, D)
    params = tuple((w.astype(jnp.float32) for w in (qkv_weight, out_weight, expand_weight, reduce_weight, norm_gains, biases, expand_bias)))
    probe = jnp.zeros_like(inputs)

    def forward(first_in, weights, nudge):
        lower = tuple((w[0] for w in weights))
        upper = tuple((w[1] for w in weights))
        between = low_back(low(run_layer(first_in, alive, lower)) + nudge)
        return (run_layer(between, alive, upper), between)
    final, pullback, between = jax.vjp(forward, inputs, params, probe, has_aux=True)
    back_in, weight_grads, between_grad = pullback(cotangent.astype(jnp.float32).reshape(final.shape))
    shaped = (MICRO, IMAGES, SEQ, D)
    section_outputs = jnp.stack([between.reshape(shaped), final.reshape(shaped)]).astype(jnp.bfloat16)
    input_grads = jnp.stack([back_in.reshape(shaped), between_grad.reshape(shaped)]).astype(jnp.bfloat16)
    return (section_outputs, input_grads, weight_grads[0], weight_grads[1], weight_grads[2], weight_grads[3], weight_grads[4], weight_grads[5], weight_grads[6])
```

```python
from functools import partial

import jax
import jax.numpy as jnp
from jax import lax
from jax.experimental import pallas as pl
from jax.experimental.pallas import tpu as pltpu
from jax.sharding import PartitionSpec as P

HEADS = 16
EPSILON = 1e-06
NEGATIVE = -1e30
F32 = jnp.float32
BF16 = jnp.bfloat16
VMEM_LIMIT = 58 * 2**20
ROOT_HALF = 0.7071067811865476
ROOT_TAU = 0.3989422804014327
ROWS = 32
ANY = pl.BlockSpec(memory_space=pl.ANY)
VMEM = pl.BlockSpec(memory_space=pltpu.VMEM)
SMEM = pl.BlockSpec(memory_space=pltpu.SMEM)
GAIN0, GAIN1, SHIFT0, SHIFT1, QUERY, VALUE, OUT, FEED, EXPAND = range(9)


def padded(length):
    return -(-length // 16) * 16


def contract(left, right, left_dim, right_dim):
    return lax.dot_general(
        left, right, (((left_dim,), (right_dim,)), ((), ())), preferred_element_type=F32
    )


def standardized(values):
    center = values - jnp.mean(values, axis=-1, keepdims=True)
    spread = jnp.mean(center * center, axis=-1, keepdims=True)
    scale = lax.rsqrt(spread + EPSILON)
    return center * scale, scale


def norm_pull(grad, gain, unit, scale):
    scaled = grad * gain
    mean = jnp.mean(scaled, axis=-1, keepdims=True)
    along = jnp.mean(scaled * unit, axis=-1, keepdims=True)
    return scale * (scaled - mean - unit * along)


def call(body, name, operands, specs, outs, scratch, flops):
    moved = sum(o.size * o.dtype.itemsize for o in operands)
    out_shape = [jax.ShapeDtypeStruct(shape, dtype) for shape, dtype in outs]
    moved += sum(o.size * o.dtype.itemsize for o in out_shape)
    return pl.pallas_call(
        body,
        out_shape=out_shape,
        in_specs=specs,
        out_specs=[VMEM] * len(outs),
        scratch_shapes=scratch,
        compiler_params=pltpu.CompilerParams(vmem_limit_bytes=VMEM_LIMIT),
        cost_estimate=pl.CostEstimate(flops=flops, bytes_accessed=moved, transcendentals=0),
        name=name,
    )(*operands)


def start_pieces(pieces, order_ref, target, sems, slot, columns):
    rows = pieces[0].shape[0]
    copies = []
    for index, piece in enumerate(pieces):
        where = pl.multiple_of(order_ref[index] * rows, rows)
        copy = pltpu.make_async_copy(
            piece.at[:, columns], target.at[pl.ds(where, rows), columns], sems.at[slot, index]
        )
        copy.start()
        copies.append(copy)
    return copies


def wait_all(copies):
    for copy in copies:
        copy.wait()


def start_chosen(section, lower, upper, target, sem):
    if lower is upper:
        copy = pltpu.make_async_copy(lower, target, sem)
        copy.start()
        return copy

    @pl.when(section == 0)
    def _():
        pltpu.make_async_copy(lower, target, sem).start()

    @pl.when(section != 0)
    def _():
        pltpu.make_async_copy(upper, target, sem).start()

    return pltpu.make_async_copy(lower, target, sem)


def each_chunk(count, length, whole, tail):
    full = length // ROWS
    for image in range(count):

        def step(index, carry, image=image):
            whole(image, pl.multiple_of(index * ROWS, ROWS))
            return carry

        lax.fori_loop(0, full, step, 0)
        if length > full * ROWS:
            tail(image, full * ROWS)


def row_at(image, space, row):
    return pl.multiple_of(image * space + row, 16)


def attention_forward(lower, upper, pieces, params, meta, keep):
    count, length, width = lower.shape
    space = padded(length)
    rows = count * space
    parts = len(pieces)
    head = width // HEADS
    pair = 2 * head
    scale = head**-0.5
    same = lower is upper
    extra = length % ROWS
    rest = space - length // ROWS * ROWS

    def body(*refs):
        refs = list(refs)
        low = refs.pop(0)
        up = low if same else refs.pop(0)
        weight = [refs.pop(0) for _ in range(parts)]
        vec, info = refs.pop(0), refs.pop(0)
        if keep:
            norm, packed, mixed, logs = (refs.pop(0) for _ in range(4))
        else:
            mixed = refs.pop(0)
        x, stage, full, x_sem, w_sem = (refs.pop(0) for _ in range(5))
        if not keep:
            norm, packed = (refs.pop(0) for _ in range(2))
        else:
            columns = refs.pop(0)
        section = info[parts]
        take = start_chosen(section, low, up, x, x_sem)
        loads = [
            start_pieces(weight, info, full, w_sem, block, pl.ds(block * width, width))
            for block in range(3)
        ]
        take.wait()
        gain, shift = vec[GAIN0 : GAIN0 + 1], vec[SHIFT0 : SHIFT0 + 1]
        stage[...] = jnp.zeros_like(stage)

        def whole(image, row):
            unit, _ = standardized(x[image, pl.ds(row, ROWS)].astype(F32))
            norm[pl.ds(row_at(image, space, row), ROWS)] = (unit * gain + shift).astype(BF16)

        def tail(image, row):
            unit, _ = standardized(x[image, row:length].astype(F32))
            stage[0:extra] = unit * gain + shift
            norm[pl.ds(image * space + row, rest)] = stage[0:rest].astype(BF16)

        each_chunk(count, length, whole, tail)
        for block in range(3):
            wait_all(loads[block])
            done = contract(norm[...], full[:, block * width : (block + 1) * width], 1, 0)
            if block != 1:
                bias = QUERY if block == 0 else VALUE
                done = done + vec[bias : bias + 1]
            packed[:, block * width : (block + 1) * width] = done.astype(BF16)
        lane = lax.broadcasted_iota(jnp.int32, (space, pair), 1)
        left = lane < head
        live = lax.broadcasted_iota(jnp.int32, (space, pair), 0) < length
        key_live = lax.broadcasted_iota(jnp.int32, (space, space), 1) < length
        for image in range(count):
            span = pl.ds(image * space, space)

            def heads(index, carry, span=span):
                def part(block):
                    offset = pl.multiple_of(block * width + index * pair, pair)
                    return packed[span, pl.ds(offset, pair)].astype(F32)

                query, key, value = part(0) * scale, part(1).astype(BF16), part(2)
                found = []
                tops = []
                for side in range(2):
                    mine = left if side == 0 else ~left
                    asked = jnp.where(mine, query, 0.0).astype(BF16)
                    held = jnp.where(live, jnp.where(mine, value, 1.0), 0.0).astype(BF16)
                    scores = jnp.where(key_live, contract(asked, key, 1, 1), NEGATIVE)
                    top = jnp.max(scores, axis=-1, keepdims=True)
                    raised = jnp.exp(scores - top).astype(BF16)
                    found.append(contract(raised, held, 1, 0))
                    tops.append(top)
                upper_part = jnp.where(left, found[0], found[1])
                total = jnp.where(left, found[1], found[0])
                turned = pltpu.roll(total, head, 1)
                offset = pl.multiple_of(index * pair, pair)
                mixed[span, pl.ds(offset, pair)] = (upper_part / turned).astype(BF16)
                if keep:
                    logged = jnp.log(turned)
                    first = tops[0] + logged[:, 0:1]
                    second = tops[1] + logged[:, head : head + 1]
                    held = columns[...]
                    held = jnp.where(lane == 2 * index, first, held)
                    columns[...] = jnp.where(lane == 2 * index + 1, second, held)
                return carry

            if keep:
                columns[...] = jnp.zeros_like(columns)
            lax.fori_loop(0, HEADS // 2, heads, 0)
            if keep:
                logs[image] = columns[...].T[0:HEADS]

    outs = [((rows, width), BF16)]
    scratch = [
        pltpu.VMEM((count, length, width), BF16),
        pltpu.VMEM((ROWS, width), F32),
        pltpu.VMEM((width, 3 * width), BF16),
        pltpu.SemaphoreType.DMA,
        pltpu.SemaphoreType.DMA((3, parts)),
    ]
    if keep:
        outs = (
            [((rows, width), BF16), ((rows, 3 * width), BF16)]
            + outs
            + [((count, HEADS, space), F32)]
        )
        scratch += [pltpu.VMEM((space, pair), F32)]
    else:
        scratch += [pltpu.VMEM((rows, width), BF16), pltpu.VMEM((rows, 3 * width), BF16)]
    inputs = [lower] if same else [lower, upper]
    return call(
        body,
        "attention_forward",
        inputs + list(pieces) + [params, meta],
        [ANY] * (len(inputs) + parts) + [VMEM, SMEM],
        outs,
        scratch,
        2 * rows * width * (3 * width + 2 * space),
    )


def hidden_forward(lower, upper, mixed, out_pieces, pieces, params, meta, keep):
    count, length, width = lower.shape
    space = padded(length)
    rows = count * space
    parts = len(pieces)
    inner = pieces[0].shape[1]
    same = lower is upper
    extra = length % ROWS
    rest = space - length // ROWS * ROWS
    blocks = inner // width

    def body(*refs):
        refs = list(refs)
        low = refs.pop(0)
        up = low if same else refs.pop(0)
        attended = refs.pop(0)
        project = [refs.pop(0) for _ in range(parts)]
        expand = [refs.pop(0) for _ in range(parts)]
        vec, info = refs.pop(0), refs.pop(0)
        middle, active = refs.pop(0), refs.pop(0)
        if keep:
            second, slope = refs.pop(0), refs.pop(0)
        x, full_out, full, x_sem, o_sem, w_sem = (refs.pop(0) for _ in range(6))
        if not keep:
            second = refs.pop(0)
        section = info[parts]
        take = start_chosen(section, low, up, x, x_sem)
        first_load = start_pieces(project, info, full_out, o_sem, 0, pl.ds(0, width))
        loads = [
            start_pieces(expand, info, full, w_sem, block, pl.ds(block * width, width))
            for block in range(blocks)
        ]
        wait_all(first_load)
        middle[...] = contract(attended[...], full_out[...], 1, 0) + vec[OUT : OUT + 1]
        take.wait()
        gain, shift = vec[GAIN1 : GAIN1 + 1], vec[SHIFT1 : SHIFT1 + 1]

        def whole(image, row):
            here = pl.ds(row_at(image, space, row), ROWS)
            total = middle[here] + x[image, pl.ds(row, ROWS)].astype(F32)
            middle[here] = total
            unit, _ = standardized(total)
            second[here] = (unit * gain + shift).astype(BF16)

        def tail(image, row):
            start = image * space + row
            middle[pl.ds(start, extra)] += x[image, row:length].astype(F32)
            unit, _ = standardized(middle[pl.ds(start, rest)])
            second[pl.ds(start, rest)] = (unit * gain + shift).astype(BF16)

        each_chunk(count, length, whole, tail)
        for block in range(blocks):
            wait_all(loads[block])
            part = slice(block * width, (block + 1) * width)
            value = contract(second[...], full[:, part], 1, 0) + vec[EXPAND + block - 0 : EXPAND + block + 1]
            share = 0.5 + 0.5 * lax.erf(value * ROOT_HALF)
            active[:, part] = (value * share).astype(BF16)
            if keep:
                density = ROOT_TAU * jnp.exp(-0.5 * value * value)
                slope[:, part] = (share + value * density).astype(BF16)

    outs = [((rows, width), F32), ((rows, inner), BF16)]
    scratch = [
        pltpu.VMEM((count, length, width), BF16),
        pltpu.VMEM((width, width), BF16),
        pltpu.VMEM((width, inner), BF16),
        pltpu.SemaphoreType.DMA,
        pltpu.SemaphoreType.DMA((1, parts)),
        pltpu.SemaphoreType.DMA((blocks, parts)),
    ]
    if keep:
        outs += [((rows, width), BF16), ((rows, inner), BF16)]
    else:
        scratch += [pltpu.VMEM((rows, width), BF16)]
    inputs = [lower] if same else [lower, upper]
    return call(
        body,
        "hidden_forward",
        inputs + [mixed] + list(out_pieces) + list(pieces) + [params, meta],
        [ANY] * len(inputs) + [VMEM] + [ANY] * (2 * parts) + [VMEM, SMEM],
        outs,
        scratch,
        2 * rows * width * (width + inner),
    )


def output_forward(middle, active, pieces, params, meta, count, length):
    rows, width = middle.shape
    inner = active.shape[1]
    space = padded(length)
    parts = len(pieces)
    half = width // 2

    def body(*refs):
        refs = list(refs)
        mid, act = refs.pop(0), refs.pop(0)
        reduce = [refs.pop(0) for _ in range(parts)]
        vec, info, result, full, w_sem = refs
        loads = [
            start_pieces(reduce, info, full, w_sem, block, pl.ds(block * half, half))
            for block in range(2)
        ]
        for block in range(2):
            wait_all(loads[block])
            part = slice(block * half, (block + 1) * half)
            value = contract(act[...], full[:, part], 1, 0) + mid[:, part] + vec[FEED : FEED + 1, part]
            for image in range(count):
                alive = jnp.where(info[parts + 1 + image] > 0, 1.0, 0.0)
                kept = value[image * space : image * space + length] * alive
                result[image, :, part] = kept.astype(BF16)

    return call(
        body,
        "output_forward",
        [middle, active] + list(pieces) + [params, meta],
        [VMEM, VMEM] + [ANY] * parts + [VMEM, SMEM],
        [((count, length, width), BF16)],
        [
            pltpu.VMEM((inner, width), BF16),
            pltpu.SemaphoreType.DMA((2, parts)),
        ],
        2 * rows * width * inner,
    )[0]


def hidden_backward(upstream, kept_low, kept_up, out_weights, weights, params, meta):
    count, length, width = upstream.shape
    space = padded(length)
    rows = count * space
    parts = len(weights)
    inner = weights[0].shape[1]
    same = kept_low[0] is kept_up[0]
    extra = length % ROWS
    rest = space - length // ROWS * ROWS
    half = width // 2
    deep = out_weights[0].shape[0]

    def body(*refs):
        refs = list(refs)
        grad = refs.pop(0)
        slope_low, middle_low = refs.pop(0), refs.pop(0)
        slope_up, middle_up = (slope_low, middle_low) if same else (refs.pop(0), refs.pop(0))
        reduce = [refs.pop(0) for _ in range(parts)]
        expand = [refs.pop(0) for _ in range(parts)]
        vec, info = refs.pop(0), refs.pop(0)
        hidden, mid_grad, branch, sums, inner_sums = (refs.pop(0) for _ in range(5))
        feed, second, slope, middle, full_out, full, k_sem, o_sem, w_sem = refs
        section = info[parts]
        for_slope = start_chosen(section, slope_low, slope_up, slope, k_sem.at[0])
        first_load = [
            start_pieces([piece], info_at(info, index), full_out, o_sem.at[pl.ds(index, 1)], 0, pl.ds(0, width))
            for index, piece in enumerate(reduce)
        ]
        for_middle = start_chosen(section, middle_low, middle_up, middle, k_sem.at[1])
        load = start_pieces(expand, info, full, w_sem, 0, pl.ds(0, inner))
        for image in range(count):
            alive = jnp.where(info[parts + 1 + image] > 0, 1.0, 0.0)
            feed[pl.ds(image * space + length // 16 * 16, space - length // 16 * 16)] = jnp.zeros(
                (space - length // 16 * 16, width), BF16
            )
            feed[pl.ds(image * space, length)] = (grad[image].astype(F32) * alive).astype(BF16)
        for_slope.wait()
        for index in range(parts):
            wait_all(first_load[index])
            where = pl.multiple_of(info[index] * deep, deep)
            value = contract(feed[...], full_out[pl.ds(where, deep)], 1, 1)
            value = (value * slope[:, pl.ds(where, deep)].astype(F32)).astype(BF16)
            hidden[:, pl.ds(where, deep)] = value
            inner_sums[:, pl.ds(where, deep)] = jnp.sum(value.astype(F32), axis=0, keepdims=True)
        wait_all(load)
        for block in range(2):
            second[:, block * half : (block + 1) * half] = contract(
                hidden[...], full[block * half : (block + 1) * half], 1, 1
            )
        for_middle.wait()
        gain = vec[GAIN1 : GAIN1 + 1]
        sums[...] = jnp.zeros_like(sums)

        def step(index, carry):
            here = pl.ds(pl.multiple_of(index * 16, 16), 16)
            unit, scale = standardized(middle[here])
            down = second[here]
            top = feed[here].astype(F32)
            total = top + norm_pull(down, gain, unit, scale)
            low = total.astype(BF16)
            mid_grad[here] = total
            branch[here] = low
            sums[0:1] += jnp.sum(down * unit, axis=0, keepdims=True)
            sums[1:2] += jnp.sum(down, axis=0, keepdims=True)
            sums[2:3] += jnp.sum(low.astype(F32), axis=0, keepdims=True)
            sums[3:4] += jnp.sum(top, axis=0, keepdims=True)
            return carry

        lax.fori_loop(0, rows // 16, step, 0)

    kept = list(kept_low) if same else list(kept_low) + list(kept_up)
    return call(
        body,
        "hidden_backward",
        [upstream] + kept + list(out_weights) + list(weights) + [params, meta],
        [VMEM] + [ANY] * (len(kept) + 2 * parts) + [VMEM, SMEM],
        [
            ((rows, inner), BF16),
            ((rows, width), F32),
            ((rows, width), BF16),
            ((8, width), F32),
            ((1, inner), F32),
        ],
        [
            pltpu.VMEM((rows, width), BF16),
            pltpu.VMEM((rows, width), F32),
            pltpu.VMEM((rows, inner), BF16),
            pltpu.VMEM((rows, width), F32),
            pltpu.VMEM((inner, width), BF16),
            pltpu.VMEM((width, inner), BF16),
            pltpu.SemaphoreType.DMA((2,)),
            pltpu.SemaphoreType.DMA((parts, 1)),
            pltpu.SemaphoreType.DMA((1, parts)),
        ],
        4 * rows * width * inner,
    )


class info_at:
    def __init__(self, ref, index):
        self.ref, self.index = ref, index

    def __getitem__(self, index):
        return self.ref[self.index + index]


def attention_backward(
    branch, mid_grad, lower, upper, kept_low, kept_up, out_weights, weights, params, meta
):
    count, length, width = lower.shape
    space = padded(length)
    rows = count * space
    parts = len(weights)
    head = width // HEADS
    pair = 2 * head
    scale = head**-0.5
    same = kept_low[0] is kept_up[0]
    same_in = lower is upper
    extra = length % ROWS
    rest = space - length // ROWS * ROWS
    half = width // 2

    def body(*refs):
        refs = list(refs)
        low_grad, top_grad = refs.pop(0), refs.pop(0)
        low = refs.pop(0)
        up = low if same_in else refs.pop(0)
        packed_low, mixed_low, logs_low = (refs.pop(0) for _ in range(3))
        packed_up, mixed_up, logs_up = (
            (packed_low, mixed_low, logs_low) if same else (refs.pop(0) for _ in range(3))
        )
        project = [refs.pop(0) for _ in range(parts)]
        query_key_value = [refs.pop(0) for _ in range(parts)]
        vec, info = refs.pop(0), refs.pop(0)
        result, grads, sums = (refs.pop(0) for _ in range(3))
        x, packed, mixed, logs, down, normal, stage, full_out, full, k_sem, o_sem, w_sem = refs
        section = info[parts]
        first_load = start_pieces(project, info, full_out, o_sem, 0, pl.ds(0, width))
        takes = [
            start_chosen(section, one, two, target, k_sem.at[index])
            for index, (one, two, target) in enumerate(
                (
                    (mixed_low, mixed_up, mixed),
                    (packed_low, packed_up, packed),
                    (logs_low, logs_up, logs),
                    (low, up, x),
                )
            )
        ]
        load = start_pieces(query_key_value, info, full, w_sem, 0, pl.ds(0, 3 * width))
        wait_all(first_load)
        down[...] = contract(low_grad[...], full_out[...], 1, 1).astype(BF16)
        wait_all(takes)
        owner = lax.shift_right_logical(
            lax.broadcasted_iota(jnp.int32, (HEADS, width), 1), head.bit_length() - 1
        )
        chosen = jnp.where(
            owner == lax.broadcasted_iota(jnp.int32, (HEADS, width), 0), 1.0, 0.0
        ).astype(BF16)
        left = lax.broadcasted_iota(jnp.int32, (space, pair), 1) < head
        live = lax.broadcasted_iota(jnp.int32, (space, pair), 0) < length
        key_live = lax.broadcasted_iota(jnp.int32, (space, space), 0) < length
        for image in range(count):
            span = pl.ds(image * space, space)
            product = down[span].astype(F32) * mixed[span].astype(F32)
            coarse = product.astype(BF16)
            fine = (product - coarse.astype(F32)).astype(BF16)
            stage[0:HEADS, 0:space] = contract(chosen, coarse, 1, 1) + contract(chosen, fine, 1, 1)

            def heads(index, carry, span=span, image=image):
                def part(block):
                    offset = pl.multiple_of(block * width + index * pair, pair)
                    return packed[span, pl.ds(offset, pair)]

                query, key, value = part(0), part(1), part(2)
                wide = key.astype(F32) * scale
                value = value.astype(F32)
                arrived = down[span, pl.ds(pl.multiple_of(index * pair, pair), pair)]
                found = []
                for side in range(2):
                    mine = left if side == 0 else ~left
                    log = logs[image, pl.ds(2 * index + side, 1), :]
                    dot = stage[pl.ds(2 * index + side, 1), 0:space]
                    scores = contract(jnp.where(mine, wide, 0.0).astype(BF16), query, 1, 1)
                    chance = jnp.exp(jnp.where(key_live, scores - log, NEGATIVE))
                    back = contract(jnp.where(mine, value, 0.0).astype(BF16), arrived, 1, 1)
                    change = (chance * (back - dot)).astype(BF16)
                    found.append(
                        (
                            contract(change, key, 0, 0),
                            contract(change, query, 1, 0),
                            contract(chance.astype(BF16), arrived, 1, 0),
                        )
                    )
                for block, factor in enumerate((scale, scale, 1.0)):
                    total = jnp.where(left, found[0][block], found[1][block]) * factor
                    offset = pl.multiple_of(block * width + index * pair, pair)
                    grads[span, pl.ds(offset, pair)] = jnp.where(live, total, 0.0).astype(BF16)
                return carry

            lax.fori_loop(0, HEADS // 2, heads, 0)
        wait_all(load)
        for block in range(2):
            normal[:, block * half : (block + 1) * half] = contract(
                grads[...], full[block * half : (block + 1) * half], 1, 1
            )
        gain = vec[GAIN0 : GAIN0 + 1]
        sums[...] = jnp.zeros_like(sums)
        sums[2:3] = jnp.sum(grads[:, 0:width].astype(F32), axis=0, keepdims=True)
        sums[3:4] = jnp.sum(grads[:, 2 * width : 3 * width].astype(F32), axis=0, keepdims=True)

        def step(value, grad, top):
            unit, rate = standardized(value)
            sums[0:1] += jnp.sum(grad * unit, axis=0, keepdims=True)
            sums[1:2] += jnp.sum(grad, axis=0, keepdims=True)
            return top + norm_pull(grad, gain, unit, rate)

        def whole(image, row):
            here = pl.ds(row_at(image, space, row), ROWS)
            value = x[image, pl.ds(row, ROWS)].astype(F32)
            result[image, pl.ds(row, ROWS)] = step(value, normal[here], top_grad[here]).astype(BF16)

        def tail(image, row):
            here = pl.ds(image * space + row, extra)
            value = x[image, row:length].astype(F32)
            result[image, row:length] = step(value, normal[here], top_grad[here]).astype(BF16)

        each_chunk(count, length, whole, tail)

    kept = list(kept_low) if same else list(kept_low) + list(kept_up)
    inputs = [lower] if same_in else [lower, upper]
    return call(
        body,
        "attention_backward",
        [branch, mid_grad] + inputs + kept + list(out_weights) + list(weights) + [params, meta],
        [VMEM, VMEM] + [ANY] * (len(inputs) + len(kept) + 2 * parts) + [VMEM, SMEM],
        [((count, length, width), BF16), ((rows, 3 * width), BF16), ((8, width), F32)],
        [
            pltpu.VMEM((count, length, width), BF16),
            pltpu.VMEM((rows, 3 * width), BF16),
            pltpu.VMEM((rows, width), BF16),
            pltpu.VMEM((count, HEADS, space), F32),
            pltpu.VMEM((rows, width), BF16),
            pltpu.VMEM((rows, width), F32),
            pltpu.VMEM((HEADS, 2 * pair), F32),
            pltpu.VMEM((width, width), BF16),
            pltpu.VMEM((width, 3 * width), BF16),
            pltpu.SemaphoreType.DMA((4,)),
            pltpu.SemaphoreType.DMA((1, parts)),
            pltpu.SemaphoreType.DMA((1, parts)),
        ],
        2 * rows * width * (4 * width + 5 * space),
    )


def weight_gradient(kept, lowers, uppers, meta, parts, quarter, rows_of, columns_of, name):
    micro = len(kept)
    first_row, height = rows_of
    first_column, breadth = columns_of
    rows = kept[0].shape[0]

    def body(*refs):
        refs = list(refs)
        left = [refs.pop(0) for _ in range(micro)]
        low = [refs.pop(0) for _ in range(micro)]
        up = [refs.pop(0) for _ in range(micro)]
        info = refs.pop(0)
        outs = [refs.pop(0) for _ in range(parts)]
        left_full, right_full, l_sem, r_sem = refs
        section = info[parts]
        waits = []
        for batch in range(micro):
            span = pl.ds(batch * rows, rows)
            columns = pl.ds(first_column, breadth)
            waits.append(
                start_chosen(
                    section,
                    low[batch].at[:, columns],
                    up[batch].at[:, columns],
                    right_full.at[span],
                    r_sem.at[batch],
                )
            )
        loads = []
        for part in range(parts):
            for batch in range(micro):
                start = pl.multiple_of(info[part] * quarter + first_row, 128)
                copy = pltpu.make_async_copy(
                    left[batch].at[:, pl.ds(start, height)],
                    left_full.at[part, pl.ds(batch * rows, rows)],
                    l_sem.at[part, batch],
                )
                copy.start()
                loads.append(copy)
        wait_all(waits)
        for part in range(parts):
            wait_all(loads[part * micro : (part + 1) * micro])
            outs[part][...] = contract(left_full[part], right_full[...], 0, 0).astype(BF16)

    return call(
        body,
        name,
        list(kept) + list(lowers) + list(uppers) + [meta],
        [ANY] * (3 * micro) + [SMEM],
        [((height, breadth), BF16)] * parts,
        [
            pltpu.VMEM((parts, micro * rows, height), BF16),
            pltpu.VMEM((micro * rows, breadth), BF16),
            pltpu.SemaphoreType.DMA((parts, micro)),
            pltpu.SemaphoreType.DMA((micro,)),
        ],
        2 * parts * micro * rows * height * breadth,
    )


def feed_gradient(kept, lowers, uppers, meta, parts, quarter, rows_of, count, length):
    micro = len(kept)
    first_row, height = rows_of
    rows = kept[0].shape[0]
    space = padded(length)
    width = lowers[0].shape[-1]
    base = length // 16 * 16

    def body(*refs):
        refs = list(refs)
        left = [refs.pop(0) for _ in range(micro)]
        low = [refs.pop(0) for _ in range(micro)]
        up = [refs.pop(0) for _ in range(micro)]
        info = refs.pop(0)
        outs = [refs.pop(0) for _ in range(parts)]
        left_full, taken, right_full, l_sem, r_sem = refs
        section = info[parts]
        waits = [
            start_chosen(section, low[batch], up[batch], taken.at[batch], r_sem.at[batch])
            for batch in range(micro)
        ]
        loads = []
        for part in range(parts):
            for batch in range(micro):
                start = pl.multiple_of(info[part] * quarter + first_row, 128)
                copy = pltpu.make_async_copy(
                    left[batch].at[:, pl.ds(start, height)],
                    left_full.at[part, pl.ds(batch * rows, rows)],
                    l_sem.at[part, batch],
                )
                copy.start()
                loads.append(copy)
        for batch in range(micro):
            waits[batch].wait()
            for image in range(count):
                start = batch * rows + image * space
                alive = jnp.where(info[parts + 1 + batch * count + image] > 0, 1.0, 0.0)
                right_full[pl.ds(start + base, space - base)] = jnp.zeros((space - base, width), BF16)
                right_full[pl.ds(start, length)] = (
                    taken[batch, image].astype(F32) * alive
                ).astype(BF16)
        for part in range(parts):
            wait_all(loads[part * micro : (part + 1) * micro])
            outs[part][...] = contract(left_full[part], right_full[...], 0, 0).astype(BF16)

    return call(
        body,
        "reduce_gradient",
        list(kept) + list(lowers) + list(uppers) + [meta],
        [ANY] * (3 * micro) + [SMEM],
        [((height, width), BF16)] * parts,
        [
            pltpu.VMEM((parts, micro * rows, height), BF16),
            pltpu.VMEM((micro, count, length, width), BF16),
            pltpu.VMEM((micro * rows, width), BF16),
            pltpu.SemaphoreType.DMA((parts, micro)),
            pltpu.SemaphoreType.DMA((micro,)),
        ],
        2 * parts * micro * rows * height * width,
    )


def added(*values):
    total = values[0].astype(F32)
    for value in values[1:]:
        total = total + value.astype(F32)
    return total.astype(values[0].dtype)


class FourByFour:
    parts = 4

    def __init__(self):
        self.group = lax.axis_index("group")
        self.place = lax.axis_index("replica")
        self.order = [self.group ^ part for part in range(4)]

    def core(self, block):
        return lax.ppermute(block, "group", [(i, i ^ 1) for i in range(4)])

    def across(self, block):
        return lax.ppermute(block, "group", [(i, i ^ 2) for i in range(4)])

    def gather(self, block):
        sibling = self.core(block)
        far = self.across(block)
        return [block, sibling, far, self.core(far)]

    def line(self, block, routes):
        pairs = [
            (group * 4 + source, group * 4 + target)
            for group in range(4)
            for source, target in routes[group % 2]
        ]
        return lax.ppermute(block, ("group", "replica"), pairs)

    def total(self, pieces):
        own, sibling, far, far_sibling = pieces
        sibling = self.core(sibling)
        far = self.across(added(far, self.core(far_sibling)))
        mine = added(own, sibling, far)
        inward = self.line(mine, ([(0, 1), (3, 2)], [(0, 1), (3, 2)]))
        joined = added(mine, inward)
        crossing = self.line(joined, ([(2, 1)], [(1, 2)]))
        summed = added(mine, inward, crossing)
        near = self.line(summed, ([(1, 0)], [(2, 3)]))
        inner = self.line(summed, ([(1, 2)], [(2, 1)]))
        outer = self.line(inner, ([(2, 3)], [(1, 0)]))
        odd = self.group % 2
        distance = jnp.where(odd == 0, self.place, 3 - self.place)
        return jnp.where(
            distance == 1,
            summed,
            jnp.where(distance == 0, near, jnp.where(distance == 2, inner, outer)),
        ).astype(F32)


class General:
    def __init__(self):
        self.parts = lax.axis_size("group")
        self.order = [jnp.int32(part) for part in range(self.parts)]

    def gather(self, block):
        whole = lax.all_gather(block, "group", axis=0)
        return [whole[part] for part in range(self.parts)]

    def total(self, pieces):
        mine = lax.psum_scatter(jnp.stack(pieces), "group", scatter_dimension=0)
        return lax.psum(mine, "replica").astype(F32)


def shifted(block, distance):
    devices = range(lax.axis_size("section"))
    route = [(i - distance, i) for i in devices if i - distance in devices]
    return lax.ppermute(block, "section", route)


def in_order(pieces, order):
    place = jnp.stack(order)
    stacked = []
    for block in range(len(pieces)):
        chosen = pieces[0]
        for part in range(1, len(pieces)):
            chosen = jnp.where(place[part] == block, pieces[part], chosen)
        stacked.append(chosen)
    return jnp.stack(stacked)


def out_of_order(blocks, order):
    return [lax.dynamic_index_in_dim(blocks, place, 0, keepdims=False) for place in order]


def per_device(
    images,
    cotangent,
    counts,
    qkv_weight,
    out_weight,
    expand_weight,
    reduce_weight,
    norm_gains,
    biases,
    expand_bias,
):
    micro, slots, length, width = images.shape
    section = lax.axis_index("section")
    first = section == 0
    sizes = (lax.axis_size("group"), lax.axis_size("replica"))
    net = FourByFour() if sizes == (4, 4) else General()
    parts = net.parts
    share = width // parts
    small = jnp.concatenate(
        [norm_gains[0], biases[0], expand_bias[0].reshape(-1, share)]
    )
    vectors = in_order(net.gather(small), net.order)
    qkv = net.gather(qkv_weight[0])
    out = net.gather(out_weight[0])
    expand = net.gather(expand_weight[0])
    reduce = net.gather(reduce_weight[0])
    top = vectors[:, :8].transpose(1, 0, 2).reshape(8, width)
    bottom = vectors[:, 8:].reshape(-1, width)
    params = jnp.concatenate([top, bottom]).astype(F32)
    slot = jnp.arange(slots, dtype=jnp.int32)
    alive = [(slot < counts[batch, 0]).astype(jnp.int32) for batch in range(micro)]
    head = jnp.stack(net.order + [section]).astype(jnp.int32)

    def meta(*batches):
        return jnp.concatenate([head] + [alive[batch] for batch in batches])

    batches = tuple(range(micro))
    flat = images.reshape((micro * slots, length, width))
    mixed = attention_forward(flat, flat, qkv, params, meta(*batches), False)[0]
    middle, active = hidden_forward(flat, flat, mixed, out, expand, params, meta(*batches), False)
    early = output_forward(
        middle, active, reduce, params, meta(*batches), micro * slots, length
    ).reshape(images.shape)
    incoming = [shifted(early[batch], 1) for batch in batches]
    kept = []
    late = []
    for batch in batches:
        low, up = images[batch], incoming[batch]
        norm, packed, mixed, logs = attention_forward(low, up, qkv, params, meta(batch), True)
        middle, active, second, slope = hidden_forward(
            low, up, mixed, out, expand, params, meta(batch), True
        )
        result = output_forward(middle, active, reduce, params, meta(batch), slots, length)
        late.append(result)
        kept.append((low, up, norm, packed, mixed, logs, middle, active, second, slope))
    section_outputs = jnp.stack(late)[None]

    returning = None
    upstreams, hiddens, mids, branches, grads, sent = [], [], [], [], [], []
    sums_a, sums_b, sums_c = [], [], []
    weights = [None] * 4
    for tick in range(micro + 1):
        low_batch, up_batch = max(tick - 1, 0), min(tick, micro - 1)
        upstream = cotangent[up_batch]
        if returning is not None:
            upstream = jnp.where(first, returning, upstream)
        upstreams.append(upstream)
        if tick == micro:
            left = [kept[batch][7] for batch in batches]
            quarter = left[0].shape[1] // parts
            step = quarter // 2
            weights[3] = [
                net.total(
                    feed_gradient(
                        left, upstreams[1:], upstreams[:-1], meta(*batches), parts, quarter,
                        (index * step, step), slots, length,
                    )
                )
                for index in range(2)
            ]
        low, up = kept[low_batch], kept[up_batch]
        chosen = jnp.where(first, alive[low_batch], alive[up_batch])
        info = jnp.concatenate([head, chosen])
        hidden, mid, branch, some, more = hidden_backward(
            upstream, (low[9], low[6]), (up[9], up[6]), reduce, expand, params, info
        )
        hiddens.append(hidden)
        branches.append(branch)
        sums_a.append(some)
        sums_b.append(more)
        if tick == micro:
            left = [kept[batch][8] for batch in batches]
            step = hidden.shape[1] // 2
            weights[2] = [
                net.total(
                    weight_gradient(
                        left, hiddens[1:], hiddens[:-1], meta(*batches), parts, share,
                        (0, share), (index * step, step), "expand_gradient",
                    )
                )
                for index in range(2)
            ]
            left = [kept[batch][4] for batch in batches]
            weights[1] = [
                net.total(
                    weight_gradient(
                        left, branches[1:], branches[:-1], meta(*batches), parts, share,
                        (0, share), (0, width), "project_gradient",
                    )
                )
            ]
        lower = kept[low_batch][0]
        upper = kept[up_batch][1]
        result, grad, some = attention_backward(
            branch, mid, lower, upper, low[3:6], up[3:6], out, qkv, params, info
        )
        grads.append(grad)
        sums_c.append(some)
        sent.append(result)
        if tick < micro:
            returning = shifted(result, -1)
    left = [kept[batch][2] for batch in batches]
    step = 3 * width // 2
    weights[0] = [
        net.total(
            weight_gradient(
                left, grads[1:], grads[:-1], meta(*batches), parts, share,
                (0, share), (index * step, step), "qkv_gradient",
            )
        )
        for index in range(2)
    ]
    input_grads = jnp.stack(
        [jnp.where(first, sent[batch + 1], sent[batch]) for batch in batches]
    )[None]

    def over_batches(values):
        return sum(jnp.where(first, values[batch + 1], values[batch]) for batch in batches)

    some, more, rest = over_batches(sums_a), over_batches(sums_b), over_batches(sums_c)
    rows = jnp.concatenate(
        [rest[0:1], some[0:1], rest[1:2], some[1:2], rest[2:4], some[2:4]]
    )
    rows = rows.reshape(8, parts, share).transpose(1, 0, 2)
    rows = jnp.concatenate([rows, more.reshape(parts, -1, share)], axis=1)
    vector = net.total(out_of_order(rows, net.order))
    return (
        section_outputs,
        input_grads,
        jnp.concatenate(weights[0], axis=1)[None],
        jnp.concatenate(weights[1], axis=1)[None],
        jnp.concatenate(weights[2], axis=1)[None],
        jnp.concatenate(weights[3], axis=0)[None],
        vector[None, 0:2],
        vector[None, 2:8],
        vector[8:].reshape(1, -1),
    )


def solution(mesh):
    placed = (
        P(None, ("group", "replica"), None, None),
        P(None, ("group", "replica"), None, None),
        P(None, ("group", "replica")),
        P("section", "group", None),
        P("section", "group", None),
        P("section", "group", None),
        P("section", "group", None),
        P("section", None, "group"),
        P("section", None, "group"),
        P("section", "group"),
    )
    return jax.shard_map(
        per_device,
        mesh=mesh,
        in_specs=placed,
        out_specs=(
            P("section", None, ("group", "replica"), None, None),
            P("section", None, ("group", "replica"), None, None),
            P("section", "group", None),
            P("section", "group", None),
            P("section", "group", None),
            P("section", "group", None),
            P("section", None, "group"),
            P("section", None, "group"),
            P("section", "group"),
        ),
        check_vma=False,
    )
```

```python
from functools import partial

import jax
import jax.numpy as jnp
from jax import lax
from jax.experimental import pallas as pl
from jax.experimental.pallas import tpu as pltpu
from jax.sharding import PartitionSpec as P

HEADS = 16
EPSILON = 1e-06
NEGATIVE = -1e30
F32 = jnp.float32
BF16 = jnp.bfloat16
VMEM_LIMIT = 58 * 2**20
ROOT_HALF = 0.7071067811865476
ROOT_TAU = 0.3989422804014327
ANY = pl.BlockSpec(memory_space=pl.ANY)
VMEM = pl.BlockSpec(memory_space=pltpu.VMEM)
SMEM = pl.BlockSpec(memory_space=pltpu.SMEM)
COST = 64
SEND_FIRST = {4: (3, 1, 2, 0)}
GAIN0, GAIN1, SHIFT0, SHIFT1, QUERY, VALUE, OUT, FEED, EXPAND = range(9)


def padded(length):
    return -(-length // 16) * 16


def contract(left, right, left_dim, right_dim):
    return lax.dot_general(
        left, right, (((left_dim,), (right_dim,)), ((), ())), preferred_element_type=F32
    )


def standardized(values):
    center = values - jnp.mean(values, axis=-1, keepdims=True)
    spread = jnp.mean(center * center, axis=-1, keepdims=True)
    scale = lax.rsqrt(spread + EPSILON)
    return center * scale, scale


def norm_pull(grad, gain, unit, scale):
    scaled = grad * gain
    mean = jnp.mean(scaled, axis=-1, keepdims=True)
    along = jnp.mean(scaled * unit, axis=-1, keepdims=True)
    return scale * (scaled - mean - unit * along)


def call(body, name, operands, specs, outs, scratch, flops):
    moved = sum(o.size * o.dtype.itemsize for o in operands)
    out_shape = [jax.ShapeDtypeStruct(shape, dtype) for shape, dtype in outs]
    moved += sum(o.size * o.dtype.itemsize for o in out_shape)
    return pl.pallas_call(
        body,
        out_shape=out_shape,
        in_specs=specs,
        out_specs=[VMEM] * len(outs),
        scratch_shapes=scratch,
        compiler_params=pltpu.CompilerParams(vmem_limit_bytes=VMEM_LIMIT),
        cost_estimate=pl.CostEstimate(flops=flops // COST, bytes_accessed=moved // COST, transcendentals=0),
        name=name,
    )(*operands)


def start_pieces(pieces, order_ref, target, sems, slot, columns):
    rows = pieces[0].shape[0]
    copies = []
    for index, piece in enumerate(pieces):
        where = pl.multiple_of(order_ref[index] * rows, rows)
        copy = pltpu.make_async_copy(
            piece.at[:, columns], target.at[pl.ds(where, rows), columns], sems.at[slot, index]
        )
        copy.start()
        copies.append(copy)
    return copies


def wait_all(copies):
    for copy in copies:
        copy.wait()


def start_chosen(section, lower, upper, target, sem):
    if lower is upper:
        copy = pltpu.make_async_copy(lower, target, sem)
        copy.start()
        return copy

    @pl.when(section == 0)
    def _():
        pltpu.make_async_copy(lower, target, sem).start()

    @pl.when(section != 0)
    def _():
        pltpu.make_async_copy(upper, target, sem).start()

    return pltpu.make_async_copy(lower, target, sem)


def eights(values):
    return jnp.sum(values.reshape(-1, 8, values.shape[-1]), axis=0)


def attention_stage(x, vec, norm, packed, mixed, logs, columns, full, loads, count, length):
    rows, width = x.shape
    space = rows // count
    head = width // HEADS
    pair = 2 * head
    scale = head**-0.5
    gain, shift = vec[GAIN0 : GAIN0 + 1], vec[SHIFT0 : SHIFT0 + 1]

    def step(here):
        unit, _ = standardized(x[here].astype(F32))
        norm[here] = (unit * gain + shift).astype(BF16)

    step(pl.ds(0, rows))
    for block in range(3):
        wait_all(loads[block])
        done = contract(norm[...], full[:, block * width : (block + 1) * width], 1, 0)
        if block != 1:
            bias = QUERY if block == 0 else VALUE
            done = done + vec[bias : bias + 1]
        packed[:, block * width : (block + 1) * width] = done.astype(BF16)
    lane = lax.broadcasted_iota(jnp.int32, (space, pair), 1)
    left = lane < head
    live = lax.broadcasted_iota(jnp.int32, (space, pair), 0) < length
    key_live = lax.broadcasted_iota(jnp.int32, (space, space), 1) < length
    columns[...] = jnp.zeros_like(columns)

    def heads(index, carry):
        for image in range(count):
            span = pl.ds(image * space, space)

            def part(block):
                offset = pl.multiple_of(block * width + index * pair, pair)
                return packed[span, pl.ds(offset, pair)]

            query, key, value = part(0).astype(F32) * scale, part(1), part(2).astype(F32)
            found = []
            tops = []
            for side in range(2):
                mine = left if side == 0 else ~left
                asked = jnp.where(mine, query, 0.0).astype(BF16)
                held = jnp.where(live, jnp.where(mine, value, 1.0), 0.0).astype(BF16)
                scores = jnp.where(key_live, contract(asked, key, 1, 1), NEGATIVE)
                top = jnp.max(scores, axis=-1, keepdims=True)
                raised = jnp.exp(scores - top).astype(BF16)
                found.append(contract(raised, held, 1, 0))
                tops.append(top)
            inside = jnp.where(left, found[0], found[1])
            total = jnp.where(left, found[1], found[0])
            turned = pltpu.roll(total, head, 1)
            offset = pl.multiple_of(index * pair, pair)
            mixed[span, pl.ds(offset, pair)] = (inside / turned).astype(BF16)
            logged = jnp.log(turned)
            first = tops[0] + logged[:, 0:1]
            second = tops[1] + logged[:, head : head + 1]
            known = columns[image]
            known = jnp.where(lane == 2 * index, first, known)
            columns[image] = jnp.where(lane == 2 * index + 1, second, known)
        return carry

    lax.fori_loop(0, HEADS // 2, heads, 0)
    for image in range(count):
        logs[image] = columns[image].T[0:HEADS]


def hidden_stage(x, vec, mixed, middle, active, second, slope, full_out, full, first_load, loads):
    rows, width = x.shape
    wait_all(first_load)
    gain, shift, bias = vec[GAIN1 : GAIN1 + 1], vec[SHIFT1 : SHIFT1 + 1], vec[OUT : OUT + 1]
    middle[...] = contract(mixed[...], full_out[...], 1, 0)

    def step(here):
        total = middle[here] + x[here].astype(F32) + bias
        middle[here] = total
        unit, _ = standardized(total)
        second[here] = (unit * gain + shift).astype(BF16)

    step(pl.ds(0, rows))
    for block, load in enumerate(loads):
        wait_all(load)
        part = slice(block * width, (block + 1) * width)
        value = contract(second[...], full[:, part], 1, 0) + vec[EXPAND + block - 0 : EXPAND + block + 1]
        share = 0.5 + 0.5 * lax.erf(value * ROOT_HALF)
        active[:, part] = (value * share).astype(BF16)
        density = ROOT_TAU * jnp.exp(-0.5 * value * value)
        slope[:, part] = (share + value * density).astype(BF16)


def forward(lower, upper, mixed_in, qkv, out, expand, params, meta, count, length):
    rows, width = lower.shape
    space = rows // count
    pair = 2 * width // HEADS
    attend, feed = qkv is not None, expand is not None
    parts = len(qkv if attend else expand)
    inner = expand[0].shape[1] if feed else 0
    blocks = inner // width
    same = lower is upper

    def body(*refs):
        refs = list(refs)
        low = refs.pop(0)
        up = low if same else refs.pop(0)
        if not attend:
            arrived = refs.pop(0)
        lists = [[refs.pop(0) for _ in range(parts)] for _ in range(attend + 2 * feed)]
        vec, info = refs.pop(0), refs.pop(0)
        if attend:
            norm, packed, mixed, logs = (refs.pop(0) for _ in range(4))
        if feed:
            middle, active, second, slope = (refs.pop(0) for _ in range(4))
        x, x_sem = refs.pop(0), refs.pop(0)
        section = info[parts]
        take = start_chosen(section, low, up, x, x_sem.at[0])
        if attend:
            columns, full, a_sem = (refs.pop(0) for _ in range(3))
            weight = lists.pop(0)
            loads = [
                start_pieces(weight, info, full, a_sem, block, pl.ds(block * width, width))
                for block in range(3)
            ]
        if feed:
            full_out, full_in, o_sem, w_sem = (refs.pop(0) for _ in range(4))
            if not attend:
                mixed = refs.pop(0)
                extra = pltpu.make_async_copy(arrived, mixed, x_sem.at[1])
                extra.start()
            first_load = start_pieces(lists[0], info, full_out, o_sem, 0, pl.ds(0, width))
            inner_loads = [
                start_pieces(lists[1], info, full_in, w_sem, block, pl.ds(block * width, width))
                for block in range(blocks)
            ]
        take.wait()
        if attend:
            attention_stage(
                x, vec, norm, packed, mixed, logs, columns, full, loads, count, length
            )
        if feed:
            if not attend:
                extra.wait()
            hidden_stage(
                x, vec, mixed, middle, active, second, slope, full_out, full_in, first_load,
                inner_loads,
            )

    outs, inputs = [], [lower] if same else [lower, upper]
    scratch = [pltpu.VMEM((rows, width), BF16), pltpu.SemaphoreType.DMA((2,))]
    flops = 0
    if attend:
        outs += [
            ((rows, width), BF16),
            ((rows, 3 * width), BF16),
            ((rows, width), BF16),
            ((count, HEADS, space), F32),
        ]
        scratch += [
            pltpu.VMEM((count, space, pair), F32),
            pltpu.VMEM((width, 3 * width), BF16),
            pltpu.SemaphoreType.DMA((3, parts)),
        ]
        flops += 2 * rows * width * (3 * width + 2 * space)
    else:
        inputs += [mixed_in]
    if feed:
        outs += [
            ((rows, width), F32),
            ((rows, inner), BF16),
            ((rows, width), BF16),
            ((rows, inner), BF16),
        ]
        scratch += [
            pltpu.VMEM((width, width), BF16),
            pltpu.VMEM((width, inner), BF16),
            pltpu.SemaphoreType.DMA((1, parts)),
            pltpu.SemaphoreType.DMA((blocks, parts)),
        ]
        if not attend:
            scratch += [pltpu.VMEM((rows, width), BF16)]
        flops += 2 * rows * width * (width + inner)
    weights = (list(qkv) if attend else []) + (list(out) + list(expand) if feed else [])
    return call(
        body,
        "forward" + "_attend" * attend + "_feed" * feed,
        inputs + weights + [params, meta],
        [ANY] * (len(inputs) + len(weights)) + [VMEM, SMEM],
        outs,
        scratch,
        flops,
    )


def output_forward(middle, active, pieces, params, meta, count):
    rows, width = middle.shape
    inner = active.shape[1]
    space = rows // count
    parts = len(pieces)
    blocks = 2
    part_width = width // blocks

    def body(*refs):
        refs = list(refs)
        mid_in, act_in = refs.pop(0), refs.pop(0)
        reduce = [refs.pop(0) for _ in range(parts)]
        vec, info, result, mid, act, full, x_sem, w_sem = refs
        copies = [
            pltpu.make_async_copy(act_in, act, x_sem.at[0]),
            pltpu.make_async_copy(mid_in, mid, x_sem.at[1]),
        ]
        copies[0].start()
        loads = [
            start_pieces(reduce, info, full, w_sem, block, pl.ds(block * part_width, part_width))
            for block in range(blocks)
        ]
        copies[1].start()
        copies[0].wait()
        for block in range(blocks):
            wait_all(loads[block])
            if block == 0:
                copies[1].wait()
            part = slice(block * part_width, (block + 1) * part_width)
            value = contract(act[...], full[:, part], 1, 0) + mid[:, part] + vec[FEED : FEED + 1, part]
            for image in range(count):
                alive = jnp.where(info[parts + 1 + image] > 0, 1.0, 0.0)
                here = slice(image * space, (image + 1) * space)
                result[here, part] = (value[here] * alive).astype(BF16)

    return call(
        body,
        "output_forward",
        [middle, active] + list(pieces) + [params, meta],
        [ANY] * (2 + parts) + [VMEM, SMEM],
        [((rows, width), BF16)],
        [
            pltpu.VMEM((rows, width), F32),
            pltpu.VMEM((rows, inner), BF16),
            pltpu.VMEM((inner, width), BF16),
            pltpu.SemaphoreType.DMA((2,)),
            pltpu.SemaphoreType.DMA((blocks, parts)),
        ],
        2 * rows * width * inner,
    )[0]


def hidden_back_stage(
    grad, vec, info, feed, slope, middle, hidden, second, mid_grad, branch, sums, inner_sums, full_out,
    full, deep, first_load, load, for_slope, for_middle, tallies, count, parts,
):
    rows, width = grad.shape
    space = rows // count
    half = width // 2
    for image in range(count):
        alive = jnp.where(info[parts + 1 + image] > 0, 1.0, 0.0)
        here = slice(image * space, (image + 1) * space)
        feed[here] = (grad[here].astype(F32) * alive).astype(BF16)
    for_slope.wait()
    for index in range(parts):
        wait_all(first_load[index])
        where = pl.multiple_of(info[index] * deep, deep)
        value = contract(feed[...], full_out[pl.ds(where, deep)], 1, 1)
        value = (value * slope[:, pl.ds(where, deep)].astype(F32)).astype(BF16)
        hidden[:, pl.ds(where, deep)] = value
        inner_sums[:, pl.ds(where, deep)] = jnp.sum(value.astype(F32), axis=0, keepdims=True)
    wait_all(load)
    for block in range(2):
        second[:, block * half : (block + 1) * half] = contract(
            hidden[...], full[block * half : (block + 1) * half], 1, 1
        )
    for_middle.wait()
    gain = vec[GAIN1 : GAIN1 + 1]
    tallies[...] = jnp.zeros_like(tallies)

    def step(here):
        unit, scale = standardized(middle[here])
        down = second[here]
        top = feed[here].astype(F32)
        total = top + norm_pull(down, gain, unit, scale)
        low = total.astype(BF16)
        mid_grad[here] = total
        branch[here] = low
        tallies[0] += eights(down * unit)
        tallies[1] += eights(down)
        tallies[2] += eights(low.astype(F32))
        tallies[3] += eights(top)

    step(pl.ds(0, rows))
    for index in range(4):
        sums[index : index + 1] = jnp.sum(tallies[index], axis=0, keepdims=True)


def attention_back_stage(
    x, vec, branch, mid_grad, packed, mixed, logs, grads, result, sums, down, normal, stage, full_out,
    full, first_load, load, takes, tallies, count, length,
):
    rows, width = x.shape
    space = rows // count
    head = width // HEADS
    pair = 2 * head
    scale = head**-0.5
    half = width // 2
    wait_all(first_load)
    down[...] = contract(branch[...], full_out[...], 1, 1).astype(BF16)
    wait_all(takes)
    owner = lax.shift_right_logical(
        lax.broadcasted_iota(jnp.int32, (HEADS, width), 1), head.bit_length() - 1
    )
    chosen = jnp.where(
        owner == lax.broadcasted_iota(jnp.int32, (HEADS, width), 0), 1.0, 0.0
    ).astype(BF16)
    left = lax.broadcasted_iota(jnp.int32, (space, pair), 1) < head
    live = lax.broadcasted_iota(jnp.int32, (space, pair), 0) < length
    key_live = lax.broadcasted_iota(jnp.int32, (space, space), 0) < length
    for image in range(count):
        span = pl.ds(image * space, space)
        product = down[span].astype(F32) * mixed[span].astype(F32)
        coarse = product.astype(BF16)
        fine = (product - coarse.astype(F32)).astype(BF16)
        stage[image, :, 0:space] = contract(chosen, coarse, 1, 1) + contract(chosen, fine, 1, 1)

    def heads(index, carry):
        for image in range(count):
            span = pl.ds(image * space, space)

            def part(block):
                offset = pl.multiple_of(block * width + index * pair, pair)
                return packed[span, pl.ds(offset, pair)]

            query, key, value = part(0), part(1), part(2)
            wide = key.astype(F32) * scale
            value = value.astype(F32)
            arrived = down[span, pl.ds(pl.multiple_of(index * pair, pair), pair)]
            found = []
            for side in range(2):
                mine = left if side == 0 else ~left
                log = logs[image, pl.ds(2 * index + side, 1), :]
                dot = stage[image, pl.ds(2 * index + side, 1), 0:space]
                scores = contract(jnp.where(mine, wide, 0.0).astype(BF16), query, 1, 1)
                chance = jnp.exp(jnp.where(key_live, scores - log, NEGATIVE))
                back = contract(jnp.where(mine, value, 0.0).astype(BF16), arrived, 1, 1)
                change = (chance * (back - dot)).astype(BF16)
                found.append(
                    (
                        contract(change, key, 0, 0),
                        contract(change, query, 1, 0),
                        contract(chance.astype(BF16), arrived, 1, 0),
                    )
                )
            for block, factor in enumerate((scale, scale, 1.0)):
                total = jnp.where(left, found[0][block], found[1][block]) * factor
                offset = pl.multiple_of(block * width + index * pair, pair)
                grads[span, pl.ds(offset, pair)] = jnp.where(live, total, 0.0).astype(BF16)
        return carry

    lax.fori_loop(0, HEADS // 2, heads, 0)
    wait_all(load)
    for block in range(2):
        normal[:, block * half : (block + 1) * half] = contract(
            grads[...], full[block * half : (block + 1) * half], 1, 1
        )
    gain = vec[GAIN0 : GAIN0 + 1]
    tallies[...] = jnp.zeros_like(tallies)

    def step(here):
        unit, rate = standardized(x[here].astype(F32))
        grad = normal[here]
        tallies[0] += eights(grad * unit)
        tallies[1] += eights(grad)
        result[here] = (mid_grad[here] + norm_pull(grad, gain, unit, rate)).astype(BF16)

    step(pl.ds(0, rows))
    for index in range(2):
        sums[index : index + 1] = jnp.sum(tallies[index], axis=0, keepdims=True)
    sums[2:3] = jnp.sum(grads[:, 0:width].astype(F32), axis=0, keepdims=True)
    sums[3:4] = jnp.sum(grads[:, 2 * width : 3 * width].astype(F32), axis=0, keepdims=True)


def backward(
    start, lower, upper, kept_low, kept_up, reduce, expand, out, qkv, params, meta, count, length
):
    feed, attend = reduce is not None, qkv is not None
    rows, width = start[0].shape
    space = rows // count
    pair = 2 * width // HEADS
    parts = len(reduce if feed else qkv)
    inner = expand[0].shape[1] if feed else 0
    deep = reduce[0].shape[0] if feed else 0
    both = feed and attend
    choices = []
    if feed:
        choices += [(kept_low[0], kept_up[0]), (kept_low[1], kept_up[1])]
        if start[0] is not start[1]:
            choices += [start]
    if attend:
        choices += [(kept_low[index], kept_up[index]) for index in (2, 3, 4)]
        choices += [(lower, upper)]
    plain = [start[0]] if feed and start[0] is start[1] else [] if feed else list(start)
    operands = []
    for low, up in choices:
        operands += [low] if low is up else [low, up]

    def body(*refs):
        refs = list(refs)
        firsts = [refs.pop(0) for _ in plain]
        pairs = []
        for low, up in choices:
            one = refs.pop(0)
            pairs.append((one, one if low is up else refs.pop(0)))
        lists = [[refs.pop(0) for _ in range(parts)] for _ in range(2 * feed + 2 * attend)]
        vec, info = refs.pop(0), refs.pop(0)
        section = info[parts]
        if feed:
            hidden, branch, feed_sums, inner_sums = (refs.pop(0) for _ in range(4))
            mid_grad = None if both else refs.pop(0)
        if attend:
            result, grads, sums = (refs.pop(0) for _ in range(3))
        tallies, x_sem = refs.pop(0), refs.pop(0)
        if feed:
            grad, keep, slope, middle, second, full_out, full, o_sem, w_sem = (
                refs.pop(0) for _ in range(9)
            )
            if both:
                mid_grad = refs.pop(0)
            begin = pairs.pop(2) if start[0] is not start[1] else (firsts[0], firsts[0])
            take = start_chosen(section, *begin, grad, x_sem.at[0])
            for_slope = start_chosen(section, *pairs.pop(0), slope, x_sem.at[1])
            first_load = [
                start_pieces(
                    [piece], Shifted(info, index), full_out, o_sem.at[pl.ds(index, 1)], 0,
                    pl.ds(0, width),
                )
                for index, piece in enumerate(lists.pop(0))
            ]
            for_middle = start_chosen(section, *pairs.pop(0), middle, x_sem.at[2])
            load = start_pieces(lists.pop(0), info, full, w_sem, 0, pl.ds(0, inner))
        if attend:
            x, packed, mixed, logs, down, normal, stage, full_o, full_q, p_sem, q_sem = (
                refs.pop(0) for _ in range(11)
            )
            if not feed:
                branch, mid_grad = refs.pop(0), refs.pop(0)
                givens = [
                    pltpu.make_async_copy(source, target, x_sem.at[index])
                    for index, (source, target) in enumerate(zip(firsts, (branch, mid_grad)))
                ]
                for given in givens:
                    given.start()
            project_load = start_pieces(lists.pop(0), info, full_o, p_sem, 0, pl.ds(0, width))
            takes = [
                start_chosen(section, *pairs[index], target, x_sem.at[3 + index])
                for index, target in ((1, mixed), (0, packed), (2, logs), (3, x))
            ]
            last_load = start_pieces(lists.pop(0), info, full_q, q_sem, 0, pl.ds(0, 3 * width))
            if not feed:
                wait_all(givens)
        if feed:
            take.wait()
            hidden_back_stage(
                grad, vec, info, keep, slope, middle, hidden, second, mid_grad, branch, feed_sums,
                inner_sums, full_out, full, deep, first_load, load, for_slope, for_middle, tallies,
                count, parts,
            )
        if attend:
            attention_back_stage(
                x, vec, branch, mid_grad, packed, mixed, logs, grads, result, sums, down, normal,
                stage, full_o, full_q, project_load, last_load, takes, tallies, count, length,
            )

    outs = []
    scratch = [pltpu.VMEM((4, 8, width), F32), pltpu.SemaphoreType.DMA((7,))]
    flops = 0
    if feed:
        outs += [
            ((rows, inner), BF16),
            ((rows, width), BF16),
            ((8, width), F32),
            ((1, inner), F32),
        ]
        if not both:
            outs += [((rows, width), F32)]
        scratch += [
            pltpu.VMEM((rows, width), BF16),
            pltpu.VMEM((rows, width), BF16),
            pltpu.VMEM((rows, inner), BF16),
            pltpu.VMEM((rows, width), F32),
            pltpu.VMEM((rows, width), F32),
            pltpu.VMEM((inner, width), BF16),
            pltpu.VMEM((width, inner), BF16),
            pltpu.SemaphoreType.DMA((parts, 1)),
            pltpu.SemaphoreType.DMA((1, parts)),
        ]
        if both:
            scratch += [pltpu.VMEM((rows, width), F32)]
        flops += 4 * rows * width * inner
    if attend:
        outs += [((rows, width), BF16), ((rows, 3 * width), BF16), ((8, width), F32)]
        scratch += [
            pltpu.VMEM((rows, width), BF16),
            pltpu.VMEM((rows, 3 * width), BF16),
            pltpu.VMEM((rows, width), BF16),
            pltpu.VMEM((count, HEADS, space), F32),
            pltpu.VMEM((rows, width), BF16),
            pltpu.VMEM((rows, width), F32),
            pltpu.VMEM((count, HEADS, 2 * pair), F32),
            pltpu.VMEM((width, width), BF16),
            pltpu.VMEM((width, 3 * width), BF16),
            pltpu.SemaphoreType.DMA((1, parts)),
            pltpu.SemaphoreType.DMA((1, parts)),
        ]
        if not feed:
            scratch += [pltpu.VMEM((rows, width), BF16), pltpu.VMEM((rows, width), F32)]
        flops += 2 * rows * width * (4 * width + 5 * space)
    weights = (list(reduce) + list(expand) if feed else []) + (
        list(out) + list(qkv) if attend else []
    )
    return call(
        body,
        "backward" + "_feed" * feed + "_attend" * attend,
        plain + operands + weights + [params, meta],
        [ANY] * (len(plain) + len(operands) + len(weights)) + [VMEM, SMEM],
        outs,
        scratch,
        flops,
    )


class Shifted:
    def __init__(self, ref, index):
        self.ref, self.index = ref, index

    def __getitem__(self, index):
        return self.ref[self.index + index]


def weight_gradient(left_pairs, pairs, meta, parts, quarter, rows_of, columns_of, name, count=0):
    micro = len(pairs)
    first_row, height = rows_of
    first_column, breadth = columns_of
    rows = pairs[0][0].shape[0]

    def body(*refs):
        refs = list(refs)
        left_low = [refs.pop(0) for _ in range(micro)]
        left_up = [refs.pop(0) for _ in range(micro)]
        low = [refs.pop(0) for _ in range(micro)]
        up = [refs.pop(0) for _ in range(micro)]
        info = refs.pop(0)
        outs = [refs.pop(0) for _ in range(2)]
        left_full, right_full, l_sem, r_sem = refs
        section = info[parts]
        waits = []
        for batch in range(micro):
            span = pl.ds(batch * rows, rows)
            columns = pl.ds(first_column, breadth)
            waits.append(
                start_chosen(
                    section,
                    low[batch].at[:, columns],
                    up[batch].at[:, columns],
                    right_full.at[span],
                    r_sem.at[batch],
                )
            )
        loads = []
        for part in range(parts):
            for batch in range(micro):
                start = pl.multiple_of(info[part] * quarter + first_row, 128)
                loads.append(
                    start_chosen(
                        section,
                        left_low[batch].at[:, pl.ds(start, height)],
                        left_up[batch].at[:, pl.ds(start, height)],
                        left_full.at[part, pl.ds(batch * rows, rows)],
                        l_sem.at[part, batch],
                    )
                )
        wait_all(waits)
        if count:
            space = rows // count
            for image in range(micro * count):
                alive = jnp.where(info[parts + 1 + image] > 0, 1.0, 0.0)
                here = slice(image * space, (image + 1) * space)
                right_full[here] = (right_full[here].astype(F32) * alive).astype(BF16)
        for part in SEND_FIRST[parts] if parts in SEND_FIRST else range(parts):
            wait_all(loads[part * micro : (part + 1) * micro])
            outs[part % 2][part // 2] = contract(left_full[part], right_full[...], 0, 0).astype(BF16)

    return call(
        body,
        name,
        [pair[side] for group in (left_pairs, pairs) for side in range(2) for pair in group] + [meta],
        [ANY] * (4 * micro) + [SMEM],
        [((parts // 2, height, breadth), BF16)] * 2,
        [
            pltpu.VMEM((parts, micro * rows, height), BF16),
            pltpu.VMEM((micro * rows, breadth), BF16),
            pltpu.SemaphoreType.DMA((parts, micro)),
            pltpu.SemaphoreType.DMA((micro,)),
        ],
        2 * parts * micro * rows * height * breadth,
    )


def after(value, *earlier):
    return lax.optimization_barrier((value,) + earlier)[0]


def added(*values):
    total = values[0].astype(F32)
    for value in values[1:]:
        total = total + value.astype(F32)
    return total.astype(values[0].dtype)


class FourByFour:
    parts = 4

    def __init__(self):
        self.group = lax.axis_index("group")
        self.place = lax.axis_index("replica")
        self.order = [self.group ^ part for part in range(4)]

    def core(self, block):
        return lax.ppermute(block, "group", [(i, i ^ 1) for i in range(4)])

    def across(self, block):
        return lax.ppermute(block, "group", [(i, i ^ 2) for i in range(4)])

    def gather(self, blocks):
        far, sibling = [], []
        for index, block in enumerate(blocks):
            far.append(self.across(after(block, far[index - 2]) if index > 1 else block))
            sibling.append(self.core(after(block, sibling[-1]) if index else block))

        def pieces(index, token):
            distant = far[index] if token is None else after(far[index], token)
            return [blocks[index], sibling[index], far[index], self.core(distant)]

        return [partial(pieces, index) for index in range(len(blocks))]

    def total(self, keep, send):
        got = self.core(send)
        token = yield
        far = after(keep[1], token)
        far = added(far, got[1])
        passed = self.across(far)
        token = yield far
        mine = added(after(keep[0], token), got[0], passed)
        inward = lax.ppermute(mine, "replica", [(0, 1), (3, 2)])
        token = yield mine
        joined = added(after(mine, token), inward)
        crossing = lax.ppermute(joined, "replica", [(1, 2), (2, 1)])
        token = yield joined
        summed = added(after(joined, token), crossing)
        outward = lax.ppermute(summed, "replica", [(1, 0), (2, 3)])
        token = yield summed
        inner = (self.place == 1) | (self.place == 2)
        yield jnp.where(inner, after(summed, token), outward).astype(F32)


class General:
    def __init__(self):
        self.parts = lax.axis_size("group")
        self.order = [jnp.int32(part) for part in range(self.parts)]

    def gather(self, blocks):
        found = []
        for block in blocks:
            whole = lax.all_gather(block, "group", axis=0)
            found.append([whole[part] for part in range(self.parts)])
        return [lambda token, pieces=pieces: pieces for pieces in found]

    def total(self, keep, send):
        yield
        mixed = jnp.stack([keep, send], axis=1)
        mixed = mixed.reshape((-1,) + keep.shape[1:])
        mine = lax.psum_scatter(mixed, "group", scatter_dimension=0)
        yield mine
        yield lax.psum(mine, "replica").astype(F32)


def shifted(block, distance):
    devices = range(lax.axis_size("section"))
    route = [(i - distance, i) for i in devices if i - distance in devices]
    return lax.ppermute(block, "section", route)


def in_order(pieces, order):
    place = jnp.stack(order)
    stacked = []
    for block in range(len(pieces)):
        chosen = pieces[0]
        for part in range(1, len(pieces)):
            chosen = jnp.where(place[part] == block, pieces[part], chosen)
        stacked.append(chosen)
    return jnp.stack(stacked)


class Sequence:
    def __init__(self, net):
        self.net, self.sums, self.results, self.token = net, {}, {}, jnp.zeros((8, 128), F32)

    def now(self, value):
        return after(value, self.token)

    def ran(self, value):
        self.token = value

    def add(self, name, keep, send):
        steps = self.net.total(keep, send)
        next(steps)
        self.sums[name] = steps

    def step(self, *names):
        for name in names:
            try:
                self.results[name] = self.token = self.sums[name].send(self.token)
            except StopIteration:
                continue

    def finish(self, name):
        while True:
            try:
                self.results[name] = self.sums[name].send(self.token)
            except StopIteration:
                return self.results[name]


def per_device(
    images,
    cotangent,
    counts,
    qkv_weight,
    out_weight,
    expand_weight,
    reduce_weight,
    norm_gains,
    biases,
    expand_bias,
):
    micro, slots, length, width = images.shape
    space = padded(length)
    section = lax.axis_index("section")
    first = section == 0
    sizes = (lax.axis_size("group"), lax.axis_size("replica"))
    net = FourByFour() if sizes == (4, 4) else General()
    parts = net.parts
    share = width // parts
    batches = tuple(range(micro))
    small = jnp.concatenate([norm_gains[0], biases[0], expand_bias[0].reshape(-1, share)])
    vectors, qkv, out, expand, reduce = net.gather(
        [small, qkv_weight[0], out_weight[0], expand_weight[0], reduce_weight[0]]
    )
    vectors = in_order(vectors(None), net.order)
    top = vectors[:, :8].transpose(1, 0, 2).reshape(8, width)
    bottom = vectors[:, 8:].reshape(-1, width)
    params = jnp.concatenate([top, bottom]).astype(F32)
    slot = jnp.arange(slots, dtype=jnp.int32)
    alive = [(slot < counts[batch, 0]).astype(jnp.int32) for batch in batches]
    head = jnp.stack(net.order + [section]).astype(jnp.int32)

    def meta(*values):
        return jnp.concatenate((head,) + values)

    def rows_of(array):
        full = jnp.pad(array, ((0, 0), (0, 0), (0, space - length), (0, 0)))
        return [full[batch].reshape(slots * space, width) for batch in batches]

    def images_of(array):
        return array.reshape(slots, space, width)[:, :length]

    inputs, targets = rows_of(images), rows_of(cotangent)
    infos = [meta(alive[batch]) for batch in batches]
    info = meta(*alive)

    qkv = qkv(params)
    attended = []
    for batch in batches:
        start = inputs[batch] if batch == 0 else after(inputs[batch], attended[-1][0])
        attended.append(
            forward(start, start, None, qkv, None, None, params, infos[batch], slots, length)
        )
    out = out(attended[-1][0])
    expand = expand(out[3])
    fed = []
    for batch in batches:
        start = inputs[batch] if batch == 0 else after(inputs[batch], fed[-1][0])
        fed.append(
            forward(start, start, attended[batch][2], None, out, expand, params, infos[batch], slots, length)
        )
    reduce = reduce(fed[-1][0])
    early, incoming = [], []
    for batch in batches:
        middle, active = fed[batch][:2]
        if batch:
            active = after(active, early[-1])
        early.append(output_forward(middle, active, reduce, params, infos[batch], slots))
        incoming.append(shifted(early[batch], 1))
    low = [attended[batch] + fed[batch] for batch in batches]

    def kept_of(values):
        norm, packed, mixed, logs, middle, active, second, slope = values
        return (slope, middle, packed, mixed, logs)

    up, results, grads, hiddens, branches = [], [], [], [], []
    sums_a, sums_b, sums_c, returning = [], [], [], []
    token = early[-1]
    for batch in batches:
        start = after(incoming[batch], token)
        up.append(
            forward(start, start, None, qkv, out, expand, params, infos[batch], slots, length)
        )
        if batch == 0:
            pair, sides = (targets[0], targets[0]), (up[0], up[0])
            lower, chosen = incoming[0], infos[0]
        else:
            pair, sides = (returning[batch - 1], targets[batch]), (low[batch - 1], up[batch])
            lower = inputs[batch - 1]
            chosen = meta(jnp.where(first, alive[batch - 1], alive[batch]))
        hidden, branch, some, more, result, grad, rest = backward(
            pair, lower, incoming[batch], kept_of(sides[0]), kept_of(sides[1]), reduce, expand, out,
            qkv, params, chosen, slots, length,
        )
        token = result
        hiddens.append(hidden)
        branches.append(branch)
        grads.append(grad)
        results.append(result)
        sums_a.append(some)
        sums_b.append(more)
        sums_c.append(rest)
        returning.append(shifted(result, -1))
    late = []
    for batch in batches:
        active = after(up[batch][5], token)
        late.append(output_forward(up[batch][4], active, reduce, params, infos[batch], slots))
        token = late[-1]

    last = micro - 1
    run = Sequence(net)
    run.ran(token)
    inner = expand[0].shape[1]
    names = ("norm", "packed", "mixed", "logs", "middle", "active", "second", "slope")

    def left_of(name):
        index = names.index(name)
        return [(low[batch][index], up[batch][index]) for batch in batches]

    def gradient(name, left, pairs, quarter, rows, columns, count=0):
        pairs = [(run.now(pairs[0][0]), pairs[0][1])] + pairs[1:]
        keep, send = weight_gradient(
            left, pairs, info, parts, quarter, rows, columns, name, count
        )
        run.ran(keep)
        run.add(name, keep, send)

    deep = inner // parts
    pairs = [(returning[batch], targets[batch]) for batch in batches]
    for index in range(2):
        step = deep // 2
        gradient(
            f"reduce{index}", left_of("active"), pairs, deep, (index * step, step), (0, width), slots
        )
    run.step("reduce0", "reduce1")
    start = run.now(returning[last])
    hidden, branch, some, more, mid = backward(
        (start, start), None, None, kept_of(low[last]), kept_of(low[last]), reduce, expand, None,
        None, params, infos[last], slots, length,
    )
    run.ran(branch)
    hiddens.append(hidden)
    branches.append(branch)
    sums_a.append(some)
    sums_b.append(more)
    run.step("reduce0")
    pairs = [(hiddens[batch + 1], hiddens[batch]) for batch in batches]
    for index in range(2):
        step = inner // 2
        gradient(
            f"expand{index}", left_of("second"), pairs, share, (0, share), (index * step, step)
        )
    run.step("expand0", "expand1", "reduce1", "reduce0")
    start = run.now(branch)
    result, grad, rest = backward(
        (start, mid), inputs[last], inputs[last], kept_of(low[last]), kept_of(low[last]), None, None,
        out, qkv, params, infos[last], slots, length,
    )
    run.ran(result)
    results.append(result)
    grads.append(grad)
    sums_c.append(rest)
    run.step("reduce0", "reduce1", "expand0")
    pairs = [(grads[batch + 1], grads[batch]) for batch in batches]
    for index in range(2):
        step = 3 * width // 2
        gradient(f"qkv{index}", left_of("norm"), pairs, share, (0, share), (index * step, step))
        if index == 0:
            run.step("expand0", "reduce1")
    run.step("qkv0", "qkv1", "expand1", "expand0")
    pairs = [(branches[batch + 1], branches[batch]) for batch in batches]
    gradient("project", left_of("mixed"), pairs, share, (0, share), (0, width))

    def over_batches(values):
        return sum(jnp.where(first, values[batch + 1], values[batch]) for batch in batches)

    some, more, rest = over_batches(sums_a), over_batches(sums_b), over_batches(sums_c)
    rows = jnp.concatenate([rest[0:1], some[0:1], rest[1:2], some[1:2], rest[2:4], some[2:4]])
    rows = rows.reshape(8, parts, share).transpose(1, 0, 2)
    rows = jnp.concatenate([rows, more.reshape(parts, -1, share)], axis=1)
    blocks = [lax.dynamic_index_in_dim(rows, place, 0, keepdims=False) for place in net.order]
    run.add("vector", jnp.stack(blocks[0::2]), jnp.stack(blocks[1::2]))
    run.step(
        "project", "vector", "qkv0", "vector", "expand1", "vector", "qkv1", "vector", "qkv0", "project",
        "expand1", "qkv1", "qkv0", "project", "qkv1", "project",
    )
    weights = {name: run.finish(name) for name in run.sums}
    vector = weights["vector"]

    def chosen(lowers, uppers):
        return jnp.stack(
            [images_of(jnp.where(first, low, up)) for low, up in zip(lowers, uppers)]
        )[None]

    return (
        chosen(early, late),
        chosen(results[1:], results[:-1]),
        jnp.concatenate([weights["qkv0"], weights["qkv1"]], axis=1)[None],
        weights["project"][None],
        jnp.concatenate([weights["expand0"], weights["expand1"]], axis=1)[None],
        jnp.concatenate([weights["reduce0"], weights["reduce1"]], axis=0)[None],
        vector[None, 0:2],
        vector[None, 2:8],
        vector[8:].reshape(1, -1),
    )


def solution(mesh):
    placed = (
        P(None, ("group", "replica"), None, None),
        P(None, ("group", "replica"), None, None),
        P(None, ("group", "replica")),
        P("section", "group", None),
        P("section", "group", None),
        P("section", "group", None),
        P("section", "group", None),
        P("section", None, "group"),
        P("section", None, "group"),
        P("section", "group"),
    )
    return jax.shard_map(
        per_device,
        mesh=mesh,
        in_specs=placed,
        out_specs=(
            P("section", None, ("group", "replica"), None, None),
            P("section", None, ("group", "replica"), None, None),
            P("section", "group", None),
            P("section", "group", None),
            P("section", "group", None),
            P("section", "group", None),
            P("section", None, "group"),
            P("section", None, "group"),
            P("section", "group"),
        ),
        check_vma=False,
    )
```

```python
from functools import partial

import jax
import jax.numpy as jnp
from jax import lax
from jax.experimental import pallas as pl
from jax.experimental.pallas import tpu as pltpu
from jax.sharding import PartitionSpec as P

HEADS = 16
EPSILON = 1e-06
NEGATIVE = -1e30
F32 = jnp.float32
BF16 = jnp.bfloat16
VMEM_LIMIT = 58 * 2**20
ROOT_HALF = 0.7071067811865476
ROOT_TAU = 0.3989422804014327
ANY = pl.BlockSpec(memory_space=pl.ANY)
VMEM = pl.BlockSpec(memory_space=pltpu.VMEM)
SMEM = pl.BlockSpec(memory_space=pltpu.SMEM)
GAIN0, GAIN1, SHIFT0, SHIFT1, QUERY, VALUE, OUT, FEED, EXPAND = range(9)


def padded(length):
    return -(-length // 16) * 16


def contract(left, right, left_dim, right_dim):
    return lax.dot_general(
        left, right, (((left_dim,), (right_dim,)), ((), ())), preferred_element_type=F32
    )


def standardized(values):
    center = values - jnp.mean(values, axis=-1, keepdims=True)
    spread = jnp.mean(center * center, axis=-1, keepdims=True)
    scale = lax.rsqrt(spread + EPSILON)
    return center * scale, scale


def norm_pull(grad, gain, unit, scale):
    scaled = grad * gain
    mean = jnp.mean(scaled, axis=-1, keepdims=True)
    along = jnp.mean(scaled * unit, axis=-1, keepdims=True)
    return scale * (scaled - mean - unit * along)


def call(body, name, operands, specs, outs, scratch, flops, weight=1.0 / 64):
    moved = sum(o.size * o.dtype.itemsize for o in operands)
    out_shape = [jax.ShapeDtypeStruct(shape, dtype) for shape, dtype in outs]
    moved += sum(o.size * o.dtype.itemsize for o in out_shape)
    return pl.pallas_call(
        body,
        out_shape=out_shape,
        in_specs=specs,
        out_specs=[VMEM] * len(outs),
        scratch_shapes=scratch,
        compiler_params=pltpu.CompilerParams(vmem_limit_bytes=VMEM_LIMIT),
        cost_estimate=pl.CostEstimate(flops=int(flops * weight), bytes_accessed=int(moved * weight), transcendentals=0),
        name=name,
    )(*operands)


def start_pieces(pieces, order_ref, target, sems, slot, columns):
    rows = pieces[0].shape[0]
    copies = []
    for index, piece in enumerate(pieces):
        where = pl.multiple_of(order_ref[index] * rows, rows)
        copy = pltpu.make_async_copy(
            piece.at[:, columns], target.at[pl.ds(where, rows), columns], sems.at[slot, index]
        )
        copy.start()
        copies.append(copy)
    return copies


def wait_all(copies):
    for copy in copies:
        copy.wait()


def start_chosen(section, lower, upper, target, sem, same=False):
    if lower is upper or same:
        copy = pltpu.make_async_copy(lower, target, sem)
        copy.start()
        return copy

    @pl.when(section == 0)
    def _():
        pltpu.make_async_copy(lower, target, sem).start()

    @pl.when(section != 0)
    def _():
        pltpu.make_async_copy(upper, target, sem).start()

    return pltpu.make_async_copy(lower, target, sem)


def eights(values):
    return jnp.sum(values.reshape(-1, 8, values.shape[-1]), axis=0)


def attention_stage(x, vec, norm, packed, mixed, logs, columns, full, loads, count, length):
    rows, width = x.shape
    space = rows // count
    head = width // HEADS
    pair = 2 * head
    scale = head**-0.5
    gain, shift = vec[GAIN0 : GAIN0 + 1], vec[SHIFT0 : SHIFT0 + 1]

    def step(here):
        unit, _ = standardized(x[here].astype(F32))
        norm[here] = (unit * gain + shift).astype(BF16)

    step(pl.ds(0, rows))
    for block in range(3):
        wait_all(loads[block])
        done = contract(norm[...], full[:, block * width : (block + 1) * width], 1, 0)
        if block != 1:
            bias = QUERY if block == 0 else VALUE
            done = done + vec[bias : bias + 1]
        packed[:, block * width : (block + 1) * width] = done.astype(BF16)
    lane = lax.broadcasted_iota(jnp.int32, (space, pair), 1)
    left = lane < head
    live = lax.broadcasted_iota(jnp.int32, (space, pair), 0) < length
    key_live = lax.broadcasted_iota(jnp.int32, (space, space), 1) < length
    columns[...] = jnp.zeros_like(columns)

    def heads(index, carry):
        for image in range(count):
            span = pl.ds(image * space, space)

            def part(block):
                offset = pl.multiple_of(block * width + index * pair, pair)
                return packed[span, pl.ds(offset, pair)]

            query, key, value = part(0).astype(F32) * scale, part(1), part(2).astype(F32)
            found = []
            tops = []
            for side in range(2):
                mine = left if side == 0 else ~left
                asked = jnp.where(mine, query, 0.0).astype(BF16)
                held = jnp.where(live, jnp.where(mine, value, 1.0), 0.0).astype(BF16)
                scores = jnp.where(key_live, contract(asked, key, 1, 1), NEGATIVE)
                top = jnp.max(scores, axis=-1, keepdims=True)
                raised = jnp.exp(scores - top).astype(BF16)
                found.append(contract(raised, held, 1, 0))
                tops.append(top)
            inside = jnp.where(left, found[0], found[1])
            total = jnp.where(left, found[1], found[0])
            turned = pltpu.roll(total, head, 1)
            offset = pl.multiple_of(index * pair, pair)
            mixed[span, pl.ds(offset, pair)] = (inside / turned).astype(BF16)
            logged = jnp.log(turned)
            first = tops[0] + logged[:, 0:1]
            second = tops[1] + logged[:, head : head + 1]
            known = columns[image]
            known = jnp.where(lane == 2 * index, first, known)
            columns[image] = jnp.where(lane == 2 * index + 1, second, known)
        return carry

    lax.fori_loop(0, HEADS // 2, heads, 0)
    for image in range(count):
        logs[image] = columns[image].T[0:HEADS]


def hidden_stage(x, vec, mixed, middle, active, second, slope, full_out, full, first_load, loads):
    rows, width = x.shape
    wait_all(first_load)
    gain, shift, bias = vec[GAIN1 : GAIN1 + 1], vec[SHIFT1 : SHIFT1 + 1], vec[OUT : OUT + 1]
    middle[...] = contract(mixed[...], full_out[...], 1, 0)

    def step(here):
        total = middle[here] + x[here].astype(F32) + bias
        middle[here] = total
        unit, _ = standardized(total)
        second[here] = (unit * gain + shift).astype(BF16)

    step(pl.ds(0, rows))
    for block, load in enumerate(loads):
        wait_all(load)
        part = slice(block * width, (block + 1) * width)
        value = contract(second[...], full[:, part], 1, 0) + vec[EXPAND + block : EXPAND + block + 1]
        share = 0.5 + 0.5 * lax.erf(value * ROOT_HALF)
        active[:, part] = (value * share).astype(BF16)
        density = ROOT_TAU * jnp.exp(-0.5 * value * value)
        slope[:, part] = (share + value * density).astype(BF16)


def forward(
    lower, upper, mixed_in, qkv, out, expand, params, meta, count, length, weight=1.0 / 64
):
    rows, width = lower.shape
    space = rows // count
    pair = 2 * width // HEADS
    attend, feed = qkv is not None, expand is not None
    both = attend and feed
    parts = len(qkv if attend else expand)
    inner = expand[0].shape[1] if feed else 0
    blocks = inner // width
    same = lower is upper

    def body(*refs):
        refs = list(refs)
        low = refs.pop(0)
        up = low if same else refs.pop(0)
        if not attend:
            arrived = refs.pop(0)
        lists = [[refs.pop(0) for _ in range(parts)] for _ in range(attend + 2 * feed)]
        vec, info = refs.pop(0), refs.pop(0)
        if both:
            left, packed, logs, middle, slope = (refs.pop(0) for _ in range(5))
            active, second, mixed, norm = (
                left.at[:, pl.ds(start, size)]
                for start, size in ((0, inner), *((inner + width * i, width) for i in range(3)))
            )
        elif attend:
            norm, packed, mixed, logs = (refs.pop(0) for _ in range(4))
        else:
            middle, active, second, slope = (refs.pop(0) for _ in range(4))
        x, x_sem = refs.pop(0), refs.pop(0)
        section = info[parts]
        take = start_chosen(section, low, up, x, x_sem.at[0])
        if attend:
            columns, full, a_sem = (refs.pop(0) for _ in range(3))
            weight = lists.pop(0)
            loads = [
                start_pieces(weight, info, full, a_sem, block, pl.ds(block * width, width))
                for block in range(3)
            ]
        if feed:
            full_out, full_in, o_sem, w_sem = (refs.pop(0) for _ in range(4))
            if not attend:
                mixed = refs.pop(0)
                extra = pltpu.make_async_copy(arrived, mixed, x_sem.at[1])
                extra.start()
            first_load = start_pieces(lists[0], info, full_out, o_sem, 0, pl.ds(0, width))
            inner_loads = [
                start_pieces(lists[1], info, full_in, w_sem, block, pl.ds(block * width, width))
                for block in range(blocks)
            ]
        take.wait()
        if attend:
            attention_stage(
                x, vec, norm, packed, mixed, logs, columns, full, loads, count, length
            )
        if feed:
            if not attend:
                extra.wait()
            hidden_stage(
                x, vec, mixed, middle, active, second, slope, full_out, full_in, first_load,
                inner_loads,
            )

    outs, inputs = [], [lower] if same else [lower, upper]
    scratch = [pltpu.VMEM((rows, width), BF16), pltpu.SemaphoreType.DMA((2,))]
    flops = 0
    if attend:
        outs += [
            ((rows, width), BF16),
            ((rows, 3 * width), BF16),
            ((rows, width), BF16),
            ((count, HEADS, space), F32),
        ]
        scratch += [
            pltpu.VMEM((count, space, pair), F32),
            pltpu.VMEM((width, 3 * width), BF16),
            pltpu.SemaphoreType.DMA((3, parts)),
        ]
        flops += 2 * rows * width * (3 * width + 2 * space)
    else:
        inputs += [mixed_in]
    if feed:
        outs += [
            ((rows, width), F32),
            ((rows, inner), BF16),
            ((rows, width), BF16),
            ((rows, inner), BF16),
        ]
        scratch += [
            pltpu.VMEM((width, width), BF16),
            pltpu.VMEM((width, inner), BF16),
            pltpu.SemaphoreType.DMA((1, parts)),
            pltpu.SemaphoreType.DMA((blocks, parts)),
        ]
        if not attend:
            scratch += [pltpu.VMEM((rows, width), BF16)]
        flops += 2 * rows * width * (width + inner)
    if both:
        outs = [((rows, inner + 3 * width), BF16), outs[1], outs[3], outs[4], outs[7]]
    weights = (list(qkv) if attend else []) + (list(out) + list(expand) if feed else [])
    return call(
        body,
        "forward" + "_attend" * attend + "_feed" * feed,
        inputs + weights + [params, meta],
        [ANY] * (len(inputs) + len(weights)) + [VMEM, SMEM],
        outs,
        scratch,
        flops,
        weight,
    )


def output_forward(middle, active, pieces, params, meta, count, weight=1.0 / 64):
    rows, width = middle.shape
    inner = len(pieces) * pieces[0].shape[0]
    space = rows // count
    parts = len(pieces)
    blocks = 2
    part_width = width // blocks

    def body(*refs):
        refs = list(refs)
        mid_in, act_in = refs.pop(0), refs.pop(0)
        reduce = [refs.pop(0) for _ in range(parts)]
        vec, info, result, mid, act, full, x_sem, w_sem = refs
        copies = [
            pltpu.make_async_copy(act_in.at[:, pl.ds(0, inner)], act, x_sem.at[0]),
            pltpu.make_async_copy(mid_in, mid, x_sem.at[1]),
        ]
        copies[0].start()
        loads = [
            start_pieces(reduce, info, full, w_sem, block, pl.ds(block * part_width, part_width))
            for block in range(blocks)
        ]
        copies[1].start()
        copies[0].wait()
        for block in range(blocks):
            wait_all(loads[block])
            if block == 0:
                copies[1].wait()
            part = slice(block * part_width, (block + 1) * part_width)
            value = contract(act[...], full[:, part], 1, 0) + mid[:, part] + vec[FEED : FEED + 1, part]
            for image in range(count):
                alive = jnp.where(info[parts + 1 + image] > 0, 1.0, 0.0)
                here = slice(image * space, (image + 1) * space)
                result[here, part] = (value[here] * alive).astype(BF16)

    return call(
        body,
        "output_forward",
        [middle, active] + list(pieces) + [params, meta],
        [ANY] * (2 + parts) + [VMEM, SMEM],
        [((rows, width), BF16)],
        [
            pltpu.VMEM((rows, width), F32),
            pltpu.VMEM((rows, inner), BF16),
            pltpu.VMEM((inner, width), BF16),
            pltpu.SemaphoreType.DMA((2,)),
            pltpu.SemaphoreType.DMA((blocks, parts)),
        ],
        2 * rows * width * inner,
        weight,
    )[0]


def hidden_back_stage(
    grad, vec, info, feed, slope, middle, hidden, second, mid_grad, branch, sums, inner_sums, full_out,
    full, deep, first_load, load, for_slope, for_middle, tallies, count, parts,
):
    rows, width = grad.shape
    space = rows // count
    half = width // 2
    for image in range(count):
        alive = jnp.where(info[parts + 1 + image] > 0, 1.0, 0.0)
        here = slice(image * space, (image + 1) * space)
        feed[here] = (grad[here].astype(F32) * alive).astype(BF16)
    for_slope.wait()
    for index in range(parts):
        wait_all(first_load[index])
        where = pl.multiple_of(info[index] * deep, deep)
        value = contract(feed[...], full_out[pl.ds(where, deep)], 1, 1)
        value = (value * slope[:, pl.ds(where, deep)].astype(F32)).astype(BF16)
        hidden[:, pl.ds(where, deep)] = value
        inner_sums[:, pl.ds(where, deep)] = jnp.sum(value.astype(F32), axis=0, keepdims=True)
    wait_all(load)
    for block in range(2):
        second[:, block * half : (block + 1) * half] = contract(
            hidden[...], full[block * half : (block + 1) * half], 1, 1
        )
    for_middle.wait()
    gain = vec[GAIN1 : GAIN1 + 1]
    tallies[...] = jnp.zeros_like(tallies)

    def step(here):
        unit, scale = standardized(middle[here])
        down = second[here]
        top = feed[here].astype(F32)
        total = top + norm_pull(down, gain, unit, scale)
        low = total.astype(BF16)
        mid_grad[here] = total
        branch[here] = low
        tallies[0] += eights(down * unit)
        tallies[1] += eights(down)
        tallies[2] += eights(low.astype(F32))
        tallies[3] += eights(top)

    step(pl.ds(0, rows))
    for index in range(4):
        sums[index : index + 1] = jnp.sum(tallies[index], axis=0, keepdims=True)


def attention_back_stage(
    x, vec, branch, mid_grad, packed, mixed, logs, grads, result, sums, down, normal, stage, full_out,
    full, first_load, load, takes, tallies, count, length,
):
    rows, width = x.shape
    space = rows // count
    head = width // HEADS
    pair = 2 * head
    scale = head**-0.5
    half = width // 2
    wait_all(first_load)
    down[...] = contract(branch[...], full_out[...], 1, 1).astype(BF16)
    wait_all(takes)
    owner = lax.shift_right_logical(
        lax.broadcasted_iota(jnp.int32, (HEADS, width), 1), head.bit_length() - 1
    )
    chosen = jnp.where(
        owner == lax.broadcasted_iota(jnp.int32, (HEADS, width), 0), 1.0, 0.0
    ).astype(BF16)
    left = lax.broadcasted_iota(jnp.int32, (space, pair), 1) < head
    live = lax.broadcasted_iota(jnp.int32, (space, pair), 0) < length
    key_live = lax.broadcasted_iota(jnp.int32, (space, space), 0) < length
    for image in range(count):
        span = pl.ds(image * space, space)
        product = down[span].astype(F32) * mixed[span].astype(F32)
        coarse = product.astype(BF16)
        fine = (product - coarse.astype(F32)).astype(BF16)
        stage[image, :, 0:space] = contract(chosen, coarse, 1, 1) + contract(chosen, fine, 1, 1)

    def heads(index, carry):
        for image in range(count):
            span = pl.ds(image * space, space)

            def part(block):
                offset = pl.multiple_of(block * width + index * pair, pair)
                return packed[span, pl.ds(offset, pair)]

            query, key, value = part(0), part(1), part(2)
            wide = key.astype(F32) * scale
            value = value.astype(F32)
            arrived = down[span, pl.ds(pl.multiple_of(index * pair, pair), pair)]
            found = []
            for side in range(2):
                mine = left if side == 0 else ~left
                log = logs[image, pl.ds(2 * index + side, 1), :]
                dot = stage[image, pl.ds(2 * index + side, 1), 0:space]
                scores = contract(jnp.where(mine, wide, 0.0).astype(BF16), query, 1, 1)
                chance = jnp.exp(jnp.where(key_live, scores - log, NEGATIVE))
                back = contract(jnp.where(mine, value, 0.0).astype(BF16), arrived, 1, 1)
                change = (chance * (back - dot)).astype(BF16)
                found.append(
                    (
                        contract(change, key, 0, 0),
                        contract(change, query, 1, 0),
                        contract(chance.astype(BF16), arrived, 1, 0),
                    )
                )
            for block, factor in enumerate((scale, scale, 1.0)):
                total = jnp.where(left, found[0][block], found[1][block]) * factor
                offset = pl.multiple_of(block * width + index * pair, pair)
                grads[span, pl.ds(offset, pair)] = jnp.where(live, total, 0.0).astype(BF16)
        return carry

    lax.fori_loop(0, HEADS // 2, heads, 0)
    wait_all(load)
    for block in range(2):
        normal[:, block * half : (block + 1) * half] = contract(
            grads[...], full[block * half : (block + 1) * half], 1, 1
        )
    gain = vec[GAIN0 : GAIN0 + 1]
    tallies[...] = jnp.zeros_like(tallies)

    def step(here):
        unit, rate = standardized(x[here].astype(F32))
        grad = normal[here]
        tallies[0] += eights(grad * unit)
        tallies[1] += eights(grad)
        result[here] = (mid_grad[here] + norm_pull(grad, gain, unit, rate)).astype(BF16)

    step(pl.ds(0, rows))
    for index in range(2):
        sums[index : index + 1] = jnp.sum(tallies[index], axis=0, keepdims=True)
    sums[2:3] = jnp.sum(grads[:, 0:width].astype(F32), axis=0, keepdims=True)
    sums[3:4] = jnp.sum(grads[:, 2 * width : 3 * width].astype(F32), axis=0, keepdims=True)


def backward(
    start, lower, upper, kept_low, kept_up, reduce, expand, out, qkv, params, meta, count, length,
    mixed_at, weight=1.0 / 64,
):
    feed, attend = reduce is not None, qkv is not None
    rows, width = start[0].shape
    space = rows // count
    pair = 2 * width // HEADS
    parts = len(reduce if feed else qkv)
    inner = expand[0].shape[1] if feed else 0
    deep = reduce[0].shape[0] if feed else 0
    both = feed and attend
    choices = []
    if feed:
        choices += [(kept_low[0], kept_up[0]), (kept_low[1], kept_up[1])]
        if start[0] is not start[1]:
            choices += [start]
    if attend:
        choices += [(kept_low[index], kept_up[index]) for index in (2, 3, 4)]
        choices += [(lower, upper)]
    plain = [start[0]] if feed and start[0] is start[1] else [] if feed else list(start)
    operands = []
    for low, up in choices:
        operands += [low] if low is up else [low, up]

    def body(*refs):
        refs = list(refs)
        firsts = [refs.pop(0) for _ in plain]
        pairs = []
        for low, up in choices:
            one = refs.pop(0)
            pairs.append((one, one if low is up else refs.pop(0)))
        lists = [[refs.pop(0) for _ in range(parts)] for _ in range(2 * feed + 2 * attend)]
        vec, info = refs.pop(0), refs.pop(0)
        section = info[parts]
        if feed:
            right, feed_sums, inner_sums = (refs.pop(0) for _ in range(3))
            hidden = right.at[:, pl.ds(0, inner)]
            branch = right.at[:, pl.ds(inner, width)]
            mid_grad = None if both else refs.pop(0)
        if attend:
            grads, result, sums = (refs.pop(0) for _ in range(3)) if not both else (None, refs.pop(0), refs.pop(0))
        if both:
            feed_grad = right.at[:, pl.ds(inner + width, width)]
            grads = right.at[:, pl.ds(inner + 2 * width, 3 * width)]
        tallies, x_sem = refs.pop(0), refs.pop(0)
        if feed:
            grad, slope, middle, second, full_out, full, o_sem, w_sem = (
                refs.pop(0) for _ in range(8)
            )
            if both:
                mid_grad, keep = refs.pop(0), feed_grad
            else:
                keep = refs.pop(0)
            begin = pairs.pop(2) if start[0] is not start[1] else (firsts[0], firsts[0])
            take = start_chosen(section, *begin, grad, x_sem.at[0])
            for_slope = start_chosen(section, *pairs.pop(0), slope, x_sem.at[1])
            first_load = [
                start_pieces(
                    [piece], Shifted(info, index), full_out, o_sem.at[pl.ds(index, 1)], 0,
                    pl.ds(0, width),
                )
                for index, piece in enumerate(lists.pop(0))
            ]
            for_middle = start_chosen(section, *pairs.pop(0), middle, x_sem.at[2])
            load = start_pieces(lists.pop(0), info, full, w_sem, 0, pl.ds(0, inner))
        if attend:
            x, packed, mixed, logs, down, normal, stage, full_o, full_q, p_sem, q_sem = (
                refs.pop(0) for _ in range(11)
            )
            if not feed:
                branch, mid_grad = refs.pop(0), refs.pop(0)
                givens = [
                    pltpu.make_async_copy(source, target, x_sem.at[index])
                    for index, (source, target) in enumerate(zip(firsts, (branch, mid_grad)))
                ]
                for given in givens:
                    given.start()
            project_load = start_pieces(lists.pop(0), info, full_o, p_sem, 0, pl.ds(0, width))
            sames = [one is two for one, two in pairs]
            pairs[1] = tuple(one.at[:, pl.ds(mixed_at, width)] for one in pairs[1])
            takes = [
                start_chosen(section, *pairs[index], target, x_sem.at[3 + index], sames[index])
                for index, target in ((1, mixed), (0, packed), (2, logs), (3, x))
            ]
            last_load = start_pieces(lists.pop(0), info, full_q, q_sem, 0, pl.ds(0, 3 * width))
            if not feed:
                wait_all(givens)
        if feed:
            take.wait()
            hidden_back_stage(
                grad, vec, info, keep, slope, middle, hidden, second, mid_grad, branch, feed_sums,
                inner_sums, full_out, full, deep, first_load, load, for_slope, for_middle, tallies,
                count, parts,
            )
        if attend:
            attention_back_stage(
                x, vec, branch, mid_grad, packed, mixed, logs, grads, result, sums, down, normal,
                stage, full_o, full_q, project_load, last_load, takes, tallies, count, length,
            )

    outs = []
    scratch = [pltpu.VMEM((4, 8, width), F32), pltpu.SemaphoreType.DMA((7,))]
    flops = 0
    if feed:
        outs += [
            ((rows, inner + (5 if both else 1) * width), BF16),
            ((8, width), F32),
            ((1, inner), F32),
        ]
        if not both:
            outs += [((rows, width), F32)]
        scratch += [
            pltpu.VMEM((rows, width), BF16),
            pltpu.VMEM((rows, inner), BF16),
            pltpu.VMEM((rows, width), F32),
            pltpu.VMEM((rows, width), F32),
            pltpu.VMEM((inner, width), BF16),
            pltpu.VMEM((width, inner), BF16),
            pltpu.SemaphoreType.DMA((parts, 1)),
            pltpu.SemaphoreType.DMA((1, parts)),
        ]
        scratch += [pltpu.VMEM((rows, width), F32 if both else BF16)]
        flops += 4 * rows * width * inner
    if attend:
        outs += [] if both else [((rows, 3 * width), BF16)]
        outs += [((rows, width), BF16), ((8, width), F32)]
        scratch += [
            pltpu.VMEM((rows, width), BF16),
            pltpu.VMEM((rows, 3 * width), BF16),
            pltpu.VMEM((rows, width), BF16),
            pltpu.VMEM((count, HEADS, space), F32),
            pltpu.VMEM((rows, width), BF16),
            pltpu.VMEM((rows, width), F32),
            pltpu.VMEM((count, HEADS, 2 * pair), F32),
            pltpu.VMEM((width, width), BF16),
            pltpu.VMEM((width, 3 * width), BF16),
            pltpu.SemaphoreType.DMA((1, parts)),
            pltpu.SemaphoreType.DMA((1, parts)),
        ]
        if not feed:
            scratch += [pltpu.VMEM((rows, width), BF16), pltpu.VMEM((rows, width), F32)]
        flops += 2 * rows * width * (4 * width + 5 * space)
    weights = (list(reduce) + list(expand) if feed else []) + (
        list(out) + list(qkv) if attend else []
    )
    return call(
        body,
        "backward" + "_feed" * feed + "_attend" * attend,
        plain + operands + weights + [params, meta],
        [ANY] * (len(plain) + len(operands) + len(weights)) + [VMEM, SMEM],
        outs,
        scratch,
        flops,
        weight,
    )


class Shifted:
    def __init__(self, ref, index):
        self.ref, self.index = ref, index

    def __getitem__(self, index):
        return self.ref[self.index + index]


def weight_gradient(lefts, rights, meta, parts, blocks, quarter, rows_of, columns_of, name):
    terms = len(lefts)
    first_row, height = rows_of
    first_column, breadth = columns_of
    rows = lefts[0].shape[0]
    operands = list(lefts)
    places = []
    for pair in rights:
        found = []
        for array, _ in pair:
            if not any(array is other for other in operands):
                operands.append(array)
            found.append(next(i for i, other in enumerate(operands) if other is array))
        places.append(found)

    def body(*refs):
        sources, info = refs[: len(operands)], refs[len(operands)]
        results = refs[len(operands) + 1 : len(operands) + 1 + len(blocks)]
        left_full, right_full, l_sem, r_sem = refs[len(operands) + 1 + len(blocks) :]
        section = info[parts]
        waits = []
        for term in range(terms):
            sides = [
                sources[place].at[:, pl.ds(column + first_column, breadth)]
                for place, (_, column) in zip(places[term], rights[term])
            ]
            same = rights[term][0] is rights[term][1]
            target = right_full.at[pl.ds(term * rows, rows)]
            waits.append(start_chosen(section, *sides, target, r_sem.at[term], same))
        loads = []
        for index, block in enumerate(blocks):
            start = pl.multiple_of(info[block] * quarter + first_row, 128)
            for term in range(terms):
                copy = pltpu.make_async_copy(
                    sources[term].at[:, pl.ds(start, height)],
                    left_full.at[index, pl.ds(term * rows, rows)],
                    l_sem.at[index, term],
                )
                copy.start()
                loads.append(copy)
        wait_all(waits)
        for index in reversed(range(len(blocks))):
            wait_all(loads[index * terms : (index + 1) * terms])
            results[index][...] = contract(left_full[index], right_full[...], 0, 0).astype(BF16)

    return call(
        body,
        name,
        operands + [meta],
        [ANY] * len(operands) + [SMEM],
        [((height, breadth), BF16)] * len(blocks),
        [
            pltpu.VMEM((len(blocks), terms * rows, height), BF16),
            pltpu.VMEM((terms * rows, breadth), BF16),
            pltpu.SemaphoreType.DMA((len(blocks), terms)),
            pltpu.SemaphoreType.DMA((terms,)),
        ],
        2 * len(blocks) * terms * rows * height * breadth,
    )


def after(value, *earlier):
    return lax.optimization_barrier((value,) + earlier)[0]


def added(*values):
    total = values[0].astype(F32)
    for value in values[1:]:
        total = total + value.astype(F32)
    return total.astype(values[0].dtype)


class FourByFour:
    parts = 4
    blocks = (0, 2)

    def __init__(self):
        self.begun = 0
        self.group = lax.axis_index("group")
        self.place = lax.axis_index("replica")
        self.order = [self.group ^ part for part in range(4)]

    def core(self, block):
        return lax.ppermute(block, "group", [(i, i ^ 1) for i in range(4)])

    def across(self, block):
        return lax.ppermute(block, "group", [(i, i ^ 2) for i in range(4)])

    def gather(self, blocks):
        far, sibling = [], []
        for index, block in enumerate(blocks):
            far.append(self.across(after(block, far[index - 2]) if index > 1 else block))
            sibling.append(self.core(after(block, sibling[-1]) if index else block))

        def pieces(index, token):
            distant = far[index] if token is None else after(far[index], token)
            return [blocks[index], sibling[index], far[index], self.core(distant)]

        return [partial(pieces, index) for index in range(len(blocks))]

    def shared(self, block):
        return [block, self.core(block)]

    def total(self, blocks, own):
        passed = self.across(blocks[1])
        token = yield
        mine = added(after(blocks[0], token), passed)
        if not own:
            turn = [(place + self.begun) % 4 for place in range(4)]
            self.begun += 1
            whole = lax.psum(mine, "replica", axis_index_groups=[turn])
            token = yield mine
            yield after(whole, token)
            return
        inward = lax.ppermute(mine, "replica", [(0, 1), (3, 2)])
        token = yield mine
        joined = added(after(mine, token), inward)
        crossing = lax.ppermute(joined, "replica", [(1, 2), (2, 1)])
        token = yield joined
        summed = added(after(joined, token), crossing)
        outward = lax.ppermute(summed, "replica", [(1, 0), (2, 3)])
        token = yield summed
        inner = (self.place == 1) | (self.place == 2)
        yield jnp.where(inner, after(summed, token), outward)


class General:
    def __init__(self):
        self.parts = lax.axis_size("group")
        self.blocks = tuple(range(self.parts))
        self.order = [jnp.int32(part) for part in range(self.parts)]

    def gather(self, blocks):
        found = []
        for block in blocks:
            whole = lax.all_gather(block, "group", axis=0)
            found.append([whole[part] for part in range(self.parts)])
        return [lambda token, pieces=pieces: pieces for pieces in found]

    def shared(self, block):
        return [block]

    def total(self, blocks, own):
        yield
        mine = lax.psum_scatter(jnp.stack(blocks), "group", scatter_dimension=0)
        yield mine
        yield lax.psum(mine, "replica")


def shifted(block, distance):
    devices = range(lax.axis_size("section"))
    route = [(i - distance, i) for i in devices if i - distance in devices]
    return lax.ppermute(block, "section", route)


def in_order(pieces, order):
    place = jnp.stack(order)
    stacked = []
    for block in range(len(pieces)):
        chosen = pieces[0]
        for part in range(1, len(pieces)):
            chosen = jnp.where(place[part] == block, pieces[part], chosen)
        stacked.append(chosen)
    return jnp.stack(stacked)


class Sequence:
    def __init__(self, net, token):
        self.net, self.sums, self.results, self.token = net, {}, {}, token

    def now(self, value):
        return after(value, self.token)

    def ran(self, value):
        self.token = value

    def add(self, name, blocks, own):
        self.sums[name] = self.net.total(blocks, own)
        next(self.sums[name])

    def step(self, *names):
        for name in names:
            try:
                self.results[name] = self.token = self.sums[name].send(self.token)
            except StopIteration:
                continue

    def finish(self, name):
        while True:
            try:
                self.results[name] = self.sums[name].send(self.token)
            except StopIteration:
                return self.results[name]


def per_device(
    images,
    cotangent,
    counts,
    qkv_weight,
    out_weight,
    expand_weight,
    reduce_weight,
    norm_gains,
    biases,
    expand_bias,
):
    micro, slots, length, width = images.shape
    space = padded(length)
    section = lax.axis_index("section")
    first = section == 0
    sizes = (lax.axis_size("group"), lax.axis_size("replica"))
    net = FourByFour() if sizes == (4, 4) else General()
    parts = net.parts
    share = width // parts
    batches = tuple(range(micro))

    def rows_of(array):
        full = jnp.pad(array, ((0, 0), (0, 0), (0, space - length), (0, 0)))
        return [full[batch].reshape(slots * space, width) for batch in batches]

    def images_of(array):
        return array.reshape(slots, space, width)[:, :length]

    inputs, targets = rows_of(images), rows_of(cotangent)
    small = jnp.concatenate([norm_gains[0], biases[0], expand_bias[0].reshape(-1, share)])
    vectors, qkv, out, expand, reduce = net.gather(
        [small, qkv_weight[0], out_weight[0], expand_weight[0], reduce_weight[0]]
    )
    vectors = in_order(vectors(after(inputs[0], *inputs[1:], *targets)), net.order)
    top = vectors[:, :8].transpose(1, 0, 2).reshape(8, width)
    bottom = vectors[:, 8:].reshape(-1, width)
    params = jnp.concatenate([top, bottom]).astype(F32)
    slot = jnp.arange(slots, dtype=jnp.int32)
    alive = [(slot < counts[batch, 0]).astype(jnp.int32) for batch in batches]
    head = jnp.stack(net.order + [section]).astype(jnp.int32)

    def meta(*values):
        return jnp.concatenate((head,) + values)

    infos = [meta(alive[batch]) for batch in batches]
    info = meta(*alive)

    qkv = qkv(params)
    attended = []
    for batch in batches:
        start = inputs[batch] if batch == 0 else after(inputs[batch], attended[-1][2])
        attended.append(
            forward(start, start, None, qkv, None, None, params, infos[batch], slots, length)
        )
    out = out(attended[-1][2])
    expand = expand(out[-1])
    fed = []
    for batch in batches:
        start = inputs[batch] if batch == 0 else after(inputs[batch], fed[-1][0])
        fed.append(
            forward(start, start, attended[batch][2], None, out, expand, params, infos[batch], slots, length)
        )
    reduce = reduce(fed[-1][0])
    early, incoming = [], []
    for batch in batches:
        middle, active = fed[batch][:2]
        if batch:
            active = after(active, early[-1])
        early.append(output_forward(middle, active, reduce, params, infos[batch], slots))
        incoming.append(shifted(early[batch], 1))

    inner = expand[0].shape[1]
    mixed_at = inner + width
    kept, lefts, rights, results = [], [], [], []
    sums_a, sums_b, sums_c, returning = [], [], [], []
    token = early[-1]
    for batch in batches:
        start = after(incoming[batch], token)
        left, packed, logs, middle, slope = forward(
            inputs[batch], start, None, qkv, out, expand, params, infos[batch], slots, length, 8.0
        )
        kept.append((slope, middle, packed, left, logs))
        lefts.append(net.shared(left))
        if batch == 0:
            pair, sides = (targets[0], targets[0]), (kept[0], kept[0])
            lower, chosen = incoming[0], infos[0]
        else:
            pair = (returning[batch - 1], targets[batch])
            sides = (kept[batch - 1], kept[batch])
            lower = inputs[batch - 1]
            chosen = meta(jnp.where(first, alive[batch - 1], alive[batch]))
        right, some, more, result, rest = backward(
            pair, lower, incoming[batch], sides[0], sides[1], reduce, expand, out, qkv, params, chosen,
            slots, length, mixed_at, 8.0,
        )
        token = result
        rights.append(net.shared(right))
        results.append(result)
        sums_a.append(some)
        sums_b.append(more)
        sums_c.append(rest)
        returning.append(shifted(result, -1))
    late = []
    for batch in batches:
        ready = lefts[batch][1:] + (rights[batch][1:] if batch < micro - 1 else [])
        active = after(kept[batch][3], token, *ready)
        late.append(output_forward(kept[batch][1], active, reduce, params, infos[batch], slots, 8.0))
        token = late[-1]

    last = micro - 1
    run = Sequence(net, token)
    arrived = run.now(returning[last])
    living = jnp.repeat(alive[last] > 0, space)[:, None]
    masked = net.shared(jnp.where(living, arrived, jnp.zeros_like(arrived)))
    many = len(masked)

    def gradient(name, left_at, final, final_at, right_at, quarter, rows, columns, own):
        left = [lefts[batch][side] for batch in batches for side in range(many)]
        right = []
        for batch in batches:
            for side in range(many):
                upper = (rights[batch][side], right_at)
                lower = (final[side], final_at) if batch == last else (rights[batch + 1][side], right_at)
                right.append((lower, upper))
        blocks = weight_gradient(
            left, right, run.now(info), parts, net.blocks, quarter, (left_at + rows[0], rows[1]), columns,
            name,
        )
        run.ran(blocks[0])
        return blocks

    def summed(name, *rest):
        run.add(name, gradient(name, *rest), rest[-1])

    def reduce_part(index, own):
        deep = inner // parts
        step = deep // 2
        summed(
            f"reduce{index}", 0, masked, 0, inner + width, deep, (index * step, step), (0, width), own
        )

    reduce_part(0, False)
    start = run.now(arrived)
    final, some, more, mid = backward(
        (start, start), None, None, kept[last], kept[last], reduce, expand, None, None, params,
        infos[last], slots, length, mixed_at,
    )
    run.ran(final)
    branch = final[:, inner:]
    finals, branches = net.shared(final[:, :inner]), net.shared(branch)
    sums_a.append(some)
    sums_b.append(more)
    reduce_part(1, False)
    run.step("reduce0")
    summed("project", mixed_at, branches, 0, inner, share, (0, share), (0, width), False)
    grads, result, rest = backward(
        (run.now(branch), mid), inputs[last], inputs[last], kept[last], kept[last], None, None, out, qkv,
        params, infos[last], slots, length, mixed_at, 16.0,
    )
    run.ran(result)
    grads = net.shared(grads)
    results.append(result)
    sums_c.append(rest)
    run.step("reduce1", "project")

    def expand_part(index, own):
        step = inner // 2
        summed(f"expand{index}", inner, finals, 0, 0, share, (0, share), (index * step, step), own)

    expand_part(0, True)
    run.step("reduce0")
    expand_part(1, True)

    def over_batches(values):
        return sum(jnp.where(first, values[batch + 1], values[batch]) for batch in batches)

    some, more, rest = over_batches(sums_a), over_batches(sums_b), over_batches(sums_c)
    rows = jnp.concatenate([rest[0:1], some[0:1], rest[1:2], some[1:2], rest[2:4], some[2:4]])
    rows = rows.reshape(8, parts, share).transpose(1, 0, 2)
    rows = jnp.concatenate([rows, more.reshape(parts, -1, share)], axis=1)
    rows = sum(net.shared(rows))
    rows = jnp.stack(
        [lax.dynamic_index_in_dim(rows, net.order[block], 0, keepdims=False) for block in net.blocks]
    )
    count, step = rows.shape[1], width // 2
    rows = rows.reshape(len(net.blocks), -1)
    rows = jnp.pad(rows, ((0, 0), (0, -rows.shape[1] % (16 * step)))).reshape(len(net.blocks), -1, step)

    def qkv_part(index):
        begin, breadth = ((0, 3 * step), (3 * step, 2 * step), (5 * step, step))[index]
        return gradient(
            f"qkv{index}", inner + 2 * width, grads, 0, inner + 2 * width, share, (0, share),
            (begin, breadth), True,
        )

    run.add("qkv0", qkv_part(0), True)
    run.add("qkv1", qkv_part(1), True)
    blocks = qkv_part(2)
    run.add("qkv2", [jnp.concatenate([one, two]) for one, two in zip(blocks, rows.astype(BF16))], True)
    run.step(
        "expand0", "reduce1", "expand1", "expand0", "project", "qkv0", "expand1", "qkv1", "expand0", "qkv2", "qkv0", "qkv1", "expand1",
        "qkv2", "expand0", "qkv0", "expand1", "qkv1", "qkv2", "qkv0", "qkv1", "qkv2",
    )
    weights = {name: run.finish(name) for name in run.sums}
    vector = weights["qkv2"][share:].reshape(-1)[: count * share].reshape(count, share).astype(F32)

    def chosen(lowers, uppers):
        return jnp.stack(
            [images_of(jnp.where(first, low, up)) for low, up in zip(lowers, uppers)]
        )[None]

    def joined(axis, *names):
        return jnp.concatenate([weights[name] for name in names], axis=axis).astype(F32)[None]

    return (
        chosen(early, late),
        chosen(results[1:], results[:-1]),
        jnp.concatenate([weights["qkv0"], weights["qkv1"], weights["qkv2"][:share]], axis=1).astype(F32)[None],
        weights["project"].astype(F32)[None],
        joined(1, "expand0", "expand1"),
        joined(0, "reduce0", "reduce1"),
        vector[None, 0:2],
        vector[None, 2:8],
        vector[8:].reshape(1, -1),
    )


def solution(mesh):
    placed = (
        P(None, ("group", "replica"), None, None),
        P(None, ("group", "replica"), None, None),
        P(None, ("group", "replica")),
        P("section", "group", None),
        P("section", "group", None),
        P("section", "group", None),
        P("section", "group", None),
        P("section", None, "group"),
        P("section", None, "group"),
        P("section", "group"),
    )
    return jax.shard_map(
        per_device,
        mesh=mesh,
        in_specs=placed,
        out_specs=(
            P("section", None, ("group", "replica"), None, None),
            P("section", None, ("group", "replica"), None, None),
            P("section", "group", None),
            P("section", "group", None),
            P("section", "group", None),
            P("section", "group", None),
            P("section", None, "group"),
            P("section", None, "group"),
            P("section", "group"),
        ),
        check_vma=False,
    )
```

```python
from functools import partial

import jax
import jax.numpy as jnp
from jax import lax
from jax.experimental import pallas as pl
from jax.experimental.pallas import tpu as pltpu
from jax.sharding import PartitionSpec as P

HEADS = 16
EPSILON = 1e-06
NEGATIVE = -1e30
F32 = jnp.float32
BF16 = jnp.bfloat16
VMEM_LIMIT = 58 * 2**20
ROOT_HALF = 0.7071067811865476
ROOT_TAU = 0.3989422804014327
ANY = pl.BlockSpec(memory_space=pl.ANY)
VMEM = pl.BlockSpec(memory_space=pltpu.VMEM)
SMEM = pl.BlockSpec(memory_space=pltpu.SMEM)
GAIN0, GAIN1, SHIFT0, SHIFT1, QUERY, VALUE, OUT, FEED, EXPAND = range(9)


def padded(length):
    return -(-length // 16) * 16


def contract(left, right, left_dim, right_dim):
    return lax.dot_general(
        left, right, (((left_dim,), (right_dim,)), ((), ())), preferred_element_type=F32
    )


def standardized(values):
    center = values - jnp.mean(values, axis=-1, keepdims=True)
    spread = jnp.mean(center * center, axis=-1, keepdims=True)
    scale = lax.rsqrt(spread + EPSILON)
    return center * scale, scale


def norm_pull(grad, gain, unit, scale):
    scaled = grad * gain
    mean = jnp.mean(scaled, axis=-1, keepdims=True)
    along = jnp.mean(scaled * unit, axis=-1, keepdims=True)
    return scale * (scaled - mean - unit * along)


def call(body, name, operands, specs, outs, scratch, flops, weight=1.0 / 64):
    moved = sum(o.size * o.dtype.itemsize for o in operands)
    out_shape = [jax.ShapeDtypeStruct(shape, dtype) for shape, dtype in outs]
    moved += sum(o.size * o.dtype.itemsize for o in out_shape)
    return pl.pallas_call(
        body,
        out_shape=out_shape,
        in_specs=specs,
        out_specs=[VMEM] * len(outs),
        scratch_shapes=scratch,
        compiler_params=pltpu.CompilerParams(vmem_limit_bytes=VMEM_LIMIT),
        cost_estimate=pl.CostEstimate(flops=int(flops * weight), bytes_accessed=int(moved * weight), transcendentals=0),
        name=name,
    )(*operands)


def flat(groups):
    return [piece for group in groups for piece in group]


def start_pieces(pieces, info, first, target, sems, slot, columns):
    copies = []
    for index, piece in enumerate(pieces):
        rows = piece.shape[0]
        where = pl.multiple_of(info[first + index] * rows, rows)
        copy = pltpu.make_async_copy(
            piece.at[:, columns], target.at[pl.ds(where, rows), columns], sems.at[slot, index]
        )
        copy.start()
        copies.append(copy)
    return copies


def wait_all(copies):
    for copy in copies:
        copy.wait()


def start_chosen(section, lower, upper, target, sem, same=False):
    if lower is upper or same:
        copy = pltpu.make_async_copy(lower, target, sem)
        copy.start()
        return copy

    @pl.when(section == 0)
    def _():
        pltpu.make_async_copy(lower, target, sem).start()

    @pl.when(section != 0)
    def _():
        pltpu.make_async_copy(upper, target, sem).start()

    return pltpu.make_async_copy(lower, target, sem)


def eights(values):
    return jnp.sum(values.reshape(-1, 8, values.shape[-1]), axis=0)


def attention_stage(x, vec, norm, packed, mixed, logs, columns, full, loads, count, length):
    rows, width = x.shape
    space = rows // count
    head = width // HEADS
    pair = 2 * head
    scale = head**-0.5
    gain, shift = vec[GAIN0 : GAIN0 + 1], vec[SHIFT0 : SHIFT0 + 1]

    def step(here):
        unit, _ = standardized(x[here].astype(F32))
        norm[here] = (unit * gain + shift).astype(BF16)

    step(pl.ds(0, rows))
    for block in range(3):
        wait_all(loads[block])
        done = contract(norm[...], full[:, block * width : (block + 1) * width], 1, 0)
        if block != 1:
            bias = QUERY if block == 0 else VALUE
            done = done + vec[bias : bias + 1]
        packed[:, block * width : (block + 1) * width] = done.astype(BF16)
    lane = lax.broadcasted_iota(jnp.int32, (space, pair), 1)
    left = lane < head
    live = lax.broadcasted_iota(jnp.int32, (space, pair), 0) < length
    key_live = lax.broadcasted_iota(jnp.int32, (space, space), 1) < length
    columns[...] = jnp.zeros_like(columns)

    def heads(index, carry):
        for image in range(count):
            span = pl.ds(image * space, space)

            def part(block):
                offset = pl.multiple_of(block * width + index * pair, pair)
                return packed[span, pl.ds(offset, pair)]

            query, key, value = part(0).astype(F32) * scale, part(1), part(2).astype(F32)
            found = []
            tops = []
            for side in range(2):
                mine = left if side == 0 else ~left
                asked = jnp.where(mine, query, 0.0).astype(BF16)
                held = jnp.where(live, jnp.where(mine, value, 1.0), 0.0).astype(BF16)
                scores = jnp.where(key_live, contract(asked, key, 1, 1), NEGATIVE)
                top = jnp.max(scores, axis=-1, keepdims=True)
                raised = jnp.exp(scores - top).astype(BF16)
                found.append(contract(raised, held, 1, 0))
                tops.append(top)
            inside = jnp.where(left, found[0], found[1])
            total = jnp.where(left, found[1], found[0])
            turned = pltpu.roll(total, head, 1)
            offset = pl.multiple_of(index * pair, pair)
            mixed[span, pl.ds(offset, pair)] = (inside / turned).astype(BF16)
            if logs is None:
                continue
            logged = jnp.log(turned)
            first = tops[0] + logged[:, 0:1]
            second = tops[1] + logged[:, head : head + 1]
            known = columns[image]
            known = jnp.where(lane == 2 * index, first, known)
            columns[image] = jnp.where(lane == 2 * index + 1, second, known)
        return carry

    lax.fori_loop(0, HEADS // 2, heads, 0)
    if logs is not None:
        for image in range(count):
            logs[image] = columns[image].T[0:HEADS]


def hidden_stage(x, vec, mixed, middle, active, second, slope, full_out, full, first_load, loads):
    rows, width = x.shape
    wait_all(first_load)
    gain, shift, bias = vec[GAIN1 : GAIN1 + 1], vec[SHIFT1 : SHIFT1 + 1], vec[OUT : OUT + 1]
    middle[...] = contract(mixed[...], full_out[...], 1, 0)

    def step(here):
        total = middle[here] + x[here].astype(F32) + bias
        middle[here] = total
        unit, _ = standardized(total)
        second[here] = (unit * gain + shift).astype(BF16)

    step(pl.ds(0, rows))
    for block, load in enumerate(loads):
        wait_all(load)
        part = slice(block * width, (block + 1) * width)
        value = contract(second[...], full[:, part], 1, 0) + vec[EXPAND + block : EXPAND + block + 1]
        share = 0.5 + 0.5 * lax.erf(value * ROOT_HALF)
        active[:, part] = (value * share).astype(BF16)
        if slope is not None:
            density = ROOT_TAU * jnp.exp(-0.5 * value * value)
            slope[:, part] = (share + value * density).astype(BF16)


def forward(
    lower, upper, mixed_in, qkv, out, expand, params, meta, count, length, weight=1.0 / 64
):
    rows, width = lower.shape
    space = rows // count
    pair = 2 * width // HEADS
    attend, feed = qkv is not None, expand is not None
    both = attend and feed
    parts = len(qkv if attend else expand)
    many = len(flat(qkv if attend else expand))
    spots = parts + 1 + count
    inner = expand[0][0].shape[1] if feed else 0
    blocks = inner // width
    same = lower is upper

    def body(*refs):
        refs = list(refs)
        low = refs.pop(0)
        up = low if same else refs.pop(0)
        if not attend:
            arrived = refs.pop(0)
        lists = [[refs.pop(0) for _ in range(many)] for _ in range(attend + 2 * feed)]
        vec, info = refs.pop(0), refs.pop(0)
        if both:
            left, packed, logs, middle, slope = (refs.pop(0) for _ in range(5))
            active, second, mixed, norm = (
                left.at[:, pl.ds(start, size)]
                for start, size in ((0, inner), *((inner + width * i, width) for i in range(3)))
            )
        elif attend:
            mixed = refs.pop(0)
        else:
            middle, active = refs.pop(0), refs.pop(0)
        x, x_sem = refs.pop(0), refs.pop(0)
        section = info[parts]
        take = start_chosen(section, low, up, x, x_sem.at[0])
        if attend:
            columns, full, a_sem = (refs.pop(0) for _ in range(3))
            if not both:
                norm, packed, logs = refs.pop(0), refs.pop(0), None
            weight = lists.pop(0)
            loads = [
                start_pieces(weight, info, spots, full, a_sem, block, pl.ds(block * width, width))
                for block in range(3)
            ]
        if feed:
            full_out, full_in, o_sem, w_sem = (refs.pop(0) for _ in range(4))
            if not attend:
                mixed, second, slope = refs.pop(0), refs.pop(0), None
                extra = pltpu.make_async_copy(arrived, mixed, x_sem.at[1])
                extra.start()
            first_load = start_pieces(lists[0], info, spots, full_out, o_sem, 0, pl.ds(0, width))
            inner_loads = [
                start_pieces(lists[1], info, spots, full_in, w_sem, block, pl.ds(block * width, width))
                for block in range(blocks)
            ]
        take.wait()
        if attend:
            attention_stage(
                x, vec, norm, packed, mixed, logs, columns, full, loads, count, length
            )
        if feed:
            if not attend:
                extra.wait()
            hidden_stage(
                x, vec, mixed, middle, active, second, slope, full_out, full_in, first_load,
                inner_loads,
            )

    outs, inputs = [], [lower] if same else [lower, upper]
    scratch = [pltpu.VMEM((rows, width), BF16), pltpu.SemaphoreType.DMA((2,))]
    flops = 0
    if attend:
        outs += [
            ((rows, width), BF16),
            ((rows, 3 * width), BF16),
            ((rows, width), BF16),
            ((count, HEADS, space), F32),
        ]
        scratch += [
            pltpu.VMEM((count, space, pair), F32),
            pltpu.VMEM((width, 3 * width), BF16),
            pltpu.SemaphoreType.DMA((3, many)),
        ]
        if not feed:
            scratch += [pltpu.VMEM((rows, width), BF16), pltpu.VMEM((rows, 3 * width), BF16)]
        flops += 2 * rows * width * (3 * width + 2 * space)
    else:
        inputs += [mixed_in]
    if feed:
        outs += [
            ((rows, width), F32),
            ((rows, inner), BF16),
            ((rows, width), BF16),
            ((rows, inner), BF16),
        ]
        scratch += [
            pltpu.VMEM((width, width), BF16),
            pltpu.VMEM((width, inner), BF16),
            pltpu.SemaphoreType.DMA((1, many)),
            pltpu.SemaphoreType.DMA((blocks, many)),
        ]
        if not attend:
            scratch += [pltpu.VMEM((rows, width), BF16), pltpu.VMEM((rows, width), BF16)]
        flops += 2 * rows * width * (width + inner)
    if both:
        outs = [((rows, inner + 3 * width), BF16), outs[1], outs[3], outs[4], outs[7]]
    else:
        outs = [outs[2]] if attend else outs[:2]
    weights = (flat(qkv) if attend else []) + (flat(out) + flat(expand) if feed else [])
    return call(
        body,
        "forward" + "_attend" * attend + "_feed" * feed,
        inputs + weights + [params, meta],
        [ANY] * (len(inputs) + len(weights)) + [VMEM, SMEM],
        outs,
        scratch,
        flops,
        weight,
    )


def output_forward(middle, active, pieces, params, meta, count, weight=1.0 / 64):
    rows, width = middle.shape
    inner = sum(piece.shape[0] for piece in flat(pieces))
    space = rows // count
    parts, many = len(pieces), len(flat(pieces))
    spots = parts + 1 + count
    blocks = 2
    part_width = width // blocks

    def body(*refs):
        refs = list(refs)
        mid_in, act_in = refs.pop(0), refs.pop(0)
        reduce = [refs.pop(0) for _ in range(many)]
        vec, info, result, mid, act, full, x_sem, w_sem = refs
        copies = [
            pltpu.make_async_copy(act_in.at[:, pl.ds(0, inner)], act, x_sem.at[0]),
            pltpu.make_async_copy(mid_in, mid, x_sem.at[1]),
        ]
        copies[0].start()
        loads = [
            start_pieces(reduce, info, spots, full, w_sem, block, pl.ds(block * part_width, part_width))
            for block in range(blocks)
        ]
        copies[1].start()
        copies[0].wait()
        for block in range(blocks):
            wait_all(loads[block])
            if block == 0:
                copies[1].wait()
            part = slice(block * part_width, (block + 1) * part_width)
            value = contract(act[...], full[:, part], 1, 0) + mid[:, part] + vec[FEED : FEED + 1, part]
            for image in range(count):
                alive = jnp.where(info[parts + 1 + image] > 0, 1.0, 0.0)
                here = slice(image * space, (image + 1) * space)
                result[here, part] = (value[here] * alive).astype(BF16)

    return call(
        body,
        "output_forward",
        [middle, active] + flat(pieces) + [params, meta],
        [ANY] * (2 + many) + [VMEM, SMEM],
        [((rows, width), BF16)],
        [
            pltpu.VMEM((rows, width), F32),
            pltpu.VMEM((rows, inner), BF16),
            pltpu.VMEM((inner, width), BF16),
            pltpu.SemaphoreType.DMA((2,)),
            pltpu.SemaphoreType.DMA((blocks, many)),
        ],
        2 * rows * width * inner,
        weight,
    )[0]


def hidden_back_stage(
    grad, vec, info, feed, slope, middle, hidden, second, mid_grad, branch, sums, inner_sums, full_out,
    full, deep, first_load, load, for_slope, for_middle, tallies, count, parts,
):
    rows, width = grad.shape
    space = rows // count
    half = width // 2
    for image in range(count):
        alive = jnp.where(info[parts + 1 + image] > 0, 1.0, 0.0)
        here = slice(image * space, (image + 1) * space)
        feed[here] = (grad[here].astype(F32) * alive).astype(BF16)
    for_slope.wait()
    for index in range(parts):
        wait_all(first_load[index])
        where = pl.multiple_of(info[index] * deep, deep)
        value = contract(feed[...], full_out[pl.ds(where, deep)], 1, 1)
        value = (value * slope[:, pl.ds(where, deep)].astype(F32)).astype(BF16)
        hidden[:, pl.ds(where, deep)] = value
        inner_sums[:, pl.ds(where, deep)] = jnp.sum(value.astype(F32), axis=0, keepdims=True)
    wait_all(load)
    for block in range(2):
        second[:, block * half : (block + 1) * half] = contract(
            hidden[...], full[block * half : (block + 1) * half], 1, 1
        )
    for_middle.wait()
    gain = vec[GAIN1 : GAIN1 + 1]
    tallies[...] = jnp.zeros_like(tallies)

    def step(here):
        unit, scale = standardized(middle[here])
        down = second[here]
        top = feed[here].astype(F32)
        total = top + norm_pull(down, gain, unit, scale)
        low = total.astype(BF16)
        mid_grad[here] = total
        branch[here] = low
        tallies[0] += eights(down * unit)
        tallies[1] += eights(down)
        tallies[2] += eights(low.astype(F32))
        tallies[3] += eights(top)

    step(pl.ds(0, rows))
    for index in range(4):
        sums[index : index + 1] = jnp.sum(tallies[index], axis=0, keepdims=True)


def attention_back_stage(
    x, vec, branch, mid_grad, packed, mixed, logs, grads, result, sums, down, normal, stage, full_out,
    full, first_load, load, takes, tallies, count, length,
):
    rows, width = x.shape
    space = rows // count
    head = width // HEADS
    pair = 2 * head
    scale = head**-0.5
    half = width // 2
    wait_all(first_load)
    down[...] = contract(branch[...], full_out[...], 1, 1).astype(BF16)
    wait_all(takes)
    owner = lax.shift_right_logical(
        lax.broadcasted_iota(jnp.int32, (HEADS, width), 1), head.bit_length() - 1
    )
    chosen = jnp.where(
        owner == lax.broadcasted_iota(jnp.int32, (HEADS, width), 0), 1.0, 0.0
    ).astype(BF16)
    left = lax.broadcasted_iota(jnp.int32, (space, pair), 1) < head
    live = lax.broadcasted_iota(jnp.int32, (space, pair), 0) < length
    key_live = lax.broadcasted_iota(jnp.int32, (space, space), 0) < length
    for image in range(count):
        span = pl.ds(image * space, space)
        product = down[span].astype(F32) * mixed[span].astype(F32)
        coarse = product.astype(BF16)
        fine = (product - coarse.astype(F32)).astype(BF16)
        stage[image, :, 0:space] = contract(chosen, coarse, 1, 1) + contract(chosen, fine, 1, 1)

    def heads(index, carry):
        for image in range(count):
            span = pl.ds(image * space, space)

            def part(block):
                offset = pl.multiple_of(block * width + index * pair, pair)
                return packed[span, pl.ds(offset, pair)]

            query, key, value = part(0), part(1), part(2)
            wide = key.astype(F32) * scale
            value = value.astype(F32)
            arrived = down[span, pl.ds(pl.multiple_of(index * pair, pair), pair)]
            found = []
            for side in range(2):
                mine = left if side == 0 else ~left
                log = logs[image, pl.ds(2 * index + side, 1), :]
                dot = stage[image, pl.ds(2 * index + side, 1), 0:space]
                scores = contract(jnp.where(mine, wide, 0.0).astype(BF16), query, 1, 1)
                chance = jnp.exp(jnp.where(key_live, scores - log, NEGATIVE))
                back = contract(jnp.where(mine, value, 0.0).astype(BF16), arrived, 1, 1)
                change = (chance * (back - dot)).astype(BF16)
                found.append(
                    (
                        contract(change, key, 0, 0),
                        contract(change, query, 1, 0),
                        contract(chance.astype(BF16), arrived, 1, 0),
                    )
                )
            for block, factor in enumerate((scale, scale, 1.0)):
                total = jnp.where(left, found[0][block], found[1][block]) * factor
                offset = pl.multiple_of(block * width + index * pair, pair)
                grads[span, pl.ds(offset, pair)] = jnp.where(live, total, 0.0).astype(BF16)
        return carry

    lax.fori_loop(0, HEADS // 2, heads, 0)
    wait_all(load)
    for block in range(2):
        normal[:, block * half : (block + 1) * half] = contract(
            grads[...], full[block * half : (block + 1) * half], 1, 1
        )
    gain = vec[GAIN0 : GAIN0 + 1]
    tallies[...] = jnp.zeros_like(tallies)

    def step(here):
        unit, rate = standardized(x[here].astype(F32))
        grad = normal[here]
        tallies[0] += eights(grad * unit)
        tallies[1] += eights(grad)
        result[here] = (mid_grad[here] + norm_pull(grad, gain, unit, rate)).astype(BF16)

    step(pl.ds(0, rows))
    for index in range(2):
        sums[index : index + 1] = jnp.sum(tallies[index], axis=0, keepdims=True)
    sums[2:3] = jnp.sum(grads[:, 0:width].astype(F32), axis=0, keepdims=True)
    sums[3:4] = jnp.sum(grads[:, 2 * width : 3 * width].astype(F32), axis=0, keepdims=True)


def backward(
    start, lower, upper, kept_low, kept_up, reduce, expand, out, qkv, params, meta, count, length,
    mixed_at, weight=1.0 / 64,
):
    feed, attend = reduce is not None, qkv is not None
    rows, width = start[0].shape
    space = rows // count
    pair = 2 * width // HEADS
    parts = len(reduce if feed else qkv)
    many = len(flat(reduce if feed else qkv))
    spots = parts + 1 + count
    inner = expand[0][0].shape[1] if feed else 0
    deep = inner // parts
    both = feed and attend
    choices = []
    if feed:
        choices += [(kept_low[0], kept_up[0]), (kept_low[1], kept_up[1])]
        if start[0] is not start[1]:
            choices += [start]
    if attend:
        choices += [(kept_low[index], kept_up[index]) for index in (2, 3, 4)]
        choices += [(lower, upper)]
    plain = [start[0]] if feed and start[0] is start[1] else [] if feed else list(start)
    operands = []
    for low, up in choices:
        operands += [low] if low is up else [low, up]

    def body(*refs):
        refs = list(refs)
        firsts = [refs.pop(0) for _ in plain]
        pairs = []
        for low, up in choices:
            one = refs.pop(0)
            pairs.append((one, one if low is up else refs.pop(0)))
        lists = [[refs.pop(0) for _ in range(many)] for _ in range(2 * feed + 2 * attend)]
        vec, info = refs.pop(0), refs.pop(0)
        section = info[parts]
        if feed:
            right, feed_sums, inner_sums = (refs.pop(0) for _ in range(3))
            hidden = right.at[:, pl.ds(0, inner)]
            branch = right.at[:, pl.ds(inner, width)]
            mid_grad = None if both else refs.pop(0)
        if attend:
            grads, result, sums = (refs.pop(0) for _ in range(3)) if not both else (None, refs.pop(0), refs.pop(0))
        if both:
            feed_grad = right.at[:, pl.ds(inner + width, width)]
            grads = right.at[:, pl.ds(inner + 2 * width, 3 * width)]
        tallies, x_sem = refs.pop(0), refs.pop(0)
        if feed:
            grad, slope, middle, second, full_out, full, o_sem, w_sem = (
                refs.pop(0) for _ in range(8)
            )
            if both:
                mid_grad, keep = refs.pop(0), feed_grad
            else:
                keep = refs.pop(0)
            begin = pairs.pop(2) if start[0] is not start[1] else (firsts[0], firsts[0])
            take = start_chosen(section, *begin, grad, x_sem.at[0])
            for_slope = start_chosen(section, *pairs.pop(0), slope, x_sem.at[1])
            every = start_pieces(lists.pop(0), info, spots, full_out, o_sem, 0, pl.ds(0, width))
            first_load = [[every.pop(0) for _ in group] for group in reduce]
            for_middle = start_chosen(section, *pairs.pop(0), middle, x_sem.at[2])
            load = start_pieces(lists.pop(0), info, spots, full, w_sem, 0, pl.ds(0, inner))
        if attend:
            x, packed, mixed, logs, down, normal, stage, full_o, full_q, p_sem, q_sem = (
                refs.pop(0) for _ in range(11)
            )
            if not feed:
                branch, mid_grad = refs.pop(0), refs.pop(0)
                givens = [
                    pltpu.make_async_copy(source, target, x_sem.at[index])
                    for index, (source, target) in enumerate(zip(firsts, (branch, mid_grad)))
                ]
                for given in givens:
                    given.start()
            project_load = start_pieces(lists.pop(0), info, spots, full_o, p_sem, 0, pl.ds(0, width))
            sames = [one is two for one, two in pairs]
            pairs[1] = tuple(one.at[:, pl.ds(mixed_at, width)] for one in pairs[1])
            takes = [
                start_chosen(section, *pairs[index], target, x_sem.at[3 + index], sames[index])
                for index, target in ((1, mixed), (0, packed), (2, logs), (3, x))
            ]
            last_load = start_pieces(lists.pop(0), info, spots, full_q, q_sem, 0, pl.ds(0, 3 * width))
            if not feed:
                wait_all(givens)
        if feed:
            take.wait()
            hidden_back_stage(
                grad, vec, info, keep, slope, middle, hidden, second, mid_grad, branch, feed_sums,
                inner_sums, full_out, full, deep, first_load, load, for_slope, for_middle, tallies,
                count, parts,
            )
        if attend:
            attention_back_stage(
                x, vec, branch, mid_grad, packed, mixed, logs, grads, result, sums, down, normal,
                stage, full_o, full_q, project_load, last_load, takes, tallies, count, length,
            )

    outs = []
    scratch = [pltpu.VMEM((4, 8, width), F32), pltpu.SemaphoreType.DMA((7,))]
    flops = 0
    if feed:
        outs += [
            ((rows, inner + (5 if both else 1) * width), BF16),
            ((8, width), F32),
            ((1, inner), F32),
        ]
        if not both:
            outs += [((rows, width), F32)]
        scratch += [
            pltpu.VMEM((rows, width), BF16),
            pltpu.VMEM((rows, inner), BF16),
            pltpu.VMEM((rows, width), F32),
            pltpu.VMEM((rows, width), F32),
            pltpu.VMEM((inner, width), BF16),
            pltpu.VMEM((width, inner), BF16),
            pltpu.SemaphoreType.DMA((1, many)),
            pltpu.SemaphoreType.DMA((1, many)),
        ]
        scratch += [pltpu.VMEM((rows, width), F32 if both else BF16)]
        flops += 4 * rows * width * inner
    if attend:
        outs += [] if both else [((rows, 3 * width), BF16)]
        outs += [((rows, width), BF16), ((8, width), F32)]
        scratch += [
            pltpu.VMEM((rows, width), BF16),
            pltpu.VMEM((rows, 3 * width), BF16),
            pltpu.VMEM((rows, width), BF16),
            pltpu.VMEM((count, HEADS, space), F32),
            pltpu.VMEM((rows, width), BF16),
            pltpu.VMEM((rows, width), F32),
            pltpu.VMEM((count, HEADS, 2 * pair), F32),
            pltpu.VMEM((width, width), BF16),
            pltpu.VMEM((width, 3 * width), BF16),
            pltpu.SemaphoreType.DMA((1, many)),
            pltpu.SemaphoreType.DMA((1, many)),
        ]
        if not feed:
            scratch += [pltpu.VMEM((rows, width), BF16), pltpu.VMEM((rows, width), F32)]
        flops += 2 * rows * width * (4 * width + 5 * space)
    weights = (flat(reduce) + flat(expand) if feed else []) + (
        flat(out) + flat(qkv) if attend else []
    )
    return call(
        body,
        "backward" + "_feed" * feed + "_attend" * attend,
        plain + operands + weights + [params, meta],
        [ANY] * (len(plain) + len(operands) + len(weights)) + [VMEM, SMEM],
        outs,
        scratch,
        flops,
        weight,
    )


def weight_gradient(
    lefts, rights, meta, parts, blocks, quarter, rows_of, columns_of, name, weight=1.0 / 64
):
    terms = len(lefts)
    first_row, height = rows_of
    first_column, breadth = columns_of
    rows = lefts[0].shape[0]
    operands = list(lefts)
    places = []
    for pair in rights:
        found = []
        for array, _ in pair:
            if not any(array is other for other in operands):
                operands.append(array)
            found.append(next(i for i, other in enumerate(operands) if other is array))
        places.append(found)

    def body(*refs):
        sources, info = refs[: len(operands)], refs[len(operands)]
        results = refs[len(operands) + 1 : len(operands) + 1 + len(blocks)]
        left_full, right_full, l_sem, r_sem = refs[len(operands) + 1 + len(blocks) :]
        section = info[parts]
        waits = []
        for term in range(terms):
            sides = [
                sources[place].at[:, pl.ds(column + first_column, breadth)]
                for place, (_, column) in zip(places[term], rights[term])
            ]
            same = rights[term][0] is rights[term][1]
            target = right_full.at[pl.ds(term * rows, rows)]
            waits.append(start_chosen(section, *sides, target, r_sem.at[term], same))
        loads = []
        for index, block in enumerate(blocks):
            start = pl.multiple_of(info[block] * quarter + first_row, 128)
            for term in range(terms):
                copy = pltpu.make_async_copy(
                    sources[term].at[:, pl.ds(start, height)],
                    left_full.at[index, pl.ds(term * rows, rows)],
                    l_sem.at[index, term],
                )
                copy.start()
                loads.append(copy)
        wait_all(waits)
        for index in reversed(range(len(blocks))):
            wait_all(loads[index * terms : (index + 1) * terms])
            results[index][...] = contract(left_full[index], right_full[...], 0, 0).astype(BF16)

    return call(
        body,
        name,
        operands + [meta],
        [ANY] * len(operands) + [SMEM],
        [((height, breadth), BF16)] * len(blocks),
        [
            pltpu.VMEM((len(blocks), terms * rows, height), BF16),
            pltpu.VMEM((terms * rows, breadth), BF16),
            pltpu.SemaphoreType.DMA((len(blocks), terms)),
            pltpu.SemaphoreType.DMA((terms,)),
        ],
        2 * len(blocks) * terms * rows * height * breadth,
        weight,
    )


def after(value, *earlier):
    return lax.optimization_barrier((value,) + earlier)[0]


def added(*values):
    total = values[0].astype(F32)
    for value in values[1:]:
        total = total + value.astype(F32)
    return total.astype(values[0].dtype)


class FourByFour:
    parts = 4
    blocks = (0, 2)

    def __init__(self):
        self.begun = 0
        self.group = lax.axis_index("group")
        self.place = lax.axis_index("replica")
        self.order = [self.group ^ part for part in range(4)]
        odd = self.place % 2
        halves = [2 * self.order[part] + half for part in (2, 3) for half in (odd, 1 - odd)]
        self.spots = self.order[:2] + halves

    def core(self, block):
        return lax.ppermute(block, "group", [(i, i ^ 1) for i in range(4)])

    def across(self, block):
        return lax.ppermute(block, "group", [(i, i ^ 2) for i in range(4)])

    def beside(self, block):
        return lax.ppermute(block, "replica", [(i, i ^ 1) for i in range(4)])

    def gather(self, small, blocks):
        far, halves, sibling = self.across(small), [], []
        odd = self.place % 2
        for index, block in enumerate(blocks):
            rows = block.shape[0] // 2
            half = lax.dynamic_slice_in_dim(block, odd * rows, rows)
            half = after(half, far if index < 2 else halves[index - 2])
            halves.append(self.across(half))
            sibling.append(self.core(after(block, sibling[-1]) if index else block))
        others = []
        for half in halves:
            others.append(self.beside(after(half, others[-1]) if others else half))

        def pieces(index, *tokens):
            one, two = (after(half, *tokens) for half in (halves[index], others[index]))
            return [
                [blocks[index]],
                [sibling[index]],
                [halves[index], others[index]],
                [self.core(one), self.core(two)],
            ]

        near = self.core(small)
        return [small, near, far, self.core(far)], [
            partial(pieces, index) for index in range(len(blocks))
        ]

    def shared(self, block):
        return [block, self.core(block)]

    def total(self, blocks, own):
        passed = self.across(blocks[1])
        token = yield
        mine = added(after(blocks[0], token), passed)
        if not own:
            turn = [(place + self.begun) % 4 for place in range(4)]
            self.begun += 1
            whole = lax.psum(mine, "replica", axis_index_groups=[turn])
            token = yield mine
            yield after(whole, token)
            return
        inward = lax.ppermute(mine, "replica", [(0, 1), (3, 2)])
        token = yield mine
        joined = added(after(mine, token), inward)
        crossing = lax.ppermute(joined, "replica", [(1, 2), (2, 1)])
        token = yield joined
        summed = added(after(joined, token), crossing)
        outward = lax.ppermute(summed, "replica", [(1, 0), (2, 3)])
        token = yield summed
        inner = (self.place == 1) | (self.place == 2)
        yield jnp.where(inner, after(summed, token), outward)


class General:
    def __init__(self):
        self.parts = lax.axis_size("group")
        self.blocks = tuple(range(self.parts))
        self.order = self.spots = [jnp.int32(part) for part in range(self.parts)]

    def gather(self, small, blocks):
        def pieces(block):
            whole = lax.all_gather(block, "group", axis=0)
            return [whole[part] for part in range(self.parts)]

        found = [[[piece] for piece in pieces(block)] for block in blocks]
        return pieces(small), [lambda *tokens, groups=groups: groups for groups in found]

    def shared(self, block):
        return [block]

    def total(self, blocks, own):
        yield
        mine = lax.psum_scatter(jnp.stack(blocks), "group", scatter_dimension=0)
        yield mine
        yield lax.psum(mine, "replica")


def shifted(block, distance):
    devices = range(lax.axis_size("section"))
    route = [(i - distance, i) for i in devices if i - distance in devices]
    return lax.ppermute(block, "section", route)


def in_order(pieces, order):
    place = jnp.stack(order)
    stacked = []
    for block in range(len(pieces)):
        chosen = pieces[0]
        for part in range(1, len(pieces)):
            chosen = jnp.where(place[part] == block, pieces[part], chosen)
        stacked.append(chosen)
    return jnp.stack(stacked)


class Sequence:
    def __init__(self, net, token):
        self.net, self.sums, self.results, self.token = net, {}, {}, token

    def now(self, value):
        return after(value, self.token)

    def ran(self, value):
        self.token = value

    def add(self, name, blocks, own):
        self.sums[name] = self.net.total(blocks, own)
        next(self.sums[name])

    def step(self, *names):
        for name in names:
            try:
                self.results[name] = self.token = self.sums[name].send(self.token)
            except StopIteration:
                continue

    def finish(self, name):
        while True:
            try:
                self.results[name] = self.sums[name].send(self.token)
            except StopIteration:
                return self.results[name]


def per_device(
    images,
    cotangent,
    counts,
    qkv_weight,
    out_weight,
    expand_weight,
    reduce_weight,
    norm_gains,
    biases,
    expand_bias,
):
    micro, slots, length, width = images.shape
    space = padded(length)
    section = lax.axis_index("section")
    first = section == 0
    sizes = (lax.axis_size("group"), lax.axis_size("replica"))
    net = FourByFour() if sizes == (4, 4) else General()
    parts = net.parts
    share = width // parts
    batches = tuple(range(micro))

    def rows_of(array):
        fulls = [jnp.pad(array[batch], ((0, 0), (0, space - length), (0, 0))) for batch in batches]
        return [full.reshape(slots * space, width) for full in fulls]

    def images_of(array):
        return array.reshape(slots, space, width)[:, :length]

    inputs, targets = rows_of(images), rows_of(cotangent)
    small = jnp.concatenate([norm_gains[0], biases[0], expand_bias[0].reshape(-1, share)])
    vectors, (qkv, out, expand, reduce) = net.gather(
        small, [qkv_weight[0], out_weight[0], expand_weight[0], reduce_weight[0]]
    )
    vectors = in_order(vectors, net.order)
    top = vectors[:, :8].transpose(1, 0, 2).reshape(8, width)
    bottom = vectors[:, 8:].reshape(-1, width)
    params = jnp.concatenate([top, bottom]).astype(F32)
    slot = jnp.arange(slots, dtype=jnp.int32)
    alive = [(slot < counts[batch, 0]).astype(jnp.int32) for batch in batches]
    head = jnp.stack(net.order + [section]).astype(jnp.int32)

    spots = jnp.stack(net.spots).astype(jnp.int32)

    def meta(living):
        return jnp.concatenate([head, living, spots])

    infos = [meta(alive[batch]) for batch in batches]

    qkv = qkv(params, *inputs, *targets)
    attended = []
    for batch in batches:
        start = inputs[batch] if batch == 0 else after(inputs[batch], attended[-1][0])
        attended.append(
            forward(start, start, None, qkv, None, None, params, infos[batch], slots, length)
        )
    out = out(attended[-1][0])
    expand = expand(out[-1][0])
    fed = []
    for batch in batches:
        start = inputs[batch] if batch == 0 else after(inputs[batch], fed[-1][0])
        fed.append(
            forward(start, start, attended[batch][0], None, out, expand, params, infos[batch], slots, length)
        )
    reduce = reduce(fed[-1][0])
    early, incoming = [], []
    for batch in batches:
        middle, active = fed[batch][:2]
        if batch:
            active = after(active, early[-1])
        early.append(output_forward(middle, active, reduce, params, infos[batch], slots))
        incoming.append(shifted(early[batch], 1))

    inner = expand[0][0].shape[1]
    mixed_at = inner + width
    kept, lefts, rights, results = [], [], [], []
    sums_a, sums_b, sums_c, returning = [], [], [], []
    token = early[-1]
    for batch in batches:
        start = after(incoming[batch], token)
        left, packed, logs, middle, slope = forward(
            inputs[batch], start, None, qkv, out, expand, params, infos[batch], slots, length, 8.0
        )
        kept.append((slope, middle, packed, left, logs))
        lefts.append(net.shared(left))
        if batch == 0:
            pair, sides = (targets[0], targets[0]), (kept[0], kept[0])
            lower, chosen = incoming[0], infos[0]
        else:
            pair = (returning[batch - 1], targets[batch])
            sides = (kept[batch - 1], kept[batch])
            lower = inputs[batch - 1]
            chosen = meta(jnp.where(first, alive[batch - 1], alive[batch]))
        right, some, more, result, rest = backward(
            pair, lower, incoming[batch], sides[0], sides[1], reduce, expand, out, qkv, params, chosen,
            slots, length, mixed_at, 8.0,
        )
        token = result
        rights.append(net.shared(right))
        results.append(result)
        sums_a.append(some)
        sums_b.append(more)
        sums_c.append(rest)
        returning.append(shifted(result, -1))
    late = []
    for batch in batches:
        ready = lefts[batch][1:] + (rights[batch][1:] if batch < micro - 1 else [])
        active = after(kept[batch][3], token, *ready)
        late.append(output_forward(kept[batch][1], active, reduce, params, infos[batch], slots, 8.0))
        token = late[-1]

    last = micro - 1
    run = Sequence(net, token)
    arrived = run.now(returning[last])
    living = jnp.repeat(alive[last] > 0, space)[:, None]
    masked = net.shared(jnp.where(living, arrived, jnp.zeros_like(arrived)))
    many = len(masked)

    def gradient(name, left_at, final, final_at, right_at, quarter, rows, columns, own, weight=1.0 / 64):
        left = [lefts[batch][side] for batch in batches for side in range(many)]
        right = []
        for batch in batches:
            for side in range(many):
                upper = (rights[batch][side], right_at)
                lower = (final[side], final_at) if batch == last else (rights[batch + 1][side], right_at)
                right.append((lower, upper))
        blocks = weight_gradient(
            left, right, run.now(head), parts, net.blocks, quarter, (left_at + rows[0], rows[1]), columns,
            name, weight,
        )
        run.ran(blocks[0])
        return blocks

    def summed(name, *rest):
        run.add(name, gradient(name, *rest), rest[7])

    def reduce_part(index, own, weight=1.0 / 64):
        deep = inner // parts
        step = deep // 2
        summed(
            f"reduce{index}", 0, masked, 0, inner + width, deep, (index * step, step), (0, width), own,
            weight,
        )

    reduce_part(0, False)
    start = run.now(arrived)
    final, some, more, mid = backward(
        (start, start), None, None, kept[last], kept[last], reduce, expand, None, None, params,
        infos[last], slots, length, mixed_at,
    )
    run.ran(final)
    branch = final[:, inner:]
    finals, branches = net.shared(final[:, :inner]), net.shared(branch)
    sums_a.append(some)
    sums_b.append(more)
    run.step("reduce0")
    reduce_part(1, False, 16.0)

    def expand_part(index, cut, own):
        begin, step = cut
        summed(f"expand{index}", inner, finals, 0, 0, share, (0, share), (begin, step), own)

    quarter = inner // 4
    expand_part(0, (0, 2 * quarter), True)
    expand_part(1, (2 * quarter, quarter), True)
    expand_part(2, (3 * quarter, quarter), True)
    run.step("reduce1")
    summed("project", mixed_at, branches, 0, inner, share, (0, share), (0, width), True)
    grads, result, rest = backward(
        (run.now(branch), mid), inputs[last], inputs[last], kept[last], kept[last], None, None, out, qkv,
        params, infos[last], slots, length, mixed_at, 16.0,
    )
    run.ran(result)
    grads = net.shared(grads)
    results.append(result)
    sums_c.append(rest)
    run.step("expand0")

    def over_batches(values):
        return sum(jnp.where(first, values[batch + 1], values[batch]) for batch in batches)

    some, more, rest = over_batches(sums_a), over_batches(sums_b), over_batches(sums_c)
    rows = jnp.concatenate([rest[0:1], some[0:1], rest[1:2], some[1:2], rest[2:4], some[2:4]])
    rows = rows.reshape(8, parts, share).transpose(1, 0, 2)
    rows = jnp.concatenate([rows, more.reshape(parts, -1, share)], axis=1)
    rows = sum(net.shared(rows))
    rows = jnp.stack(
        [lax.dynamic_index_in_dim(rows, net.order[block], 0, keepdims=False) for block in net.blocks]
    )
    count, step = rows.shape[1], width // 2
    rows = rows.reshape(len(net.blocks), -1)
    rows = jnp.pad(rows, ((0, 0), (0, -rows.shape[1] % (32 * step)))).reshape(len(net.blocks), -1, 2 * step)

    def qkv_part(index):
        begin, breadth = ((0, 2 * step), (2 * step, 2 * step), (4 * step, 2 * step))[index]
        return gradient(
            f"qkv{index}", inner + 2 * width, grads, 0, inner + 2 * width, share, (0, share),
            (begin, breadth), True,
        )

    run.add("qkv0", qkv_part(0), True)
    run.step("expand1")
    run.add("qkv1", qkv_part(1), True)
    run.step("expand0", "reduce0")
    blocks = qkv_part(2)
    run.add("qkv2", [jnp.concatenate([one, two]) for one, two in zip(blocks, rows.astype(BF16))], True)
    run.step(
        "expand2", "reduce1", "project", "expand1", "expand2", "expand0", "qkv0", "expand1", "qkv1", "project",
        "expand2", "qkv2", "qkv0", "expand0", "expand1", "qkv1", "project", "expand2", "qkv0", "qkv2", "project",
        "qkv1", "qkv0", "qkv2", "qkv1", "qkv2",
    )
    weights = {name: run.finish(name) for name in run.sums}
    vector = weights["qkv2"][share:].reshape(-1)[: count * share].reshape(count, share).astype(F32)

    def chosen(lowers, uppers):
        return jnp.stack(
            [images_of(jnp.where(first, low, up)) for low, up in zip(lowers, uppers)]
        )[None]

    def joined(axis, *names):
        return jnp.concatenate([weights[name] for name in names], axis=axis).astype(F32)[None]

    return (
        chosen(early, late),
        chosen(results[1:], results[:-1]),
        jnp.concatenate([weights["qkv0"], weights["qkv1"], weights["qkv2"][:share]], axis=1).astype(F32)[None],
        weights["project"].astype(F32)[None],
        joined(1, "expand0", "expand1", "expand2"),
        joined(0, "reduce0", "reduce1"),
        vector[None, 0:2],
        vector[None, 2:8],
        vector[8:].reshape(1, -1),
    )


def solution(mesh):
    placed = (
        P(None, ("group", "replica"), None, None),
        P(None, ("group", "replica"), None, None),
        P(None, ("group", "replica")),
        P("section", "group", None),
        P("section", "group", None),
        P("section", "group", None),
        P("section", "group", None),
        P("section", None, "group"),
        P("section", None, "group"),
        P("section", "group"),
    )
    return jax.shard_map(
        per_device,
        mesh=mesh,
        in_specs=placed,
        out_specs=(
            P("section", None, ("group", "replica"), None, None),
            P("section", None, ("group", "replica"), None, None),
            P("section", "group", None),
            P("section", "group", None),
            P("section", "group", None),
            P("section", "group", None),
            P("section", None, "group"),
            P("section", None, "group"),
            P("section", "group"),
        ),
        check_vma=False,
    )
```

```python
from functools import partial

import jax
import jax.numpy as jnp
from jax import lax
from jax.experimental import pallas as pl
from jax.experimental.pallas import tpu as pltpu
from jax.sharding import PartitionSpec as P

HEADS = 16
EPSILON = 1e-06
NEGATIVE = -1e30
F32 = jnp.float32
BF16 = jnp.bfloat16
LIGHT, HEAVY = 1.0 / 64, 16.0
VMEM_LIMIT = 58 * 2**20
ROOT_HALF = 0.7071067811865476
ROOT_TAU = 0.3989422804014327
ANY = pl.BlockSpec(memory_space=pl.ANY)
VMEM = pl.BlockSpec(memory_space=pltpu.VMEM)
SMEM = pl.BlockSpec(memory_space=pltpu.SMEM)
GAIN0, GAIN1, SHIFT0, SHIFT1, QUERY, VALUE, OUT, FEED, EXPAND = range(9)


def padded(length):
    return -(-length // 16) * 16


def contract(left, right, left_dim, right_dim):
    return lax.dot_general(
        left, right, (((left_dim,), (right_dim,)), ((), ())), preferred_element_type=F32
    )


def standardized(values):
    center = values - jnp.mean(values, axis=-1, keepdims=True)
    spread = jnp.mean(center * center, axis=-1, keepdims=True)
    scale = lax.rsqrt(spread + EPSILON)
    return center * scale, scale


def norm_pull(grad, gain, unit, scale):
    scaled = grad * gain
    mean = jnp.mean(scaled, axis=-1, keepdims=True)
    along = jnp.mean(scaled * unit, axis=-1, keepdims=True)
    return scale * (scaled - mean - unit * along)


def call(body, name, operands, specs, outs, scratch, flops, weight=LIGHT):
    moved = sum(o.size * o.dtype.itemsize for o in operands)
    out_shape = [jax.ShapeDtypeStruct(shape, dtype) for shape, dtype in outs]
    moved += sum(o.size * o.dtype.itemsize for o in out_shape)
    return pl.pallas_call(
        body,
        out_shape=out_shape,
        in_specs=specs,
        out_specs=[VMEM] * len(outs),
        scratch_shapes=scratch,
        compiler_params=pltpu.CompilerParams(vmem_limit_bytes=VMEM_LIMIT),
        cost_estimate=pl.CostEstimate(flops=int(flops * weight), bytes_accessed=int(moved * weight), transcendentals=0),
        name=name,
    )(*operands)


def flat(groups):
    return [piece for group in groups for piece in group]


def start_pieces(pieces, info, first, target, sems, slot, columns, shift=0):
    begin, size = columns
    columns = pl.ds(begin, size)
    copies = []
    for index, piece in enumerate(pieces):
        rows = piece.shape[0]
        where = pl.multiple_of(info[first + index] * rows, rows)
        copy = pltpu.make_async_copy(
            piece.at[:, pl.ds(begin + shift, size)],
            target.at[pl.ds(where, rows), columns],
            sems.at[slot, index],
        )
        copy.start()
        copies.append(copy)
    return copies


def wait_all(copies):
    for copy in copies:
        copy.wait()


def start_chosen(section, lower, upper, target, sem, same=False):
    if lower is upper or same:
        copy = pltpu.make_async_copy(lower, target, sem)
        copy.start()
        return copy

    @pl.when(section == 0)
    def _():
        pltpu.make_async_copy(lower, target, sem).start()

    @pl.when(section != 0)
    def _():
        pltpu.make_async_copy(upper, target, sem).start()

    return pltpu.make_async_copy(lower, target, sem)


def eights(values):
    return jnp.sum(values.reshape(-1, 8, values.shape[-1]), axis=0)


def attention_stage(x, vec, norm, packed, mixed, logs, columns, full, loads, count, length):
    rows, width = x.shape
    space = rows // count
    head = width // HEADS
    pair = 2 * head
    scale = head**-0.5
    gain, shift = vec[GAIN0 : GAIN0 + 1], vec[SHIFT0 : SHIFT0 + 1]

    def step(here):
        unit, _ = standardized(x[here].astype(F32))
        norm[here] = (unit * gain + shift).astype(BF16)

    step(pl.ds(0, rows))
    for block in range(3):
        wait_all(loads[block])
        done = contract(norm[...], full[:, block * width : (block + 1) * width], 1, 0)
        if block != 1:
            bias = QUERY if block == 0 else VALUE
            done = done + vec[bias : bias + 1]
        packed[:, block * width : (block + 1) * width] = done.astype(BF16)
    lane = lax.broadcasted_iota(jnp.int32, (space, pair), 1)
    left = lane < head
    live = lax.broadcasted_iota(jnp.int32, (space, pair), 0) < length
    key_live = lax.broadcasted_iota(jnp.int32, (space, space), 1) < length
    columns[...] = jnp.zeros_like(columns)

    def heads(index, carry):
        for image in range(count):
            span = pl.ds(image * space, space)

            def part(block):
                offset = pl.multiple_of(block * width + index * pair, pair)
                return packed[span, pl.ds(offset, pair)]

            query, key, value = part(0).astype(F32) * scale, part(1), part(2).astype(F32)
            found = []
            tops = []
            for side in range(2):
                mine = left if side == 0 else ~left
                asked = jnp.where(mine, query, 0.0).astype(BF16)
                held = jnp.where(live, jnp.where(mine, value, 1.0), 0.0).astype(BF16)
                scores = jnp.where(key_live, contract(asked, key, 1, 1), NEGATIVE)
                top = jnp.max(scores, axis=-1, keepdims=True)
                raised = jnp.exp(scores - top).astype(BF16)
                found.append(contract(raised, held, 1, 0))
                tops.append(top)
            inside = jnp.where(left, found[0], found[1])
            total = jnp.where(left, found[1], found[0])
            turned = pltpu.roll(total, head, 1)
            offset = pl.multiple_of(index * pair, pair)
            mixed[span, pl.ds(offset, pair)] = (inside / turned).astype(BF16)
            if logs is None:
                continue
            logged = jnp.log(turned)
            first = tops[0] + logged[:, 0:1]
            second = tops[1] + logged[:, head : head + 1]
            known = columns[image]
            known = jnp.where(lane == 2 * index, first, known)
            columns[image] = jnp.where(lane == 2 * index + 1, second, known)
        return carry

    lax.fori_loop(0, HEADS // 2, heads, 0)
    if logs is not None:
        for image in range(count):
            logs[image] = columns[image].T[0:HEADS]


def hidden_stage(x, vec, mixed, middle, active, second, slope, full_out, full, first_load, loads):
    rows, width = x.shape
    wait_all(first_load)
    gain, shift, bias = vec[GAIN1 : GAIN1 + 1], vec[SHIFT1 : SHIFT1 + 1], vec[OUT : OUT + 1]
    middle[...] = contract(mixed[...], full_out[...], 1, 0)

    def step(here):
        total = middle[here] + x[here].astype(F32) + bias
        middle[here] = total
        unit, _ = standardized(total)
        second[here] = (unit * gain + shift).astype(BF16)

    step(pl.ds(0, rows))
    for block, load in enumerate(loads):
        wait_all(load)
        part = slice(block * width, (block + 1) * width)
        value = contract(second[...], full[:, part], 1, 0) + vec[EXPAND + block : EXPAND + block + 1]
        share = 0.5 + 0.5 * lax.erf(value * ROOT_HALF)
        active[:, part] = (value * share).astype(BF16)
        if slope is not None:
            density = ROOT_TAU * jnp.exp(-0.5 * value * value)
            slope[:, part] = (share + value * density).astype(BF16)


def forward(
    lower, upper, mixed_in, qkv, wide, params, meta, count, length, weight=LIGHT
):
    rows, width = lower.shape
    space = rows // count
    pair = 2 * width // HEADS
    attend, feed = qkv is not None, wide is not None
    both = attend and feed
    parts = len(qkv if attend else wide)
    many = len(flat(qkv if attend else wide))
    spots = parts + 1 + count
    inner = wide[0][0].shape[1] - width if feed else 0
    blocks = inner // width
    same = lower is upper

    def body(*refs):
        refs = list(refs)
        low = refs.pop(0)
        up = low if same else refs.pop(0)
        if not attend:
            arrived = refs.pop(0)
        lists = [[refs.pop(0) for _ in range(many)] for _ in range(attend + 2 * feed)]
        vec, info = refs.pop(0), refs.pop(0)
        if both:
            left, packed, logs, middle, slope = (refs.pop(0) for _ in range(5))
            active, second, mixed, norm = (
                left.at[:, pl.ds(start, size)]
                for start, size in ((0, inner), *((inner + width * i, width) for i in range(3)))
            )
        elif attend:
            mixed = refs.pop(0)
        else:
            middle, active = refs.pop(0), refs.pop(0)
        x, x_sem = refs.pop(0), refs.pop(0)
        section = info[parts]
        take = start_chosen(section, low, up, x, x_sem.at[0])
        if attend:
            columns, full, a_sem = (refs.pop(0) for _ in range(3))
            if not both:
                norm, packed, logs = refs.pop(0), refs.pop(0), None
            weight = lists.pop(0)
            loads = [
                start_pieces(weight, info, spots, full, a_sem, block, (block * width, width))
                for block in range(3)
            ]
        if feed:
            full_out, full_in, o_sem, w_sem = (refs.pop(0) for _ in range(4))
            if not attend:
                mixed, second, slope = refs.pop(0), refs.pop(0), None
                extra = pltpu.make_async_copy(arrived, mixed, x_sem.at[1])
                extra.start()
            first_load = start_pieces(lists[0], info, spots, full_out, o_sem, 0, (0, width))
            inner_loads = [
                start_pieces(lists[1], info, spots, full_in, w_sem, block, (block * width, width), width)
                for block in range(blocks)
            ]
        take.wait()
        if attend:
            attention_stage(
                x, vec, norm, packed, mixed, logs, columns, full, loads, count, length
            )
        if feed:
            if not attend:
                extra.wait()
            hidden_stage(
                x, vec, mixed, middle, active, second, slope, full_out, full_in, first_load,
                inner_loads,
            )

    outs, inputs = [], [lower] if same else [lower, upper]
    scratch = [pltpu.VMEM((rows, width), BF16), pltpu.SemaphoreType.DMA((2,))]
    flops = 0
    if attend:
        outs += [
            ((rows, width), BF16),
            ((rows, 3 * width), BF16),
            ((rows, width), BF16),
            ((count, HEADS, space), F32),
        ]
        scratch += [
            pltpu.VMEM((count, space, pair), F32),
            pltpu.VMEM((width, 3 * width), BF16),
            pltpu.SemaphoreType.DMA((3, many)),
        ]
        if not feed:
            scratch += [pltpu.VMEM((rows, width), BF16), pltpu.VMEM((rows, 3 * width), BF16)]
        flops += 2 * rows * width * (3 * width + 2 * space)
    else:
        inputs += [mixed_in]
    if feed:
        outs += [
            ((rows, width), F32),
            ((rows, inner), BF16),
            ((rows, width), BF16),
            ((rows, inner), BF16),
        ]
        scratch += [
            pltpu.VMEM((width, width), BF16),
            pltpu.VMEM((width, inner), BF16),
            pltpu.SemaphoreType.DMA((1, many)),
            pltpu.SemaphoreType.DMA((blocks, many)),
        ]
        if not attend:
            scratch += [pltpu.VMEM((rows, width), BF16), pltpu.VMEM((rows, width), BF16)]
        flops += 2 * rows * width * (width + inner)
    if both:
        outs = [((rows, inner + 3 * width), BF16), outs[1], outs[3], outs[4], outs[7]]
    else:
        outs = [outs[2]] if attend else outs[:2]
    weights = (flat(qkv) if attend else []) + (2 * flat(wide) if feed else [])
    return call(
        body,
        "forward" + "_attend" * attend + "_feed" * feed,
        inputs + weights + [params, meta],
        [ANY] * (len(inputs) + len(weights)) + [VMEM, SMEM],
        outs,
        scratch,
        flops,
        weight,
    )


def output_forward(middle, active, pieces, params, meta, count, weight=LIGHT):
    rows, width = middle.shape
    inner = sum(piece.shape[0] for piece in flat(pieces))
    space = rows // count
    parts, many = len(pieces), len(flat(pieces))
    spots = parts + 1 + count
    blocks = 2
    part_width = width // blocks

    def body(*refs):
        refs = list(refs)
        mid_in, act_in = refs.pop(0), refs.pop(0)
        reduce = [refs.pop(0) for _ in range(many)]
        vec, info, result, mid, act, full, x_sem, w_sem = refs
        copies = [
            pltpu.make_async_copy(act_in.at[:, pl.ds(0, inner)], act, x_sem.at[0]),
            pltpu.make_async_copy(mid_in, mid, x_sem.at[1]),
        ]
        copies[0].start()
        loads = [
            start_pieces(reduce, info, spots, full, w_sem, block, (block * part_width, part_width))
            for block in range(blocks)
        ]
        copies[1].start()
        copies[0].wait()
        for block in range(blocks):
            wait_all(loads[block])
            if block == 0:
                copies[1].wait()
            part = slice(block * part_width, (block + 1) * part_width)
            value = contract(act[...], full[:, part], 1, 0) + mid[:, part] + vec[FEED : FEED + 1, part]
            for image in range(count):
                alive = jnp.where(info[parts + 1 + image] > 0, 1.0, 0.0)
                here = slice(image * space, (image + 1) * space)
                result[here, part] = (value[here] * alive).astype(BF16)

    return call(
        body,
        "output_forward",
        [middle, active] + flat(pieces) + [params, meta],
        [ANY] * (2 + many) + [VMEM, SMEM],
        [((rows, width), BF16)],
        [
            pltpu.VMEM((rows, width), F32),
            pltpu.VMEM((rows, inner), BF16),
            pltpu.VMEM((inner, width), BF16),
            pltpu.SemaphoreType.DMA((2,)),
            pltpu.SemaphoreType.DMA((blocks, many)),
        ],
        2 * rows * width * inner,
        weight,
    )[0]


def hidden_back_stage(
    grad, vec, info, feed, slope, middle, hidden, second, mid_grad, branch, sums, inner_sums, full_out,
    full, deep, first_load, load, for_slope, for_middle, tallies, count, parts,
):
    rows, width = grad.shape
    space = rows // count
    half = width // 2
    for image in range(count):
        alive = jnp.where(info[parts + 1 + image] > 0, 1.0, 0.0)
        here = slice(image * space, (image + 1) * space)
        feed[here] = (grad[here].astype(F32) * alive).astype(BF16)
    for_slope.wait()
    for index in range(parts):
        wait_all(first_load[index])
        where = pl.multiple_of(info[index] * deep, deep)
        value = contract(feed[...], full_out[pl.ds(where, deep)], 1, 1)
        value = (value * slope[:, pl.ds(where, deep)].astype(F32)).astype(BF16)
        hidden[:, pl.ds(where, deep)] = value
        inner_sums[:, pl.ds(where, deep)] = jnp.sum(value.astype(F32), axis=0, keepdims=True)
    wait_all(load)
    for block in range(2):
        second[:, block * half : (block + 1) * half] = contract(
            hidden[...], full[block * half : (block + 1) * half], 1, 1
        )
    for_middle.wait()
    gain = vec[GAIN1 : GAIN1 + 1]
    tallies[...] = jnp.zeros_like(tallies)

    def step(here):
        unit, scale = standardized(middle[here])
        down = second[here]
        top = feed[here].astype(F32)
        total = top + norm_pull(down, gain, unit, scale)
        low = total.astype(BF16)
        mid_grad[here] = total
        branch[here] = low
        tallies[0] += eights(down * unit)
        tallies[1] += eights(down)
        tallies[2] += eights(low.astype(F32))
        tallies[3] += eights(top)

    step(pl.ds(0, rows))
    for index in range(4):
        sums[index : index + 1] = jnp.sum(tallies[index], axis=0, keepdims=True)


def attention_back_stage(
    x, vec, branch, mid_grad, packed, mixed, logs, grads, result, sums, down, normal, stage, full_out,
    full, first_load, load, takes, tallies, count, length,
):
    rows, width = x.shape
    space = rows // count
    head = width // HEADS
    pair = 2 * head
    scale = head**-0.5
    half = width // 2
    wait_all(first_load)
    down[...] = contract(branch[...], full_out[...], 1, 1).astype(BF16)
    wait_all(takes)
    owner = lax.shift_right_logical(
        lax.broadcasted_iota(jnp.int32, (HEADS, width), 1), head.bit_length() - 1
    )
    chosen = jnp.where(
        owner == lax.broadcasted_iota(jnp.int32, (HEADS, width), 0), 1.0, 0.0
    ).astype(BF16)
    left = lax.broadcasted_iota(jnp.int32, (space, pair), 1) < head
    live = lax.broadcasted_iota(jnp.int32, (space, pair), 0) < length
    key_live = lax.broadcasted_iota(jnp.int32, (space, space), 0) < length
    for image in range(count):
        span = pl.ds(image * space, space)
        product = down[span].astype(F32) * mixed[span].astype(F32)
        coarse = product.astype(BF16)
        fine = (product - coarse.astype(F32)).astype(BF16)
        stage[image, :, 0:space] = contract(chosen, coarse, 1, 1) + contract(chosen, fine, 1, 1)

    def heads(index, carry):
        for image in range(count):
            span = pl.ds(image * space, space)

            def part(block):
                offset = pl.multiple_of(block * width + index * pair, pair)
                return packed[span, pl.ds(offset, pair)]

            query, key, value = part(0), part(1), part(2)
            wide = key.astype(F32) * scale
            value = value.astype(F32)
            arrived = down[span, pl.ds(pl.multiple_of(index * pair, pair), pair)]
            found = []
            for side in range(2):
                mine = left if side == 0 else ~left
                log = logs[image, pl.ds(2 * index + side, 1), :]
                dot = stage[image, pl.ds(2 * index + side, 1), 0:space]
                scores = contract(jnp.where(mine, wide, 0.0).astype(BF16), query, 1, 1)
                chance = jnp.exp(jnp.where(key_live, scores - log, NEGATIVE))
                back = contract(jnp.where(mine, value, 0.0).astype(BF16), arrived, 1, 1)
                change = (chance * (back - dot)).astype(BF16)
                found.append(
                    (
                        contract(change, key, 0, 0),
                        contract(change, query, 1, 0),
                        contract(chance.astype(BF16), arrived, 1, 0),
                    )
                )
            for block, factor in enumerate((scale, scale, 1.0)):
                total = jnp.where(left, found[0][block], found[1][block]) * factor
                offset = pl.multiple_of(block * width + index * pair, pair)
                grads[span, pl.ds(offset, pair)] = jnp.where(live, total, 0.0).astype(BF16)
        return carry

    lax.fori_loop(0, HEADS // 2, heads, 0)
    wait_all(load)
    for block in range(2):
        normal[:, block * half : (block + 1) * half] = contract(
            grads[...], full[block * half : (block + 1) * half], 1, 1
        )
    gain = vec[GAIN0 : GAIN0 + 1]
    tallies[...] = jnp.zeros_like(tallies)

    def step(here):
        unit, rate = standardized(x[here].astype(F32))
        grad = normal[here]
        tallies[0] += eights(grad * unit)
        tallies[1] += eights(grad)
        result[here] = (mid_grad[here] + norm_pull(grad, gain, unit, rate)).astype(BF16)

    step(pl.ds(0, rows))
    for index in range(2):
        sums[index : index + 1] = jnp.sum(tallies[index], axis=0, keepdims=True)
    sums[2:3] = jnp.sum(grads[:, 0:width].astype(F32), axis=0, keepdims=True)
    sums[3:4] = jnp.sum(grads[:, 2 * width : 3 * width].astype(F32), axis=0, keepdims=True)


def backward(
    start, lower, upper, kept_low, kept_up, reduce, wide, qkv, params, meta, count, length,
    mixed_at, weight=LIGHT,
):
    feed, attend = reduce is not None, qkv is not None
    rows, width = start[0].shape
    space = rows // count
    pair = 2 * width // HEADS
    parts = len(reduce if feed else qkv)
    many = len(flat(reduce if feed else qkv))
    spots = parts + 1 + count
    inner = wide[0][0].shape[1] - width if feed else 0
    deep = inner // parts
    both = feed and attend
    choices = []
    if feed:
        choices += [(kept_low[0], kept_up[0]), (kept_low[1], kept_up[1])]
        if start[0] is not start[1]:
            choices += [start]
    if attend:
        choices += [(kept_low[index], kept_up[index]) for index in (2, 3, 4)]
        choices += [(lower, upper)]
    plain = [start[0]] if feed and start[0] is start[1] else [] if feed else list(start)
    operands = []
    for low, up in choices:
        operands += [low] if low is up else [low, up]

    def body(*refs):
        refs = list(refs)
        firsts = [refs.pop(0) for _ in plain]
        pairs = []
        for low, up in choices:
            one = refs.pop(0)
            pairs.append((one, one if low is up else refs.pop(0)))
        lists = [[refs.pop(0) for _ in range(many)] for _ in range(2 * feed + 2 * attend)]
        vec, info = refs.pop(0), refs.pop(0)
        section = info[parts]
        if feed:
            if both:
                right = refs.pop(0)
                hidden, branch = right.at[:, pl.ds(0, inner)], right.at[:, pl.ds(inner, width)]
            else:
                hidden, branch = refs.pop(0), refs.pop(0)
            feed_sums, inner_sums = refs.pop(0), refs.pop(0)
            mid_grad = None if both else refs.pop(0)
        if attend:
            grads, result, sums = (refs.pop(0) for _ in range(3)) if not both else (None, refs.pop(0), refs.pop(0))
        if both:
            feed_grad = right.at[:, pl.ds(inner + width, width)]
            grads = right.at[:, pl.ds(inner + 2 * width, 3 * width)]
        tallies, x_sem = refs.pop(0), refs.pop(0)
        if feed:
            grad, slope, middle, second, full_out, full, o_sem, w_sem = (
                refs.pop(0) for _ in range(8)
            )
            if both:
                mid_grad, keep = refs.pop(0), feed_grad
            else:
                keep = refs.pop(0)
            begin = pairs.pop(2) if start[0] is not start[1] else (firsts[0], firsts[0])
            take = start_chosen(section, *begin, grad, x_sem.at[0])
            for_slope = start_chosen(section, *pairs.pop(0), slope, x_sem.at[1])
            every = start_pieces(lists.pop(0), info, spots, full_out, o_sem, 0, (0, width))
            first_load = [[every.pop(0) for _ in group] for group in reduce]
            for_middle = start_chosen(section, *pairs.pop(0), middle, x_sem.at[2])
            load = start_pieces(lists.pop(0), info, spots, full, w_sem, 0, (0, inner), width)
        if attend:
            x, packed, mixed, logs, down, normal, stage, full_o, full_q, p_sem, q_sem = (
                refs.pop(0) for _ in range(11)
            )
            if not feed:
                branch, mid_grad = refs.pop(0), refs.pop(0)
                givens = [
                    pltpu.make_async_copy(source, target, x_sem.at[index])
                    for index, (source, target) in enumerate(zip(firsts, (branch, mid_grad)))
                ]
                for given in givens:
                    given.start()
            project_load = start_pieces(lists.pop(0), info, spots, full_o, p_sem, 0, (0, width))
            sames = [one is two for one, two in pairs]
            pairs[1] = tuple(one.at[:, pl.ds(mixed_at, width)] for one in pairs[1])
            takes = [
                start_chosen(section, *pairs[index], target, x_sem.at[3 + index], sames[index])
                for index, target in ((1, mixed), (0, packed), (2, logs), (3, x))
            ]
            last_load = start_pieces(lists.pop(0), info, spots, full_q, q_sem, 0, (0, 3 * width))
            if not feed:
                wait_all(givens)
        if feed:
            take.wait()
            hidden_back_stage(
                grad, vec, info, keep, slope, middle, hidden, second, mid_grad, branch, feed_sums,
                inner_sums, full_out, full, deep, first_load, load, for_slope, for_middle, tallies,
                count, parts,
            )
        if attend:
            attention_back_stage(
                x, vec, branch, mid_grad, packed, mixed, logs, grads, result, sums, down, normal,
                stage, full_o, full_q, project_load, last_load, takes, tallies, count, length,
            )

    outs = []
    scratch = [pltpu.VMEM((4, 8, width), F32), pltpu.SemaphoreType.DMA((7,))]
    flops = 0
    if feed:
        outs += [((rows, inner + 5 * width), BF16)] if both else [((rows, inner), BF16), ((rows, width), BF16)]
        outs += [
            ((8, width), F32),
            ((1, inner), F32),
        ]
        if not both:
            outs += [((rows, width), F32)]
        scratch += [
            pltpu.VMEM((rows, width), BF16),
            pltpu.VMEM((rows, inner), BF16),
            pltpu.VMEM((rows, width), F32),
            pltpu.VMEM((rows, width), F32),
            pltpu.VMEM((inner, width), BF16),
            pltpu.VMEM((width, inner), BF16),
            pltpu.SemaphoreType.DMA((1, many)),
            pltpu.SemaphoreType.DMA((1, many)),
        ]
        scratch += [pltpu.VMEM((rows, width), F32 if both else BF16)]
        flops += 4 * rows * width * inner
    if attend:
        outs += [] if both else [((rows, 3 * width), BF16)]
        outs += [((rows, width), BF16), ((8, width), F32)]
        scratch += [
            pltpu.VMEM((rows, width), BF16),
            pltpu.VMEM((rows, 3 * width), BF16),
            pltpu.VMEM((rows, width), BF16),
            pltpu.VMEM((count, HEADS, space), F32),
            pltpu.VMEM((rows, width), BF16),
            pltpu.VMEM((rows, width), F32),
            pltpu.VMEM((count, HEADS, 2 * pair), F32),
            pltpu.VMEM((width, width), BF16),
            pltpu.VMEM((width, 3 * width), BF16),
            pltpu.SemaphoreType.DMA((1, many)),
            pltpu.SemaphoreType.DMA((1, many)),
        ]
        if not feed:
            scratch += [pltpu.VMEM((rows, width), BF16), pltpu.VMEM((rows, width), F32)]
        flops += 2 * rows * width * (4 * width + 5 * space)
    weights = (flat(reduce) + flat(wide) if feed else []) + (
        flat(wide) + flat(qkv) if attend else []
    )
    return call(
        body,
        "backward" + "_feed" * feed + "_attend" * attend,
        plain + operands + weights + [params, meta],
        [ANY] * (len(plain) + len(operands) + len(weights)) + [VMEM, SMEM],
        outs,
        scratch,
        flops,
        weight,
    )


def weight_gradient(
    lefts, rights, meta, parts, blocks, quarter, rows_of, columns_of, name, weight=LIGHT
):
    terms = len(lefts)
    first_row, height = rows_of
    first_column, breadth = columns_of
    rows = lefts[0].shape[0]
    operands = list(lefts)
    places = []
    for pair in rights:
        found = []
        for array, _ in pair:
            if not any(array is other for other in operands):
                operands.append(array)
            found.append(next(i for i, other in enumerate(operands) if other is array))
        places.append(found)

    def body(*refs):
        sources, info = refs[: len(operands)], refs[len(operands)]
        results = refs[len(operands) + 1 : len(operands) + 1 + len(blocks)]
        left_full, right_full, l_sem, r_sem = refs[len(operands) + 1 + len(blocks) :]
        section = info[parts]
        waits = []
        for term in range(terms):
            sides = [
                sources[place].at[:, pl.ds(column + first_column, breadth)]
                for place, (_, column) in zip(places[term], rights[term])
            ]
            same = rights[term][0] is rights[term][1]
            target = right_full.at[pl.ds(term * rows, rows)]
            waits.append(start_chosen(section, *sides, target, r_sem.at[term], same))
        loads = []
        for index, block in enumerate(blocks):
            start = pl.multiple_of(info[block] * quarter + first_row, 128)
            for term in range(terms):
                copy = pltpu.make_async_copy(
                    sources[term].at[:, pl.ds(start, height)],
                    left_full.at[index, pl.ds(term * rows, rows)],
                    l_sem.at[index, term],
                )
                copy.start()
                loads.append(copy)
        wait_all(waits)
        for index in reversed(range(len(blocks))):
            wait_all(loads[index * terms : (index + 1) * terms])
            results[index][...] = contract(left_full[index], right_full[...], 0, 0).astype(BF16)

    return call(
        body,
        name,
        operands + [meta],
        [ANY] * len(operands) + [SMEM],
        [((height, breadth), BF16)] * len(blocks),
        [
            pltpu.VMEM((len(blocks), terms * rows, height), BF16),
            pltpu.VMEM((terms * rows, breadth), BF16),
            pltpu.SemaphoreType.DMA((len(blocks), terms)),
            pltpu.SemaphoreType.DMA((terms,)),
        ],
        2 * len(blocks) * terms * rows * height * breadth,
        weight,
    )


def after(value, *earlier):
    return lax.optimization_barrier((value,) + earlier)[0]


def added(*values):
    total = values[0].astype(F32)
    for value in values[1:]:
        total = total + value.astype(F32)
    return total.astype(values[0].dtype)


class FourByFour:
    parts = 4
    blocks = (0, 2)

    def __init__(self):
        self.group = lax.axis_index("group")
        self.place = lax.axis_index("replica")
        self.order = [self.group ^ part for part in range(4)]
        odd = self.place % 2
        halves = [2 * self.order[part] + half for part in (2, 3) for half in (odd, 1 - odd)]
        self.spots = self.order[:2] + halves

    def core(self, block):
        return lax.ppermute(block, "group", [(i, i ^ 1) for i in range(4)])

    def across(self, block):
        return lax.ppermute(block, "group", [(i, i ^ 2) for i in range(4)])

    def beside(self, block):
        return lax.ppermute(block, "replica", [(i, i ^ 1) for i in range(4)])

    def gather_small(self, block):
        near, far = self.core(block), self.across(block)
        return [block, near, far, self.core(far)]

    def gather(self, blocks, prepare):
        odd = self.place % 2
        asked = [
            lax.dynamic_slice_in_dim(block, odd * (block.shape[0] // 2), block.shape[0] // 2)
            for block in blocks
        ]
        halves, sibling = [], []
        for index, block in enumerate(blocks):
            halves.append(self.across(after(asked[index], *halves[: max(index - 1, 0)])))
            sibling.append(self.core(after(block, sibling[-1]) if index else block))
        others = []
        tokens = prepare(halves[0]) + asked[2:]
        for index, half in enumerate(halves):
            others.append(self.beside(after(half, *others[-1:], *(tokens if index == 1 else []))))

        def pieces(index, *tokens):
            one, two = (after(half, *tokens) for half in (halves[index], others[index]))
            return [
                [blocks[index]],
                [sibling[index]],
                [halves[index], others[index]],
                [self.core(one), self.core(two)],
            ]

        return [partial(pieces, index) for index in range(len(blocks))]

    def shared(self, block):
        return [block, self.core(block)]

    def total(self, blocks):
        passed = self.across(blocks[1])
        token = yield
        mine = added(after(blocks[0], token), passed)
        inward = lax.ppermute(mine, "replica", [(0, 1), (3, 2)])
        token = yield mine
        joined = added(after(mine, token), inward)
        crossing = lax.ppermute(joined, "replica", [(1, 2), (2, 1)])
        token = yield joined
        summed = added(after(joined, token), crossing)
        outward = lax.ppermute(summed, "replica", [(1, 0), (2, 3)])
        token = yield summed
        inner = (self.place == 1) | (self.place == 2)
        yield jnp.where(inner, after(summed, token), outward)


class General:
    def __init__(self):
        self.parts = lax.axis_size("group")
        self.blocks = tuple(range(self.parts))
        self.order = self.spots = [jnp.int32(part) for part in range(self.parts)]

    def gather_small(self, block):
        whole = lax.all_gather(block, "group", axis=0)
        return [whole[part] for part in range(self.parts)]

    def gather(self, blocks, prepare):
        prepare(blocks[0])
        found = [[[piece] for piece in self.gather_small(block)] for block in blocks]
        return [lambda *tokens, groups=groups: groups for groups in found]

    def shared(self, block):
        return [block]

    def total(self, blocks):
        yield
        mine = lax.psum_scatter(jnp.stack(blocks), "group", scatter_dimension=0)
        yield mine
        yield lax.psum(mine, "replica")


def shifted(block, distance):
    devices = range(lax.axis_size("section"))
    route = [(i - distance, i) for i in devices if i - distance in devices]
    return lax.ppermute(block, "section", route)


def in_order(pieces, order):
    place = jnp.stack(order)
    stacked = []
    for block in range(len(pieces)):
        chosen = pieces[0]
        for part in range(1, len(pieces)):
            chosen = jnp.where(place[part] == block, pieces[part], chosen)
        stacked.append(chosen)
    return jnp.stack(stacked)


class Sequence:
    def __init__(self, net, token):
        self.net, self.sums, self.results, self.token = net, {}, {}, token

    def now(self, value):
        return after(value, self.token)

    def ran(self, value):
        self.token = value

    def add(self, name, blocks):
        self.sums[name] = self.net.total(blocks)
        next(self.sums[name])

    def step(self, *names):
        for name in names:
            try:
                self.results[name] = self.token = self.sums[name].send(self.token)
            except StopIteration:
                continue

    def finish(self, name):
        while True:
            try:
                self.results[name] = self.sums[name].send(self.token)
            except StopIteration:
                return self.results[name]


def per_device(
    images,
    cotangent,
    counts,
    qkv_weight,
    out_weight,
    expand_weight,
    reduce_weight,
    norm_gains,
    biases,
    expand_bias,
):
    micro, slots, length, width = images.shape
    space = padded(length)
    section = lax.axis_index("section")
    first = section == 0
    sizes = (lax.axis_size("group"), lax.axis_size("replica"))
    net = FourByFour() if sizes == (4, 4) else General()
    parts = net.parts
    share = width // parts
    batches = tuple(range(micro))

    def rows_of(array):
        fulls = [jnp.pad(array[batch], ((0, 0), (0, space - length), (0, 0))) for batch in batches]
        return [full.reshape(slots * space, width) for full in fulls]

    def images_of(array):
        return array.reshape(slots, space, width)[:, :length]

    small = jnp.concatenate([norm_gains[0], biases[0], expand_bias[0].reshape(-1, share)])
    slot = jnp.arange(slots, dtype=jnp.int32)
    alive = [(slot < counts[batch, 0]).astype(jnp.int32) for batch in batches]
    head = jnp.stack(net.order + [section]).astype(jnp.int32)

    spots = jnp.stack(net.spots).astype(jnp.int32)

    def meta(living):
        return jnp.concatenate([head, living, spots])

    infos = [meta(alive[batch]) for batch in batches]
    pieces = net.gather_small(small)
    vectors = in_order(pieces, net.order)
    top = vectors[:, :8].transpose(1, 0, 2).reshape(8, width)
    bottom = vectors[:, 8:].reshape(-1, width)
    params = jnp.concatenate([top, bottom]).astype(F32)
    slot = jnp.arange(slots, dtype=jnp.int32)
    alive = [(slot < counts[batch, 0]).astype(jnp.int32) for batch in batches]
    head = jnp.stack(net.order + [section]).astype(jnp.int32)
    spots = jnp.stack(net.spots).astype(jnp.int32)

    def meta(living):
        return jnp.concatenate([head, living, spots])

    infos = [meta(alive[batch]) for batch in batches]
    inputs, targets = [], []

    def prepare(token):
        inputs.extend(rows_of(after(images, token)))
        targets.extend(rows_of(after(cotangent, token)))
        return [params, *inputs, *targets, *infos]

    qkv, wide, reduce = net.gather(
        [qkv_weight[0], jnp.concatenate([out_weight[0], expand_weight[0]], axis=1), reduce_weight[0]],
        prepare,
    )

    qkv = qkv()
    attended = []
    for batch in batches:
        start = inputs[batch] if batch == 0 else after(inputs[batch], attended[-1][0])
        attended.append(
            forward(start, start, None, qkv, None, params, infos[batch], slots, length)
        )
    wide = wide(attended[-1][0])
    fed = []
    for batch in batches:
        start = inputs[batch] if batch == 0 else after(inputs[batch], fed[-1][0])
        fed.append(
            forward(start, start, attended[batch][0], None, wide, params, infos[batch], slots, length)
        )
    reduce = reduce(fed[-1][0])
    early, incoming = [], []
    for batch in batches:
        middle, active = fed[batch][:2]
        if batch:
            active = after(active, early[-1])
        early.append(output_forward(middle, active, reduce, params, infos[batch], slots))
        incoming.append(shifted(early[batch], 1))

    inner = wide[0][0].shape[1] - width
    mixed_at = inner + width
    kept, lefts, rights, results = [], [], [], []
    sums_a, sums_b, sums_c, returning = [], [], [], []
    token = early[-1]
    for batch in batches:
        start = after(incoming[batch], token)
        left, packed, logs, middle, slope = forward(
            inputs[batch], start, None, qkv, wide, params, infos[batch], slots, length, 8.0
        )
        kept.append((slope, middle, packed, left, logs))
        lefts.append(net.shared(left))
        if batch == 0:
            pair, sides = (targets[0], targets[0]), (kept[0], kept[0])
            lower, chosen = incoming[0], infos[0]
        else:
            pair = (returning[batch - 1], targets[batch])
            sides = (kept[batch - 1], kept[batch])
            lower = inputs[batch - 1]
            chosen = meta(jnp.where(first, alive[batch - 1], alive[batch]))
        right, some, more, result, rest = backward(
            pair, lower, incoming[batch], sides[0], sides[1], reduce, wide, qkv, params, chosen,
            slots, length, mixed_at, 8.0,
        )
        token = result
        rights.append(net.shared(right))
        results.append(result)
        sums_a.append(some)
        sums_b.append(more)
        sums_c.append(rest)
        returning.append(shifted(result, -1))
    late = []
    for batch in batches:
        ready = lefts[batch][1:] + (rights[batch][1:] if batch < micro - 1 else [])
        active = after(kept[batch][3], token, *ready)
        late.append(output_forward(kept[batch][1], active, reduce, params, infos[batch], slots, 8.0))
        token = late[-1]

    last = micro - 1
    run = Sequence(net, token)
    arrived = run.now(returning[last])
    living = jnp.repeat(alive[last] > 0, space)[:, None]
    masked = net.shared(jnp.where(living, arrived, jnp.zeros_like(arrived)))
    many = len(masked)

    def gradient(name, left_at, final, final_at, right_at, quarter, rows, columns, weight=LIGHT):
        left = [lefts[batch][side] for batch in batches for side in range(many)]
        right = []
        for batch in batches:
            for side in range(many):
                upper = (rights[batch][side], right_at)
                lower = (final[side], final_at) if batch == last else (rights[batch + 1][side], right_at)
                right.append((lower, upper))
        blocks = weight_gradient(
            left, right, run.now(head), parts, net.blocks, quarter, (left_at + rows[0], rows[1]), columns,
            name, weight,
        )
        run.ran(blocks[0])
        return blocks

    def reduce_part(index, weight=LIGHT):
        step = inner // parts // 2
        blocks = gradient(
            "reduce", 0, masked, 0, inner + width, inner // parts, (index * step, step), (0, width), weight
        )
        run.add(f"reduce{index}", blocks)

    def expand_part(index):
        step = inner // 2
        blocks = gradient("expand", inner, finals, 0, 0, share, (0, share), (index * step, step))
        run.add(f"expand{index}", blocks)

    def qkv_part(index):
        step = 3 * width // 2
        at = inner + 2 * width
        run.add(f"qkv{index}", gradient("qkv", at, grads, 0, at, share, (0, share), (index * step, step)))

    reduce_part(0)
    start = run.now(arrived)
    final, branch, some, more, mid = backward(
        (start, start), None, None, kept[last], kept[last], reduce, wide, None, params, infos[last],
        slots, length, mixed_at,
    )
    run.ran(final)
    finals, branches = net.shared(final), net.shared(branch)
    sums_a.append(some)
    sums_b.append(more)
    run.step("reduce0")
    reduce_part(1, HEAVY)
    expand_part(0)
    expand_part(1)
    run.step("reduce1", "reduce0")
    grads, result, rest = backward(
        (run.now(after(branch, *branches[1:])), mid), inputs[last], inputs[last], kept[last], kept[last], None, wide, qkv,
        params, infos[last], slots, length, mixed_at, HEAVY,
    )
    run.ran(result)
    grads = net.shared(grads)
    results.append(result)
    sums_c.append(rest)
    run.step("expand0", "reduce1", "reduce0")
    qkv_part(0)
    run.step("expand1", "expand0", "reduce1", "reduce0")
    qkv_part(1)

    run.step("qkv0", "expand1", "expand0", "reduce1", "qkv1", "qkv0")

    def over_batches(values):
        return sum(jnp.where(first, values[batch + 1], values[batch]) for batch in batches)

    some, more, rest = over_batches(sums_a), over_batches(sums_b), over_batches(sums_c)
    rows = jnp.concatenate([rest[0:1], some[0:1], rest[1:2], some[1:2], rest[2:4], some[2:4]])
    rows = rows.reshape(8, parts, share).transpose(1, 0, 2)
    rows = jnp.concatenate([rows, more.reshape(parts, -1, share)], axis=1)
    rows = sum(net.shared(run.now(rows)))
    rows = jnp.stack(
        [lax.dynamic_index_in_dim(rows, net.order[block], 0, keepdims=False) for block in net.blocks]
    )
    count = rows.shape[1]
    rows = rows.reshape(len(net.blocks), -1)
    rows = jnp.pad(rows, ((0, 0), (0, -rows.shape[1] % (16 * width)))).reshape(len(net.blocks), -1, width)
    blocks = gradient("project", mixed_at, branches, 0, inner, share, (0, share), (0, width))
    run.add("project", [jnp.concatenate([one, two]) for one, two in zip(blocks, rows.astype(BF16))])
    run.step("expand1", "expand0", "qkv1", "project", "qkv0")
    outputs = [
        images_of(jnp.where(first, run.now(low), up))
        for low, up in zip(early + results[1:], late + results[:-1])
    ]
    run.step("expand1", "qkv1", "project", "qkv0", "project", "qkv1", "project")
    weights = {name: run.finish(name) for name in run.sums}
    vector = weights["project"][share:].reshape(-1)[: count * share].reshape(count, share).astype(F32)

    def joined(axis, *names):
        return jnp.concatenate([weights[name] for name in names], axis=axis).astype(F32)[None]

    return (
        jnp.stack(outputs[:micro])[None],
        jnp.stack(outputs[micro:])[None],
        joined(1, "qkv0", "qkv1"),
        weights["project"][:share].astype(F32)[None],
        joined(1, "expand0", "expand1"),
        joined(0, "reduce0", "reduce1"),
        vector[None, 0:2],
        vector[None, 2:8],
        vector[8:].reshape(1, -1),
    )


def solution(mesh):
    placed = (
        P(None, ("group", "replica"), None, None),
        P(None, ("group", "replica"), None, None),
        P(None, ("group", "replica")),
        P("section", "group", None),
        P("section", "group", None),
        P("section", "group", None),
        P("section", "group", None),
        P("section", None, "group"),
        P("section", None, "group"),
        P("section", "group"),
    )
    return jax.shard_map(
        per_device,
        mesh=mesh,
        in_specs=placed,
        out_specs=(
            P("section", None, ("group", "replica"), None, None),
            P("section", None, ("group", "replica"), None, None),
            P("section", "group", None),
            P("section", "group", None),
            P("section", "group", None),
            P("section", "group", None),
            P("section", None, "group"),
            P("section", None, "group"),
            P("section", "group"),
        ),
        check_vma=False,
    )
```

```python
from functools import partial

import jax
import jax.numpy as jnp
from jax import lax
from jax.experimental import pallas as pl
from jax.experimental.pallas import tpu as pltpu
from jax.sharding import PartitionSpec as P

HEADS = 16
EPSILON = 1e-06
NEGATIVE = -1e30
F32 = jnp.float32
BF16 = jnp.bfloat16
LIGHT, HEAVY = 1.0 / 64, 16.0
VMEM_LIMIT = 58 * 2**20
ROOT_HALF = 0.7071067811865476
ROOT_TAU = 0.3989422804014327
ANY = pl.BlockSpec(memory_space=pl.ANY)
VMEM = pl.BlockSpec(memory_space=pltpu.VMEM)
SMEM = pl.BlockSpec(memory_space=pltpu.SMEM)
GAIN0, GAIN1, SHIFT0, SHIFT1, QUERY, VALUE, OUT, FEED, EXPAND = range(9)


def padded(length):
    return -(-length // 16) * 16


def contract(left, right, left_dim, right_dim):
    return lax.dot_general(
        left, right, (((left_dim,), (right_dim,)), ((), ())), preferred_element_type=F32
    )


def standardized(values):
    center = values - jnp.mean(values, axis=-1, keepdims=True)
    spread = jnp.mean(center * center, axis=-1, keepdims=True)
    scale = lax.rsqrt(spread + EPSILON)
    return center * scale, scale


def norm_pull(grad, gain, unit, scale):
    scaled = grad * gain
    mean = jnp.mean(scaled, axis=-1, keepdims=True)
    along = jnp.mean(scaled * unit, axis=-1, keepdims=True)
    return scale * (scaled - mean - unit * along)


def call(body, name, operands, specs, outs, scratch, flops, weight=LIGHT):
    moved = sum(o.size * o.dtype.itemsize for o in operands)
    out_shape = [jax.ShapeDtypeStruct(shape, dtype) for shape, dtype in outs]
    moved += sum(o.size * o.dtype.itemsize for o in out_shape)
    return pl.pallas_call(
        body,
        out_shape=out_shape,
        in_specs=specs,
        out_specs=[VMEM] * len(outs),
        scratch_shapes=scratch,
        compiler_params=pltpu.CompilerParams(vmem_limit_bytes=VMEM_LIMIT),
        cost_estimate=pl.CostEstimate(flops=int(flops * weight), bytes_accessed=int(moved * weight), transcendentals=0),
        name=name,
    )(*operands)


def flat(groups):
    return [piece for group in groups for piece in group]


def start_pieces(pieces, info, first, target, sems, slot, columns, shift=0):
    begin, size = columns
    columns = pl.ds(begin, size)
    copies = []
    for index, piece in enumerate(pieces):
        rows = piece.shape[0]
        where = pl.multiple_of(info[first + index] * rows, rows)
        copy = pltpu.make_async_copy(
            piece.at[:, pl.ds(begin + shift, size)],
            target.at[pl.ds(where, rows), columns],
            sems.at[slot, index],
        )
        copy.start()
        copies.append(copy)
    return copies


def wait_all(copies):
    for copy in copies:
        copy.wait()


def start_chosen(section, lower, upper, target, sem, same=False):
    if lower is upper or same:
        copy = pltpu.make_async_copy(lower, target, sem)
        copy.start()
        return copy

    @pl.when(section == 0)
    def _():
        pltpu.make_async_copy(lower, target, sem).start()

    @pl.when(section != 0)
    def _():
        pltpu.make_async_copy(upper, target, sem).start()

    return pltpu.make_async_copy(lower, target, sem)


def eights(values):
    return jnp.sum(values.reshape(-1, 8, values.shape[-1]), axis=0)


def attention_stage(x, vec, norm, packed, mixed, logs, columns, full, loads, count, length):
    rows, width = x.shape
    space = rows // count
    head = width // HEADS
    pair = 2 * head
    scale = head**-0.5
    gain, shift = vec[GAIN0 : GAIN0 + 1], vec[SHIFT0 : SHIFT0 + 1]

    def step(here):
        unit, _ = standardized(x[here].astype(F32))
        norm[here] = (unit * gain + shift).astype(BF16)

    step(pl.ds(0, rows))
    for block in range(3):
        wait_all(loads[block])
        done = contract(norm[...], full[:, block * width : (block + 1) * width], 1, 0)
        if block != 1:
            bias = QUERY if block == 0 else VALUE
            done = done + vec[bias : bias + 1]
        packed[:, block * width : (block + 1) * width] = done.astype(BF16)
    lane = lax.broadcasted_iota(jnp.int32, (space, pair), 1)
    left = lane < head
    live = lax.broadcasted_iota(jnp.int32, (space, pair), 0) < length
    key_live = lax.broadcasted_iota(jnp.int32, (space, space), 1) < length
    columns[...] = jnp.zeros_like(columns)

    def heads(index, carry):
        for image in range(count):
            span = pl.ds(image * space, space)

            def part(block):
                offset = pl.multiple_of(block * width + index * pair, pair)
                return packed[span, pl.ds(offset, pair)]

            query, key, value = part(0).astype(F32) * scale, part(1), part(2).astype(F32)
            found = []
            tops = []
            for side in range(2):
                mine = left if side == 0 else ~left
                asked = jnp.where(mine, query, 0.0).astype(BF16)
                held = jnp.where(live, jnp.where(mine, value, 1.0), 0.0).astype(BF16)
                scores = jnp.where(key_live, contract(asked, key, 1, 1), NEGATIVE)
                top = jnp.max(scores, axis=-1, keepdims=True)
                raised = jnp.exp(scores - top).astype(BF16)
                found.append(contract(raised, held, 1, 0))
                tops.append(top)
            inside = jnp.where(left, found[0], found[1])
            total = jnp.where(left, found[1], found[0])
            turned = pltpu.roll(total, head, 1)
            offset = pl.multiple_of(index * pair, pair)
            mixed[span, pl.ds(offset, pair)] = (inside / turned).astype(BF16)
            if logs is None:
                continue
            logged = jnp.log(turned)
            first = tops[0] + logged[:, 0:1]
            second = tops[1] + logged[:, head : head + 1]
            known = columns[image]
            known = jnp.where(lane == 2 * index, first, known)
            columns[image] = jnp.where(lane == 2 * index + 1, second, known)
        return carry

    lax.fori_loop(0, HEADS // 2, heads, 0)
    if logs is not None:
        for image in range(count):
            logs[image] = columns[image].T[0:HEADS]


def hidden_stage(x, vec, mixed, middle, active, second, slope, full_out, full, first_load, loads):
    rows, width = x.shape
    wait_all(first_load)
    gain, shift, bias = vec[GAIN1 : GAIN1 + 1], vec[SHIFT1 : SHIFT1 + 1], vec[OUT : OUT + 1]
    middle[...] = contract(mixed[...], full_out[...], 1, 0)

    def step(here):
        total = middle[here] + x[here].astype(F32) + bias
        middle[here] = total
        unit, _ = standardized(total)
        second[here] = (unit * gain + shift).astype(BF16)

    step(pl.ds(0, rows))
    for block, load in enumerate(loads):
        wait_all(load)
        part = slice(block * width, (block + 1) * width)
        value = contract(second[...], full[:, part], 1, 0) + vec[EXPAND + block : EXPAND + block + 1]
        share = 0.5 + 0.5 * lax.erf(value * ROOT_HALF)
        active[:, part] = (value * share).astype(BF16)
        if slope is not None:
            density = ROOT_TAU * jnp.exp(-0.5 * value * value)
            slope[:, part] = (share + value * density).astype(BF16)


def forward(
    lower, upper, mixed_in, qkv, wide, params, meta, count, length, weight=LIGHT
):
    rows, width = lower.shape
    space = rows // count
    pair = 2 * width // HEADS
    attend, feed = qkv is not None, wide is not None
    both = attend and feed
    parts = len(qkv if attend else wide)
    many = len(flat(qkv if attend else wide))
    spots = parts + 1 + count
    inner = wide[0][0].shape[1] - width if feed else 0
    blocks = inner // width
    same = lower is upper

    def body(*refs):
        refs = list(refs)
        low = refs.pop(0)
        up = low if same else refs.pop(0)
        if not attend:
            arrived = refs.pop(0)
        lists = [[refs.pop(0) for _ in range(many)] for _ in range(attend + 2 * feed)]
        vec, info = refs.pop(0), refs.pop(0)
        if both:
            left, packed, logs, middle, slope = (refs.pop(0) for _ in range(5))
            active, second, mixed, norm = (
                left.at[:, pl.ds(start, size)]
                for start, size in ((0, inner), *((inner + width * i, width) for i in range(3)))
            )
        elif attend:
            mixed = refs.pop(0)
        else:
            middle, active = refs.pop(0), refs.pop(0)
        x, x_sem = refs.pop(0), refs.pop(0)
        section = info[parts]
        take = start_chosen(section, low, up, x, x_sem.at[0])
        if attend:
            columns, full, a_sem = (refs.pop(0) for _ in range(3))
            if not both:
                norm, packed, logs = refs.pop(0), refs.pop(0), None
            weight = lists.pop(0)
            loads = [
                start_pieces(weight, info, spots, full, a_sem, block, (block * width, width))
                for block in range(3)
            ]
        if feed:
            full_out, full_in, o_sem, w_sem = (refs.pop(0) for _ in range(4))
            if not attend:
                mixed, second, slope = refs.pop(0), refs.pop(0), None
                extra = pltpu.make_async_copy(arrived, mixed, x_sem.at[1])
                extra.start()
            first_load = start_pieces(lists[0], info, spots, full_out, o_sem, 0, (0, width))
            inner_loads = [
                start_pieces(lists[1], info, spots, full_in, w_sem, block, (block * width, width), width)
                for block in range(blocks)
            ]
        take.wait()
        if attend:
            attention_stage(
                x, vec, norm, packed, mixed, logs, columns, full, loads, count, length
            )
        if feed:
            if not attend:
                extra.wait()
            hidden_stage(
                x, vec, mixed, middle, active, second, slope, full_out, full_in, first_load,
                inner_loads,
            )

    outs, inputs = [], [lower] if same else [lower, upper]
    scratch = [pltpu.VMEM((rows, width), BF16), pltpu.SemaphoreType.DMA((2,))]
    flops = 0
    if attend:
        outs += [
            ((rows, width), BF16),
            ((rows, 3 * width), BF16),
            ((rows, width), BF16),
            ((count, HEADS, space), F32),
        ]
        scratch += [
            pltpu.VMEM((count, space, pair), F32),
            pltpu.VMEM((width, 3 * width), BF16),
            pltpu.SemaphoreType.DMA((3, many)),
        ]
        if not feed:
            scratch += [pltpu.VMEM((rows, width), BF16), pltpu.VMEM((rows, 3 * width), BF16)]
        flops += 2 * rows * width * (3 * width + 2 * space)
    else:
        inputs += [mixed_in]
    if feed:
        outs += [
            ((rows, width), F32),
            ((rows, inner), BF16),
            ((rows, width), BF16),
            ((rows, inner), BF16),
        ]
        scratch += [
            pltpu.VMEM((width, width), BF16),
            pltpu.VMEM((width, inner), BF16),
            pltpu.SemaphoreType.DMA((1, many)),
            pltpu.SemaphoreType.DMA((blocks, many)),
        ]
        if not attend:
            scratch += [pltpu.VMEM((rows, width), BF16), pltpu.VMEM((rows, width), BF16)]
        flops += 2 * rows * width * (width + inner)
    if both:
        outs = [((rows, inner + 3 * width), BF16), outs[1], outs[3], outs[4], outs[7]]
    else:
        outs = [outs[2]] if attend else outs[:2]
    weights = (flat(qkv) if attend else []) + (2 * flat(wide) if feed else [])
    return call(
        body,
        "forward" + "_attend" * attend + "_feed" * feed,
        inputs + weights + [params, meta],
        [ANY] * (len(inputs) + len(weights)) + [VMEM, SMEM],
        outs,
        scratch,
        flops,
        weight,
    )


def output_forward(middle, active, pieces, params, meta, count, weight=LIGHT):
    rows, width = middle.shape
    inner = sum(piece.shape[0] for piece in flat(pieces))
    space = rows // count
    parts, many = len(pieces), len(flat(pieces))
    spots = parts + 1 + count
    blocks = 2
    part_width = width // blocks

    def body(*refs):
        refs = list(refs)
        mid_in, act_in = refs.pop(0), refs.pop(0)
        reduce = [refs.pop(0) for _ in range(many)]
        vec, info, result, mid, act, full, x_sem, w_sem = refs
        copies = [
            pltpu.make_async_copy(act_in.at[:, pl.ds(0, inner)], act, x_sem.at[0]),
            pltpu.make_async_copy(mid_in, mid, x_sem.at[1]),
        ]
        copies[0].start()
        loads = [
            start_pieces(reduce, info, spots, full, w_sem, block, (block * part_width, part_width))
            for block in range(blocks)
        ]
        copies[1].start()
        copies[0].wait()
        for block in range(blocks):
            wait_all(loads[block])
            if block == 0:
                copies[1].wait()
            part = slice(block * part_width, (block + 1) * part_width)
            value = contract(act[...], full[:, part], 1, 0) + mid[:, part] + vec[FEED : FEED + 1, part]
            for image in range(count):
                alive = jnp.where(info[parts + 1 + image] > 0, 1.0, 0.0)
                here = slice(image * space, (image + 1) * space)
                result[here, part] = (value[here] * alive).astype(BF16)

    return call(
        body,
        "output_forward",
        [middle, active] + flat(pieces) + [params, meta],
        [ANY] * (2 + many) + [VMEM, SMEM],
        [((rows, width), BF16)],
        [
            pltpu.VMEM((rows, width), F32),
            pltpu.VMEM((rows, inner), BF16),
            pltpu.VMEM((inner, width), BF16),
            pltpu.SemaphoreType.DMA((2,)),
            pltpu.SemaphoreType.DMA((blocks, many)),
        ],
        2 * rows * width * inner,
        weight,
    )[0]


def hidden_back_stage(
    grad, vec, info, feed, slope, middle, hidden, second, mid_grad, branch, sums, inner_sums, full_out,
    full, deep, first_load, load, for_slope, for_middle, tallies, count, parts,
):
    rows, width = grad.shape
    space = rows // count
    half = width // 2
    for image in range(count):
        alive = jnp.where(info[parts + 1 + image] > 0, 1.0, 0.0)
        here = slice(image * space, (image + 1) * space)
        feed[here] = (grad[here].astype(F32) * alive).astype(BF16)
    for_slope.wait()
    for index in range(parts):
        wait_all(first_load[index])
        where = pl.multiple_of(info[index] * deep, deep)
        value = contract(feed[...], full_out[pl.ds(where, deep)], 1, 1)
        value = (value * slope[:, pl.ds(where, deep)].astype(F32)).astype(BF16)
        hidden[:, pl.ds(where, deep)] = value
        inner_sums[:, pl.ds(where, deep)] = jnp.sum(value.astype(F32), axis=0, keepdims=True)
    wait_all(load)
    for block in range(2):
        second[:, block * half : (block + 1) * half] = contract(
            hidden[...], full[block * half : (block + 1) * half], 1, 1
        )
    for_middle.wait()
    gain = vec[GAIN1 : GAIN1 + 1]
    tallies[...] = jnp.zeros_like(tallies)

    def step(here):
        unit, scale = standardized(middle[here])
        down = second[here]
        top = feed[here].astype(F32)
        total = top + norm_pull(down, gain, unit, scale)
        low = total.astype(BF16)
        mid_grad[here] = total
        branch[here] = low
        tallies[0] += eights(down * unit)
        tallies[1] += eights(down)
        tallies[2] += eights(low.astype(F32))
        tallies[3] += eights(top)

    step(pl.ds(0, rows))
    for index in range(4):
        sums[index : index + 1] = jnp.sum(tallies[index], axis=0, keepdims=True)


def attention_back_stage(
    x, vec, branch, mid_grad, packed, mixed, logs, grads, result, sums, down, normal, stage, full_out,
    full, first_load, load, takes, tallies, count, length,
):
    rows, width = x.shape
    space = rows // count
    head = width // HEADS
    pair = 2 * head
    scale = head**-0.5
    half = width // 2
    wait_all(first_load)
    down[...] = contract(branch[...], full_out[...], 1, 1).astype(BF16)
    wait_all(takes)
    owner = lax.shift_right_logical(
        lax.broadcasted_iota(jnp.int32, (HEADS, width), 1), head.bit_length() - 1
    )
    chosen = jnp.where(
        owner == lax.broadcasted_iota(jnp.int32, (HEADS, width), 0), 1.0, 0.0
    ).astype(BF16)
    left = lax.broadcasted_iota(jnp.int32, (space, pair), 1) < head
    live = lax.broadcasted_iota(jnp.int32, (space, pair), 0) < length
    key_live = lax.broadcasted_iota(jnp.int32, (space, space), 0) < length
    for image in range(count):
        span = pl.ds(image * space, space)
        product = down[span].astype(F32) * mixed[span].astype(F32)
        coarse = product.astype(BF16)
        fine = (product - coarse.astype(F32)).astype(BF16)
        stage[image, :, 0:space] = contract(chosen, coarse, 1, 1) + contract(chosen, fine, 1, 1)

    def heads(index, carry):
        for image in range(count):
            span = pl.ds(image * space, space)

            def part(block):
                offset = pl.multiple_of(block * width + index * pair, pair)
                return packed[span, pl.ds(offset, pair)]

            query, key, value = part(0), part(1), part(2)
            wide = key.astype(F32) * scale
            value = value.astype(F32)
            arrived = down[span, pl.ds(pl.multiple_of(index * pair, pair), pair)]
            found = []
            for side in range(2):
                mine = left if side == 0 else ~left
                log = logs[image, pl.ds(2 * index + side, 1), :]
                dot = stage[image, pl.ds(2 * index + side, 1), 0:space]
                scores = contract(jnp.where(mine, wide, 0.0).astype(BF16), query, 1, 1)
                chance = jnp.exp(jnp.where(key_live, scores - log, NEGATIVE))
                back = contract(jnp.where(mine, value, 0.0).astype(BF16), arrived, 1, 1)
                change = (chance * (back - dot)).astype(BF16)
                found.append(
                    (
                        contract(change, key, 0, 0),
                        contract(change, query, 1, 0),
                        contract(chance.astype(BF16), arrived, 1, 0),
                    )
                )
            for block, factor in enumerate((scale, scale, 1.0)):
                total = jnp.where(left, found[0][block], found[1][block]) * factor
                offset = pl.multiple_of(block * width + index * pair, pair)
                grads[span, pl.ds(offset, pair)] = jnp.where(live, total, 0.0).astype(BF16)
        return carry

    lax.fori_loop(0, HEADS // 2, heads, 0)
    wait_all(load)
    for block in range(2):
        normal[:, block * half : (block + 1) * half] = contract(
            grads[...], full[block * half : (block + 1) * half], 1, 1
        )
    gain = vec[GAIN0 : GAIN0 + 1]
    tallies[...] = jnp.zeros_like(tallies)

    def step(here):
        unit, rate = standardized(x[here].astype(F32))
        grad = normal[here]
        tallies[0] += eights(grad * unit)
        tallies[1] += eights(grad)
        result[here] = (mid_grad[here] + norm_pull(grad, gain, unit, rate)).astype(BF16)

    step(pl.ds(0, rows))
    for index in range(2):
        sums[index : index + 1] = jnp.sum(tallies[index], axis=0, keepdims=True)
    sums[2:3] = jnp.sum(grads[:, 0:width].astype(F32), axis=0, keepdims=True)
    sums[3:4] = jnp.sum(grads[:, 2 * width : 3 * width].astype(F32), axis=0, keepdims=True)


def backward(
    start, lower, upper, kept_low, kept_up, reduce, wide, qkv, params, meta, count, length,
    mixed_at, weight=LIGHT,
):
    feed, attend = reduce is not None, qkv is not None
    rows, width = start[0].shape
    space = rows // count
    pair = 2 * width // HEADS
    parts = len(reduce if feed else qkv)
    many = len(flat(reduce if feed else qkv))
    spots = parts + 1 + count
    inner = wide[0][0].shape[1] - width if feed else 0
    deep = inner // parts
    both = feed and attend
    choices = []
    if feed:
        choices += [(kept_low[0], kept_up[0]), (kept_low[1], kept_up[1])]
        if start[0] is not start[1]:
            choices += [start]
    if attend:
        choices += [(kept_low[index], kept_up[index]) for index in (2, 3, 4)]
        choices += [(lower, upper)]
    plain = [start[0]] if feed and start[0] is start[1] else [] if feed else list(start)
    operands = []
    for low, up in choices:
        operands += [low] if low is up else [low, up]

    def body(*refs):
        refs = list(refs)
        firsts = [refs.pop(0) for _ in plain]
        pairs = []
        for low, up in choices:
            one = refs.pop(0)
            pairs.append((one, one if low is up else refs.pop(0)))
        lists = [[refs.pop(0) for _ in range(many)] for _ in range(2 * feed + 2 * attend)]
        vec, info = refs.pop(0), refs.pop(0)
        section = info[parts]
        if feed:
            if both:
                right = refs.pop(0)
                hidden, branch = right.at[:, pl.ds(0, inner)], right.at[:, pl.ds(inner, width)]
            else:
                hidden, branch = refs.pop(0), refs.pop(0)
            feed_sums, inner_sums = refs.pop(0), refs.pop(0)
            mid_grad = None if both else refs.pop(0)
        if attend:
            grads, result, sums = (refs.pop(0) for _ in range(3)) if not both else (None, refs.pop(0), refs.pop(0))
        if both:
            feed_grad = right.at[:, pl.ds(inner + width, width)]
            grads = right.at[:, pl.ds(inner + 2 * width, 3 * width)]
        tallies, x_sem = refs.pop(0), refs.pop(0)
        if feed:
            grad, slope, middle, second, full_out, full, o_sem, w_sem = (
                refs.pop(0) for _ in range(8)
            )
            if both:
                mid_grad, keep = refs.pop(0), feed_grad
            else:
                keep = refs.pop(0)
            begin = pairs.pop(2) if start[0] is not start[1] else (firsts[0], firsts[0])
            take = start_chosen(section, *begin, grad, x_sem.at[0])
            for_slope = start_chosen(section, *pairs.pop(0), slope, x_sem.at[1])
            every = start_pieces(lists.pop(0), info, spots, full_out, o_sem, 0, (0, width))
            first_load = [[every.pop(0) for _ in group] for group in reduce]
            for_middle = start_chosen(section, *pairs.pop(0), middle, x_sem.at[2])
            load = start_pieces(lists.pop(0), info, spots, full, w_sem, 0, (0, inner), width)
        if attend:
            x, packed, mixed, logs, down, normal, stage, full_o, full_q, p_sem, q_sem = (
                refs.pop(0) for _ in range(11)
            )
            if not feed:
                branch, mid_grad = refs.pop(0), refs.pop(0)
                givens = [
                    pltpu.make_async_copy(source, target, x_sem.at[index])
                    for index, (source, target) in enumerate(zip(firsts, (branch, mid_grad)))
                ]
                for given in givens:
                    given.start()
            project_load = start_pieces(lists.pop(0), info, spots, full_o, p_sem, 0, (0, width))
            sames = [one is two for one, two in pairs]
            pairs[1] = tuple(one.at[:, pl.ds(mixed_at, width)] for one in pairs[1])
            takes = [
                start_chosen(section, *pairs[index], target, x_sem.at[3 + index], sames[index])
                for index, target in ((1, mixed), (0, packed), (2, logs), (3, x))
            ]
            last_load = start_pieces(lists.pop(0), info, spots, full_q, q_sem, 0, (0, 3 * width))
            if not feed:
                wait_all(givens)
        if feed:
            take.wait()
            hidden_back_stage(
                grad, vec, info, keep, slope, middle, hidden, second, mid_grad, branch, feed_sums,
                inner_sums, full_out, full, deep, first_load, load, for_slope, for_middle, tallies,
                count, parts,
            )
        if attend:
            attention_back_stage(
                x, vec, branch, mid_grad, packed, mixed, logs, grads, result, sums, down, normal,
                stage, full_o, full_q, project_load, last_load, takes, tallies, count, length,
            )

    outs = []
    scratch = [pltpu.VMEM((4, 8, width), F32), pltpu.SemaphoreType.DMA((7,))]
    flops = 0
    if feed:
        outs += [((rows, inner + 5 * width), BF16)] if both else [((rows, inner), BF16), ((rows, width), BF16)]
        outs += [
            ((8, width), F32),
            ((1, inner), F32),
        ]
        if not both:
            outs += [((rows, width), F32)]
        scratch += [
            pltpu.VMEM((rows, width), BF16),
            pltpu.VMEM((rows, inner), BF16),
            pltpu.VMEM((rows, width), F32),
            pltpu.VMEM((rows, width), F32),
            pltpu.VMEM((inner, width), BF16),
            pltpu.VMEM((width, inner), BF16),
            pltpu.SemaphoreType.DMA((1, many)),
            pltpu.SemaphoreType.DMA((1, many)),
        ]
        scratch += [pltpu.VMEM((rows, width), F32 if both else BF16)]
        flops += 4 * rows * width * inner
    if attend:
        outs += [] if both else [((rows, 3 * width), BF16)]
        outs += [((rows, width), BF16), ((8, width), F32)]
        scratch += [
            pltpu.VMEM((rows, width), BF16),
            pltpu.VMEM((rows, 3 * width), BF16),
            pltpu.VMEM((rows, width), BF16),
            pltpu.VMEM((count, HEADS, space), F32),
            pltpu.VMEM((rows, width), BF16),
            pltpu.VMEM((rows, width), F32),
            pltpu.VMEM((count, HEADS, 2 * pair), F32),
            pltpu.VMEM((width, width), BF16),
            pltpu.VMEM((width, 3 * width), BF16),
            pltpu.SemaphoreType.DMA((1, many)),
            pltpu.SemaphoreType.DMA((1, many)),
        ]
        if not feed:
            scratch += [pltpu.VMEM((rows, width), BF16), pltpu.VMEM((rows, width), F32)]
        flops += 2 * rows * width * (4 * width + 5 * space)
    weights = (flat(reduce) + flat(wide) if feed else []) + (
        flat(wide) + flat(qkv) if attend else []
    )
    return call(
        body,
        "backward" + "_feed" * feed + "_attend" * attend,
        plain + operands + weights + [params, meta],
        [ANY] * (len(plain) + len(operands) + len(weights)) + [VMEM, SMEM],
        outs,
        scratch,
        flops,
        weight,
    )


def weight_gradient(
    lefts, rights, meta, parts, blocks, quarter, rows_of, columns_of, name, weight=LIGHT
):
    terms = len(lefts)
    first_row, height = rows_of
    first_column, breadth = columns_of
    rows = lefts[0].shape[0]
    operands = list(lefts)
    places = []
    for pair in rights:
        found = []
        for array, _ in pair:
            if not any(array is other for other in operands):
                operands.append(array)
            found.append(next(i for i, other in enumerate(operands) if other is array))
        places.append(found)

    def body(*refs):
        sources, info = refs[: len(operands)], refs[len(operands)]
        results = refs[len(operands) + 1 : len(operands) + 1 + len(blocks)]
        left_full, right_full, l_sem, r_sem = refs[len(operands) + 1 + len(blocks) :]
        section = info[parts]
        waits = []
        for term in range(terms):
            sides = [
                sources[place].at[:, pl.ds(column + first_column, breadth)]
                for place, (_, column) in zip(places[term], rights[term])
            ]
            same = rights[term][0] is rights[term][1]
            target = right_full.at[pl.ds(term * rows, rows)]
            waits.append(start_chosen(section, *sides, target, r_sem.at[term], same))
        loads = []
        for index, block in enumerate(blocks):
            start = pl.multiple_of(info[block] * quarter + first_row, 128)
            for term in range(terms):
                copy = pltpu.make_async_copy(
                    sources[term].at[:, pl.ds(start, height)],
                    left_full.at[index, pl.ds(term * rows, rows)],
                    l_sem.at[index, term],
                )
                copy.start()
                loads.append(copy)
        wait_all(waits)
        for index in reversed(range(len(blocks))):
            wait_all(loads[index * terms : (index + 1) * terms])
            results[index][...] = contract(left_full[index], right_full[...], 0, 0).astype(BF16)

    return call(
        body,
        name,
        operands + [meta],
        [ANY] * len(operands) + [SMEM],
        [((height, breadth), BF16)] * len(blocks),
        [
            pltpu.VMEM((len(blocks), terms * rows, height), BF16),
            pltpu.VMEM((terms * rows, breadth), BF16),
            pltpu.SemaphoreType.DMA((len(blocks), terms)),
            pltpu.SemaphoreType.DMA((terms,)),
        ],
        2 * len(blocks) * terms * rows * height * breadth,
        weight,
    )


def after(value, *earlier):
    return lax.optimization_barrier((value,) + earlier)[0]


def added(*values):
    total = values[0].astype(F32)
    for value in values[1:]:
        total = total + value.astype(F32)
    return total.astype(values[0].dtype)


class FourByFour:
    parts = 4
    blocks = (0, 2)

    def __init__(self):
        self.group = lax.axis_index("group")
        self.place = lax.axis_index("replica")
        self.order = [self.group ^ part for part in range(4)]
        odd = self.place % 2
        halves = [2 * self.order[part] + half for part in (2, 3) for half in (odd, 1 - odd)]
        self.spots = self.order[:2] + halves

    def core(self, block):
        return lax.ppermute(block, "group", [(i, i ^ 1) for i in range(4)])

    def across(self, block):
        return lax.ppermute(block, "group", [(i, i ^ 2) for i in range(4)])

    def beside(self, block):
        return lax.ppermute(block, "replica", [(i, i ^ 1) for i in range(4)])

    def gather_small(self, block):
        near, far = self.core(block), self.across(block)
        return [block, near, far, self.core(far)]

    def gather(self, blocks, prepare):
        odd = self.place % 2
        asked = [
            lax.dynamic_slice_in_dim(block, odd * (block.shape[0] // 2), block.shape[0] // 2)
            for block in blocks
        ]
        halves, sibling = [], []
        for index, block in enumerate(blocks):
            halves.append(self.across(after(asked[index], *halves[: max(index - 1, 0)])))
            sibling.append(self.core(after(block, sibling[-1]) if index else block))
        others = []
        tokens = prepare(halves[0]) + asked[2:]
        for index, half in enumerate(halves):
            others.append(self.beside(after(half, *others[-1:], *(tokens if index == 1 else []))))

        def pieces(index, *tokens):
            one, two = (after(half, *tokens) for half in (halves[index], others[index]))
            return [
                [blocks[index]],
                [sibling[index]],
                [halves[index], others[index]],
                [self.core(one), self.core(two)],
            ]

        return [partial(pieces, index) for index in range(len(blocks))]

    def shared(self, block):
        return [block, self.core(block)]

    def total(self, blocks):
        passed = self.across(blocks[1])
        token = yield
        mine = added(after(blocks[0], token), passed)
        inward = lax.ppermute(mine, "replica", [(0, 1), (3, 2)])
        token = yield mine
        joined = added(after(mine, token), inward)
        crossing = lax.ppermute(joined, "replica", [(1, 2), (2, 1)])
        token = yield joined
        summed = added(after(joined, token), crossing)
        outward = lax.ppermute(summed, "replica", [(1, 0), (2, 3)])
        token = yield summed
        inner = (self.place == 1) | (self.place == 2)
        yield jnp.where(inner, after(summed, token), outward)


class General:
    def __init__(self):
        self.parts = lax.axis_size("group")
        self.blocks = tuple(range(self.parts))
        self.order = self.spots = [jnp.int32(part) for part in range(self.parts)]

    def gather_small(self, block):
        whole = lax.all_gather(block, "group", axis=0)
        return [whole[part] for part in range(self.parts)]

    def gather(self, blocks, prepare):
        prepare(blocks[0])
        found = [[[piece] for piece in self.gather_small(block)] for block in blocks]
        return [lambda *tokens, groups=groups: groups for groups in found]

    def shared(self, block):
        return [block]

    def total(self, blocks):
        yield
        mine = lax.psum_scatter(jnp.stack(blocks), "group", scatter_dimension=0)
        yield mine
        yield lax.psum(mine, "replica")


def shifted(block, distance):
    devices = range(lax.axis_size("section"))
    route = [(i - distance, i) for i in devices if i - distance in devices]
    return lax.ppermute(block, "section", route)


def in_order(pieces, order):
    place = jnp.stack(order)
    stacked = []
    for block in range(len(pieces)):
        chosen = pieces[0]
        for part in range(1, len(pieces)):
            chosen = jnp.where(place[part] == block, pieces[part], chosen)
        stacked.append(chosen)
    return jnp.stack(stacked)


class Sequence:
    def __init__(self, net, token):
        self.net, self.sums, self.results, self.token = net, {}, {}, token

    def now(self, value):
        return after(value, self.token)

    def ran(self, value):
        self.token = value

    def add(self, name, blocks):
        self.sums[name] = self.net.total(blocks)
        next(self.sums[name])

    def step(self, *names):
        for name in names:
            try:
                self.results[name] = self.token = self.sums[name].send(self.token)
            except StopIteration:
                continue

    def finish(self, name):
        while True:
            try:
                self.results[name] = self.sums[name].send(self.token)
            except StopIteration:
                return self.results[name]


def per_device(
    images,
    cotangent,
    counts,
    qkv_weight,
    out_weight,
    expand_weight,
    reduce_weight,
    norm_gains,
    biases,
    expand_bias,
):
    micro, slots, length, width = images.shape
    space = padded(length)
    section = lax.axis_index("section")
    first = section == 0
    sizes = (lax.axis_size("group"), lax.axis_size("replica"))
    net = FourByFour() if sizes == (4, 4) else General()
    parts = net.parts
    share = width // parts
    batches = tuple(range(micro))

    def rows_of(array):
        fulls = [jnp.pad(array[batch], ((0, 0), (0, space - length), (0, 0))) for batch in batches]
        return [full.reshape(slots * space, width) for full in fulls]

    def images_of(array):
        return array.reshape(slots, space, width)[:, :length]

    small = jnp.concatenate([norm_gains[0], biases[0], expand_bias[0].reshape(-1, share)])
    slot = jnp.arange(slots, dtype=jnp.int32)
    alive = [(slot < counts[batch, 0]).astype(jnp.int32) for batch in batches]
    head = jnp.stack(net.order + [section]).astype(jnp.int32)

    spots = jnp.stack(net.spots).astype(jnp.int32)

    def meta(living):
        return jnp.concatenate([head, living, spots])

    infos = [meta(alive[batch]) for batch in batches]
    pieces = net.gather_small(small)
    vectors = in_order(pieces, net.order)
    top = vectors[:, :8].transpose(1, 0, 2).reshape(8, width)
    bottom = vectors[:, 8:].reshape(-1, width)
    params = jnp.concatenate([top, bottom]).astype(F32)
    slot = jnp.arange(slots, dtype=jnp.int32)
    alive = [(slot < counts[batch, 0]).astype(jnp.int32) for batch in batches]
    head = jnp.stack(net.order + [section]).astype(jnp.int32)
    spots = jnp.stack(net.spots).astype(jnp.int32)

    def meta(living):
        return jnp.concatenate([head, living, spots])

    infos = [meta(alive[batch]) for batch in batches]
    inputs, targets = [], []

    def prepare(token):
        inputs.extend(rows_of(after(images, token)))
        targets.extend(rows_of(after(cotangent, token)))
        return [params, *inputs, *targets, *infos]

    qkv, wide, reduce = net.gather(
        [qkv_weight[0], jnp.concatenate([out_weight[0], expand_weight[0]], axis=1), reduce_weight[0]],
        prepare,
    )

    qkv = qkv()
    attended = []
    for batch in batches:
        start = inputs[batch] if batch == 0 else after(inputs[batch], attended[-1][0])
        attended.append(
            forward(start, start, None, qkv, None, params, infos[batch], slots, length)
        )
    wide = wide(attended[-1][0])
    fed = []
    for batch in batches:
        start = inputs[batch] if batch == 0 else after(inputs[batch], fed[-1][0])
        fed.append(
            forward(start, start, attended[batch][0], None, wide, params, infos[batch], slots, length)
        )
    reduce = reduce(fed[-1][0])
    early, incoming = [], []
    for batch in batches:
        middle, active = fed[batch][:2]
        if batch:
            active = after(active, early[-1])
        early.append(output_forward(middle, active, reduce, params, infos[batch], slots))
        incoming.append(shifted(early[batch], 1))

    inner = wide[0][0].shape[1] - width
    mixed_at = inner + width
    kept, lefts, rights, results = [], [], [], []
    sums_a, sums_b, sums_c, returning = [], [], [], []
    token = early[-1]
    for batch in batches:
        start = after(incoming[batch], token)
        left, packed, logs, middle, slope = forward(
            inputs[batch], start, None, qkv, wide, params, infos[batch], slots, length, 8.0
        )
        kept.append((slope, middle, packed, left, logs))
        lefts.append(net.shared(left))
        if batch == 0:
            pair, sides = (targets[0], targets[0]), (kept[0], kept[0])
            lower, chosen = incoming[0], infos[0]
        else:
            pair = (returning[batch - 1], targets[batch])
            sides = (kept[batch - 1], kept[batch])
            lower = inputs[batch - 1]
            chosen = meta(jnp.where(first, alive[batch - 1], alive[batch]))
        right, some, more, result, rest = backward(
            pair, lower, incoming[batch], sides[0], sides[1], reduce, wide, qkv, params, chosen,
            slots, length, mixed_at, 8.0,
        )
        token = result
        rights.append(net.shared(right))
        results.append(result)
        sums_a.append(some)
        sums_b.append(more)
        sums_c.append(rest)
        returning.append(shifted(result, -1))
    late = []
    for batch in batches:
        ready = lefts[batch][1:] + (rights[batch][1:] if batch < micro - 1 else [])
        active = after(kept[batch][3], token, *ready)
        late.append(output_forward(kept[batch][1], active, reduce, params, infos[batch], slots, 8.0))
        token = late[-1]

    last = micro - 1
    run = Sequence(net, token)
    arrived = run.now(returning[last])
    living = jnp.repeat(alive[last] > 0, space)[:, None]
    masked = net.shared(jnp.where(living, arrived, jnp.zeros_like(arrived)))
    many = len(masked)

    def gradient(name, left_at, final, final_at, right_at, quarter, rows, columns, weight=LIGHT):
        left = [lefts[batch][side] for batch in batches for side in range(many)]
        right = []
        for batch in batches:
            for side in range(many):
                upper = (rights[batch][side], right_at)
                lower = (final[side], final_at) if batch == last else (rights[batch + 1][side], right_at)
                right.append((lower, upper))
        blocks = weight_gradient(
            left, right, run.now(head), parts, net.blocks, quarter, (left_at + rows[0], rows[1]), columns,
            name, weight,
        )
        run.ran(blocks[0])
        return blocks

    def reduce_part(index, weight=LIGHT):
        step = inner // parts // 2
        blocks = gradient(
            "reduce", 0, masked, 0, inner + width, inner // parts, (index * step, step), (0, width), weight
        )
        run.add(f"reduce{index}", blocks)

    def expand_part(index):
        step = inner // 2
        blocks = gradient("expand", inner, finals, 0, 0, share, (0, share), (index * step, step))
        run.add(f"expand{index}", blocks)

    def qkv_part(index):
        step = 3 * width // 2
        at = inner + 2 * width
        return gradient("qkv", at, grads, 0, at, share, (0, share), (index * step, step))

    reduce_part(0)
    start = run.now(arrived)
    final, branch, some, more, mid = backward(
        (start, start), None, None, kept[last], kept[last], reduce, wide, None, params, infos[last],
        slots, length, mixed_at,
    )
    run.ran(final)
    finals, branches = net.shared(final), net.shared(branch)
    sums_a.append(some)
    sums_b.append(more)
    run.step("reduce0")
    reduce_part(1, HEAVY)
    expand_part(0)
    expand_part(1)
    run.step("reduce1", "reduce0")
    grads, result, rest = backward(
        (run.now(after(branch, *branches[1:])), mid), inputs[last], inputs[last], kept[last], kept[last], None, wide, qkv,
        params, infos[last], slots, length, mixed_at, HEAVY,
    )
    run.ran(result)
    grads = net.shared(grads)
    results.append(result)
    sums_c.append(rest)
    run.step("expand0", "reduce1", "reduce0")
    run.add(
        "project", gradient("project", mixed_at, branches, 0, inner, share, (0, share), (0, width), HEAVY)
    )
    run.add("qkv0", qkv_part(0))
    run.step("expand1", "expand0", "reduce1", "reduce0", "project")

    def over_batches(values):
        return sum(jnp.where(first, values[batch + 1], values[batch]) for batch in batches)

    some, more, rest = over_batches(sums_a), over_batches(sums_b), over_batches(sums_c)
    rows = jnp.concatenate([rest[0:1], some[0:1], rest[1:2], some[1:2], rest[2:4], some[2:4]])
    rows = rows.reshape(8, parts, share).transpose(1, 0, 2)
    rows = jnp.concatenate([rows, more.reshape(parts, -1, share)], axis=1)
    rows = sum(net.shared(run.now(rows)))
    rows = jnp.stack(
        [lax.dynamic_index_in_dim(rows, net.order[block], 0, keepdims=False) for block in net.blocks]
    )
    count, step = rows.shape[1], 3 * width // 2
    rows = rows.reshape(len(net.blocks), -1)
    rows = jnp.pad(rows, ((0, 0), (0, -rows.shape[1] % (16 * step)))).reshape(len(net.blocks), -1, step)
    blocks = qkv_part(1)
    run.add("qkv1", [jnp.concatenate([one, two]) for one, two in zip(blocks, rows.astype(BF16))])
    run.step(
        "qkv0", "expand1", "expand0", "project", "reduce1", "qkv1", "expand1", "qkv0", "expand0", "project"
    )
    outputs = [
        images_of(jnp.where(first, run.now(low), up))
        for low, up in zip(early + results[1:], late + results[:-1])
    ]
    run.step("qkv1", "qkv0", "expand1", "project", "qkv1", "qkv0", "qkv1")
    weights = {name: run.finish(name) for name in run.sums}
    vector = weights["qkv1"][share:].reshape(-1)[: count * share].reshape(count, share).astype(F32)

    def joined(axis, *names):
        return jnp.concatenate([weights[name] for name in names], axis=axis).astype(F32)[None]

    return (
        jnp.stack(outputs[:micro])[None],
        jnp.stack(outputs[micro:])[None],
        jnp.concatenate([weights["qkv0"], weights["qkv1"][:share]], axis=1).astype(F32)[None],
        weights["project"].astype(F32)[None],
        joined(1, "expand0", "expand1"),
        joined(0, "reduce0", "reduce1"),
        vector[None, 0:2],
        vector[None, 2:8],
        vector[8:].reshape(1, -1),
    )


def solution(mesh):
    placed = (
        P(None, ("group", "replica"), None, None),
        P(None, ("group", "replica"), None, None),
        P(None, ("group", "replica")),
        P("section", "group", None),
        P("section", "group", None),
        P("section", "group", None),
        P("section", "group", None),
        P("section", None, "group"),
        P("section", None, "group"),
        P("section", "group"),
    )
    return jax.shard_map(
        per_device,
        mesh=mesh,
        in_specs=placed,
        out_specs=(
            P("section", None, ("group", "replica"), None, None),
            P("section", None, ("group", "replica"), None, None),
            P("section", "group", None),
            P("section", "group", None),
            P("section", "group", None),
            P("section", "group", None),
            P("section", None, "group"),
            P("section", None, "group"),
            P("section", "group"),
        ),
        check_vma=False,
    )
```

```python
from functools import partial

import jax
import jax.numpy as jnp
from jax import lax
from jax.experimental import pallas as pl
from jax.experimental.pallas import tpu as pltpu
from jax.sharding import PartitionSpec as P

HEADS = 16
EPSILON = 1e-06
NEGATIVE = -1e30
F32 = jnp.float32
BF16 = jnp.bfloat16
LIGHT, HEAVY = 1.0 / 64, 16.0
VMEM_LIMIT = 58 * 2**20
ROOT_HALF = 0.7071067811865476
ROOT_TAU = 0.3989422804014327
ANY = pl.BlockSpec(memory_space=pl.ANY)
VMEM = pl.BlockSpec(memory_space=pltpu.VMEM)
SMEM = pl.BlockSpec(memory_space=pltpu.SMEM)
GAIN0, GAIN1, SHIFT0, SHIFT1, QUERY, VALUE, OUT, FEED, EXPAND = range(9)


def padded(length):
    return -(-length // 16) * 16


def contract(left, right, left_dim, right_dim):
    return lax.dot_general(
        left, right, (((left_dim,), (right_dim,)), ((), ())), preferred_element_type=F32
    )


def standardized(values):
    center = values - jnp.mean(values, axis=-1, keepdims=True)
    spread = jnp.mean(center * center, axis=-1, keepdims=True)
    scale = lax.rsqrt(spread + EPSILON)
    return center * scale, scale


def norm_pull(grad, gain, unit, scale):
    scaled = grad * gain
    mean = jnp.mean(scaled, axis=-1, keepdims=True)
    along = jnp.mean(scaled * unit, axis=-1, keepdims=True)
    return scale * (scaled - mean - unit * along)


def call(body, name, operands, specs, outs, scratch, flops, weight=LIGHT):
    moved = sum(o.size * o.dtype.itemsize for o in operands)
    out_shape = [jax.ShapeDtypeStruct(shape, dtype) for shape, dtype in outs]
    moved += sum(o.size * o.dtype.itemsize for o in out_shape)
    return pl.pallas_call(
        body,
        out_shape=out_shape,
        in_specs=specs,
        out_specs=[VMEM] * len(outs),
        scratch_shapes=scratch,
        compiler_params=pltpu.CompilerParams(vmem_limit_bytes=VMEM_LIMIT),
        cost_estimate=pl.CostEstimate(flops=int(flops * weight), bytes_accessed=int(moved * weight), transcendentals=0),
        name=name,
    )(*operands)


def flat(groups):
    return [piece for group in groups for piece in group]


def start_pieces(pieces, info, first, target, sems, slot, columns, shift=0):
    begin, size = columns
    columns = pl.ds(begin, size)
    copies = []
    for index, piece in enumerate(pieces):
        rows = piece.shape[0]
        where = pl.multiple_of(info[first + index] * rows, rows)
        copy = pltpu.make_async_copy(
            piece.at[:, pl.ds(begin + shift, size)],
            target.at[pl.ds(where, rows), columns],
            sems.at[slot, index],
        )
        copy.start()
        copies.append(copy)
    return copies


def wait_all(copies):
    for copy in copies:
        copy.wait()


def start_chosen(section, lower, upper, target, sem, same=False):
    if lower is upper or same:
        copy = pltpu.make_async_copy(lower, target, sem)
        copy.start()
        return copy

    @pl.when(section == 0)
    def _():
        pltpu.make_async_copy(lower, target, sem).start()

    @pl.when(section != 0)
    def _():
        pltpu.make_async_copy(upper, target, sem).start()

    return pltpu.make_async_copy(lower, target, sem)


def eights(values):
    return jnp.sum(values.reshape(-1, 8, values.shape[-1]), axis=0)


def attention_stage(x, vec, norm, packed, mixed, logs, columns, full, loads, count, length):
    rows, width = x.shape
    space = rows // count
    head = width // HEADS
    pair = 2 * head
    scale = head**-0.5
    gain, shift = vec[GAIN0 : GAIN0 + 1], vec[SHIFT0 : SHIFT0 + 1]

    def step(here):
        unit, _ = standardized(x[here].astype(F32))
        norm[here] = (unit * gain + shift).astype(BF16)

    step(pl.ds(0, rows))
    for block in range(3):
        wait_all(loads[block])
        done = contract(norm[...], full[:, block * width : (block + 1) * width], 1, 0)
        if block != 1:
            bias = QUERY if block == 0 else VALUE
            done = done + vec[bias : bias + 1]
        packed[:, block * width : (block + 1) * width] = done.astype(BF16)
    lane = lax.broadcasted_iota(jnp.int32, (space, pair), 1)
    left = lane < head
    live = lax.broadcasted_iota(jnp.int32, (space, pair), 0) < length
    key_live = lax.broadcasted_iota(jnp.int32, (space, space), 1) < length
    columns[...] = jnp.zeros_like(columns)

    def heads(index, carry):
        for image in range(count):
            span = pl.ds(image * space, space)

            def part(block):
                offset = pl.multiple_of(block * width + index * pair, pair)
                return packed[span, pl.ds(offset, pair)]

            query, key, value = part(0).astype(F32) * scale, part(1), part(2).astype(F32)
            found = []
            tops = []
            for side in range(2):
                mine = left if side == 0 else ~left
                asked = jnp.where(mine, query, 0.0).astype(BF16)
                held = jnp.where(live, jnp.where(mine, value, 1.0), 0.0).astype(BF16)
                scores = jnp.where(key_live, contract(asked, key, 1, 1), NEGATIVE)
                top = jnp.max(scores, axis=-1, keepdims=True)
                raised = jnp.exp(scores - top).astype(BF16)
                found.append(contract(raised, held, 1, 0))
                tops.append(top)
            inside = jnp.where(left, found[0], found[1])
            total = jnp.where(left, found[1], found[0])
            turned = pltpu.roll(total, head, 1)
            offset = pl.multiple_of(index * pair, pair)
            mixed[span, pl.ds(offset, pair)] = (inside / turned).astype(BF16)
            if logs is None:
                continue
            logged = jnp.log(turned)
            first = tops[0] + logged[:, 0:1]
            second = tops[1] + logged[:, head : head + 1]
            known = columns[image]
            known = jnp.where(lane == 2 * index, first, known)
            columns[image] = jnp.where(lane == 2 * index + 1, second, known)
        return carry

    lax.fori_loop(0, HEADS // 2, heads, 0)
    if logs is not None:
        for image in range(count):
            logs[image] = columns[image].T[0:HEADS]


def hidden_stage(x, vec, mixed, middle, active, second, slope, full_out, full, first_load, loads):
    rows, width = x.shape
    wait_all(first_load)
    gain, shift, bias = vec[GAIN1 : GAIN1 + 1], vec[SHIFT1 : SHIFT1 + 1], vec[OUT : OUT + 1]
    middle[...] = contract(mixed[...], full_out[...], 1, 0)

    def step(here):
        total = middle[here] + x[here].astype(F32) + bias
        middle[here] = total
        unit, _ = standardized(total)
        second[here] = (unit * gain + shift).astype(BF16)

    step(pl.ds(0, rows))
    for block, load in enumerate(loads):
        wait_all(load)
        part = slice(block * width, (block + 1) * width)
        value = contract(second[...], full[:, part], 1, 0) + vec[EXPAND + block : EXPAND + block + 1]
        share = 0.5 + 0.5 * lax.erf(value * ROOT_HALF)
        active[:, part] = (value * share).astype(BF16)
        if slope is not None:
            density = ROOT_TAU * jnp.exp(-0.5 * value * value)
            slope[:, part] = (share + value * density).astype(BF16)


def forward(
    lower, upper, mixed_in, qkv, wide, params, meta, count, length, weight=LIGHT
):
    rows, width = lower.shape
    space = rows // count
    pair = 2 * width // HEADS
    attend, feed = qkv is not None, wide is not None
    both = attend and feed
    parts = len(qkv if attend else wide)
    many = len(flat(qkv if attend else wide))
    spots = parts + 1 + count
    inner = wide[0][0].shape[1] - width if feed else 0
    blocks = inner // width
    same = lower is upper

    def body(*refs):
        refs = list(refs)
        low = refs.pop(0)
        up = low if same else refs.pop(0)
        if not attend:
            arrived = refs.pop(0)
        lists = [[refs.pop(0) for _ in range(many)] for _ in range(attend + 2 * feed)]
        vec, info = refs.pop(0), refs.pop(0)
        if both:
            left, packed, logs, middle, slope = (refs.pop(0) for _ in range(5))
            active, second, mixed, norm = (
                left.at[:, pl.ds(start, size)]
                for start, size in ((0, inner), *((inner + width * i, width) for i in range(3)))
            )
        elif attend:
            mixed = refs.pop(0)
        else:
            middle, active = refs.pop(0), refs.pop(0)
        x, x_sem = refs.pop(0), refs.pop(0)
        section = info[parts]
        take = start_chosen(section, low, up, x, x_sem.at[0])
        if attend:
            columns, full, a_sem = (refs.pop(0) for _ in range(3))
            if not both:
                norm, packed, logs = refs.pop(0), refs.pop(0), None
            weight = lists.pop(0)
            loads = [
                start_pieces(weight, info, spots, full, a_sem, block, (block * width, width))
                for block in range(3)
            ]
        if feed:
            full_out, full_in, o_sem, w_sem = (refs.pop(0) for _ in range(4))
            if not attend:
                mixed, second, slope = refs.pop(0), refs.pop(0), None
                extra = pltpu.make_async_copy(arrived, mixed, x_sem.at[1])
                extra.start()
            first_load = start_pieces(lists[0], info, spots, full_out, o_sem, 0, (0, width))
            inner_loads = [
                start_pieces(lists[1], info, spots, full_in, w_sem, block, (block * width, width), width)
                for block in range(blocks)
            ]
        take.wait()
        if attend:
            attention_stage(
                x, vec, norm, packed, mixed, logs, columns, full, loads, count, length
            )
        if feed:
            if not attend:
                extra.wait()
            hidden_stage(
                x, vec, mixed, middle, active, second, slope, full_out, full_in, first_load,
                inner_loads,
            )

    outs, inputs = [], [lower] if same else [lower, upper]
    scratch = [pltpu.VMEM((rows, width), BF16), pltpu.SemaphoreType.DMA((2,))]
    flops = 0
    if attend:
        outs += [
            ((rows, width), BF16),
            ((rows, 3 * width), BF16),
            ((rows, width), BF16),
            ((count, HEADS, space), F32),
        ]
        scratch += [
            pltpu.VMEM((count, space, pair), F32),
            pltpu.VMEM((width, 3 * width), BF16),
            pltpu.SemaphoreType.DMA((3, many)),
        ]
        if not feed:
            scratch += [pltpu.VMEM((rows, width), BF16), pltpu.VMEM((rows, 3 * width), BF16)]
        flops += 2 * rows * width * (3 * width + 2 * space)
    else:
        inputs += [mixed_in]
    if feed:
        outs += [
            ((rows, width), F32),
            ((rows, inner), BF16),
            ((rows, width), BF16),
            ((rows, inner), BF16),
        ]
        scratch += [
            pltpu.VMEM((width, width), BF16),
            pltpu.VMEM((width, inner), BF16),
            pltpu.SemaphoreType.DMA((1, many)),
            pltpu.SemaphoreType.DMA((blocks, many)),
        ]
        if not attend:
            scratch += [pltpu.VMEM((rows, width), BF16), pltpu.VMEM((rows, width), BF16)]
        flops += 2 * rows * width * (width + inner)
    if both:
        outs = [((rows, inner + 3 * width), BF16), outs[1], outs[3], outs[4], outs[7]]
    else:
        outs = [outs[2]] if attend else outs[:2]
    weights = (flat(qkv) if attend else []) + (2 * flat(wide) if feed else [])
    return call(
        body,
        "forward" + "_attend" * attend + "_feed" * feed,
        inputs + weights + [params, meta],
        [ANY] * (len(inputs) + len(weights)) + [VMEM, SMEM],
        outs,
        scratch,
        flops,
        weight,
    )


def output_forward(middle, active, pieces, params, meta, count, weight=LIGHT, columns=None):
    rows, width = middle.shape
    first, width = columns or (0, width)
    inner = sum(piece.shape[0] for piece in flat(pieces))
    space = rows // count
    parts, many = len(pieces), len(flat(pieces))
    spots = parts + 1 + count
    blocks = 2
    part_width = width // blocks

    def body(*refs):
        refs = list(refs)
        mid_in, act_in = refs.pop(0), refs.pop(0)
        reduce = [refs.pop(0) for _ in range(many)]
        vec, info, result, mid, act, full, x_sem, w_sem = refs
        copies = [
            pltpu.make_async_copy(act_in.at[:, pl.ds(0, inner)], act, x_sem.at[0]),
            pltpu.make_async_copy(mid_in.at[:, pl.ds(first, width)], mid, x_sem.at[1]),
        ]
        copies[0].start()
        loads = [
            start_pieces(reduce, info, spots, full, w_sem, block, (block * part_width, part_width), first)
            for block in range(blocks)
        ]
        copies[1].start()
        copies[0].wait()
        for block in range(blocks):
            wait_all(loads[block])
            if block == 0:
                copies[1].wait()
            part = slice(block * part_width, (block + 1) * part_width)
            value = contract(act[...], full[:, part], 1, 0) + mid[:, part]
            value = value + vec[FEED : FEED + 1, first + block * part_width : first + (block + 1) * part_width]
            for image in range(count):
                alive = jnp.where(info[parts + 1 + image] > 0, 1.0, 0.0)
                here = slice(image * space, (image + 1) * space)
                result[here, part] = (value[here] * alive).astype(BF16)

    return call(
        body,
        "output_forward",
        [middle, active] + flat(pieces) + [params, meta],
        [ANY] * (2 + many) + [VMEM, SMEM],
        [((rows, width), BF16)],
        [
            pltpu.VMEM((rows, width), F32),
            pltpu.VMEM((rows, inner), BF16),
            pltpu.VMEM((inner, width), BF16),
            pltpu.SemaphoreType.DMA((2,)),
            pltpu.SemaphoreType.DMA((blocks, many)),
        ],
        2 * rows * width * inner,
        weight,
    )[0]


def hidden_back_stage(
    grad, vec, info, feed, slope, middle, hidden, second, mid_grad, branch, sums, inner_sums, full_out,
    full, deep, first_load, load, for_slope, for_middle, tallies, count, parts,
):
    rows, width = grad.shape
    space = rows // count
    half = width // 2
    for image in range(count):
        alive = jnp.where(info[parts + 1 + image] > 0, 1.0, 0.0)
        here = slice(image * space, (image + 1) * space)
        feed[here] = (grad[here].astype(F32) * alive).astype(BF16)
    for_slope.wait()
    for index in range(parts):
        wait_all(first_load[index])
        where = pl.multiple_of(info[index] * deep, deep)
        value = contract(feed[...], full_out[pl.ds(where, deep)], 1, 1)
        value = (value * slope[:, pl.ds(where, deep)].astype(F32)).astype(BF16)
        hidden[:, pl.ds(where, deep)] = value
        inner_sums[:, pl.ds(where, deep)] = jnp.sum(value.astype(F32), axis=0, keepdims=True)
    wait_all(load)
    for block in range(2):
        second[:, block * half : (block + 1) * half] = contract(
            hidden[...], full[block * half : (block + 1) * half], 1, 1
        )
    for_middle.wait()
    gain = vec[GAIN1 : GAIN1 + 1]
    tallies[...] = jnp.zeros_like(tallies)

    def step(here):
        unit, scale = standardized(middle[here])
        down = second[here]
        top = feed[here].astype(F32)
        total = top + norm_pull(down, gain, unit, scale)
        low = total.astype(BF16)
        mid_grad[here] = total
        branch[here] = low
        tallies[0] += eights(down * unit)
        tallies[1] += eights(down)
        tallies[2] += eights(low.astype(F32))
        tallies[3] += eights(top)

    step(pl.ds(0, rows))
    for index in range(4):
        sums[index : index + 1] = jnp.sum(tallies[index], axis=0, keepdims=True)


def attention_back_stage(
    x, vec, branch, mid_grad, packed, mixed, logs, grads, result, sums, down, normal, stage, full_out,
    full, first_load, load, takes, tallies, count, length,
):
    rows, width = x.shape
    space = rows // count
    head = width // HEADS
    pair = 2 * head
    scale = head**-0.5
    half = width // 2
    wait_all(first_load)
    down[...] = contract(branch[...], full_out[...], 1, 1).astype(BF16)
    wait_all(takes)
    owner = lax.shift_right_logical(
        lax.broadcasted_iota(jnp.int32, (HEADS, width), 1), head.bit_length() - 1
    )
    chosen = jnp.where(
        owner == lax.broadcasted_iota(jnp.int32, (HEADS, width), 0), 1.0, 0.0
    ).astype(BF16)
    left = lax.broadcasted_iota(jnp.int32, (space, pair), 1) < head
    live = lax.broadcasted_iota(jnp.int32, (space, pair), 0) < length
    key_live = lax.broadcasted_iota(jnp.int32, (space, space), 0) < length
    for image in range(count):
        span = pl.ds(image * space, space)
        product = down[span].astype(F32) * mixed[span].astype(F32)
        coarse = product.astype(BF16)
        fine = (product - coarse.astype(F32)).astype(BF16)
        stage[image, :, 0:space] = contract(chosen, coarse, 1, 1) + contract(chosen, fine, 1, 1)

    def heads(index, carry):
        for image in range(count):
            span = pl.ds(image * space, space)

            def part(block):
                offset = pl.multiple_of(block * width + index * pair, pair)
                return packed[span, pl.ds(offset, pair)]

            query, key, value = part(0), part(1), part(2)
            wide = key.astype(F32) * scale
            value = value.astype(F32)
            arrived = down[span, pl.ds(pl.multiple_of(index * pair, pair), pair)]
            found = []
            for side in range(2):
                mine = left if side == 0 else ~left
                log = logs[image, pl.ds(2 * index + side, 1), :]
                dot = stage[image, pl.ds(2 * index + side, 1), 0:space]
                scores = contract(jnp.where(mine, wide, 0.0).astype(BF16), query, 1, 1)
                chance = jnp.exp(jnp.where(key_live, scores - log, NEGATIVE))
                back = contract(jnp.where(mine, value, 0.0).astype(BF16), arrived, 1, 1)
                change = (chance * (back - dot)).astype(BF16)
                found.append(
                    (
                        contract(change, key, 0, 0),
                        contract(change, query, 1, 0),
                        contract(chance.astype(BF16), arrived, 1, 0),
                    )
                )
            for block, factor in enumerate((scale, scale, 1.0)):
                total = jnp.where(left, found[0][block], found[1][block]) * factor
                offset = pl.multiple_of(block * width + index * pair, pair)
                grads[span, pl.ds(offset, pair)] = jnp.where(live, total, 0.0).astype(BF16)
        return carry

    lax.fori_loop(0, HEADS // 2, heads, 0)
    wait_all(load)
    for block in range(2):
        normal[:, block * half : (block + 1) * half] = contract(
            grads[...], full[block * half : (block + 1) * half], 1, 1
        )
    gain = vec[GAIN0 : GAIN0 + 1]
    tallies[...] = jnp.zeros_like(tallies)

    def step(here):
        unit, rate = standardized(x[here].astype(F32))
        grad = normal[here]
        tallies[0] += eights(grad * unit)
        tallies[1] += eights(grad)
        result[here] = (mid_grad[here] + norm_pull(grad, gain, unit, rate)).astype(BF16)

    step(pl.ds(0, rows))
    for index in range(2):
        sums[index : index + 1] = jnp.sum(tallies[index], axis=0, keepdims=True)
    sums[2:3] = jnp.sum(grads[:, 0:width].astype(F32), axis=0, keepdims=True)
    sums[3:4] = jnp.sum(grads[:, 2 * width : 3 * width].astype(F32), axis=0, keepdims=True)


def backward(
    start, lower, upper, kept_low, kept_up, reduce, wide, qkv, params, meta, count, length,
    mixed_at, weight=LIGHT,
):
    feed, attend = reduce is not None, qkv is not None
    rows, width = start[0].shape
    space = rows // count
    pair = 2 * width // HEADS
    parts = len(reduce if feed else qkv)
    many = len(flat(reduce if feed else qkv))
    spots = parts + 1 + count
    inner = wide[0][0].shape[1] - width if feed else 0
    deep = inner // parts
    both = feed and attend
    choices = []
    if feed:
        choices += [(kept_low[0], kept_up[0]), (kept_low[1], kept_up[1])]
        if start[0] is not start[1]:
            choices += [start]
    if attend:
        choices += [(kept_low[index], kept_up[index]) for index in (2, 3, 4)]
        choices += [(lower, upper)]
    plain = [start[0]] if feed and start[0] is start[1] else [] if feed else list(start)
    operands = []
    for low, up in choices:
        operands += [low] if low is up else [low, up]

    def body(*refs):
        refs = list(refs)
        firsts = [refs.pop(0) for _ in plain]
        pairs = []
        for low, up in choices:
            one = refs.pop(0)
            pairs.append((one, one if low is up else refs.pop(0)))
        lists = [[refs.pop(0) for _ in range(many)] for _ in range(2 * feed + 2 * attend)]
        vec, info = refs.pop(0), refs.pop(0)
        section = info[parts]
        if feed:
            if both:
                right = refs.pop(0)
                hidden, branch = right.at[:, pl.ds(0, inner)], right.at[:, pl.ds(inner, width)]
            else:
                hidden, branch = refs.pop(0), refs.pop(0)
            feed_sums, inner_sums = refs.pop(0), refs.pop(0)
            mid_grad = None if both else refs.pop(0)
        if attend:
            grads, result, sums = (refs.pop(0) for _ in range(3)) if not both else (None, refs.pop(0), refs.pop(0))
        if both:
            feed_grad = right.at[:, pl.ds(inner + width, width)]
            grads = right.at[:, pl.ds(inner + 2 * width, 3 * width)]
        tallies, x_sem = refs.pop(0), refs.pop(0)
        if feed:
            grad, slope, middle, second, full_out, full, o_sem, w_sem = (
                refs.pop(0) for _ in range(8)
            )
            if both:
                mid_grad, keep = refs.pop(0), feed_grad
            else:
                keep = refs.pop(0)
            begin = pairs.pop(2) if start[0] is not start[1] else (firsts[0], firsts[0])
            take = start_chosen(section, *begin, grad, x_sem.at[0])
            for_slope = start_chosen(section, *pairs.pop(0), slope, x_sem.at[1])
            every = start_pieces(lists.pop(0), info, spots, full_out, o_sem, 0, (0, width))
            first_load = [[every.pop(0) for _ in group] for group in reduce]
            for_middle = start_chosen(section, *pairs.pop(0), middle, x_sem.at[2])
            load = start_pieces(lists.pop(0), info, spots, full, w_sem, 0, (0, inner), width)
        if attend:
            x, packed, mixed, logs, down, normal, stage, full_o, full_q, p_sem, q_sem = (
                refs.pop(0) for _ in range(11)
            )
            if not feed:
                branch, mid_grad = refs.pop(0), refs.pop(0)
                givens = [
                    pltpu.make_async_copy(source, target, x_sem.at[index])
                    for index, (source, target) in enumerate(zip(firsts, (branch, mid_grad)))
                ]
                for given in givens:
                    given.start()
            project_load = start_pieces(lists.pop(0), info, spots, full_o, p_sem, 0, (0, width))
            sames = [one is two for one, two in pairs]
            pairs[1] = tuple(one.at[:, pl.ds(mixed_at, width)] for one in pairs[1])
            takes = [
                start_chosen(section, *pairs[index], target, x_sem.at[3 + index], sames[index])
                for index, target in ((1, mixed), (0, packed), (2, logs), (3, x))
            ]
            last_load = start_pieces(lists.pop(0), info, spots, full_q, q_sem, 0, (0, 3 * width))
            if not feed:
                wait_all(givens)
        if feed:
            take.wait()
            hidden_back_stage(
                grad, vec, info, keep, slope, middle, hidden, second, mid_grad, branch, feed_sums,
                inner_sums, full_out, full, deep, first_load, load, for_slope, for_middle, tallies,
                count, parts,
            )
        if attend:
            attention_back_stage(
                x, vec, branch, mid_grad, packed, mixed, logs, grads, result, sums, down, normal,
                stage, full_o, full_q, project_load, last_load, takes, tallies, count, length,
            )

    outs = []
    scratch = [pltpu.VMEM((4, 8, width), F32), pltpu.SemaphoreType.DMA((7,))]
    flops = 0
    if feed:
        outs += [((rows, inner + 5 * width), BF16)] if both else [((rows, inner), BF16), ((rows, width), BF16)]
        outs += [
            ((8, width), F32),
            ((1, inner), F32),
        ]
        if not both:
            outs += [((rows, width), F32)]
        scratch += [
            pltpu.VMEM((rows, width), BF16),
            pltpu.VMEM((rows, inner), BF16),
            pltpu.VMEM((rows, width), F32),
            pltpu.VMEM((rows, width), F32),
            pltpu.VMEM((inner, width), BF16),
            pltpu.VMEM((width, inner), BF16),
            pltpu.SemaphoreType.DMA((1, many)),
            pltpu.SemaphoreType.DMA((1, many)),
        ]
        scratch += [pltpu.VMEM((rows, width), F32 if both else BF16)]
        flops += 4 * rows * width * inner
    if attend:
        outs += [] if both else [((rows, 3 * width), BF16)]
        outs += [((rows, width), BF16), ((8, width), F32)]
        scratch += [
            pltpu.VMEM((rows, width), BF16),
            pltpu.VMEM((rows, 3 * width), BF16),
            pltpu.VMEM((rows, width), BF16),
            pltpu.VMEM((count, HEADS, space), F32),
            pltpu.VMEM((rows, width), BF16),
            pltpu.VMEM((rows, width), F32),
            pltpu.VMEM((count, HEADS, 2 * pair), F32),
            pltpu.VMEM((width, width), BF16),
            pltpu.VMEM((width, 3 * width), BF16),
            pltpu.SemaphoreType.DMA((1, many)),
            pltpu.SemaphoreType.DMA((1, many)),
        ]
        if not feed:
            scratch += [pltpu.VMEM((rows, width), BF16), pltpu.VMEM((rows, width), F32)]
        flops += 2 * rows * width * (4 * width + 5 * space)
    weights = (flat(reduce) + flat(wide) if feed else []) + (
        flat(wide) + flat(qkv) if attend else []
    )
    return call(
        body,
        "backward" + "_feed" * feed + "_attend" * attend,
        plain + operands + weights + [params, meta],
        [ANY] * (len(plain) + len(operands) + len(weights)) + [VMEM, SMEM],
        outs,
        scratch,
        flops,
        weight,
    )


def weight_gradient(
    lefts, rights, meta, parts, blocks, quarter, rows_of, columns_of, name, weight=LIGHT
):
    terms = len(lefts)
    first_row, height = rows_of
    first_column, breadth = columns_of
    rows = lefts[0].shape[0]
    operands = list(lefts)
    places = []
    for pair in rights:
        found = []
        for array, _ in pair:
            if not any(array is other for other in operands):
                operands.append(array)
            found.append(next(i for i, other in enumerate(operands) if other is array))
        places.append(found)

    def body(*refs):
        sources, info = refs[: len(operands)], refs[len(operands)]
        results = refs[len(operands) + 1 : len(operands) + 1 + len(blocks)]
        left_full, right_full, l_sem, r_sem = refs[len(operands) + 1 + len(blocks) :]
        section = info[parts]
        waits = []
        for term in range(terms):
            sides = [
                sources[place].at[:, pl.ds(column + first_column, breadth)]
                for place, (_, column) in zip(places[term], rights[term])
            ]
            same = rights[term][0] is rights[term][1]
            target = right_full.at[pl.ds(term * rows, rows)]
            waits.append(start_chosen(section, *sides, target, r_sem.at[term], same))
        loads = []
        for index, block in enumerate(blocks):
            start = pl.multiple_of(info[block] * quarter + first_row, 128)
            for term in range(terms):
                copy = pltpu.make_async_copy(
                    sources[term].at[:, pl.ds(start, height)],
                    left_full.at[index, pl.ds(term * rows, rows)],
                    l_sem.at[index, term],
                )
                copy.start()
                loads.append(copy)
        wait_all(waits)
        for index in reversed(range(len(blocks))):
            wait_all(loads[index * terms : (index + 1) * terms])
            results[index][...] = contract(left_full[index], right_full[...], 0, 0).astype(BF16)

    return call(
        body,
        name,
        operands + [meta],
        [ANY] * len(operands) + [SMEM],
        [((height, breadth), BF16)] * len(blocks),
        [
            pltpu.VMEM((len(blocks), terms * rows, height), BF16),
            pltpu.VMEM((terms * rows, breadth), BF16),
            pltpu.SemaphoreType.DMA((len(blocks), terms)),
            pltpu.SemaphoreType.DMA((terms,)),
        ],
        2 * len(blocks) * terms * rows * height * breadth,
        weight,
    )


def after(value, *earlier):
    return lax.optimization_barrier((value,) + earlier)[0]


def added(*values):
    total = values[0].astype(F32)
    for value in values[1:]:
        total = total + value.astype(F32)
    return total.astype(values[0].dtype)


class FourByFour:
    parts = 4
    blocks = (0, 2)

    def __init__(self):
        self.group = lax.axis_index("group")
        self.place = lax.axis_index("replica")
        self.order = [self.group ^ part for part in range(4)]
        odd = self.place % 2
        halves = [2 * self.order[part] + half for part in (2, 3) for half in (odd, 1 - odd)]
        self.spots = self.order[:2] + halves

    def core(self, block):
        return lax.ppermute(block, "group", [(i, i ^ 1) for i in range(4)])

    def across(self, block):
        return lax.ppermute(block, "group", [(i, i ^ 2) for i in range(4)])

    def beside(self, block):
        return lax.ppermute(block, "replica", [(i, i ^ 1) for i in range(4)])

    def gather_small(self, block):
        near, far = self.core(block), self.across(block)
        return [block, near, far, self.core(far)]

    def gather(self, blocks, prepare):
        odd = self.place % 2
        asked = [
            lax.dynamic_slice_in_dim(block, odd * (block.shape[0] // 2), block.shape[0] // 2)
            for block in blocks
        ]
        halves, sibling = [], []
        for index, block in enumerate(blocks):
            halves.append(self.across(after(asked[index], *halves[: max(index - 1, 0)])))
            sibling.append(self.core(after(block, sibling[-1]) if index else block))
        others = []
        tokens = prepare(halves[0]) + asked[2:]
        for index, half in enumerate(halves):
            earlier = others[-1:] if index == 1 else []
            others.append(self.beside(after(half, *earlier, *(tokens if index == 1 else []))))
        self.arrived = halves[-1]

        def pieces(index, *tokens):
            one, two = (after(half, *tokens) for half in (halves[index], others[index]))
            return [
                [blocks[index]],
                [sibling[index]],
                [halves[index], others[index]],
                [self.core(one), self.core(two)],
            ]

        return [partial(pieces, index) for index in range(len(blocks))]

    def shared(self, block):
        return [block, self.core(block)]

    def total(self, blocks):
        passed = self.across(blocks[1])
        token = yield
        mine = added(after(blocks[0], token), passed)
        inward = lax.ppermute(mine, "replica", [(0, 1), (3, 2)])
        token = yield mine
        joined = added(after(mine, token), inward)
        crossing = lax.ppermute(joined, "replica", [(1, 2), (2, 1)])
        token = yield joined
        summed = added(after(joined, token), crossing)
        outward = lax.ppermute(summed, "replica", [(1, 0), (2, 3)])
        token = yield summed
        inner = (self.place == 1) | (self.place == 2)
        yield jnp.where(inner, after(summed, token), outward)


class General:
    def __init__(self):
        self.parts = lax.axis_size("group")
        self.blocks = tuple(range(self.parts))
        self.order = self.spots = [jnp.int32(part) for part in range(self.parts)]

    def gather_small(self, block):
        whole = lax.all_gather(block, "group", axis=0)
        return [whole[part] for part in range(self.parts)]

    def gather(self, blocks, prepare):
        prepare(blocks[0])
        self.arrived = blocks[0]
        found = [[[piece] for piece in self.gather_small(block)] for block in blocks]
        return [lambda *tokens, groups=groups: groups for groups in found]

    def shared(self, block):
        return [block]

    def total(self, blocks):
        yield
        mine = lax.psum_scatter(jnp.stack(blocks), "group", scatter_dimension=0)
        yield mine
        yield lax.psum(mine, "replica")


def shifted(block, distance):
    devices = range(lax.axis_size("section"))
    route = [(i - distance, i) for i in devices if i - distance in devices]
    return lax.ppermute(block, "section", route)


def in_order(pieces, order):
    place = jnp.stack(order)
    stacked = []
    for block in range(len(pieces)):
        chosen = pieces[0]
        for part in range(1, len(pieces)):
            chosen = jnp.where(place[part] == block, pieces[part], chosen)
        stacked.append(chosen)
    return jnp.stack(stacked)


class Sequence:
    def __init__(self, net, token):
        self.net, self.sums, self.results, self.token = net, {}, {}, token

    def now(self, value):
        return after(value, self.token)

    def ran(self, value):
        self.token = value

    def add(self, name, blocks):
        self.sums[name] = self.net.total(blocks)
        next(self.sums[name])

    def step(self, *names):
        for name in names:
            try:
                self.results[name] = self.token = self.sums[name].send(self.token)
            except StopIteration:
                continue

    def finish(self, name):
        while True:
            try:
                self.results[name] = self.sums[name].send(self.token)
            except StopIteration:
                return self.results[name]


def per_device(
    images,
    cotangent,
    counts,
    qkv_weight,
    out_weight,
    expand_weight,
    reduce_weight,
    norm_gains,
    biases,
    expand_bias,
):
    micro, slots, length, width = images.shape
    space = padded(length)
    section = lax.axis_index("section")
    first = section == 0
    sizes = (lax.axis_size("group"), lax.axis_size("replica"))
    net = FourByFour() if sizes == (4, 4) else General()
    parts = net.parts
    share = width // parts
    batches = tuple(range(micro))

    def rows_of(array):
        fulls = [jnp.pad(array[batch], ((0, 0), (0, space - length), (0, 0))) for batch in batches]
        return [full.reshape(slots * space, width) for full in fulls]

    def images_of(array):
        return array.reshape(slots, space, width)[:, :length]

    small = jnp.concatenate([norm_gains[0], biases[0], expand_bias[0].reshape(-1, share)])
    slot = jnp.arange(slots, dtype=jnp.int32)
    alive = [(slot < counts[batch, 0]).astype(jnp.int32) for batch in batches]
    head = jnp.stack(net.order + [section]).astype(jnp.int32)

    spots = jnp.stack(net.spots).astype(jnp.int32)

    def meta(living):
        return jnp.concatenate([head, living, spots])

    infos = [meta(alive[batch]) for batch in batches]
    pieces = net.gather_small(small)
    vectors = in_order(pieces, net.order)
    top = vectors[:, :8].transpose(1, 0, 2).reshape(8, width)
    bottom = vectors[:, 8:].reshape(-1, width)
    params = jnp.concatenate([top, bottom]).astype(F32)
    slot = jnp.arange(slots, dtype=jnp.int32)
    alive = [(slot < counts[batch, 0]).astype(jnp.int32) for batch in batches]
    head = jnp.stack(net.order + [section]).astype(jnp.int32)
    spots = jnp.stack(net.spots).astype(jnp.int32)

    def meta(living):
        return jnp.concatenate([head, living, spots])

    infos = [meta(alive[batch]) for batch in batches]
    inputs, targets = [], []

    def prepare(token):
        inputs.extend(rows_of(after(images, token)))
        targets.extend(rows_of(after(cotangent, token)))
        return [params, *inputs, *targets, *infos]

    qkv, wide, reduce = net.gather(
        [qkv_weight[0], jnp.concatenate([out_weight[0], expand_weight[0]], axis=1), reduce_weight[0]],
        prepare,
    )

    qkv = qkv()
    attended = []
    for batch in batches:
        start = inputs[batch] if batch == 0 else after(inputs[batch], attended[-1][0], net.arrived)
        attended.append(
            forward(start, start, None, qkv, None, params, infos[batch], slots, length)
        )
    wide = wide(attended[-1][0])
    fed = []
    for batch in batches:
        start = inputs[batch] if batch == 0 else after(inputs[batch], fed[-1][0])
        fed.append(
            forward(start, start, attended[batch][0], None, wide, params, infos[batch], slots, length)
        )
    reduce = reduce(fed[-1][0])
    early, incoming = [], []
    for batch in batches:
        middle, active = fed[batch]
        if batch:
            active = after(active, made[-1])
        cuts = 2 if batch == 0 else 1
        made, sent = [], []
        for cut in range(cuts):
            part = width // cuts
            made.append(
                output_forward(
                    middle, after(active, *made), reduce, params, infos[batch], slots, LIGHT, (cut * part, part)
                )
            )
            sent.append(shifted(made[-1], 1))
        early.append(jnp.concatenate(made, axis=1))
        incoming.append(jnp.concatenate(sent, axis=1))

    inner = wide[0][0].shape[1] - width
    mixed_at = inner + width
    kept, lefts, rights, results = [], [], [], []
    sums_a, sums_b, sums_c, returning = [], [], [], []
    token = made[-1]
    for batch in batches:
        start = after(incoming[batch], token)
        left, packed, logs, middle, slope = forward(
            inputs[batch], start, None, qkv, wide, params, infos[batch], slots, length, 8.0
        )
        kept.append((slope, middle, packed, left, logs))
        lefts.append(net.shared(left))
        if batch == 0:
            pair, sides = (targets[0], targets[0]), (kept[0], kept[0])
            lower, chosen = incoming[0], infos[0]
        else:
            pair = (returning[batch - 1], targets[batch])
            sides = (kept[batch - 1], kept[batch])
            lower = inputs[batch - 1]
            chosen = meta(jnp.where(first, alive[batch - 1], alive[batch]))
        right, some, more, result, rest = backward(
            pair, lower, incoming[batch], sides[0], sides[1], reduce, wide, qkv, params, chosen,
            slots, length, mixed_at, 8.0,
        )
        token = result
        rights.append(net.shared(right))
        results.append(result)
        sums_a.append(some)
        sums_b.append(more)
        sums_c.append(rest)
        returning.append(shifted(result, -1))
    late = []
    for batch in batches:
        ready = lefts[batch][1:] + (rights[batch][1:] if batch < micro - 1 else [])
        active = after(kept[batch][3], token, *ready)
        late.append(output_forward(kept[batch][1], active, reduce, params, infos[batch], slots, 8.0))
        token = late[-1]

    last = micro - 1
    run = Sequence(net, token)
    arrived = run.now(returning[last])
    living = jnp.repeat(alive[last] > 0, space)[:, None]
    masked = net.shared(jnp.where(living, arrived, jnp.zeros_like(arrived)))
    many = len(masked)

    def gradient(name, left_at, final, final_at, right_at, quarter, rows, columns, weight=LIGHT):
        left = [lefts[batch][side] for batch in batches for side in range(many)]
        right = []
        for batch in batches:
            for side in range(many):
                upper = (rights[batch][side], right_at)
                lower = (final[side], final_at) if batch == last else (rights[batch + 1][side], right_at)
                right.append((lower, upper))
        blocks = weight_gradient(
            left, right, run.now(head), parts, net.blocks, quarter, (left_at + rows[0], rows[1]), columns,
            name, weight,
        )
        run.ran(blocks[0])
        return blocks

    def reduce_part(index, weight=LIGHT):
        step = inner // parts // 2
        blocks = gradient(
            "reduce", 0, masked, 0, inner + width, inner // parts, (index * step, step), (0, width), weight
        )
        run.add(f"reduce{index}", blocks)

    def expand_part(index):
        step = inner // 2
        blocks = gradient("expand", inner, finals, 0, 0, share, (0, share), (index * step, step))
        run.add(f"expand{index}", blocks)

    def qkv_part(begin, size):
        at = inner + 2 * width
        return gradient("qkv", at, grads, 0, at, share, (0, share), (begin, size))

    reduce_part(0)
    start = run.now(arrived)
    final, branch, some, more, mid = backward(
        (start, start), None, None, kept[last], kept[last], reduce, wide, None, params, infos[last],
        slots, length, mixed_at,
    )
    run.ran(final)
    finals, branches = net.shared(final), net.shared(branch)
    sums_a.append(some)
    sums_b.append(more)
    run.step("reduce0")
    reduce_part(1, HEAVY)
    expand_part(0)
    expand_part(1)
    run.step("reduce1", "reduce0")
    grads, result, rest = backward(
        (run.now(after(branch, *branches[1:])), mid), inputs[last], inputs[last], kept[last], kept[last], None, wide, qkv,
        params, infos[last], slots, length, mixed_at, HEAVY,
    )
    run.ran(result)
    grads = net.shared(grads)
    results.append(result)
    sums_c.append(rest)
    run.step("expand0", "reduce1", "reduce0")
    project = gradient("project", mixed_at, branches, 0, inner, share, (0, share), (0, width), HEAVY)
    mixed_part = qkv_part(0, width)
    run.add("mixed", [jnp.concatenate(pair, axis=1) for pair in zip(project, mixed_part)])
    run.step("expand1", "expand0", "reduce1", "reduce0")

    def over_batches(values):
        return sum(jnp.where(first, values[batch + 1], values[batch]) for batch in batches)

    some, more, rest = over_batches(sums_a), over_batches(sums_b), over_batches(sums_c)
    rows = jnp.concatenate([rest[0:1], some[0:1], rest[1:2], some[1:2], rest[2:4], some[2:4]])
    rows = rows.reshape(8, parts, share).transpose(1, 0, 2)
    rows = jnp.concatenate([rows, more.reshape(parts, -1, share)], axis=1)
    rows = sum(net.shared(run.now(rows)))
    rows = jnp.stack(
        [lax.dynamic_index_in_dim(rows, net.order[block], 0, keepdims=False) for block in net.blocks]
    )
    count, step = rows.shape[1], 2 * width
    rows = rows.reshape(len(net.blocks), -1)
    rows = jnp.pad(rows, ((0, 0), (0, -rows.shape[1] % (16 * step)))).reshape(len(net.blocks), -1, step)
    blocks = qkv_part(width, step)
    run.add("qkv", [jnp.concatenate([one, two]) for one, two in zip(blocks, rows.astype(BF16))])
    run.step("mixed", "expand1", "expand0", "reduce1", "qkv", "mixed", "expand1", "expand0", "qkv")
    outputs = [
        images_of(jnp.where(first, run.now(low), up))
        for low, up in zip(early + results[1:], late + results[:-1])
    ]
    run.step("mixed", "expand1", "qkv", "mixed", "qkv")
    weights = {name: run.finish(name) for name in run.sums}
    vector = weights["qkv"][share:].reshape(-1)[: count * share].reshape(count, share).astype(F32)

    def joined(axis, *names):
        return jnp.concatenate([weights[name] for name in names], axis=axis).astype(F32)[None]

    return (
        jnp.stack(outputs[:micro])[None],
        jnp.stack(outputs[micro:])[None],
        jnp.concatenate([weights["mixed"][:, width:], weights["qkv"][:share]], axis=1).astype(F32)[None],
        weights["mixed"][:, :width].astype(F32)[None],
        joined(1, "expand0", "expand1"),
        joined(0, "reduce0", "reduce1"),
        vector[None, 0:2],
        vector[None, 2:8],
        vector[8:].reshape(1, -1),
    )


def solution(mesh):
    placed = (
        P(None, ("group", "replica"), None, None),
        P(None, ("group", "replica"), None, None),
        P(None, ("group", "replica")),
        P("section", "group", None),
        P("section", "group", None),
        P("section", "group", None),
        P("section", "group", None),
        P("section", None, "group"),
        P("section", None, "group"),
        P("section", "group"),
    )
    return jax.shard_map(
        per_device,
        mesh=mesh,
        in_specs=placed,
        out_specs=(
            P("section", None, ("group", "replica"), None, None),
            P("section", None, ("group", "replica"), None, None),
            P("section", "group", None),
            P("section", "group", None),
            P("section", "group", None),
            P("section", "group", None),
            P("section", None, "group"),
            P("section", None, "group"),
            P("section", "group"),
        ),
        check_vma=False,
    )
```

```python
from functools import partial

import jax
import jax.numpy as jnp
from jax import lax
from jax.experimental import pallas as pl
from jax.experimental.pallas import tpu as pltpu
from jax.sharding import PartitionSpec as P

HEADS = 16
EPSILON = 1e-06
NEGATIVE = -1e30
F32 = jnp.float32
BF16 = jnp.bfloat16
LIGHT, HEAVY = 1.0 / 64, 16.0
PLAN = (
    "R0 BF r0 R1*",
    "BA r0 r1 E0*",
    "Q0 r0 r1 e0",
    "E1 q0 r0 r1",
    "e0 Q1 e1 q0",
    "r1 e0 V P0",
    "q1 e1 q0 e0",
    "p0 O q1 e1",
    "q0 p0 O O",
    "q1 e1 p0 O",
    "q1 p0",
)
LAST = "P0"
VMEM_LIMIT = 58 * 2**20
ROOT_HALF = 0.7071067811865476
ROOT_TAU = 0.3989422804014327
ANY = pl.BlockSpec(memory_space=pl.ANY)
VMEM = pl.BlockSpec(memory_space=pltpu.VMEM)
SMEM = pl.BlockSpec(memory_space=pltpu.SMEM)
GAIN0, GAIN1, SHIFT0, SHIFT1, QUERY, VALUE, OUT, FEED, EXPAND = range(9)


def padded(length):
    return -(-length // 16) * 16


def contract(left, right, left_dim, right_dim):
    return lax.dot_general(
        left, right, (((left_dim,), (right_dim,)), ((), ())), preferred_element_type=F32
    )


def standardized(values):
    center = values - jnp.mean(values, axis=-1, keepdims=True)
    spread = jnp.mean(center * center, axis=-1, keepdims=True)
    scale = lax.rsqrt(spread + EPSILON)
    return center * scale, scale


def norm_pull(grad, gain, unit, scale):
    scaled = grad * gain
    mean = jnp.mean(scaled, axis=-1, keepdims=True)
    along = jnp.mean(scaled * unit, axis=-1, keepdims=True)
    return scale * (scaled - mean - unit * along)


def call(body, name, operands, specs, outs, scratch, flops, weight=LIGHT):
    moved = sum(o.size * o.dtype.itemsize for o in operands)
    out_shape = [jax.ShapeDtypeStruct(shape, dtype) for shape, dtype in outs]
    moved += sum(o.size * o.dtype.itemsize for o in out_shape)
    return pl.pallas_call(
        body,
        out_shape=out_shape,
        in_specs=specs,
        out_specs=[VMEM] * len(outs),
        scratch_shapes=scratch,
        compiler_params=pltpu.CompilerParams(vmem_limit_bytes=VMEM_LIMIT),
        cost_estimate=pl.CostEstimate(flops=int(flops * weight), bytes_accessed=int(moved * weight), transcendentals=0),
        name=name,
    )(*operands)


def flat(groups):
    return [piece for group in groups for piece in group]


def start_pieces(pieces, info, first, target, sems, slot, columns, shift=0):
    begin, size = columns
    columns = pl.ds(begin, size)
    copies = []
    for index, piece in enumerate(pieces):
        rows = piece.shape[0]
        where = pl.multiple_of(info[first + index] * rows, rows)
        copy = pltpu.make_async_copy(
            piece.at[:, pl.ds(begin + shift, size)],
            target.at[pl.ds(where, rows), columns],
            sems.at[slot, index],
        )
        copy.start()
        copies.append(copy)
    return copies


def wait_all(copies):
    for copy in copies:
        copy.wait()


def start_chosen(section, lower, upper, target, sem, same=False):
    if lower is upper or same:
        copy = pltpu.make_async_copy(lower, target, sem)
        copy.start()
        return copy

    @pl.when(section == 0)
    def _():
        pltpu.make_async_copy(lower, target, sem).start()

    @pl.when(section != 0)
    def _():
        pltpu.make_async_copy(upper, target, sem).start()

    return pltpu.make_async_copy(lower, target, sem)


def eights(values):
    return jnp.sum(values.reshape(-1, 8, values.shape[-1]), axis=0)


def attention_stage(x, vec, norm, packed, mixed, logs, columns, full, loads, count, length):
    rows, width = x.shape
    space = rows // count
    head = width // HEADS
    pair = 2 * head
    scale = head**-0.5
    gain, shift = vec[GAIN0 : GAIN0 + 1], vec[SHIFT0 : SHIFT0 + 1]

    def step(here):
        unit, _ = standardized(x[here].astype(F32))
        norm[here] = (unit * gain + shift).astype(BF16)

    step(pl.ds(0, rows))
    for block in range(3):
        wait_all(loads[block])
        done = contract(norm[...], full[:, block * width : (block + 1) * width], 1, 0)
        if block != 1:
            bias = QUERY if block == 0 else VALUE
            done = done + vec[bias : bias + 1]
        packed[:, block * width : (block + 1) * width] = done.astype(BF16)
    lane = lax.broadcasted_iota(jnp.int32, (space, pair), 1)
    left = lane < head
    live = lax.broadcasted_iota(jnp.int32, (space, pair), 0) < length
    key_live = lax.broadcasted_iota(jnp.int32, (space, space), 1) < length
    columns[...] = jnp.zeros_like(columns)

    def heads(index, carry):
        for image in range(count):
            span = pl.ds(image * space, space)

            def part(block):
                offset = pl.multiple_of(block * width + index * pair, pair)
                return packed[span, pl.ds(offset, pair)]

            query, key, value = part(0).astype(F32) * scale, part(1), part(2).astype(F32)
            found = []
            tops = []
            for side in range(2):
                mine = left if side == 0 else ~left
                asked = jnp.where(mine, query, 0.0).astype(BF16)
                held = jnp.where(live, jnp.where(mine, value, 1.0), 0.0).astype(BF16)
                scores = jnp.where(key_live, contract(asked, key, 1, 1), NEGATIVE)
                top = jnp.max(scores, axis=-1, keepdims=True)
                raised = jnp.exp(scores - top).astype(BF16)
                found.append(contract(raised, held, 1, 0))
                tops.append(top)
            inside = jnp.where(left, found[0], found[1])
            total = jnp.where(left, found[1], found[0])
            turned = pltpu.roll(total, head, 1)
            offset = pl.multiple_of(index * pair, pair)
            mixed[span, pl.ds(offset, pair)] = (inside / turned).astype(BF16)
            if logs is None:
                continue
            logged = jnp.log(turned)
            first = tops[0] + logged[:, 0:1]
            second = tops[1] + logged[:, head : head + 1]
            known = columns[image]
            known = jnp.where(lane == 2 * index, first, known)
            columns[image] = jnp.where(lane == 2 * index + 1, second, known)
        return carry

    lax.fori_loop(0, HEADS // 2, heads, 0)
    if logs is not None:
        for image in range(count):
            logs[image] = columns[image].T[0:HEADS]


def hidden_stage(x, vec, mixed, middle, active, second, slope, full_out, full, first_load, loads):
    rows, width = x.shape
    wait_all(first_load)
    gain, shift, bias = vec[GAIN1 : GAIN1 + 1], vec[SHIFT1 : SHIFT1 + 1], vec[OUT : OUT + 1]
    middle[...] = contract(mixed[...], full_out[...], 1, 0)

    def step(here):
        total = middle[here] + x[here].astype(F32) + bias
        middle[here] = total
        unit, _ = standardized(total)
        second[here] = (unit * gain + shift).astype(BF16)

    step(pl.ds(0, rows))
    for block, load in enumerate(loads):
        wait_all(load)
        part = slice(block * width, (block + 1) * width)
        value = contract(second[...], full[:, part], 1, 0) + vec[EXPAND + block : EXPAND + block + 1]
        share = 0.5 + 0.5 * lax.erf(value * ROOT_HALF)
        active[:, part] = (value * share).astype(BF16)
        if slope is not None:
            density = ROOT_TAU * jnp.exp(-0.5 * value * value)
            slope[:, part] = (share + value * density).astype(BF16)


def forward(
    lower, upper, mixed_in, qkv, wide, params, meta, count, length, weight=LIGHT
):
    rows, width = lower.shape
    space = rows // count
    pair = 2 * width // HEADS
    attend, feed = qkv is not None, wide is not None
    both = attend and feed
    parts = len(qkv if attend else wide)
    many = len(flat(qkv if attend else wide))
    spots = parts + 1 + count
    inner = wide[0][0].shape[1] - width if feed else 0
    blocks = inner // width
    same = lower is upper

    def body(*refs):
        refs = list(refs)
        low = refs.pop(0)
        up = low if same else refs.pop(0)
        if not attend:
            arrived = refs.pop(0)
        lists = [[refs.pop(0) for _ in range(many)] for _ in range(attend + 2 * feed)]
        vec, info = refs.pop(0), refs.pop(0)
        if both:
            left, packed, logs, middle, slope = (refs.pop(0) for _ in range(5))
            active, second, mixed, norm = (
                left.at[:, pl.ds(start, size)]
                for start, size in ((0, inner), *((inner + width * i, width) for i in range(3)))
            )
        elif attend:
            mixed = refs.pop(0)
        else:
            middle, active = refs.pop(0), refs.pop(0)
        x, x_sem = refs.pop(0), refs.pop(0)
        section = info[parts]
        take = start_chosen(section, low, up, x, x_sem.at[0])
        if attend:
            columns, full, a_sem = (refs.pop(0) for _ in range(3))
            if not both:
                norm, packed, logs = refs.pop(0), refs.pop(0), None
            weight = lists.pop(0)
            loads = [
                start_pieces(weight, info, spots, full, a_sem, block, (block * width, width))
                for block in range(3)
            ]
        if feed:
            full_out, full_in, o_sem, w_sem = (refs.pop(0) for _ in range(4))
            if not attend:
                mixed, second, slope = refs.pop(0), refs.pop(0), None
                extra = pltpu.make_async_copy(arrived, mixed, x_sem.at[1])
                extra.start()
            first_load = start_pieces(lists[0], info, spots, full_out, o_sem, 0, (0, width))
            inner_loads = [
                start_pieces(lists[1], info, spots, full_in, w_sem, block, (block * width, width), width)
                for block in range(blocks)
            ]
        take.wait()
        if attend:
            attention_stage(
                x, vec, norm, packed, mixed, logs, columns, full, loads, count, length
            )
        if feed:
            if not attend:
                extra.wait()
            hidden_stage(
                x, vec, mixed, middle, active, second, slope, full_out, full_in, first_load,
                inner_loads,
            )

    outs, inputs = [], [lower] if same else [lower, upper]
    scratch = [pltpu.VMEM((rows, width), BF16), pltpu.SemaphoreType.DMA((2,))]
    flops = 0
    if attend:
        outs += [
            ((rows, width), BF16),
            ((rows, 3 * width), BF16),
            ((rows, width), BF16),
            ((count, HEADS, space), F32),
        ]
        scratch += [
            pltpu.VMEM((count, space, pair), F32),
            pltpu.VMEM((width, 3 * width), BF16),
            pltpu.SemaphoreType.DMA((3, many)),
        ]
        if not feed:
            scratch += [pltpu.VMEM((rows, width), BF16), pltpu.VMEM((rows, 3 * width), BF16)]
        flops += 2 * rows * width * (3 * width + 2 * space)
    else:
        inputs += [mixed_in]
    if feed:
        outs += [
            ((rows, width), F32),
            ((rows, inner), BF16),
            ((rows, width), BF16),
            ((rows, inner), BF16),
        ]
        scratch += [
            pltpu.VMEM((width, width), BF16),
            pltpu.VMEM((width, inner), BF16),
            pltpu.SemaphoreType.DMA((1, many)),
            pltpu.SemaphoreType.DMA((blocks, many)),
        ]
        if not attend:
            scratch += [pltpu.VMEM((rows, width), BF16), pltpu.VMEM((rows, width), BF16)]
        flops += 2 * rows * width * (width + inner)
    if both:
        outs = [((rows, inner + 3 * width), BF16), outs[1], outs[3], outs[4], outs[7]]
    else:
        outs = [outs[2]] if attend else outs[:2]
    weights = (flat(qkv) if attend else []) + (2 * flat(wide) if feed else [])
    return call(
        body,
        "forward" + "_attend" * attend + "_feed" * feed,
        inputs + weights + [params, meta],
        [ANY] * (len(inputs) + len(weights)) + [VMEM, SMEM],
        outs,
        scratch,
        flops,
        weight,
    )


def output_forward(middle, active, pieces, params, meta, count, weight=LIGHT, columns=None):
    rows, width = middle.shape
    first, width = columns or (0, width)
    inner = sum(piece.shape[0] for piece in flat(pieces))
    space = rows // count
    parts, many = len(pieces), len(flat(pieces))
    spots = parts + 1 + count
    blocks = 2
    part_width = width // blocks

    def body(*refs):
        refs = list(refs)
        mid_in, act_in = refs.pop(0), refs.pop(0)
        reduce = [refs.pop(0) for _ in range(many)]
        vec, info, result, mid, act, full, x_sem, w_sem = refs
        copies = [
            pltpu.make_async_copy(act_in.at[:, pl.ds(0, inner)], act, x_sem.at[0]),
            pltpu.make_async_copy(mid_in.at[:, pl.ds(first, width)], mid, x_sem.at[1]),
        ]
        copies[0].start()
        loads = [
            start_pieces(reduce, info, spots, full, w_sem, block, (block * part_width, part_width), first)
            for block in range(blocks)
        ]
        copies[1].start()
        copies[0].wait()
        for block in range(blocks):
            wait_all(loads[block])
            if block == 0:
                copies[1].wait()
            part = slice(block * part_width, (block + 1) * part_width)
            value = contract(act[...], full[:, part], 1, 0) + mid[:, part]
            value = value + vec[FEED : FEED + 1, first + block * part_width : first + (block + 1) * part_width]
            for image in range(count):
                alive = jnp.where(info[parts + 1 + image] > 0, 1.0, 0.0)
                here = slice(image * space, (image + 1) * space)
                result[here, part] = (value[here] * alive).astype(BF16)

    return call(
        body,
        "output_forward",
        [middle, active] + flat(pieces) + [params, meta],
        [ANY] * (2 + many) + [VMEM, SMEM],
        [((rows, width), BF16)],
        [
            pltpu.VMEM((rows, width), F32),
            pltpu.VMEM((rows, inner), BF16),
            pltpu.VMEM((inner, width), BF16),
            pltpu.SemaphoreType.DMA((2,)),
            pltpu.SemaphoreType.DMA((blocks, many)),
        ],
        2 * rows * width * inner,
        weight,
    )[0]


def hidden_back_stage(
    grad, vec, info, feed, slope, middle, hidden, second, mid_grad, branch, sums, inner_sums, full_out,
    full, deep, first_load, load, for_slope, for_middle, tallies, count, parts,
):
    rows, width = grad.shape
    space = rows // count
    half = width // 2
    for image in range(count):
        alive = jnp.where(info[parts + 1 + image] > 0, 1.0, 0.0)
        here = slice(image * space, (image + 1) * space)
        feed[here] = (grad[here].astype(F32) * alive).astype(BF16)
    for_slope.wait()
    for index in range(parts):
        wait_all(first_load[index])
        where = pl.multiple_of(info[index] * deep, deep)
        value = contract(feed[...], full_out[pl.ds(where, deep)], 1, 1)
        value = (value * slope[:, pl.ds(where, deep)].astype(F32)).astype(BF16)
        hidden[:, pl.ds(where, deep)] = value
        inner_sums[:, pl.ds(where, deep)] = jnp.sum(value.astype(F32), axis=0, keepdims=True)
    wait_all(load)
    for block in range(2):
        second[:, block * half : (block + 1) * half] = contract(
            hidden[...], full[block * half : (block + 1) * half], 1, 1
        )
    for_middle.wait()
    gain = vec[GAIN1 : GAIN1 + 1]
    tallies[...] = jnp.zeros_like(tallies)

    def step(here):
        unit, scale = standardized(middle[here])
        down = second[here]
        top = feed[here].astype(F32)
        total = top + norm_pull(down, gain, unit, scale)
        low = total.astype(BF16)
        mid_grad[here] = total
        branch[here] = low
        tallies[0] += eights(down * unit)
        tallies[1] += eights(down)
        tallies[2] += eights(low.astype(F32))
        tallies[3] += eights(top)

    step(pl.ds(0, rows))
    for index in range(4):
        sums[index : index + 1] = jnp.sum(tallies[index], axis=0, keepdims=True)


def attention_back_stage(
    x, vec, branch, mid_grad, packed, mixed, logs, grads, result, sums, down, normal, stage, full_out,
    full, first_load, load, takes, tallies, count, length,
):
    rows, width = x.shape
    space = rows // count
    head = width // HEADS
    pair = 2 * head
    scale = head**-0.5
    half = width // 2
    wait_all(first_load)
    down[...] = contract(branch[...], full_out[...], 1, 1).astype(BF16)
    wait_all(takes)
    owner = lax.shift_right_logical(
        lax.broadcasted_iota(jnp.int32, (HEADS, width), 1), head.bit_length() - 1
    )
    chosen = jnp.where(
        owner == lax.broadcasted_iota(jnp.int32, (HEADS, width), 0), 1.0, 0.0
    ).astype(BF16)
    left = lax.broadcasted_iota(jnp.int32, (space, pair), 1) < head
    live = lax.broadcasted_iota(jnp.int32, (space, pair), 0) < length
    key_live = lax.broadcasted_iota(jnp.int32, (space, space), 0) < length
    for image in range(count):
        span = pl.ds(image * space, space)
        product = down[span].astype(F32) * mixed[span].astype(F32)
        coarse = product.astype(BF16)
        fine = (product - coarse.astype(F32)).astype(BF16)
        stage[image, :, 0:space] = contract(chosen, coarse, 1, 1) + contract(chosen, fine, 1, 1)

    def heads(index, carry):
        for image in range(count):
            span = pl.ds(image * space, space)

            def part(block):
                offset = pl.multiple_of(block * width + index * pair, pair)
                return packed[span, pl.ds(offset, pair)]

            query, key, value = part(0), part(1), part(2)
            wide = key.astype(F32) * scale
            value = value.astype(F32)
            arrived = down[span, pl.ds(pl.multiple_of(index * pair, pair), pair)]
            found = []
            for side in range(2):
                mine = left if side == 0 else ~left
                log = logs[image, pl.ds(2 * index + side, 1), :]
                dot = stage[image, pl.ds(2 * index + side, 1), 0:space]
                scores = contract(jnp.where(mine, wide, 0.0).astype(BF16), query, 1, 1)
                chance = jnp.exp(jnp.where(key_live, scores - log, NEGATIVE))
                back = contract(jnp.where(mine, value, 0.0).astype(BF16), arrived, 1, 1)
                change = (chance * (back - dot)).astype(BF16)
                found.append(
                    (
                        contract(change, key, 0, 0),
                        contract(change, query, 1, 0),
                        contract(chance.astype(BF16), arrived, 1, 0),
                    )
                )
            for block, factor in enumerate((scale, scale, 1.0)):
                total = jnp.where(left, found[0][block], found[1][block]) * factor
                offset = pl.multiple_of(block * width + index * pair, pair)
                grads[span, pl.ds(offset, pair)] = jnp.where(live, total, 0.0).astype(BF16)
        return carry

    lax.fori_loop(0, HEADS // 2, heads, 0)
    wait_all(load)
    for block in range(2):
        normal[:, block * half : (block + 1) * half] = contract(
            grads[...], full[block * half : (block + 1) * half], 1, 1
        )
    gain = vec[GAIN0 : GAIN0 + 1]
    tallies[...] = jnp.zeros_like(tallies)

    def step(here):
        unit, rate = standardized(x[here].astype(F32))
        grad = normal[here]
        tallies[0] += eights(grad * unit)
        tallies[1] += eights(grad)
        result[here] = (mid_grad[here] + norm_pull(grad, gain, unit, rate)).astype(BF16)

    step(pl.ds(0, rows))
    for index in range(2):
        sums[index : index + 1] = jnp.sum(tallies[index], axis=0, keepdims=True)
    sums[2:3] = jnp.sum(grads[:, 0:width].astype(F32), axis=0, keepdims=True)
    sums[3:4] = jnp.sum(grads[:, 2 * width : 3 * width].astype(F32), axis=0, keepdims=True)


def backward(
    start, lower, upper, kept_low, kept_up, reduce, wide, qkv, params, meta, count, length,
    mixed_at, weight=LIGHT,
):
    feed, attend = reduce is not None, qkv is not None
    rows, width = start[0].shape
    space = rows // count
    pair = 2 * width // HEADS
    parts = len(reduce if feed else qkv)
    many = len(flat(reduce if feed else qkv))
    spots = parts + 1 + count
    inner = wide[0][0].shape[1] - width if feed else 0
    deep = inner // parts
    both = feed and attend
    choices = []
    if feed:
        choices += [(kept_low[0], kept_up[0]), (kept_low[1], kept_up[1])]
        if start[0] is not start[1]:
            choices += [start]
    if attend:
        choices += [(kept_low[index], kept_up[index]) for index in (2, 3, 4)]
        choices += [(lower, upper)]
    plain = [start[0]] if feed and start[0] is start[1] else [] if feed else list(start)
    operands = []
    for low, up in choices:
        operands += [low] if low is up else [low, up]

    def body(*refs):
        refs = list(refs)
        firsts = [refs.pop(0) for _ in plain]
        pairs = []
        for low, up in choices:
            one = refs.pop(0)
            pairs.append((one, one if low is up else refs.pop(0)))
        lists = [[refs.pop(0) for _ in range(many)] for _ in range(2 * feed + 2 * attend)]
        vec, info = refs.pop(0), refs.pop(0)
        section = info[parts]
        if feed:
            if both:
                right = refs.pop(0)
                hidden, branch = right.at[:, pl.ds(0, inner)], right.at[:, pl.ds(inner, width)]
            else:
                hidden, branch = refs.pop(0), refs.pop(0)
            feed_sums, inner_sums = refs.pop(0), refs.pop(0)
            mid_grad = None if both else refs.pop(0)
        if attend:
            grads, result, sums = (refs.pop(0) for _ in range(3)) if not both else (None, refs.pop(0), refs.pop(0))
        if both:
            feed_grad = right.at[:, pl.ds(inner + width, width)]
            grads = right.at[:, pl.ds(inner + 2 * width, 3 * width)]
        tallies, x_sem = refs.pop(0), refs.pop(0)
        if feed:
            grad, slope, middle, second, full_out, full, o_sem, w_sem = (
                refs.pop(0) for _ in range(8)
            )
            if both:
                mid_grad, keep = refs.pop(0), feed_grad
            else:
                keep = refs.pop(0)
            begin = pairs.pop(2) if start[0] is not start[1] else (firsts[0], firsts[0])
            take = start_chosen(section, *begin, grad, x_sem.at[0])
            for_slope = start_chosen(section, *pairs.pop(0), slope, x_sem.at[1])
            every = start_pieces(lists.pop(0), info, spots, full_out, o_sem, 0, (0, width))
            first_load = [[every.pop(0) for _ in group] for group in reduce]
            for_middle = start_chosen(section, *pairs.pop(0), middle, x_sem.at[2])
            load = start_pieces(lists.pop(0), info, spots, full, w_sem, 0, (0, inner), width)
        if attend:
            x, packed, mixed, logs, down, normal, stage, full_o, full_q, p_sem, q_sem = (
                refs.pop(0) for _ in range(11)
            )
            if not feed:
                branch, mid_grad = refs.pop(0), refs.pop(0)
                givens = [
                    pltpu.make_async_copy(source, target, x_sem.at[index])
                    for index, (source, target) in enumerate(zip(firsts, (branch, mid_grad)))
                ]
                for given in givens:
                    given.start()
            project_load = start_pieces(lists.pop(0), info, spots, full_o, p_sem, 0, (0, width))
            sames = [one is two for one, two in pairs]
            pairs[1] = tuple(one.at[:, pl.ds(mixed_at, width)] for one in pairs[1])
            takes = [
                start_chosen(section, *pairs[index], target, x_sem.at[3 + index], sames[index])
                for index, target in ((1, mixed), (0, packed), (2, logs), (3, x))
            ]
            last_load = start_pieces(lists.pop(0), info, spots, full_q, q_sem, 0, (0, 3 * width))
            if not feed:
                wait_all(givens)
        if feed:
            take.wait()
            hidden_back_stage(
                grad, vec, info, keep, slope, middle, hidden, second, mid_grad, branch, feed_sums,
                inner_sums, full_out, full, deep, first_load, load, for_slope, for_middle, tallies,
                count, parts,
            )
        if attend:
            attention_back_stage(
                x, vec, branch, mid_grad, packed, mixed, logs, grads, result, sums, down, normal,
                stage, full_o, full_q, project_load, last_load, takes, tallies, count, length,
            )

    outs = []
    scratch = [pltpu.VMEM((4, 8, width), F32), pltpu.SemaphoreType.DMA((7,))]
    flops = 0
    if feed:
        outs += [((rows, inner + 5 * width), BF16)] if both else [((rows, inner), BF16), ((rows, width), BF16)]
        outs += [
            ((8, width), F32),
            ((1, inner), F32),
        ]
        if not both:
            outs += [((rows, width), F32)]
        scratch += [
            pltpu.VMEM((rows, width), BF16),
            pltpu.VMEM((rows, inner), BF16),
            pltpu.VMEM((rows, width), F32),
            pltpu.VMEM((rows, width), F32),
            pltpu.VMEM((inner, width), BF16),
            pltpu.VMEM((width, inner), BF16),
            pltpu.SemaphoreType.DMA((1, many)),
            pltpu.SemaphoreType.DMA((1, many)),
        ]
        scratch += [pltpu.VMEM((rows, width), F32 if both else BF16)]
        flops += 4 * rows * width * inner
    if attend:
        outs += [] if both else [((rows, 3 * width), BF16)]
        outs += [((rows, width), BF16), ((8, width), F32)]
        scratch += [
            pltpu.VMEM((rows, width), BF16),
            pltpu.VMEM((rows, 3 * width), BF16),
            pltpu.VMEM((rows, width), BF16),
            pltpu.VMEM((count, HEADS, space), F32),
            pltpu.VMEM((rows, width), BF16),
            pltpu.VMEM((rows, width), F32),
            pltpu.VMEM((count, HEADS, 2 * pair), F32),
            pltpu.VMEM((width, width), BF16),
            pltpu.VMEM((width, 3 * width), BF16),
            pltpu.SemaphoreType.DMA((1, many)),
            pltpu.SemaphoreType.DMA((1, many)),
        ]
        if not feed:
            scratch += [pltpu.VMEM((rows, width), BF16), pltpu.VMEM((rows, width), F32)]
        flops += 2 * rows * width * (4 * width + 5 * space)
    weights = (flat(reduce) + flat(wide) if feed else []) + (
        flat(wide) + flat(qkv) if attend else []
    )
    return call(
        body,
        "backward" + "_feed" * feed + "_attend" * attend,
        plain + operands + weights + [params, meta],
        [ANY] * (len(plain) + len(operands) + len(weights)) + [VMEM, SMEM],
        outs,
        scratch,
        flops,
        weight,
    )


def weight_gradient(
    lefts, rights, meta, parts, blocks, quarter, rows_of, columns_of, name, weight=LIGHT
):
    terms = len(lefts)
    first_row, height = rows_of
    first_column, breadth = columns_of
    rows = lefts[0].shape[0]
    operands = list(lefts)
    places = []
    for pair in rights:
        found = []
        for array, _ in pair:
            if not any(array is other for other in operands):
                operands.append(array)
            found.append(next(i for i, other in enumerate(operands) if other is array))
        places.append(found)

    def body(*refs):
        sources, info = refs[: len(operands)], refs[len(operands)]
        results = refs[len(operands) + 1 : len(operands) + 1 + len(blocks)]
        left_full, right_full, l_sem, r_sem = refs[len(operands) + 1 + len(blocks) :]
        section = info[parts]
        waits = []
        for term in range(terms):
            sides = [
                sources[place].at[:, pl.ds(column + first_column, breadth)]
                for place, (_, column) in zip(places[term], rights[term])
            ]
            same = rights[term][0] is rights[term][1]
            target = right_full.at[pl.ds(term * rows, rows)]
            waits.append(start_chosen(section, *sides, target, r_sem.at[term], same))
        loads = []
        for index, block in enumerate(blocks):
            start = pl.multiple_of(info[block] * quarter + first_row, 128)
            for term in range(terms):
                copy = pltpu.make_async_copy(
                    sources[term].at[:, pl.ds(start, height)],
                    left_full.at[index, pl.ds(term * rows, rows)],
                    l_sem.at[index, term],
                )
                copy.start()
                loads.append(copy)
        wait_all(waits)
        for index in reversed(range(len(blocks))):
            wait_all(loads[index * terms : (index + 1) * terms])
            results[index][...] = contract(left_full[index], right_full[...], 0, 0).astype(BF16)

    return call(
        body,
        name,
        operands + [meta],
        [ANY] * len(operands) + [SMEM],
        [((height, breadth), BF16)] * len(blocks),
        [
            pltpu.VMEM((len(blocks), terms * rows, height), BF16),
            pltpu.VMEM((terms * rows, breadth), BF16),
            pltpu.SemaphoreType.DMA((len(blocks), terms)),
            pltpu.SemaphoreType.DMA((terms,)),
        ],
        2 * len(blocks) * terms * rows * height * breadth,
        weight,
    )


def after(value, *earlier):
    return lax.optimization_barrier((value,) + earlier)[0]


def added(*values):
    total = values[0].astype(F32)
    for value in values[1:]:
        total = total + value.astype(F32)
    return total.astype(values[0].dtype)


class FourByFour:
    parts = 4
    blocks = (0, 2)

    def __init__(self):
        self.group = lax.axis_index("group")
        self.place = lax.axis_index("replica")
        self.order = [self.group ^ part for part in range(4)]
        odd = self.place % 2
        halves = [2 * self.order[part] + half for part in (2, 3) for half in (odd, 1 - odd)]
        self.spots = self.order[:2] + halves

    def core(self, block):
        return lax.ppermute(block, "group", [(i, i ^ 1) for i in range(4)])

    def across(self, block):
        return lax.ppermute(block, "group", [(i, i ^ 2) for i in range(4)])

    def beside(self, block):
        return lax.ppermute(block, "replica", [(i, i ^ 1) for i in range(4)])

    def gather_small(self, block):
        near, far = self.core(block), self.across(block)
        return [block, near, far, self.core(far)]

    def gather(self, blocks, prepare):
        odd = self.place % 2
        asked = [
            lax.dynamic_slice_in_dim(block, odd * (block.shape[0] // 2), block.shape[0] // 2)
            for block in blocks
        ]
        halves, sibling = [], []
        for index, block in enumerate(blocks):
            halves.append(self.across(after(asked[index], *halves[: max(index - 1, 0)])))
            sibling.append(self.core(after(block, sibling[-1]) if index else block))
        others = []
        tokens = prepare(halves[0]) + asked[2:]
        for index, half in enumerate(halves):
            earlier = others[-1:] if index == 1 else []
            others.append(self.beside(after(half, *earlier, *(tokens if index == 1 else []))))
        self.arrived = halves[-1]

        def pieces(index, *tokens):
            one, two = (after(half, *tokens) for half in (halves[index], others[index]))
            return [
                [blocks[index]],
                [sibling[index]],
                [halves[index], others[index]],
                [self.core(one), self.core(two)],
            ]

        return [partial(pieces, index) for index in range(len(blocks))]

    def shared(self, block):
        return [block, self.core(block)]

    def total(self, blocks):
        passed = self.across(blocks[1])
        token = yield
        mine = added(after(blocks[0], token), passed)
        inward = lax.ppermute(mine, "replica", [(0, 1), (3, 2)])
        token = yield mine
        joined = added(after(mine, token), inward)
        crossing = lax.ppermute(joined, "replica", [(1, 2), (2, 1)])
        token = yield joined
        summed = added(after(joined, token), crossing)
        outward = lax.ppermute(summed, "replica", [(1, 0), (2, 3)])
        token = yield summed
        inner = (self.place == 1) | (self.place == 2)
        yield jnp.where(inner, after(summed, token), outward)


class General:
    def __init__(self):
        self.parts = lax.axis_size("group")
        self.blocks = tuple(range(self.parts))
        self.order = self.spots = [jnp.int32(part) for part in range(self.parts)]

    def gather_small(self, block):
        whole = lax.all_gather(block, "group", axis=0)
        return [whole[part] for part in range(self.parts)]

    def gather(self, blocks, prepare):
        prepare(blocks[0])
        self.arrived = blocks[0]
        found = [[[piece] for piece in self.gather_small(block)] for block in blocks]
        return [lambda *tokens, groups=groups: groups for groups in found]

    def shared(self, block):
        return [block]

    def total(self, blocks):
        yield
        mine = lax.psum_scatter(jnp.stack(blocks), "group", scatter_dimension=0)
        yield mine
        yield lax.psum(mine, "replica")


def shifted(block, distance):
    devices = range(lax.axis_size("section"))
    route = [(i - distance, i) for i in devices if i - distance in devices]
    return lax.ppermute(block, "section", route)


def in_order(pieces, order):
    place = jnp.stack(order)
    stacked = []
    for block in range(len(pieces)):
        chosen = pieces[0]
        for part in range(1, len(pieces)):
            chosen = jnp.where(place[part] == block, pieces[part], chosen)
        stacked.append(chosen)
    return jnp.stack(stacked)


class Sequence:
    def __init__(self, net, token):
        self.net, self.sums, self.results, self.token = net, {}, {}, token

    def now(self, value):
        return after(value, self.token)

    def ran(self, value):
        self.token = value

    def add(self, name, blocks):
        self.sums[name] = self.net.total(blocks)
        next(self.sums[name])

    def step(self, *names):
        for name in names:
            try:
                self.results[name] = self.token = self.sums[name].send(self.token)
            except StopIteration:
                continue

    def finish(self, name):
        while True:
            try:
                self.results[name] = self.sums[name].send(self.token)
            except StopIteration:
                return self.results[name]


def per_device(
    images,
    cotangent,
    counts,
    qkv_weight,
    out_weight,
    expand_weight,
    reduce_weight,
    norm_gains,
    biases,
    expand_bias,
):
    micro, slots, length, width = images.shape
    space = padded(length)
    section = lax.axis_index("section")
    first = section == 0
    sizes = (lax.axis_size("group"), lax.axis_size("replica"))
    net = FourByFour() if sizes == (4, 4) else General()
    parts = net.parts
    share = width // parts
    batches = tuple(range(micro))

    def rows_of(array):
        fulls = [jnp.pad(array[batch], ((0, 0), (0, space - length), (0, 0))) for batch in batches]
        return [full.reshape(slots * space, width) for full in fulls]

    def images_of(array):
        return array.reshape(slots, space, width)[:, :length]

    small = jnp.concatenate([norm_gains[0], biases[0], expand_bias[0].reshape(-1, share)])
    slot = jnp.arange(slots, dtype=jnp.int32)
    alive = [(slot < counts[batch, 0]).astype(jnp.int32) for batch in batches]
    head = jnp.stack(net.order + [section]).astype(jnp.int32)

    spots = jnp.stack(net.spots).astype(jnp.int32)

    def meta(living):
        return jnp.concatenate([head, living, spots])

    infos = [meta(alive[batch]) for batch in batches]
    pieces = net.gather_small(small)
    vectors = in_order(pieces, net.order)
    top = vectors[:, :8].transpose(1, 0, 2).reshape(8, width)
    bottom = vectors[:, 8:].reshape(-1, width)
    params = jnp.concatenate([top, bottom]).astype(F32)
    slot = jnp.arange(slots, dtype=jnp.int32)
    alive = [(slot < counts[batch, 0]).astype(jnp.int32) for batch in batches]
    head = jnp.stack(net.order + [section]).astype(jnp.int32)
    spots = jnp.stack(net.spots).astype(jnp.int32)

    def meta(living):
        return jnp.concatenate([head, living, spots])

    infos = [meta(alive[batch]) for batch in batches]
    inputs, targets = [], []

    def prepare(token):
        inputs.extend(rows_of(after(images, token)))
        targets.extend(rows_of(after(cotangent, token)))
        return [params, *inputs, *targets, *infos]

    qkv, wide, reduce = net.gather(
        [qkv_weight[0], jnp.concatenate([out_weight[0], expand_weight[0]], axis=1), reduce_weight[0]],
        prepare,
    )

    qkv = qkv()
    attended = []
    for batch in batches:
        start = inputs[batch] if batch == 0 else after(inputs[batch], attended[-1][0], net.arrived)
        attended.append(
            forward(start, start, None, qkv, None, params, infos[batch], slots, length)
        )
    wide = wide(attended[-1][0])
    fed = []
    for batch in batches:
        start = inputs[batch] if batch == 0 else after(inputs[batch], fed[-1][0])
        fed.append(
            forward(start, start, attended[batch][0], None, wide, params, infos[batch], slots, length)
        )
    reduce = reduce(fed[-1][0])
    early, incoming = [], []
    for batch in batches:
        middle, active = fed[batch]
        if batch:
            active = after(active, made[-1])
        cuts = 2 if batch == 0 else 1
        made, sent = [], []
        for cut in range(cuts):
            part = width // cuts
            made.append(
                output_forward(
                    middle, after(active, *made), reduce, params, infos[batch], slots, LIGHT, (cut * part, part)
                )
            )
            sent.append(shifted(made[-1], 1))
        early.append(jnp.concatenate(made, axis=1))
        incoming.append(jnp.concatenate(sent, axis=1))

    inner = wide[0][0].shape[1] - width
    mixed_at = inner + width
    kept, lefts, rights, results = [], [], [], []
    sums_a, sums_b, sums_c, returning = [], [], [], []
    token = made[-1]
    for batch in batches:
        start = after(incoming[batch], token)
        left, packed, logs, middle, slope = forward(
            inputs[batch], start, None, qkv, wide, params, infos[batch], slots, length, 8.0
        )
        kept.append((slope, middle, packed, left, logs))
        lefts.append(net.shared(left))
        if batch == 0:
            pair, sides = (targets[0], targets[0]), (kept[0], kept[0])
            lower, chosen = incoming[0], infos[0]
        else:
            pair = (returning[batch - 1], targets[batch])
            sides = (kept[batch - 1], kept[batch])
            lower = inputs[batch - 1]
            chosen = meta(jnp.where(first, alive[batch - 1], alive[batch]))
        right, some, more, result, rest = backward(
            pair, lower, incoming[batch], sides[0], sides[1], reduce, wide, qkv, params, chosen,
            slots, length, mixed_at, 8.0,
        )
        token = result
        rights.append(net.shared(right))
        results.append(result)
        sums_a.append(some)
        sums_b.append(more)
        sums_c.append(rest)
        returning.append(shifted(result, -1))
    late = []
    for batch in batches:
        ready = lefts[batch][1:] + (rights[batch][1:] if batch < micro - 1 else [])
        active = after(kept[batch][3], token, *ready)
        late.append(output_forward(kept[batch][1], active, reduce, params, infos[batch], slots, 8.0))
        token = late[-1]

    last = micro - 1
    run = Sequence(net, token)
    arrived = run.now(returning[last])
    living = jnp.repeat(alive[last] > 0, space)[:, None]
    masked = net.shared(jnp.where(living, arrived, jnp.zeros_like(arrived)))
    many = len(masked)

    def gradient(name, left_at, final, final_at, right_at, quarter, rows, columns, weight=LIGHT):
        left = [lefts[batch][side] for batch in batches for side in range(many)]
        right = []
        for batch in batches:
            for side in range(many):
                upper = (rights[batch][side], right_at)
                lower = (final[side], final_at) if batch == last else (rights[batch + 1][side], right_at)
                right.append((lower, upper))
        blocks = weight_gradient(
            left, right, run.now(head), parts, net.blocks, quarter, (left_at + rows[0], rows[1]), columns,
            name, weight,
        )
        run.ran(blocks[0])
        return blocks

    half, at = inner // 2, inner + 2 * width
    deep = inner // parts
    state = {"mid": None, "rows": None}

    def feed_back(weight):
        start = run.now(arrived)
        hidden, branch, some, more, mid = backward(
            (start, start), None, None, kept[last], kept[last], reduce, wide, None, params, infos[last],
            slots, length, mixed_at, weight,
        )
        run.ran(hidden)
        state.update(mid=mid, branch=branch, hidden=net.shared(hidden), branches=net.shared(branch))
        sums_a.append(some)
        sums_b.append(more)

    def attend_back(weight):
        start = run.now(after(state["branch"], *state["branches"][1:], *state["hidden"][1:]))
        grads, result, rest = backward(
            (start, state["mid"]), inputs[last], inputs[last], kept[last], kept[last], None, wide, qkv,
            params, infos[last], slots, length, mixed_at, weight,
        )
        run.ran(result)
        state["grads"] = net.shared(grads)
        results.append(result)
        sums_c.append(rest)

    def reduce_part(index, weight):
        step = deep // 2
        return gradient(
            "reduce", 0, masked, 0, inner + width, deep, (index * step, step), (0, width), weight
        )

    def expand_part(begin, size, weight):
        return gradient("expand", inner, state["hidden"], 0, 0, share, (0, share), (begin, size), weight)

    def project_part(weight):
        return gradient(
            "project", mixed_at, state["branches"], 0, inner, share, (0, share), (0, width), weight
        )

    def qkv_part(begin, size, weight):
        return gradient("qkv", at, state["grads"], 0, at, share, (0, share), (begin, size), weight)

    def over_batches(values):
        return sum(jnp.where(first, values[batch + 1], values[batch]) for batch in batches)

    def small_sums():
        some, more, rest = over_batches(sums_a), over_batches(sums_b), over_batches(sums_c)
        rows = jnp.concatenate([rest[0:1], some[0:1], rest[1:2], some[1:2], rest[2:4], some[2:4]])
        rows = rows.reshape(8, parts, share).transpose(1, 0, 2)
        rows = jnp.concatenate([rows, more.reshape(parts, -1, share)], axis=1)
        rows = sum(net.shared(run.now(rows)))
        rows = jnp.stack(
            [lax.dynamic_index_in_dim(rows, net.order[block], 0, keepdims=False) for block in net.blocks]
        )
        state["count"] = rows.shape[1]
        state["rows"] = rows.reshape(len(net.blocks), -1).astype(BF16)

    def with_small(blocks):
        step, rows = blocks[0].shape[1], state["rows"]
        rows = jnp.pad(rows, ((0, 0), (0, -rows.shape[1] % (16 * step)))).reshape(len(blocks), -1, step)
        return [jnp.concatenate([block, row]) for block, row in zip(blocks, rows)]

    outputs = []

    def assemble():
        index = len(outputs)
        low, up = (early + results[1:])[index], (late + results[:-1])[index]
        outputs.append(images_of(jnp.where(first, run.now(low), up)))

    def joined(axis, *names):
        found = [run.finish(name) for name in names]
        found = [value[:share] if name == LAST.lower() else value for name, value in zip(names, found)]
        return jnp.concatenate(found, axis=axis).astype(F32)[None]

    shapes = {"q": (1, "q0", "q1"), "p": (1, "p0"), "e": (1, "e0", "e1"), "r": (0, "r0", "r1")}
    gradients = {}

    third = 3 * width // 2
    kernels = {
        "R0": lambda weight: reduce_part(0, weight),
        "R1": lambda weight: reduce_part(1, weight),
        "E0": lambda weight: expand_part(0, half, weight),
        "E1": lambda weight: expand_part(half, half, weight),
        "Q0": lambda weight: qkv_part(0, third, weight),
        "Q1": lambda weight: qkv_part(third, third, weight),
        "P0": lambda weight: project_part(weight),
    }
    for entry in " ".join(PLAN).split():
        name, _, factor = entry.partition("*")
        weight = float(factor or HEAVY) if "*" in entry else LIGHT
        if name in kernels:
            blocks = kernels[name](weight)
            if name == LAST:
                blocks = with_small(blocks)
            run.add(name.lower(), blocks)
        elif name == "BF":
            feed_back(weight)
        elif name == "BA":
            attend_back(weight)
        elif name == "V":
            small_sums()
        elif name == "O":
            assemble()
        elif name[0] == "C":
            gradients[name[1]] = joined(*shapes[name[1]])
        else:
            run.step(name)
    while len(outputs) < 2 * micro:
        assemble()
    for name in shapes:
        if name not in gradients:
            gradients[name] = joined(*shapes[name])
    count = state["count"]
    vector = run.finish(LAST.lower())[share:].reshape(-1)[: count * share].reshape(count, share).astype(F32)
    return (
        jnp.stack(outputs[:micro])[None],
        jnp.stack(outputs[micro:])[None],
        gradients["q"],
        gradients["p"],
        gradients["e"],
        gradients["r"],
        vector[None, 0:2],
        vector[None, 2:8],
        vector[8:].reshape(1, -1),
    )


def solution(mesh):
    placed = (
        P(None, ("group", "replica"), None, None),
        P(None, ("group", "replica"), None, None),
        P(None, ("group", "replica")),
        P("section", "group", None),
        P("section", "group", None),
        P("section", "group", None),
        P("section", "group", None),
        P("section", None, "group"),
        P("section", None, "group"),
        P("section", "group"),
    )
    return jax.shard_map(
        per_device,
        mesh=mesh,
        in_specs=placed,
        out_specs=(
            P("section", None, ("group", "replica"), None, None),
            P("section", None, ("group", "replica"), None, None),
            P("section", "group", None),
            P("section", "group", None),
            P("section", "group", None),
            P("section", "group", None),
            P("section", None, "group"),
            P("section", None, "group"),
            P("section", "group"),
        ),
        check_vma=False,
    )
```

```python
from functools import partial

import jax
import jax.numpy as jnp
from jax import lax
from jax.experimental import pallas as pl
from jax.experimental.pallas import tpu as pltpu
from jax.sharding import PartitionSpec as P

HEADS = 16
EPSILON = 1e-06
NEGATIVE = -1e30
F32 = jnp.float32
BF16 = jnp.bfloat16
LIGHT, HEAVY = 1.0 / 64, 16.0
PLAN = (
    "R0 BF r0 R1*",
    "BA r0 r1 E0*",
    "Q0 r0 r1 e0",
    "E1 q0 r1 e0",
    "r0 Q1 e1 q0",
    "r1 e0 V P0",
    "e1 q1 q0 e0",
    "p0 O q1 O",
    "e1 q0 p0 O",
    "O q1 e1 p0",
    "q1 p0",
)
LAST = "P0"
VMEM_LIMIT = 58 * 2**20
ROOT_HALF = 0.7071067811865476
ROOT_TAU = 0.3989422804014327
ANY = pl.BlockSpec(memory_space=pl.ANY)
VMEM = pl.BlockSpec(memory_space=pltpu.VMEM)
SMEM = pl.BlockSpec(memory_space=pltpu.SMEM)
GAIN0, GAIN1, SHIFT0, SHIFT1, QUERY, VALUE, OUT, FEED, EXPAND = range(9)


def padded(length):
    return -(-length // 16) * 16


def contract(left, right, left_dim, right_dim):
    return lax.dot_general(
        left, right, (((left_dim,), (right_dim,)), ((), ())), preferred_element_type=F32
    )


def standardized(values):
    center = values - jnp.mean(values, axis=-1, keepdims=True)
    spread = jnp.mean(center * center, axis=-1, keepdims=True)
    scale = lax.rsqrt(spread + EPSILON)
    return center * scale, scale


def norm_pull(grad, gain, unit, scale):
    scaled = grad * gain
    mean = jnp.mean(scaled, axis=-1, keepdims=True)
    along = jnp.mean(scaled * unit, axis=-1, keepdims=True)
    return scale * (scaled - mean - unit * along)


def call(body, name, operands, specs, outs, scratch, flops, weight=LIGHT):
    moved = sum(o.size * o.dtype.itemsize for o in operands)
    out_shape = [jax.ShapeDtypeStruct(shape, dtype) for shape, dtype in outs]
    moved += sum(o.size * o.dtype.itemsize for o in out_shape)
    return pl.pallas_call(
        body,
        out_shape=out_shape,
        in_specs=specs,
        out_specs=[VMEM] * len(outs),
        scratch_shapes=scratch,
        compiler_params=pltpu.CompilerParams(vmem_limit_bytes=VMEM_LIMIT),
        cost_estimate=pl.CostEstimate(flops=int(flops * weight), bytes_accessed=int(moved * weight), transcendentals=0),
        name=name,
    )(*operands)


def flat(groups):
    return [piece for group in groups for piece in group]


def start_pieces(pieces, info, first, target, sems, slot, columns, shift=0):
    begin, size = columns
    columns = pl.ds(begin, size)
    copies = []
    for index, piece in enumerate(pieces):
        rows = piece.shape[0]
        where = pl.multiple_of(info[first + index] * rows, rows)
        copy = pltpu.make_async_copy(
            piece.at[:, pl.ds(begin + shift, size)],
            target.at[pl.ds(where, rows), columns],
            sems.at[slot, index],
        )
        copy.start()
        copies.append(copy)
    return copies


def wait_all(copies):
    for copy in copies:
        copy.wait()


def start_chosen(section, lower, upper, target, sem, same=False):
    if lower is upper or same:
        copy = pltpu.make_async_copy(lower, target, sem)
        copy.start()
        return copy

    @pl.when(section == 0)
    def _():
        pltpu.make_async_copy(lower, target, sem).start()

    @pl.when(section != 0)
    def _():
        pltpu.make_async_copy(upper, target, sem).start()

    return pltpu.make_async_copy(lower, target, sem)


def eights(values):
    return jnp.sum(values.reshape(-1, 8, values.shape[-1]), axis=0)


def attention_stage(x, vec, norm, packed, mixed, logs, columns, full, loads, count, length):
    rows, width = x.shape
    space = rows // count
    head = width // HEADS
    pair = 2 * head
    scale = head**-0.5
    gain, shift = vec[GAIN0 : GAIN0 + 1], vec[SHIFT0 : SHIFT0 + 1]

    def step(here):
        unit, _ = standardized(x[here].astype(F32))
        norm[here] = (unit * gain + shift).astype(BF16)

    step(pl.ds(0, rows))
    for block in range(3):
        wait_all(loads[block])
        done = contract(norm[...], full[:, block * width : (block + 1) * width], 1, 0)
        if block != 1:
            bias = QUERY if block == 0 else VALUE
            done = done + vec[bias : bias + 1]
        packed[:, block * width : (block + 1) * width] = done.astype(BF16)
    lane = lax.broadcasted_iota(jnp.int32, (space, pair), 1)
    left = lane < head
    live = lax.broadcasted_iota(jnp.int32, (space, pair), 0) < length
    key_live = lax.broadcasted_iota(jnp.int32, (space, space), 1) < length
    columns[...] = jnp.zeros_like(columns)

    def heads(index, carry):
        for image in range(count):
            span = pl.ds(image * space, space)

            def part(block):
                offset = pl.multiple_of(block * width + index * pair, pair)
                return packed[span, pl.ds(offset, pair)]

            query, key, value = part(0).astype(F32) * scale, part(1), part(2).astype(F32)
            found = []
            tops = []
            for side in range(2):
                mine = left if side == 0 else ~left
                asked = jnp.where(mine, query, 0.0).astype(BF16)
                held = jnp.where(live, jnp.where(mine, value, 1.0), 0.0).astype(BF16)
                scores = jnp.where(key_live, contract(asked, key, 1, 1), NEGATIVE)
                top = jnp.max(scores, axis=-1, keepdims=True)
                raised = jnp.exp(scores - top).astype(BF16)
                found.append(contract(raised, held, 1, 0))
                tops.append(top)
            inside = jnp.where(left, found[0], found[1])
            total = jnp.where(left, found[1], found[0])
            turned = pltpu.roll(total, head, 1)
            offset = pl.multiple_of(index * pair, pair)
            mixed[span, pl.ds(offset, pair)] = (inside / turned).astype(BF16)
            if logs is None:
                continue
            logged = jnp.log(turned)
            first = tops[0] + logged[:, 0:1]
            second = tops[1] + logged[:, head : head + 1]
            known = columns[image]
            known = jnp.where(lane == 2 * index, first, known)
            columns[image] = jnp.where(lane == 2 * index + 1, second, known)
        return carry

    lax.fori_loop(0, HEADS // 2, heads, 0)
    if logs is not None:
        for image in range(count):
            logs[image] = columns[image].T[0:HEADS]


def hidden_stage(x, vec, mixed, middle, active, second, slope, full_out, full, first_load, loads):
    rows, width = x.shape
    wait_all(first_load)
    gain, shift, bias = vec[GAIN1 : GAIN1 + 1], vec[SHIFT1 : SHIFT1 + 1], vec[OUT : OUT + 1]
    middle[...] = contract(mixed[...], full_out[...], 1, 0)

    def step(here):
        total = middle[here] + x[here].astype(F32) + bias
        middle[here] = total
        unit, _ = standardized(total)
        second[here] = (unit * gain + shift).astype(BF16)

    step(pl.ds(0, rows))
    for block, load in enumerate(loads):
        wait_all(load)
        part = slice(block * width, (block + 1) * width)
        value = contract(second[...], full[:, part], 1, 0) + vec[EXPAND + block : EXPAND + block + 1]
        share = 0.5 + 0.5 * lax.erf(value * ROOT_HALF)
        active[:, part] = (value * share).astype(BF16)
        if slope is not None:
            density = ROOT_TAU * jnp.exp(-0.5 * value * value)
            slope[:, part] = (share + value * density).astype(BF16)


def forward(
    lower, upper, mixed_in, qkv, wide, params, meta, count, length, weight=LIGHT
):
    rows, width = lower.shape
    space = rows // count
    pair = 2 * width // HEADS
    attend, feed = qkv is not None, wide is not None
    both = attend and feed
    parts = len(qkv if attend else wide)
    many = len(flat(qkv if attend else wide))
    spots = parts + 1 + count
    inner = wide[0][0].shape[1] - width if feed else 0
    blocks = inner // width
    same = lower is upper

    def body(*refs):
        refs = list(refs)
        low = refs.pop(0)
        up = low if same else refs.pop(0)
        if not attend:
            arrived = refs.pop(0)
        lists = [[refs.pop(0) for _ in range(many)] for _ in range(attend + 2 * feed)]
        vec, info = refs.pop(0), refs.pop(0)
        if both:
            left, packed, logs, middle, slope = (refs.pop(0) for _ in range(5))
            active, second, mixed, norm = (
                left.at[:, pl.ds(start, size)]
                for start, size in ((0, inner), *((inner + width * i, width) for i in range(3)))
            )
        elif attend:
            mixed = refs.pop(0)
        else:
            middle, active = refs.pop(0), refs.pop(0)
        x, x_sem = refs.pop(0), refs.pop(0)
        section = info[parts]
        take = start_chosen(section, low, up, x, x_sem.at[0])
        if attend:
            columns, full, a_sem = (refs.pop(0) for _ in range(3))
            if not both:
                norm, packed, logs = refs.pop(0), refs.pop(0), None
            weight = lists.pop(0)
            loads = [
                start_pieces(weight, info, spots, full, a_sem, block, (block * width, width))
                for block in range(3)
            ]
        if feed:
            full_out, full_in, o_sem, w_sem = (refs.pop(0) for _ in range(4))
            if not attend:
                mixed, second, slope = refs.pop(0), refs.pop(0), None
                extra = pltpu.make_async_copy(arrived, mixed, x_sem.at[1])
                extra.start()
            first_load = start_pieces(lists[0], info, spots, full_out, o_sem, 0, (0, width))
            inner_loads = [
                start_pieces(lists[1], info, spots, full_in, w_sem, block, (block * width, width), width)
                for block in range(blocks)
            ]
        take.wait()
        if attend:
            attention_stage(
                x, vec, norm, packed, mixed, logs, columns, full, loads, count, length
            )
        if feed:
            if not attend:
                extra.wait()
            hidden_stage(
                x, vec, mixed, middle, active, second, slope, full_out, full_in, first_load,
                inner_loads,
            )

    outs, inputs = [], [lower] if same else [lower, upper]
    scratch = [pltpu.VMEM((rows, width), BF16), pltpu.SemaphoreType.DMA((2,))]
    flops = 0
    if attend:
        outs += [
            ((rows, width), BF16),
            ((rows, 3 * width), BF16),
            ((rows, width), BF16),
            ((count, HEADS, space), F32),
        ]
        scratch += [
            pltpu.VMEM((count, space, pair), F32),
            pltpu.VMEM((width, 3 * width), BF16),
            pltpu.SemaphoreType.DMA((3, many)),
        ]
        if not feed:
            scratch += [pltpu.VMEM((rows, width), BF16), pltpu.VMEM((rows, 3 * width), BF16)]
        flops += 2 * rows * width * (3 * width + 2 * space)
    else:
        inputs += [mixed_in]
    if feed:
        outs += [
            ((rows, width), F32),
            ((rows, inner), BF16),
            ((rows, width), BF16),
            ((rows, inner), BF16),
        ]
        scratch += [
            pltpu.VMEM((width, width), BF16),
            pltpu.VMEM((width, inner), BF16),
            pltpu.SemaphoreType.DMA((1, many)),
            pltpu.SemaphoreType.DMA((blocks, many)),
        ]
        if not attend:
            scratch += [pltpu.VMEM((rows, width), BF16), pltpu.VMEM((rows, width), BF16)]
        flops += 2 * rows * width * (width + inner)
    if both:
        outs = [((rows, inner + 3 * width), BF16), outs[1], outs[3], outs[4], outs[7]]
    else:
        outs = [outs[2]] if attend else outs[:2]
    weights = (flat(qkv) if attend else []) + (2 * flat(wide) if feed else [])
    return call(
        body,
        "forward" + "_attend" * attend + "_feed" * feed,
        inputs + weights + [params, meta],
        [ANY] * (len(inputs) + len(weights)) + [VMEM, SMEM],
        outs,
        scratch,
        flops,
        weight,
    )


def output_forward(middle, active, pieces, params, meta, count, weight=LIGHT):
    rows, width = middle.shape
    inner = sum(piece.shape[0] for piece in flat(pieces))
    space = rows // count
    parts, many = len(pieces), len(flat(pieces))
    spots = parts + 1 + count
    deep = inner // parts

    def body(*refs):
        refs = list(refs)
        mid_in, act_in = refs.pop(0), refs.pop(0)
        reduce = [refs.pop(0) for _ in range(many)]
        vec, info, result, mid, act, full, total, x_sem, w_sem = refs
        every = start_pieces(reduce[:1], info, spots, full, w_sem, 0, (0, width))
        columns = [pl.ds(pl.multiple_of(info[index] * deep, deep), deep) for index in range(parts)]
        takes = []
        for index in range(parts):
            takes.append(
                pltpu.make_async_copy(act_in.at[:, columns[index]], act.at[index], x_sem.at[index])
            )
            takes[-1].start()
            if index == 0:
                every += start_pieces(
                    reduce[1:], info, spots + 1, full, w_sem.at[:, pl.ds(1, many - 1)], 0, (0, width)
                )
        last = pltpu.make_async_copy(mid_in, mid, x_sem.at[parts])
        last.start()
        for index, group in enumerate(pieces):
            takes[index].wait()
            wait_all([every.pop(0) for _ in group])
            value = contract(act[index], full[columns[index]], 1, 0)
            if index:
                value = value + total[...]
            if index < parts - 1:
                total[...] = value
        last.wait()
        value = value + mid[...] + vec[FEED : FEED + 1]
        for image in range(count):
            alive = jnp.where(info[parts + 1 + image] > 0, 1.0, 0.0)
            here = slice(image * space, (image + 1) * space)
            result[here] = (value[here] * alive).astype(BF16)

    return call(
        body,
        "output_forward",
        [middle, active] + flat(pieces) + [params, meta],
        [ANY] * (2 + many) + [VMEM, SMEM],
        [((rows, width), BF16)],
        [
            pltpu.VMEM((rows, width), F32),
            pltpu.VMEM((parts, rows, deep), BF16),
            pltpu.VMEM((inner, width), BF16),
            pltpu.VMEM((rows, width), F32),
            pltpu.SemaphoreType.DMA((parts + 1,)),
            pltpu.SemaphoreType.DMA((1, many)),
        ],
        2 * rows * width * inner,
        weight,
    )[0]


def hidden_back_stage(
    grad, vec, info, feed, slope, middle, hidden, second, mid_grad, branch, sums, inner_sums, full_out,
    full, deep, first_load, load, for_slope, for_middle, tallies, count, parts,
):
    rows, width = grad.shape
    space = rows // count
    half = width // 2
    for image in range(count):
        alive = jnp.where(info[parts + 1 + image] > 0, 1.0, 0.0)
        here = slice(image * space, (image + 1) * space)
        feed[here] = (grad[here].astype(F32) * alive).astype(BF16)
    for_slope.wait()
    for index in range(parts):
        wait_all(first_load[index])
        where = pl.multiple_of(info[index] * deep, deep)
        value = contract(feed[...], full_out[pl.ds(where, deep)], 1, 1)
        value = (value * slope[:, pl.ds(where, deep)].astype(F32)).astype(BF16)
        hidden[:, pl.ds(where, deep)] = value
        inner_sums[:, pl.ds(where, deep)] = jnp.sum(value.astype(F32), axis=0, keepdims=True)
    wait_all(load)
    for block in range(2):
        second[:, block * half : (block + 1) * half] = contract(
            hidden[...], full[block * half : (block + 1) * half], 1, 1
        )
    for_middle.wait()
    gain = vec[GAIN1 : GAIN1 + 1]
    tallies[...] = jnp.zeros_like(tallies)

    def step(here):
        unit, scale = standardized(middle[here])
        down = second[here]
        top = feed[here].astype(F32)
        total = top + norm_pull(down, gain, unit, scale)
        low = total.astype(BF16)
        mid_grad[here] = total
        branch[here] = low
        tallies[0] += eights(down * unit)
        tallies[1] += eights(down)
        tallies[2] += eights(low.astype(F32))
        tallies[3] += eights(top)

    step(pl.ds(0, rows))
    for index in range(4):
        sums[index : index + 1] = jnp.sum(tallies[index], axis=0, keepdims=True)


def attention_back_stage(
    x, vec, branch, mid_grad, packed, mixed, logs, grads, result, sums, down, normal, stage, full_out,
    full, first_load, load, takes, tallies, count, length,
):
    rows, width = x.shape
    space = rows // count
    head = width // HEADS
    pair = 2 * head
    scale = head**-0.5
    half = width // 2
    wait_all(first_load)
    down[...] = contract(branch[...], full_out[...], 1, 1).astype(BF16)
    wait_all(takes)
    owner = lax.shift_right_logical(
        lax.broadcasted_iota(jnp.int32, (HEADS, width), 1), head.bit_length() - 1
    )
    chosen = jnp.where(
        owner == lax.broadcasted_iota(jnp.int32, (HEADS, width), 0), 1.0, 0.0
    ).astype(BF16)
    left = lax.broadcasted_iota(jnp.int32, (space, pair), 1) < head
    live = lax.broadcasted_iota(jnp.int32, (space, pair), 0) < length
    key_live = lax.broadcasted_iota(jnp.int32, (space, space), 0) < length
    for image in range(count):
        span = pl.ds(image * space, space)
        product = down[span].astype(F32) * mixed[span].astype(F32)
        coarse = product.astype(BF16)
        fine = (product - coarse.astype(F32)).astype(BF16)
        stage[image, :, 0:space] = contract(chosen, coarse, 1, 1) + contract(chosen, fine, 1, 1)

    def heads(index, carry):
        for image in range(count):
            span = pl.ds(image * space, space)

            def part(block):
                offset = pl.multiple_of(block * width + index * pair, pair)
                return packed[span, pl.ds(offset, pair)]

            query, key, value = part(0), part(1), part(2)
            wide = key.astype(F32) * scale
            value = value.astype(F32)
            arrived = down[span, pl.ds(pl.multiple_of(index * pair, pair), pair)]
            found = []
            for side in range(2):
                mine = left if side == 0 else ~left
                log = logs[image, pl.ds(2 * index + side, 1), :]
                dot = stage[image, pl.ds(2 * index + side, 1), 0:space]
                scores = contract(jnp.where(mine, wide, 0.0).astype(BF16), query, 1, 1)
                chance = jnp.exp(jnp.where(key_live, scores - log, NEGATIVE))
                back = contract(jnp.where(mine, value, 0.0).astype(BF16), arrived, 1, 1)
                change = (chance * (back - dot)).astype(BF16)
                found.append(
                    (
                        contract(change, key, 0, 0),
                        contract(change, query, 1, 0),
                        contract(chance.astype(BF16), arrived, 1, 0),
                    )
                )
            for block, factor in enumerate((scale, scale, 1.0)):
                total = jnp.where(left, found[0][block], found[1][block]) * factor
                offset = pl.multiple_of(block * width + index * pair, pair)
                grads[span, pl.ds(offset, pair)] = jnp.where(live, total, 0.0).astype(BF16)
        return carry

    lax.fori_loop(0, HEADS // 2, heads, 0)
    wait_all(load)
    for block in range(2):
        normal[:, block * half : (block + 1) * half] = contract(
            grads[...], full[block * half : (block + 1) * half], 1, 1
        )
    gain = vec[GAIN0 : GAIN0 + 1]
    tallies[...] = jnp.zeros_like(tallies)

    def step(here):
        unit, rate = standardized(x[here].astype(F32))
        grad = normal[here]
        tallies[0] += eights(grad * unit)
        tallies[1] += eights(grad)
        result[here] = (mid_grad[here] + norm_pull(grad, gain, unit, rate)).astype(BF16)

    step(pl.ds(0, rows))
    for index in range(2):
        sums[index : index + 1] = jnp.sum(tallies[index], axis=0, keepdims=True)
    sums[2:3] = jnp.sum(grads[:, 0:width].astype(F32), axis=0, keepdims=True)
    sums[3:4] = jnp.sum(grads[:, 2 * width : 3 * width].astype(F32), axis=0, keepdims=True)


def backward(
    start, lower, upper, kept_low, kept_up, reduce, wide, qkv, params, meta, count, length,
    mixed_at, weight=LIGHT,
):
    feed, attend = reduce is not None, qkv is not None
    rows, width = start[0].shape
    space = rows // count
    pair = 2 * width // HEADS
    parts = len(reduce if feed else qkv)
    many = len(flat(reduce if feed else qkv))
    spots = parts + 1 + count
    inner = wide[0][0].shape[1] - width if feed else 0
    deep = inner // parts
    both = feed and attend
    choices = []
    if feed:
        choices += [(kept_low[0], kept_up[0]), (kept_low[1], kept_up[1])]
        if start[0] is not start[1]:
            choices += [start]
    if attend:
        choices += [(kept_low[index], kept_up[index]) for index in (2, 3, 4)]
        choices += [(lower, upper)]
    plain = [start[0]] if feed and start[0] is start[1] else [] if feed else list(start)
    operands = []
    for low, up in choices:
        operands += [low] if low is up else [low, up]

    def body(*refs):
        refs = list(refs)
        firsts = [refs.pop(0) for _ in plain]
        pairs = []
        for low, up in choices:
            one = refs.pop(0)
            pairs.append((one, one if low is up else refs.pop(0)))
        lists = [[refs.pop(0) for _ in range(many)] for _ in range(2 * feed + 2 * attend)]
        vec, info = refs.pop(0), refs.pop(0)
        section = info[parts]
        if feed:
            if both:
                right = refs.pop(0)
                hidden, branch = right.at[:, pl.ds(0, inner)], right.at[:, pl.ds(inner, width)]
            else:
                hidden, branch = refs.pop(0), refs.pop(0)
            feed_sums, inner_sums = refs.pop(0), refs.pop(0)
            mid_grad = None if both else refs.pop(0)
        if attend:
            grads, result, sums = (refs.pop(0) for _ in range(3)) if not both else (None, refs.pop(0), refs.pop(0))
        if both:
            feed_grad = right.at[:, pl.ds(inner + width, width)]
            grads = right.at[:, pl.ds(inner + 2 * width, 3 * width)]
        tallies, x_sem = refs.pop(0), refs.pop(0)
        if feed:
            grad, slope, middle, second, full_out, full, o_sem, w_sem = (
                refs.pop(0) for _ in range(8)
            )
            if both:
                mid_grad, keep = refs.pop(0), feed_grad
            else:
                keep = refs.pop(0)
            begin = pairs.pop(2) if start[0] is not start[1] else (firsts[0], firsts[0])
            take = start_chosen(section, *begin, grad, x_sem.at[0])
            for_slope = start_chosen(section, *pairs.pop(0), slope, x_sem.at[1])
            every = start_pieces(lists.pop(0), info, spots, full_out, o_sem, 0, (0, width))
            first_load = [[every.pop(0) for _ in group] for group in reduce]
            for_middle = start_chosen(section, *pairs.pop(0), middle, x_sem.at[2])
            load = start_pieces(lists.pop(0), info, spots, full, w_sem, 0, (0, inner), width)
        if attend:
            x, packed, mixed, logs, down, normal, stage, full_o, full_q, p_sem, q_sem = (
                refs.pop(0) for _ in range(11)
            )
            if not feed:
                branch, mid_grad = refs.pop(0), refs.pop(0)
                givens = [
                    pltpu.make_async_copy(source, target, x_sem.at[index])
                    for index, (source, target) in enumerate(zip(firsts, (branch, mid_grad)))
                ]
                for given in givens:
                    given.start()
            project_load = start_pieces(lists.pop(0), info, spots, full_o, p_sem, 0, (0, width))
            sames = [one is two for one, two in pairs]
            pairs[1] = tuple(one.at[:, pl.ds(mixed_at, width)] for one in pairs[1])
            takes = [
                start_chosen(section, *pairs[index], target, x_sem.at[3 + index], sames[index])
                for index, target in ((1, mixed), (0, packed), (2, logs), (3, x))
            ]
            last_load = start_pieces(lists.pop(0), info, spots, full_q, q_sem, 0, (0, 3 * width))
            if not feed:
                wait_all(givens)
        if feed:
            take.wait()
            hidden_back_stage(
                grad, vec, info, keep, slope, middle, hidden, second, mid_grad, branch, feed_sums,
                inner_sums, full_out, full, deep, first_load, load, for_slope, for_middle, tallies,
                count, parts,
            )
        if attend:
            attention_back_stage(
                x, vec, branch, mid_grad, packed, mixed, logs, grads, result, sums, down, normal,
                stage, full_o, full_q, project_load, last_load, takes, tallies, count, length,
            )

    outs = []
    scratch = [pltpu.VMEM((4, 8, width), F32), pltpu.SemaphoreType.DMA((7,))]
    flops = 0
    if feed:
        outs += [((rows, inner + 5 * width), BF16)] if both else [((rows, inner), BF16), ((rows, width), BF16)]
        outs += [
            ((8, width), F32),
            ((1, inner), F32),
        ]
        if not both:
            outs += [((rows, width), F32)]
        scratch += [
            pltpu.VMEM((rows, width), BF16),
            pltpu.VMEM((rows, inner), BF16),
            pltpu.VMEM((rows, width), F32),
            pltpu.VMEM((rows, width), F32),
            pltpu.VMEM((inner, width), BF16),
            pltpu.VMEM((width, inner), BF16),
            pltpu.SemaphoreType.DMA((1, many)),
            pltpu.SemaphoreType.DMA((1, many)),
        ]
        scratch += [pltpu.VMEM((rows, width), F32 if both else BF16)]
        flops += 4 * rows * width * inner
    if attend:
        outs += [] if both else [((rows, 3 * width), BF16)]
        outs += [((rows, width), BF16), ((8, width), F32)]
        scratch += [
            pltpu.VMEM((rows, width), BF16),
            pltpu.VMEM((rows, 3 * width), BF16),
            pltpu.VMEM((rows, width), BF16),
            pltpu.VMEM((count, HEADS, space), F32),
            pltpu.VMEM((rows, width), BF16),
            pltpu.VMEM((rows, width), F32),
            pltpu.VMEM((count, HEADS, 2 * pair), F32),
            pltpu.VMEM((width, width), BF16),
            pltpu.VMEM((width, 3 * width), BF16),
            pltpu.SemaphoreType.DMA((1, many)),
            pltpu.SemaphoreType.DMA((1, many)),
        ]
        if not feed:
            scratch += [pltpu.VMEM((rows, width), BF16), pltpu.VMEM((rows, width), F32)]
        flops += 2 * rows * width * (4 * width + 5 * space)
    weights = (flat(reduce) + flat(wide) if feed else []) + (
        flat(wide) + flat(qkv) if attend else []
    )
    return call(
        body,
        "backward" + "_feed" * feed + "_attend" * attend,
        plain + operands + weights + [params, meta],
        [ANY] * (len(plain) + len(operands) + len(weights)) + [VMEM, SMEM],
        outs,
        scratch,
        flops,
        weight,
    )


def weight_gradient(
    lefts, rights, meta, parts, blocks, quarter, rows_of, columns_of, name, weight=LIGHT
):
    terms = len(lefts)
    first_row, height = rows_of
    first_column, breadth = columns_of
    rows = lefts[0].shape[0]
    operands = list(lefts)
    places = []
    for pair in rights:
        found = []
        for array, _ in pair:
            if not any(array is other for other in operands):
                operands.append(array)
            found.append(next(i for i, other in enumerate(operands) if other is array))
        places.append(found)

    def body(*refs):
        sources, info = refs[: len(operands)], refs[len(operands)]
        results = refs[len(operands) + 1 : len(operands) + 1 + len(blocks)]
        left_full, right_full, l_sem, r_sem = refs[len(operands) + 1 + len(blocks) :]
        section = info[parts]
        waits = []
        for term in range(terms):
            sides = [
                sources[place].at[:, pl.ds(column + first_column, breadth)]
                for place, (_, column) in zip(places[term], rights[term])
            ]
            same = rights[term][0] is rights[term][1]
            target = right_full.at[pl.ds(term * rows, rows)]
            waits.append(start_chosen(section, *sides, target, r_sem.at[term], same))
        loads = []
        for index, block in enumerate(blocks):
            start = pl.multiple_of(info[block] * quarter + first_row, 128)
            for term in range(terms):
                copy = pltpu.make_async_copy(
                    sources[term].at[:, pl.ds(start, height)],
                    left_full.at[index, pl.ds(term * rows, rows)],
                    l_sem.at[index, term],
                )
                copy.start()
                loads.append(copy)
        wait_all(waits)
        for index in reversed(range(len(blocks))):
            wait_all(loads[index * terms : (index + 1) * terms])
            results[index][...] = contract(left_full[index], right_full[...], 0, 0).astype(BF16)

    return call(
        body,
        name,
        operands + [meta],
        [ANY] * len(operands) + [SMEM],
        [((height, breadth), BF16)] * len(blocks),
        [
            pltpu.VMEM((len(blocks), terms * rows, height), BF16),
            pltpu.VMEM((terms * rows, breadth), BF16),
            pltpu.SemaphoreType.DMA((len(blocks), terms)),
            pltpu.SemaphoreType.DMA((terms,)),
        ],
        2 * len(blocks) * terms * rows * height * breadth,
        weight,
    )


def after(value, *earlier):
    return lax.optimization_barrier((value,) + earlier)[0]


def added(*values):
    total = values[0].astype(F32)
    for value in values[1:]:
        total = total + value.astype(F32)
    return total.astype(values[0].dtype)


class FourByFour:
    parts = 4
    blocks = (0, 2)

    def __init__(self):
        self.group = lax.axis_index("group")
        self.place = lax.axis_index("replica")
        self.order = [self.group ^ part for part in range(4)]
        odd = self.place % 2
        halves = [2 * self.order[part] + half for part in (2, 3) for half in (odd, 1 - odd)]
        self.spots = self.order[:2] + halves

    def core(self, block):
        return lax.ppermute(block, "group", [(i, i ^ 1) for i in range(4)])

    def across(self, block):
        return lax.ppermute(block, "group", [(i, i ^ 2) for i in range(4)])

    def beside(self, block):
        return lax.ppermute(block, "replica", [(i, i ^ 1) for i in range(4)])

    def gather_small(self, block):
        near, far = self.core(block), self.across(block)
        return [block, near, far, self.core(far)]

    def gather(self, blocks, prepare):
        odd = self.place % 2
        asked = [
            lax.dynamic_slice_in_dim(block, odd * (block.shape[0] // 2), block.shape[0] // 2)
            for block in blocks
        ]
        halves, sibling = [], []
        for index, block in enumerate(blocks):
            halves.append(self.across(after(asked[index], *halves[: max(index - 1, 0)])))
            sibling.append(self.core(after(block, sibling[-1]) if index else block))
        others = []
        tokens = prepare(halves[0]) + asked[2:]
        for index, half in enumerate(halves):
            earlier = others[-1:] if index == 1 else []
            others.append(self.beside(after(half, *earlier, *(tokens if index == 1 else []))))
        self.arrived, self.swapped = halves[-1], others[-1]

        def pieces(index, before_one=(), before_two=()):
            one, two = after(halves[index], *before_one), after(others[index], *before_two)
            return [
                [blocks[index]],
                [sibling[index]],
                [halves[index], others[index]],
                [self.core(one), self.core(two)],
            ]

        return [partial(pieces, index) for index in range(len(blocks))]

    def shared(self, block):
        return [block, self.core(block)]

    def total(self, blocks):
        passed = self.across(blocks[1])
        token = yield
        mine = added(after(blocks[0], token), passed)
        inward = lax.ppermute(mine, "replica", [(0, 1), (3, 2)])
        token = yield mine
        joined = added(after(mine, token), inward)
        crossing = lax.ppermute(joined, "replica", [(1, 2), (2, 1)])
        token = yield joined
        summed = added(after(joined, token), crossing)
        outward = lax.ppermute(summed, "replica", [(1, 0), (2, 3)])
        token = yield summed
        inner = (self.place == 1) | (self.place == 2)
        yield jnp.where(inner, after(summed, token), outward)


class General:
    def __init__(self):
        self.parts = lax.axis_size("group")
        self.blocks = tuple(range(self.parts))
        self.order = self.spots = [jnp.int32(part) for part in range(self.parts)]

    def gather_small(self, block):
        whole = lax.all_gather(block, "group", axis=0)
        return [whole[part] for part in range(self.parts)]

    def gather(self, blocks, prepare):
        prepare(blocks[0])
        self.arrived = self.swapped = blocks[0]
        found = [[[piece] for piece in self.gather_small(block)] for block in blocks]
        return [lambda *tokens, groups=groups: groups for groups in found]

    def shared(self, block):
        return [block]

    def total(self, blocks):
        yield
        mine = lax.psum_scatter(jnp.stack(blocks), "group", scatter_dimension=0)
        yield mine
        yield lax.psum(mine, "replica")


def shifted(block, distance):
    devices = range(lax.axis_size("section"))
    route = [(i - distance, i) for i in devices if i - distance in devices]
    return lax.ppermute(block, "section", route)


def in_order(pieces, order):
    place = jnp.stack(order)
    stacked = []
    for block in range(len(pieces)):
        chosen = pieces[0]
        for part in range(1, len(pieces)):
            chosen = jnp.where(place[part] == block, pieces[part], chosen)
        stacked.append(chosen)
    return jnp.stack(stacked)


class Sequence:
    def __init__(self, net, token):
        self.net, self.sums, self.results, self.token = net, {}, {}, token

    def now(self, value):
        return after(value, self.token)

    def ran(self, value):
        self.token = value

    def add(self, name, blocks):
        self.sums[name] = self.net.total(blocks)
        next(self.sums[name])

    def step(self, *names):
        for name in names:
            try:
                self.results[name] = self.token = self.sums[name].send(self.token)
            except StopIteration:
                continue

    def finish(self, name):
        while True:
            try:
                self.results[name] = self.sums[name].send(self.token)
            except StopIteration:
                return self.results[name]


def per_device(
    images,
    cotangent,
    counts,
    qkv_weight,
    out_weight,
    expand_weight,
    reduce_weight,
    norm_gains,
    biases,
    expand_bias,
):
    micro, slots, length, width = images.shape
    space = padded(length)
    section = lax.axis_index("section")
    first = section == 0
    sizes = (lax.axis_size("group"), lax.axis_size("replica"))
    net = FourByFour() if sizes == (4, 4) else General()
    parts = net.parts
    share = width // parts
    batches = tuple(range(micro))

    def rows_of(array):
        fulls = [jnp.pad(array[batch], ((0, 0), (0, space - length), (0, 0))) for batch in batches]
        return [full.reshape(slots * space, width) for full in fulls]

    def images_of(array):
        return array.reshape(slots, space, width)[:, :length]

    small = jnp.concatenate([norm_gains[0], biases[0], expand_bias[0].reshape(-1, share)])
    slot = jnp.arange(slots, dtype=jnp.int32)
    alive = [(slot < counts[batch, 0]).astype(jnp.int32) for batch in batches]
    head = jnp.stack(net.order + [section]).astype(jnp.int32)

    spots = jnp.stack(net.spots).astype(jnp.int32)

    def meta(living):
        return jnp.concatenate([head, living, spots])

    infos = [meta(alive[batch]) for batch in batches]
    pieces = net.gather_small(small)
    vectors = in_order(pieces, net.order)
    top = vectors[:, :8].transpose(1, 0, 2).reshape(8, width)
    bottom = vectors[:, 8:].reshape(-1, width)
    params = jnp.concatenate([top, bottom]).astype(F32)
    slot = jnp.arange(slots, dtype=jnp.int32)
    alive = [(slot < counts[batch, 0]).astype(jnp.int32) for batch in batches]
    head = jnp.stack(net.order + [section]).astype(jnp.int32)
    spots = jnp.stack(net.spots).astype(jnp.int32)

    def meta(living):
        return jnp.concatenate([head, living, spots])

    infos = [meta(alive[batch]) for batch in batches]
    inputs, targets = [], []

    def prepare(token):
        inputs.extend(rows_of(after(images, token)))
        targets.extend(rows_of(after(cotangent, token)))
        return [params, *inputs, *targets, *infos]

    qkv, wide, reduce = net.gather(
        [qkv_weight[0], jnp.concatenate([out_weight[0], expand_weight[0]], axis=1), reduce_weight[0]],
        prepare,
    )

    qkv = qkv()
    attended = []
    for batch in batches:
        start = inputs[batch] if batch == 0 else after(inputs[batch], attended[-1][0], net.arrived)
        attended.append(
            forward(start, start, None, qkv, None, params, infos[batch], slots, length)
        )
    wide = wide(attended[0], attended[-1])
    fed = []
    for batch in batches:
        start = inputs[batch] if batch == 0 else after(inputs[batch], fed[-1][0], net.swapped)
        fed.append(
            forward(start, start, attended[batch][0], None, wide, params, infos[batch], slots, length)
        )
    reduce = reduce(attended[-1], fed[0][:1])
    early, incoming = [], []
    for batch in batches:
        middle, active = fed[batch]
        if batch:
            active = after(active, early[-1])
        early.append(output_forward(middle, active, reduce, params, infos[batch], slots))
        incoming.append(shifted(early[batch], 1))

    inner = wide[0][0].shape[1] - width
    mixed_at = inner + width
    kept, lefts, rights, results = [], [], [], []
    sums_a, sums_b, sums_c, returning = [], [], [], []
    token = early[-1]
    for batch in batches:
        start = after(incoming[batch], token)
        left, packed, logs, middle, slope = forward(
            inputs[batch], start, None, qkv, wide, params, infos[batch], slots, length, 8.0
        )
        kept.append((slope, middle, packed, left, logs))
        lefts.append(net.shared(left))
        if batch == 0:
            pair, sides = (targets[0], targets[0]), (kept[0], kept[0])
            lower, chosen = incoming[0], infos[0]
        else:
            pair = (returning[batch - 1], targets[batch])
            sides = (kept[batch - 1], kept[batch])
            lower = inputs[batch - 1]
            chosen = meta(jnp.where(first, alive[batch - 1], alive[batch]))
        right, some, more, result, rest = backward(
            pair, lower, incoming[batch], sides[0], sides[1], reduce, wide, qkv, params, chosen,
            slots, length, mixed_at, 8.0,
        )
        token = result
        rights.append(net.shared(right))
        results.append(result)
        sums_a.append(some)
        sums_b.append(more)
        sums_c.append(rest)
        returning.append(shifted(result, -1))
    late = []
    for batch in batches:
        ready = lefts[batch][1:] + (rights[batch][1:] if batch < micro - 1 else [])
        active = after(kept[batch][3], token, *ready)
        late.append(output_forward(kept[batch][1], active, reduce, params, infos[batch], slots, 8.0))
        token = late[-1]

    last = micro - 1
    run = Sequence(net, token)
    arrived = run.now(returning[last])
    living = jnp.repeat(alive[last] > 0, space)[:, None]
    masked = net.shared(jnp.where(living, arrived, jnp.zeros_like(arrived)))
    many = len(masked)

    def gradient(name, left_at, final, final_at, right_at, quarter, rows, columns, weight=LIGHT):
        left = [lefts[batch][side] for batch in batches for side in range(many)]
        right = []
        for batch in batches:
            for side in range(many):
                upper = (rights[batch][side], right_at)
                lower = (final[side], final_at) if batch == last else (rights[batch + 1][side], right_at)
                right.append((lower, upper))
        blocks = weight_gradient(
            left, right, run.now(head), parts, net.blocks, quarter, (left_at + rows[0], rows[1]), columns,
            name, weight,
        )
        run.ran(blocks[0])
        return blocks

    half, at = inner // 2, inner + 2 * width
    deep = inner // parts
    state = {"mid": None, "rows": None}

    def feed_back(weight):
        start = run.now(arrived)
        hidden, branch, some, more, mid = backward(
            (start, start), None, None, kept[last], kept[last], reduce, wide, None, params, infos[last],
            slots, length, mixed_at, weight,
        )
        run.ran(hidden)
        state.update(mid=mid, branch=branch, hidden=net.shared(hidden), branches=net.shared(branch))
        sums_a.append(some)
        sums_b.append(more)

    def attend_back(weight):
        start = run.now(after(state["branch"], *state["branches"][1:], *state["hidden"][1:]))
        grads, result, rest = backward(
            (start, state["mid"]), inputs[last], inputs[last], kept[last], kept[last], None, wide, qkv,
            params, infos[last], slots, length, mixed_at, weight,
        )
        run.ran(result)
        state["grads"] = net.shared(grads)
        results.append(result)
        sums_c.append(rest)

    def reduce_part(index, weight):
        step = deep // 2
        return gradient(
            "reduce", 0, masked, 0, inner + width, deep, (index * step, step), (0, width), weight
        )

    def expand_part(begin, size, weight):
        return gradient("expand", inner, state["hidden"], 0, 0, share, (0, share), (begin, size), weight)

    def project_part(weight):
        return gradient(
            "project", mixed_at, state["branches"], 0, inner, share, (0, share), (0, width), weight
        )

    def qkv_part(begin, size, weight):
        return gradient("qkv", at, state["grads"], 0, at, share, (0, share), (begin, size), weight)

    def over_batches(values):
        return sum(jnp.where(first, values[batch + 1], values[batch]) for batch in batches)

    def small_sums():
        some, more, rest = over_batches(sums_a), over_batches(sums_b), over_batches(sums_c)
        rows = jnp.concatenate([rest[0:1], some[0:1], rest[1:2], some[1:2], rest[2:4], some[2:4]])
        rows = rows.reshape(8, parts, share).transpose(1, 0, 2)
        rows = jnp.concatenate([rows, more.reshape(parts, -1, share)], axis=1)
        rows = sum(net.shared(run.now(rows)))
        rows = jnp.stack(
            [lax.dynamic_index_in_dim(rows, net.order[block], 0, keepdims=False) for block in net.blocks]
        )
        state["count"] = rows.shape[1]
        state["rows"] = rows.reshape(len(net.blocks), -1).astype(BF16)

    def with_small(blocks):
        step, rows = blocks[0].shape[1], state["rows"]
        rows = jnp.pad(rows, ((0, 0), (0, -rows.shape[1] % (16 * step)))).reshape(len(blocks), -1, step)
        return [jnp.concatenate([block, row]) for block, row in zip(blocks, rows)]

    outputs = []

    def assemble():
        index = len(outputs)
        low, up = (early + results[1:])[index], (late + results[:-1])[index]
        outputs.append(images_of(jnp.where(first, run.now(low), up)))

    def joined(axis, *names):
        found = [run.finish(name) for name in names]
        found = [value[:share] if name == LAST.lower() else value for name, value in zip(names, found)]
        return jnp.concatenate(found, axis=axis).astype(F32)[None]

    shapes = {"q": (1, "q0", "q1"), "p": (1, "p0"), "e": (1, "e0", "e1"), "r": (0, "r0", "r1")}
    gradients = {}

    third = 3 * width // 2
    kernels = {
        "R0": lambda weight: reduce_part(0, weight),
        "R1": lambda weight: reduce_part(1, weight),
        "E0": lambda weight: expand_part(0, half, weight),
        "E1": lambda weight: expand_part(half, half, weight),
        "Q0": lambda weight: qkv_part(0, third, weight),
        "Q1": lambda weight: qkv_part(third, third, weight),
        "P0": lambda weight: project_part(weight),
    }
    for entry in " ".join(PLAN).split():
        name, _, factor = entry.partition("*")
        weight = float(factor or HEAVY) if "*" in entry else LIGHT
        if name in kernels:
            blocks = kernels[name](weight)
            if name == LAST:
                blocks = with_small(blocks)
            run.add(name.lower(), blocks)
        elif name == "BF":
            feed_back(weight)
        elif name == "BA":
            attend_back(weight)
        elif name == "V":
            small_sums()
        elif name == "O":
            assemble()
        elif name[0] == "C":
            gradients[name[1]] = joined(*shapes[name[1]])
        else:
            run.step(name)
    while len(outputs) < 2 * micro:
        assemble()
    for name in shapes:
        if name not in gradients:
            gradients[name] = joined(*shapes[name])
    count = state["count"]
    vector = run.finish(LAST.lower())[share:].reshape(-1)[: count * share].reshape(count, share).astype(F32)
    return (
        jnp.stack(outputs[:micro])[None],
        jnp.stack(outputs[micro:])[None],
        gradients["q"],
        gradients["p"],
        gradients["e"],
        gradients["r"],
        vector[None, 0:2],
        vector[None, 2:8],
        vector[8:].reshape(1, -1),
    )


def solution(mesh):
    placed = (
        P(None, ("group", "replica"), None, None),
        P(None, ("group", "replica"), None, None),
        P(None, ("group", "replica")),
        P("section", "group", None),
        P("section", "group", None),
        P("section", "group", None),
        P("section", "group", None),
        P("section", None, "group"),
        P("section", None, "group"),
        P("section", "group"),
    )
    return jax.shard_map(
        per_device,
        mesh=mesh,
        in_specs=placed,
        out_specs=(
            P("section", None, ("group", "replica"), None, None),
            P("section", None, ("group", "replica"), None, None),
            P("section", "group", None),
            P("section", "group", None),
            P("section", "group", None),
            P("section", "group", None),
            P("section", None, "group"),
            P("section", None, "group"),
            P("section", "group"),
        ),
        check_vma=False,
    )
```

```python
from functools import partial

import jax
import jax.numpy as jnp
from jax import lax
from jax.experimental import pallas as pl
from jax.experimental.pallas import tpu as pltpu
from jax.sharding import PartitionSpec as P

HEADS = 16
EPSILON = 1e-06
NEGATIVE = -1e30
F32 = jnp.float32
BF16 = jnp.bfloat16
LIGHT, HEAVY = 1.0 / 64, 16.0
PLAN = (
    "R0 BF r0 R1*",
    "BA r0 r1 E0*",
    "r1 Q0 r0 e0",
    "E1 q0 r1 e0",
    "r0 Q1 e1 q0",
    "r1 e0 V P0",
    "e1 q1 O q0",
    "e0 p0 q1 O",
    "e1 q0 p0 O",
    "O q1 e1 p0",
    "q1 p0",
)
LAST = "P0"
VMEM_LIMIT = 58 * 2**20
ROOT_HALF = 0.7071067811865476
ROOT_TAU = 0.3989422804014327
ANY = pl.BlockSpec(memory_space=pl.ANY)
VMEM = pl.BlockSpec(memory_space=pltpu.VMEM)
SMEM = pl.BlockSpec(memory_space=pltpu.SMEM)
GAIN0, GAIN1, SHIFT0, SHIFT1, QUERY, VALUE, OUT, FEED, EXPAND = range(9)


def padded(length):
    return -(-length // 16) * 16


def contract(left, right, left_dim, right_dim):
    return lax.dot_general(
        left, right, (((left_dim,), (right_dim,)), ((), ())), preferred_element_type=F32
    )


def standardized(values):
    center = values - jnp.mean(values, axis=-1, keepdims=True)
    spread = jnp.mean(center * center, axis=-1, keepdims=True)
    scale = lax.rsqrt(spread + EPSILON)
    return center * scale, scale


def norm_pull(grad, gain, unit, scale):
    scaled = grad * gain
    mean = jnp.mean(scaled, axis=-1, keepdims=True)
    along = jnp.mean(scaled * unit, axis=-1, keepdims=True)
    return scale * (scaled - mean - unit * along)


def call(body, name, operands, specs, outs, scratch, flops, weight=LIGHT):
    moved = sum(o.size * o.dtype.itemsize for o in operands)
    out_shape = [jax.ShapeDtypeStruct(shape, dtype) for shape, dtype in outs]
    moved += sum(o.size * o.dtype.itemsize for o in out_shape)
    return pl.pallas_call(
        body,
        out_shape=out_shape,
        in_specs=specs,
        out_specs=[VMEM] * len(outs),
        scratch_shapes=scratch,
        compiler_params=pltpu.CompilerParams(vmem_limit_bytes=VMEM_LIMIT),
        cost_estimate=pl.CostEstimate(flops=int(flops * weight), bytes_accessed=int(moved * weight), transcendentals=0),
        name=name,
    )(*operands)


def flat(groups):
    return [piece for group in groups for piece in group]


def start_pieces(pieces, info, first, target, sems, slot, columns, block, shift=0):
    begin, size = columns
    columns = pl.ds(begin, size)
    copies = []
    for index, piece in enumerate(pieces):
        rows = piece.shape[0]
        where = pl.multiple_of(info[first + index] * (block // 4), block // 4)
        copy = pltpu.make_async_copy(
            piece.at[:, pl.ds(begin + shift, size)],
            target.at[pl.ds(where, rows), columns],
            sems.at[slot, index],
        )
        copy.start()
        copies.append(copy)
    return copies


def wait_all(copies):
    for copy in copies:
        copy.wait()


def start_chosen(section, lower, upper, target, sem, same=False):
    if lower is upper or same:
        copy = pltpu.make_async_copy(lower, target, sem)
        copy.start()
        return copy

    @pl.when(section == 0)
    def _():
        pltpu.make_async_copy(lower, target, sem).start()

    @pl.when(section != 0)
    def _():
        pltpu.make_async_copy(upper, target, sem).start()

    return pltpu.make_async_copy(lower, target, sem)


def eights(values):
    return jnp.sum(values.reshape(-1, 8, values.shape[-1]), axis=0)


def attention_stage(x, vec, norm, packed, mixed, logs, columns, full, loads, count, length):
    rows, width = x.shape
    space = rows // count
    head = width // HEADS
    pair = 2 * head
    scale = head**-0.5
    gain, shift = vec[GAIN0 : GAIN0 + 1], vec[SHIFT0 : SHIFT0 + 1]

    def step(here):
        unit, _ = standardized(x[here].astype(F32))
        norm[here] = (unit * gain + shift).astype(BF16)

    step(pl.ds(0, rows))
    for block in range(3):
        wait_all(loads[block])
        done = contract(norm[...], full[:, block * width : (block + 1) * width], 1, 0)
        if block != 1:
            bias = QUERY if block == 0 else VALUE
            done = done + vec[bias : bias + 1]
        packed[:, block * width : (block + 1) * width] = done.astype(BF16)
    lane = lax.broadcasted_iota(jnp.int32, (space, pair), 1)
    left = lane < head
    live = lax.broadcasted_iota(jnp.int32, (space, pair), 0) < length
    key_live = lax.broadcasted_iota(jnp.int32, (space, space), 1) < length
    columns[...] = jnp.zeros_like(columns)

    def heads(index, carry):
        for image in range(count):
            span = pl.ds(image * space, space)

            def part(block):
                offset = pl.multiple_of(block * width + index * pair, pair)
                return packed[span, pl.ds(offset, pair)]

            query, key, value = part(0).astype(F32) * scale, part(1), part(2).astype(F32)
            found = []
            tops = []
            for side in range(2):
                mine = left if side == 0 else ~left
                asked = jnp.where(mine, query, 0.0).astype(BF16)
                held = jnp.where(live, jnp.where(mine, value, 1.0), 0.0).astype(BF16)
                scores = jnp.where(key_live, contract(asked, key, 1, 1), NEGATIVE)
                top = jnp.max(scores, axis=-1, keepdims=True)
                raised = jnp.exp(scores - top).astype(BF16)
                found.append(contract(raised, held, 1, 0))
                tops.append(top)
            inside = jnp.where(left, found[0], found[1])
            total = jnp.where(left, found[1], found[0])
            turned = pltpu.roll(total, head, 1)
            offset = pl.multiple_of(index * pair, pair)
            mixed[span, pl.ds(offset, pair)] = (inside / turned).astype(BF16)
            if logs is None:
                continue
            logged = jnp.log(turned)
            first = tops[0] + logged[:, 0:1]
            second = tops[1] + logged[:, head : head + 1]
            known = columns[image]
            known = jnp.where(lane == 2 * index, first, known)
            columns[image] = jnp.where(lane == 2 * index + 1, second, known)
        return carry

    lax.fori_loop(0, HEADS // 2, heads, 0)
    if logs is not None:
        for image in range(count):
            logs[image] = columns[image].T[0:HEADS]


def hidden_stage(x, vec, mixed, middle, active, second, slope, full_out, full, first_load, loads):
    rows, width = x.shape
    wait_all(first_load)
    gain, shift, bias = vec[GAIN1 : GAIN1 + 1], vec[SHIFT1 : SHIFT1 + 1], vec[OUT : OUT + 1]
    middle[...] = contract(mixed[...], full_out[...], 1, 0)

    def step(here):
        total = middle[here] + x[here].astype(F32) + bias
        middle[here] = total
        unit, _ = standardized(total)
        second[here] = (unit * gain + shift).astype(BF16)

    step(pl.ds(0, rows))
    for block, load in enumerate(loads):
        wait_all(load)
        part = slice(block * width, (block + 1) * width)
        value = contract(second[...], full[:, part], 1, 0) + vec[EXPAND + block : EXPAND + block + 1]
        share = 0.5 + 0.5 * lax.erf(value * ROOT_HALF)
        active[:, part] = (value * share).astype(BF16)
        if slope is not None:
            density = ROOT_TAU * jnp.exp(-0.5 * value * value)
            slope[:, part] = (share + value * density).astype(BF16)


def forward(
    lower, upper, mixed_in, qkv, wide, params, meta, count, length, weight=LIGHT
):
    rows, width = lower.shape
    space = rows // count
    pair = 2 * width // HEADS
    attend, feed = qkv is not None, wide is not None
    both = attend and feed
    parts = len(qkv if attend else wide)
    many = len(flat(qkv if attend else wide))
    spots = parts + 1 + count
    inner = wide[0][0].shape[1] - width if feed else 0
    share = width // parts
    blocks = inner // width
    same = lower is upper

    def body(*refs):
        refs = list(refs)
        low = refs.pop(0)
        up = low if same else refs.pop(0)
        if not attend:
            arrived = refs.pop(0)
        lists = [[refs.pop(0) for _ in range(many)] for _ in range(attend + 2 * feed)]
        vec, info = refs.pop(0), refs.pop(0)
        if both:
            left, packed, logs, middle, slope = (refs.pop(0) for _ in range(5))
            active, second, mixed, norm = (
                left.at[:, pl.ds(start, size)]
                for start, size in ((0, inner), *((inner + width * i, width) for i in range(3)))
            )
        elif attend:
            mixed = refs.pop(0)
        else:
            middle, active = refs.pop(0), refs.pop(0)
        x, x_sem = refs.pop(0), refs.pop(0)
        section = info[parts]
        take = start_chosen(section, low, up, x, x_sem.at[0])
        if attend:
            columns, full, a_sem = (refs.pop(0) for _ in range(3))
            if not both:
                norm, packed, logs = refs.pop(0), refs.pop(0), None
            weight = lists.pop(0)
            loads = [
                start_pieces(weight, info, spots, full, a_sem, block, (block * width, width), share)
                for block in range(3)
            ]
        if feed:
            full_out, full_in, o_sem, w_sem = (refs.pop(0) for _ in range(4))
            if not attend:
                mixed, second, slope = refs.pop(0), refs.pop(0), None
                extra = pltpu.make_async_copy(arrived, mixed, x_sem.at[1])
                extra.start()
            first_load = start_pieces(lists[0], info, spots, full_out, o_sem, 0, (0, width), share)
            inner_loads = [
                start_pieces(lists[1], info, spots, full_in, w_sem, block, (block * width, width), share, width)
                for block in range(blocks)
            ]
        take.wait()
        if attend:
            attention_stage(
                x, vec, norm, packed, mixed, logs, columns, full, loads, count, length
            )
        if feed:
            if not attend:
                extra.wait()
            hidden_stage(
                x, vec, mixed, middle, active, second, slope, full_out, full_in, first_load,
                inner_loads,
            )

    outs, inputs = [], [lower] if same else [lower, upper]
    scratch = [pltpu.VMEM((rows, width), BF16), pltpu.SemaphoreType.DMA((2,))]
    flops = 0
    if attend:
        outs += [
            ((rows, width), BF16),
            ((rows, 3 * width), BF16),
            ((rows, width), BF16),
            ((count, HEADS, space), F32),
        ]
        scratch += [
            pltpu.VMEM((count, space, pair), F32),
            pltpu.VMEM((width, 3 * width), BF16),
            pltpu.SemaphoreType.DMA((3, many)),
        ]
        if not feed:
            scratch += [pltpu.VMEM((rows, width), BF16), pltpu.VMEM((rows, 3 * width), BF16)]
        flops += 2 * rows * width * (3 * width + 2 * space)
    else:
        inputs += [mixed_in]
    if feed:
        outs += [
            ((rows, width), F32),
            ((rows, inner), BF16),
            ((rows, width), BF16),
            ((rows, inner), BF16),
        ]
        scratch += [
            pltpu.VMEM((width, width), BF16),
            pltpu.VMEM((width, inner), BF16),
            pltpu.SemaphoreType.DMA((1, many)),
            pltpu.SemaphoreType.DMA((blocks, many)),
        ]
        if not attend:
            scratch += [pltpu.VMEM((rows, width), BF16), pltpu.VMEM((rows, width), BF16)]
        flops += 2 * rows * width * (width + inner)
    if both:
        outs = [((rows, inner + 3 * width), BF16), outs[1], outs[3], outs[4], outs[7]]
    else:
        outs = [outs[2]] if attend else outs[:2]
    weights = (flat(qkv) if attend else []) + (2 * flat(wide) if feed else [])
    return call(
        body,
        "forward" + "_attend" * attend + "_feed" * feed,
        inputs + weights + [params, meta],
        [ANY] * (len(inputs) + len(weights)) + [VMEM, SMEM],
        outs,
        scratch,
        flops,
        weight,
    )


def output_forward(middle, active, pieces, params, meta, count, weight=LIGHT):
    rows, width = middle.shape
    inner = sum(piece.shape[0] for piece in flat(pieces))
    space = rows // count
    parts, many = len(pieces), len(flat(pieces))
    spots = parts + 1 + count
    deep = inner // parts

    def body(*refs):
        refs = list(refs)
        mid_in, act_in = refs.pop(0), refs.pop(0)
        reduce = [refs.pop(0) for _ in range(many)]
        vec, info, result, mid, act, full, total, x_sem, w_sem = refs
        every = start_pieces(reduce[:1], info, spots + many, full, w_sem, 0, (0, width), deep)
        columns = [pl.ds(pl.multiple_of(info[index] * deep, deep), deep) for index in range(parts)]
        takes = []
        for index in range(parts):
            takes.append(
                pltpu.make_async_copy(act_in.at[:, columns[index]], act.at[index], x_sem.at[index])
            )
            takes[-1].start()
            if index == 0:
                every += start_pieces(
                    reduce[1:], info, spots + many + 1, full, w_sem.at[:, pl.ds(1, many - 1)], 0,
                    (0, width), deep,
                )
        last = pltpu.make_async_copy(mid_in, mid, x_sem.at[parts])
        last.start()
        for index, group in enumerate(pieces):
            takes[index].wait()
            wait_all([every.pop(0) for _ in group])
            value = contract(act[index], full[columns[index]], 1, 0)
            if index:
                value = value + total[...]
            if index < parts - 1:
                total[...] = value
        last.wait()
        value = value + mid[...] + vec[FEED : FEED + 1]
        for image in range(count):
            alive = jnp.where(info[parts + 1 + image] > 0, 1.0, 0.0)
            here = slice(image * space, (image + 1) * space)
            result[here] = (value[here] * alive).astype(BF16)

    return call(
        body,
        "output_forward",
        [middle, active] + flat(pieces) + [params, meta],
        [ANY] * (2 + many) + [VMEM, SMEM],
        [((rows, width), BF16)],
        [
            pltpu.VMEM((rows, width), F32),
            pltpu.VMEM((parts, rows, deep), BF16),
            pltpu.VMEM((inner, width), BF16),
            pltpu.VMEM((rows, width), F32),
            pltpu.SemaphoreType.DMA((parts + 1,)),
            pltpu.SemaphoreType.DMA((1, many)),
        ],
        2 * rows * width * inner,
        weight,
    )[0]


def hidden_back_stage(
    grad, vec, info, feed, slope, middle, hidden, second, mid_grad, branch, sums, inner_sums, full_out,
    full, deep, first_load, load, for_slope, for_middle, tallies, count, parts,
):
    rows, width = grad.shape
    space = rows // count
    half = width // 2
    for image in range(count):
        alive = jnp.where(info[parts + 1 + image] > 0, 1.0, 0.0)
        here = slice(image * space, (image + 1) * space)
        feed[here] = (grad[here].astype(F32) * alive).astype(BF16)
    for_slope.wait()
    for index in range(parts):
        wait_all(first_load[index])
        where = pl.multiple_of(info[index] * deep, deep)
        value = contract(feed[...], full_out[pl.ds(where, deep)], 1, 1)
        value = (value * slope[:, pl.ds(where, deep)].astype(F32)).astype(BF16)
        hidden[:, pl.ds(where, deep)] = value
        inner_sums[:, pl.ds(where, deep)] = jnp.sum(value.astype(F32), axis=0, keepdims=True)
    wait_all(load)
    for block in range(2):
        second[:, block * half : (block + 1) * half] = contract(
            hidden[...], full[block * half : (block + 1) * half], 1, 1
        )
    for_middle.wait()
    gain = vec[GAIN1 : GAIN1 + 1]
    tallies[...] = jnp.zeros_like(tallies)

    def step(here):
        unit, scale = standardized(middle[here])
        down = second[here]
        top = feed[here].astype(F32)
        total = top + norm_pull(down, gain, unit, scale)
        low = total.astype(BF16)
        mid_grad[here] = total
        branch[here] = low
        tallies[0] += eights(down * unit)
        tallies[1] += eights(down)
        tallies[2] += eights(low.astype(F32))
        tallies[3] += eights(top)

    step(pl.ds(0, rows))
    for index in range(4):
        sums[index : index + 1] = jnp.sum(tallies[index], axis=0, keepdims=True)


def attention_back_stage(
    x, vec, branch, mid_grad, packed, mixed, logs, grads, result, sums, down, normal, stage, full_out,
    full, first_load, load, takes, tallies, count, length,
):
    rows, width = x.shape
    space = rows // count
    head = width // HEADS
    pair = 2 * head
    scale = head**-0.5
    half = width // 2
    wait_all(first_load)
    down[...] = contract(branch[...], full_out[...], 1, 1).astype(BF16)
    wait_all(takes)
    owner = lax.shift_right_logical(
        lax.broadcasted_iota(jnp.int32, (HEADS, width), 1), head.bit_length() - 1
    )
    chosen = jnp.where(
        owner == lax.broadcasted_iota(jnp.int32, (HEADS, width), 0), 1.0, 0.0
    ).astype(BF16)
    left = lax.broadcasted_iota(jnp.int32, (space, pair), 1) < head
    live = lax.broadcasted_iota(jnp.int32, (space, pair), 0) < length
    key_live = lax.broadcasted_iota(jnp.int32, (space, space), 0) < length
    for image in range(count):
        span = pl.ds(image * space, space)
        product = down[span].astype(F32) * mixed[span].astype(F32)
        coarse = product.astype(BF16)
        fine = (product - coarse.astype(F32)).astype(BF16)
        stage[image, :, 0:space] = contract(chosen, coarse, 1, 1) + contract(chosen, fine, 1, 1)

    def heads(index, carry):
        for image in range(count):
            span = pl.ds(image * space, space)

            def part(block):
                offset = pl.multiple_of(block * width + index * pair, pair)
                return packed[span, pl.ds(offset, pair)]

            query, key, value = part(0), part(1), part(2)
            wide = key.astype(F32) * scale
            value = value.astype(F32)
            arrived = down[span, pl.ds(pl.multiple_of(index * pair, pair), pair)]
            found = []
            for side in range(2):
                mine = left if side == 0 else ~left
                log = logs[image, pl.ds(2 * index + side, 1), :]
                dot = stage[image, pl.ds(2 * index + side, 1), 0:space]
                scores = contract(jnp.where(mine, wide, 0.0).astype(BF16), query, 1, 1)
                chance = jnp.exp(jnp.where(key_live, scores - log, NEGATIVE))
                back = contract(jnp.where(mine, value, 0.0).astype(BF16), arrived, 1, 1)
                change = (chance * (back - dot)).astype(BF16)
                found.append(
                    (
                        contract(change, key, 0, 0),
                        contract(change, query, 1, 0),
                        contract(chance.astype(BF16), arrived, 1, 0),
                    )
                )
            for block, factor in enumerate((scale, scale, 1.0)):
                total = jnp.where(left, found[0][block], found[1][block]) * factor
                offset = pl.multiple_of(block * width + index * pair, pair)
                grads[span, pl.ds(offset, pair)] = jnp.where(live, total, 0.0).astype(BF16)
        return carry

    lax.fori_loop(0, HEADS // 2, heads, 0)
    wait_all(load)
    for block in range(2):
        normal[:, block * half : (block + 1) * half] = contract(
            grads[...], full[block * half : (block + 1) * half], 1, 1
        )
    gain = vec[GAIN0 : GAIN0 + 1]
    tallies[...] = jnp.zeros_like(tallies)

    def step(here):
        unit, rate = standardized(x[here].astype(F32))
        grad = normal[here]
        tallies[0] += eights(grad * unit)
        tallies[1] += eights(grad)
        result[here] = (mid_grad[here] + norm_pull(grad, gain, unit, rate)).astype(BF16)

    step(pl.ds(0, rows))
    for index in range(2):
        sums[index : index + 1] = jnp.sum(tallies[index], axis=0, keepdims=True)
    sums[2:3] = jnp.sum(grads[:, 0:width].astype(F32), axis=0, keepdims=True)
    sums[3:4] = jnp.sum(grads[:, 2 * width : 3 * width].astype(F32), axis=0, keepdims=True)


def backward(
    start, lower, upper, kept_low, kept_up, reduce, wide, qkv, params, meta, count, length,
    mixed_at, weight=LIGHT,
):
    feed, attend = reduce is not None, qkv is not None
    rows, width = start[0].shape
    space = rows // count
    pair = 2 * width // HEADS
    parts = len(reduce if feed else qkv)
    many = len(flat(reduce if feed else qkv))
    spots = parts + 1 + count
    inner = wide[0][0].shape[1] - width if feed else 0
    deep, share = inner // parts, width // parts
    both = feed and attend
    choices = []
    if feed:
        choices += [(kept_low[0], kept_up[0]), (kept_low[1], kept_up[1])]
        if start[0] is not start[1]:
            choices += [start]
    if attend:
        choices += [(kept_low[index], kept_up[index]) for index in (2, 3, 4)]
        choices += [(lower, upper)]
    plain = [start[0]] if feed and start[0] is start[1] else [] if feed else list(start)
    operands = []
    for low, up in choices:
        operands += [low] if low is up else [low, up]

    def body(*refs):
        refs = list(refs)
        firsts = [refs.pop(0) for _ in plain]
        pairs = []
        for low, up in choices:
            one = refs.pop(0)
            pairs.append((one, one if low is up else refs.pop(0)))
        lists = [[refs.pop(0) for _ in range(many)] for _ in range(2 * feed + 2 * attend)]
        vec, info = refs.pop(0), refs.pop(0)
        section = info[parts]
        if feed:
            if both:
                right = refs.pop(0)
                hidden, branch = right.at[:, pl.ds(0, inner)], right.at[:, pl.ds(inner, width)]
            else:
                hidden, branch = refs.pop(0), refs.pop(0)
            feed_sums, inner_sums = refs.pop(0), refs.pop(0)
            mid_grad = None if both else refs.pop(0)
        if attend:
            grads, result, sums = (refs.pop(0) for _ in range(3)) if not both else (None, refs.pop(0), refs.pop(0))
        if both:
            feed_grad = right.at[:, pl.ds(inner + width, width)]
            grads = right.at[:, pl.ds(inner + 2 * width, 3 * width)]
        tallies, x_sem = refs.pop(0), refs.pop(0)
        if feed:
            grad, slope, middle, second, full_out, full, o_sem, w_sem = (
                refs.pop(0) for _ in range(8)
            )
            if both:
                mid_grad, keep = refs.pop(0), feed_grad
            else:
                keep = refs.pop(0)
            begin = pairs.pop(2) if start[0] is not start[1] else (firsts[0], firsts[0])
            take = start_chosen(section, *begin, grad, x_sem.at[0])
            for_slope = start_chosen(section, *pairs.pop(0), slope, x_sem.at[1])
            every = start_pieces(lists.pop(0), info, spots + many, full_out, o_sem, 0, (0, width), deep)
            first_load = [[every.pop(0) for _ in group] for group in reduce]
            for_middle = start_chosen(section, *pairs.pop(0), middle, x_sem.at[2])
            load = start_pieces(lists.pop(0), info, spots, full, w_sem, 0, (0, inner), share, width)
        if attend:
            x, packed, mixed, logs, down, normal, stage, full_o, full_q, p_sem, q_sem = (
                refs.pop(0) for _ in range(11)
            )
            if not feed:
                branch, mid_grad = refs.pop(0), refs.pop(0)
                givens = [
                    pltpu.make_async_copy(source, target, x_sem.at[index])
                    for index, (source, target) in enumerate(zip(firsts, (branch, mid_grad)))
                ]
                for given in givens:
                    given.start()
            project_load = start_pieces(lists.pop(0), info, spots, full_o, p_sem, 0, (0, width), share)
            sames = [one is two for one, two in pairs]
            pairs[1] = tuple(one.at[:, pl.ds(mixed_at, width)] for one in pairs[1])
            takes = [
                start_chosen(section, *pairs[index], target, x_sem.at[3 + index], sames[index])
                for index, target in ((1, mixed), (0, packed), (2, logs), (3, x))
            ]
            last_load = start_pieces(lists.pop(0), info, spots, full_q, q_sem, 0, (0, 3 * width), share)
            if not feed:
                wait_all(givens)
        if feed:
            take.wait()
            hidden_back_stage(
                grad, vec, info, keep, slope, middle, hidden, second, mid_grad, branch, feed_sums,
                inner_sums, full_out, full, deep, first_load, load, for_slope, for_middle, tallies,
                count, parts,
            )
        if attend:
            attention_back_stage(
                x, vec, branch, mid_grad, packed, mixed, logs, grads, result, sums, down, normal,
                stage, full_o, full_q, project_load, last_load, takes, tallies, count, length,
            )

    outs = []
    scratch = [pltpu.VMEM((4, 8, width), F32), pltpu.SemaphoreType.DMA((7,))]
    flops = 0
    if feed:
        outs += [((rows, inner + 5 * width), BF16)] if both else [((rows, inner), BF16), ((rows, width), BF16)]
        outs += [
            ((8, width), F32),
            ((1, inner), F32),
        ]
        if not both:
            outs += [((rows, width), F32)]
        scratch += [
            pltpu.VMEM((rows, width), BF16),
            pltpu.VMEM((rows, inner), BF16),
            pltpu.VMEM((rows, width), F32),
            pltpu.VMEM((rows, width), F32),
            pltpu.VMEM((inner, width), BF16),
            pltpu.VMEM((width, inner), BF16),
            pltpu.SemaphoreType.DMA((1, many)),
            pltpu.SemaphoreType.DMA((1, many)),
        ]
        scratch += [pltpu.VMEM((rows, width), F32 if both else BF16)]
        flops += 4 * rows * width * inner
    if attend:
        outs += [] if both else [((rows, 3 * width), BF16)]
        outs += [((rows, width), BF16), ((8, width), F32)]
        scratch += [
            pltpu.VMEM((rows, width), BF16),
            pltpu.VMEM((rows, 3 * width), BF16),
            pltpu.VMEM((rows, width), BF16),
            pltpu.VMEM((count, HEADS, space), F32),
            pltpu.VMEM((rows, width), BF16),
            pltpu.VMEM((rows, width), F32),
            pltpu.VMEM((count, HEADS, 2 * pair), F32),
            pltpu.VMEM((width, width), BF16),
            pltpu.VMEM((width, 3 * width), BF16),
            pltpu.SemaphoreType.DMA((1, many)),
            pltpu.SemaphoreType.DMA((1, many)),
        ]
        if not feed:
            scratch += [pltpu.VMEM((rows, width), BF16), pltpu.VMEM((rows, width), F32)]
        flops += 2 * rows * width * (4 * width + 5 * space)
    weights = (flat(reduce) + flat(wide) if feed else []) + (
        flat(wide) + flat(qkv) if attend else []
    )
    return call(
        body,
        "backward" + "_feed" * feed + "_attend" * attend,
        plain + operands + weights + [params, meta],
        [ANY] * (len(plain) + len(operands) + len(weights)) + [VMEM, SMEM],
        outs,
        scratch,
        flops,
        weight,
    )


def weight_gradient(
    lefts, rights, meta, parts, blocks, quarter, rows_of, columns_of, name, weight=LIGHT
):
    terms = len(lefts)
    first_row, height = rows_of
    first_column, breadth = columns_of
    step = breadth // 2
    rows = lefts[0].shape[0]
    operands = list(lefts)
    places = []
    for pair in rights:
        found = []
        for array, _ in pair:
            if not any(array is other for other in operands):
                operands.append(array)
            found.append(next(i for i, other in enumerate(operands) if other is array))
        places.append(found)

    def body(*refs):
        sources, info = refs[: len(operands)], refs[len(operands)]
        results = refs[len(operands) + 1 : len(operands) + 1 + len(blocks)]
        left_full, right_full, l_sem, r_sem = refs[len(operands) + 1 + len(blocks) :]
        section = info[parts]

        def start_lefts():
            loads = [[] for _ in blocks]
            for index, block in reversed(list(enumerate(blocks))):
                start = pl.multiple_of(info[block] * quarter + first_row, 128)
                for term in range(terms):
                    copy = pltpu.make_async_copy(
                        sources[term].at[:, pl.ds(start, height)],
                        left_full.at[index, pl.ds(term * rows, rows)],
                        l_sem.at[index, term],
                    )
                    copy.start()
                    loads[index].append(copy)
            return loads

        waits = [[], []]
        for cut in range(2):
            for term in range(terms):
                sides = [
                    sources[place].at[:, pl.ds(column + first_column + cut * step, step)]
                    for place, (_, column) in zip(places[term], rights[term])
                ]
                same = rights[term][0] is rights[term][1]
                target = right_full.at[cut, pl.ds(term * rows, rows)]
                waits[cut].append(start_chosen(section, *sides, target, r_sem.at[cut, term], same))
            if cut == 0:
                loads = start_lefts()
        for cut in range(2):
            wait_all(waits[cut])
            for index in reversed(range(len(blocks))):
                if cut == 0:
                    wait_all(loads[index])
                done = contract(left_full[index], right_full[cut], 0, 0)
                results[index][:, cut * step : (cut + 1) * step] = done.astype(BF16)

    return call(
        body,
        name,
        operands + [meta],
        [ANY] * len(operands) + [SMEM],
        [((height, breadth), BF16)] * len(blocks),
        [
            pltpu.VMEM((len(blocks), terms * rows, height), BF16),
            pltpu.VMEM((2, terms * rows, step), BF16),
            pltpu.SemaphoreType.DMA((len(blocks), terms)),
            pltpu.SemaphoreType.DMA((2, terms)),
        ],
        2 * len(blocks) * terms * rows * height * breadth,
        weight,
    )


def after(value, *earlier):
    return lax.optimization_barrier((value,) + earlier)[0]


def added(*values):
    total = values[0].astype(F32)
    for value in values[1:]:
        total = total + value.astype(F32)
    return total.astype(values[0].dtype)


class FourByFour:
    parts = 4
    blocks = (0, 2)

    def __init__(self):
        self.group = lax.axis_index("group")
        self.place = lax.axis_index("replica")
        self.order = [self.group ^ part for part in range(4)]
        odd = self.place % 2
        near = [4 * self.order[part] for part in (0, 1)]
        far = [4 * self.order[part] for part in (2, 3)]
        self.spots = near + [block + place for block in far for place in (2 * odd, 2 - 2 * odd)]
        self.last_spots = near + [block + place for block in far for place in (odd, 3 - 3 * odd)]

    def core(self, block):
        return lax.ppermute(block, "group", [(i, i ^ 1) for i in range(4)])

    def across(self, block):
        return lax.ppermute(block, "group", [(i, i ^ 2) for i in range(4)])

    def beside(self, block):
        return lax.ppermute(block, "replica", [(i, i ^ 1) for i in range(4)])

    def gather_small(self, block):
        near, far = self.core(block), self.across(block)
        return [block, near, far, self.core(far)]

    def gather(self, blocks, prepare):
        odd = self.place % 2
        quarters = [block.shape[0] // 4 for block in blocks]
        asked = [
            lax.dynamic_slice_in_dim(block, 2 * odd * rows, 2 * rows)
            for block, rows in zip(blocks[:-1], quarters)
        ]
        asked.append(lax.dynamic_slice_in_dim(blocks[-1], odd * quarters[-1], 3 * quarters[-1]))
        halves, sibling = [], []
        for index, block in enumerate(blocks):
            halves.append(self.across(after(asked[index], *halves[: max(index - 1, 0)])))
            sibling.append(self.core(after(block, sibling[-1]) if index else block))
        others = []
        tokens = prepare(halves[0]) + asked[2:]
        swaps = halves[:-1] + [
            lax.dynamic_slice_in_dim(halves[-1], 2 * odd * quarters[-1], quarters[-1])
        ]
        for index, half in enumerate(swaps):
            earlier = others[-1:] if index == 1 else []
            others.append(self.beside(after(half, *earlier, *(tokens if index == 1 else []))))
        self.swapped = others[-1]

        def pieces(index, before_one=(), before_two=()):
            one, two = after(halves[index], *before_one), after(others[index], *before_two)
            return [
                [blocks[index]],
                [sibling[index]],
                [halves[index], others[index]],
                [self.core(one), self.core(two)],
            ]

        return [partial(pieces, index) for index in range(len(blocks))]

    def shared(self, block):
        return [block, self.core(block)]

    def total(self, blocks):
        passed = self.across(blocks[1])
        token = yield
        mine = added(after(blocks[0], token), passed)
        inward = lax.ppermute(mine, "replica", [(0, 1), (3, 2)])
        token = yield mine
        joined = added(after(mine, token), inward)
        crossing = lax.ppermute(joined, "replica", [(1, 2), (2, 1)])
        token = yield joined
        summed = added(after(joined, token), crossing)
        outward = lax.ppermute(summed, "replica", [(1, 0), (2, 3)])
        token = yield summed
        inner = (self.place == 1) | (self.place == 2)
        yield jnp.where(inner, after(summed, token), outward)


class General:
    def __init__(self):
        self.parts = lax.axis_size("group")
        self.blocks = tuple(range(self.parts))
        self.order = [jnp.int32(part) for part in range(self.parts)]
        self.spots = self.last_spots = [4 * part for part in self.order]

    def gather_small(self, block):
        whole = lax.all_gather(block, "group", axis=0)
        return [whole[part] for part in range(self.parts)]

    def gather(self, blocks, prepare):
        prepare(blocks[0])
        self.swapped = blocks[0]
        found = [[[piece] for piece in self.gather_small(block)] for block in blocks]
        return [lambda *tokens, groups=groups: groups for groups in found]

    def shared(self, block):
        return [block]

    def total(self, blocks):
        yield
        mine = lax.psum_scatter(jnp.stack(blocks), "group", scatter_dimension=0)
        yield mine
        yield lax.psum(mine, "replica")


def shifted(block, distance):
    devices = range(lax.axis_size("section"))
    route = [(i - distance, i) for i in devices if i - distance in devices]
    return lax.ppermute(block, "section", route)


def in_order(pieces, order):
    place = jnp.stack(order)
    stacked = []
    for block in range(len(pieces)):
        chosen = pieces[0]
        for part in range(1, len(pieces)):
            chosen = jnp.where(place[part] == block, pieces[part], chosen)
        stacked.append(chosen)
    return jnp.stack(stacked)


class Sequence:
    def __init__(self, net, token):
        self.net, self.sums, self.results, self.token = net, {}, {}, token

    def now(self, value):
        return after(value, self.token)

    def ran(self, value):
        self.token = value

    def add(self, name, blocks):
        self.sums[name] = self.net.total(blocks)
        next(self.sums[name])

    def step(self, *names):
        for name in names:
            try:
                self.results[name] = self.token = self.sums[name].send(self.token)
            except StopIteration:
                continue

    def finish(self, name):
        while True:
            try:
                self.results[name] = self.sums[name].send(self.token)
            except StopIteration:
                return self.results[name]


def per_device(
    images,
    cotangent,
    counts,
    qkv_weight,
    out_weight,
    expand_weight,
    reduce_weight,
    norm_gains,
    biases,
    expand_bias,
):
    micro, slots, length, width = images.shape
    space = padded(length)
    section = lax.axis_index("section")
    first = section == 0
    sizes = (lax.axis_size("group"), lax.axis_size("replica"))
    net = FourByFour() if sizes == (4, 4) else General()
    parts = net.parts
    share = width // parts
    batches = tuple(range(micro))

    def rows_of(array):
        fulls = [jnp.pad(array[batch], ((0, 0), (0, space - length), (0, 0))) for batch in batches]
        return [full.reshape(slots * space, width) for full in fulls]

    def images_of(array):
        return array.reshape(slots, space, width)[:, :length]

    small = jnp.concatenate([norm_gains[0], biases[0], expand_bias[0].reshape(-1, share)])
    slot = jnp.arange(slots, dtype=jnp.int32)
    alive = [(slot < counts[batch, 0]).astype(jnp.int32) for batch in batches]
    head = jnp.stack(net.order + [section]).astype(jnp.int32)

    spots = jnp.stack(net.spots + net.last_spots).astype(jnp.int32)

    def meta(living):
        return jnp.concatenate([head, living, spots])

    infos = [meta(alive[batch]) for batch in batches]
    pieces = net.gather_small(small)
    vectors = in_order(pieces, net.order)
    top = vectors[:, :8].transpose(1, 0, 2).reshape(8, width)
    bottom = vectors[:, 8:].reshape(-1, width)
    params = jnp.concatenate([top, bottom]).astype(F32)
    slot = jnp.arange(slots, dtype=jnp.int32)
    alive = [(slot < counts[batch, 0]).astype(jnp.int32) for batch in batches]
    head = jnp.stack(net.order + [section]).astype(jnp.int32)
    spots = jnp.stack(net.spots + net.last_spots).astype(jnp.int32)

    def meta(living):
        return jnp.concatenate([head, living, spots])

    infos = [meta(alive[batch]) for batch in batches]
    inputs, targets = [], []

    def prepare(token):
        inputs.extend(rows_of(after(images, token)))
        targets.extend(rows_of(after(cotangent, token)))
        return [params, *inputs, *targets, *infos]

    qkv, wide, reduce = net.gather(
        [qkv_weight[0], jnp.concatenate([out_weight[0], expand_weight[0]], axis=1), reduce_weight[0]],
        prepare,
    )

    qkv = qkv()
    attended = []
    for batch in batches:
        start = inputs[batch] if batch == 0 else after(inputs[batch], attended[-1][0])
        attended.append(
            forward(start, start, None, qkv, None, params, infos[batch], slots, length)
        )
    wide = wide(attended[0], attended[-1])
    fed = []
    for batch in batches:
        start = inputs[batch] if batch == 0 else after(inputs[batch], fed[-1][0], net.swapped)
        fed.append(
            forward(start, start, attended[batch][0], None, wide, params, infos[batch], slots, length)
        )
    reduce = reduce(attended[-1], fed[0][:1])
    early, incoming = [], []
    for batch in batches:
        middle, active = fed[batch]
        if batch:
            active = after(active, early[-1])
        early.append(output_forward(middle, active, reduce, params, infos[batch], slots))
        incoming.append(shifted(early[batch], 1))

    inner = wide[0][0].shape[1] - width
    mixed_at = inner + width
    kept, lefts, rights, results = [], [], [], []
    sums_a, sums_b, sums_c, returning = [], [], [], []
    token = early[-1]
    for batch in batches:
        start = after(incoming[batch], token)
        left, packed, logs, middle, slope = forward(
            inputs[batch], start, None, qkv, wide, params, infos[batch], slots, length, 8.0
        )
        kept.append((slope, middle, packed, left, logs))
        lefts.append(net.shared(left))
        if batch == 0:
            pair, sides = (targets[0], targets[0]), (kept[0], kept[0])
            lower, chosen = incoming[0], infos[0]
        else:
            pair = (returning[batch - 1], targets[batch])
            sides = (kept[batch - 1], kept[batch])
            lower = inputs[batch - 1]
            chosen = meta(jnp.where(first, alive[batch - 1], alive[batch]))
        right, some, more, result, rest = backward(
            pair, lower, incoming[batch], sides[0], sides[1], reduce, wide, qkv, params, chosen,
            slots, length, mixed_at, 8.0,
        )
        token = result
        rights.append(net.shared(right))
        results.append(result)
        sums_a.append(some)
        sums_b.append(more)
        sums_c.append(rest)
        returning.append(shifted(result, -1))
    late = []
    for batch in batches:
        ready = lefts[batch][1:] + (rights[batch][1:] if batch < micro - 1 else [])
        active = after(kept[batch][3], token, *ready)
        late.append(output_forward(kept[batch][1], active, reduce, params, infos[batch], slots, 8.0))
        token = late[-1]

    last = micro - 1
    run = Sequence(net, token)
    arrived = run.now(returning[last])
    living = jnp.repeat(alive[last] > 0, space)[:, None]
    masked = net.shared(jnp.where(living, arrived, jnp.zeros_like(arrived)))
    many = len(masked)

    def gradient(name, left_at, final, final_at, right_at, quarter, rows, columns, weight=LIGHT):
        left = [lefts[batch][side] for batch in batches for side in range(many)]
        right = []
        for batch in batches:
            for side in range(many):
                upper = (rights[batch][side], right_at)
                lower = (final[side], final_at) if batch == last else (rights[batch + 1][side], right_at)
                right.append((lower, upper))
        blocks = weight_gradient(
            left, right, run.now(head), parts, net.blocks, quarter, (left_at + rows[0], rows[1]), columns,
            name, weight,
        )
        run.ran(blocks[0])
        return blocks

    half, at = inner // 2, inner + 2 * width
    deep = inner // parts
    state = {"mid": None, "rows": None}

    def feed_back(weight):
        start = run.now(arrived)
        hidden, branch, some, more, mid = backward(
            (start, start), None, None, kept[last], kept[last], reduce, wide, None, params, infos[last],
            slots, length, mixed_at, weight,
        )
        run.ran(hidden)
        state.update(mid=mid, branch=branch, hidden=net.shared(hidden), branches=net.shared(branch))
        sums_a.append(some)
        sums_b.append(more)

    def attend_back(weight):
        start = run.now(after(state["branch"], *state["branches"][1:], *state["hidden"][1:]))
        grads, result, rest = backward(
            (start, state["mid"]), inputs[last], inputs[last], kept[last], kept[last], None, wide, qkv,
            params, infos[last], slots, length, mixed_at, weight,
        )
        run.ran(result)
        state["grads"] = net.shared(grads)
        results.append(result)
        sums_c.append(rest)

    def reduce_part(index, weight):
        step = deep // 2
        return gradient(
            "reduce", 0, masked, 0, inner + width, deep, (index * step, step), (0, width), weight
        )

    def expand_part(begin, size, weight):
        return gradient("expand", inner, state["hidden"], 0, 0, share, (0, share), (begin, size), weight)

    def project_part(weight):
        return gradient(
            "project", mixed_at, state["branches"], 0, inner, share, (0, share), (0, width), weight
        )

    def qkv_part(begin, size, weight):
        return gradient("qkv", at, state["grads"], 0, at, share, (0, share), (begin, size), weight)

    def over_batches(values):
        return sum(jnp.where(first, values[batch + 1], values[batch]) for batch in batches)

    def small_sums():
        some, more, rest = over_batches(sums_a), over_batches(sums_b), over_batches(sums_c)
        rows = jnp.concatenate([rest[0:1], some[0:1], rest[1:2], some[1:2], rest[2:4], some[2:4]])
        rows = rows.reshape(8, parts, share).transpose(1, 0, 2)
        rows = jnp.concatenate([rows, more.reshape(parts, -1, share)], axis=1)
        rows = sum(net.shared(run.now(rows)))
        rows = jnp.stack(
            [lax.dynamic_index_in_dim(rows, net.order[block], 0, keepdims=False) for block in net.blocks]
        )
        state["count"] = rows.shape[1]
        state["rows"] = rows.reshape(len(net.blocks), -1).astype(BF16)

    def with_small(blocks):
        step, rows = blocks[0].shape[1], state["rows"]
        rows = jnp.pad(rows, ((0, 0), (0, -rows.shape[1] % (16 * step)))).reshape(len(blocks), -1, step)
        return [jnp.concatenate([block, row]) for block, row in zip(blocks, rows)]

    outputs = []

    def assemble():
        index = len(outputs)
        low, up = (early + results[1:])[index], (late + results[:-1])[index]
        outputs.append(images_of(jnp.where(first, run.now(low), up)))

    def joined(axis, *names):
        found = [run.finish(name) for name in names]
        found = [value[:share] if name == LAST.lower() else value for name, value in zip(names, found)]
        return jnp.concatenate(found, axis=axis).astype(F32)[None]

    shapes = {"q": (1, "q0", "q1"), "p": (1, "p0"), "e": (1, "e0", "e1"), "r": (0, "r0", "r1")}
    gradients = {}

    third = 3 * width // 2
    kernels = {
        "R0": lambda weight: reduce_part(0, weight),
        "R1": lambda weight: reduce_part(1, weight),
        "E0": lambda weight: expand_part(0, half, weight),
        "E1": lambda weight: expand_part(half, half, weight),
        "Q0": lambda weight: qkv_part(0, third, weight),
        "Q1": lambda weight: qkv_part(third, third, weight),
        "P0": lambda weight: project_part(weight),
    }
    for entry in " ".join(PLAN).split():
        name, _, factor = entry.partition("*")
        weight = float(factor or HEAVY) if "*" in entry else LIGHT
        if name in kernels:
            blocks = kernels[name](weight)
            if name == LAST:
                blocks = with_small(blocks)
            run.add(name.lower(), blocks)
        elif name == "BF":
            feed_back(weight)
        elif name == "BA":
            attend_back(weight)
        elif name == "V":
            small_sums()
        elif name == "O":
            assemble()
        elif name[0] == "C":
            gradients[name[1]] = joined(*shapes[name[1]])
        else:
            run.step(name)
    while len(outputs) < 2 * micro:
        assemble()
    for name in shapes:
        if name not in gradients:
            gradients[name] = joined(*shapes[name])
    count = state["count"]
    vector = run.finish(LAST.lower())[share:].reshape(-1)[: count * share].reshape(count, share).astype(F32)
    return (
        jnp.stack(outputs[:micro])[None],
        jnp.stack(outputs[micro:])[None],
        gradients["q"],
        gradients["p"],
        gradients["e"],
        gradients["r"],
        vector[None, 0:2],
        vector[None, 2:8],
        vector[8:].reshape(1, -1),
    )


def solution(mesh):
    placed = (
        P(None, ("group", "replica"), None, None),
        P(None, ("group", "replica"), None, None),
        P(None, ("group", "replica")),
        P("section", "group", None),
        P("section", "group", None),
        P("section", "group", None),
        P("section", "group", None),
        P("section", None, "group"),
        P("section", None, "group"),
        P("section", "group"),
    )
    return jax.shard_map(
        per_device,
        mesh=mesh,
        in_specs=placed,
        out_specs=(
            P("section", None, ("group", "replica"), None, None),
            P("section", None, ("group", "replica"), None, None),
            P("section", "group", None),
            P("section", "group", None),
            P("section", "group", None),
            P("section", "group", None),
            P("section", None, "group"),
            P("section", None, "group"),
            P("section", "group"),
        ),
        check_vma=False,
    )
```

```python
from functools import partial

import jax
import jax.numpy as jnp
from jax import lax
from jax.experimental import pallas as pl
from jax.experimental.pallas import tpu as pltpu
from jax.sharding import PartitionSpec as P

HEADS = 16
EPSILON = 1e-06
NEGATIVE = -1e30
F32 = jnp.float32
BF16 = jnp.bfloat16
LIGHT, HEAVY = 1.0 / 64, 16.0
PLAN = (
    "R0 BF r0 R1*",
    "BA r0 r1 E0*",
    "r1 Q0 r0 e0",
    "E1 q0 r1 e0",
    "r0 Q1 e1 q0",
    "r1 e0 V P0",
    "e1 q1 O q0",
    "e0 p0 q1 O",
    "e1 q0 p0 O",
    "O q1 e1 p0",
    "q1 p0",
)
LAST = "P0"
VMEM_LIMIT = 58 * 2**20
ROOT_HALF = 0.7071067811865476
ROOT_TAU = 0.3989422804014327
ANY = pl.BlockSpec(memory_space=pl.ANY)
VMEM = pl.BlockSpec(memory_space=pltpu.VMEM)
SMEM = pl.BlockSpec(memory_space=pltpu.SMEM)
GAIN0, GAIN1, SHIFT0, SHIFT1, QUERY, VALUE, OUT, FEED, EXPAND = range(9)


def padded(length):
    return -(-length // 16) * 16


def contract(left, right, left_dim, right_dim):
    return lax.dot_general(
        left, right, (((left_dim,), (right_dim,)), ((), ())), preferred_element_type=F32
    )


def standardized(values):
    center = values - jnp.mean(values, axis=-1, keepdims=True)
    spread = jnp.mean(center * center, axis=-1, keepdims=True)
    scale = lax.rsqrt(spread + EPSILON)
    return center * scale, scale


def norm_pull(grad, gain, unit, scale):
    scaled = grad * gain
    mean = jnp.mean(scaled, axis=-1, keepdims=True)
    along = jnp.mean(scaled * unit, axis=-1, keepdims=True)
    return scale * (scaled - mean - unit * along)


def call(body, name, operands, specs, outs, scratch, flops, weight=LIGHT):
    moved = sum(o.size * o.dtype.itemsize for o in operands)
    out_shape = [jax.ShapeDtypeStruct(shape, dtype) for shape, dtype in outs]
    moved += sum(o.size * o.dtype.itemsize for o in out_shape)
    return pl.pallas_call(
        body,
        out_shape=out_shape,
        in_specs=specs,
        out_specs=[VMEM] * len(outs),
        scratch_shapes=scratch,
        compiler_params=pltpu.CompilerParams(vmem_limit_bytes=VMEM_LIMIT),
        cost_estimate=pl.CostEstimate(flops=int(flops * weight), bytes_accessed=int(moved * weight), transcendentals=0),
        name=name,
    )(*operands)


def flat(groups):
    return [piece for group in groups for piece in group]


def start_pieces(pieces, info, first, target, sems, slot, columns, block, shift=0):
    begin, size = columns
    columns = pl.ds(begin, size)
    copies = []
    for index, piece in enumerate(pieces):
        rows = piece.shape[0]
        where = pl.multiple_of(info[first + index] * (block // 4), block // 4)
        copy = pltpu.make_async_copy(
            piece.at[:, pl.ds(begin + shift, size)],
            target.at[pl.ds(where, rows), columns],
            sems.at[slot, index],
        )
        copy.start()
        copies.append(copy)
    return copies


def wait_all(copies):
    for copy in copies:
        copy.wait()


def start_chosen(section, lower, upper, target, sem, same=False):
    if lower is upper or same:
        copy = pltpu.make_async_copy(lower, target, sem)
        copy.start()
        return copy

    @pl.when(section == 0)
    def _():
        pltpu.make_async_copy(lower, target, sem).start()

    @pl.when(section != 0)
    def _():
        pltpu.make_async_copy(upper, target, sem).start()

    return pltpu.make_async_copy(lower, target, sem)


def eights(values):
    return jnp.sum(values.reshape(-1, 8, values.shape[-1]), axis=0)


def attention_stage(x, vec, norm, packed, mixed, logs, columns, full, loads, count, length):
    rows, width = x.shape
    space = rows // count
    head = width // HEADS
    pair = 2 * head
    scale = head**-0.5
    gain, shift = vec[GAIN0 : GAIN0 + 1], vec[SHIFT0 : SHIFT0 + 1]

    def step(here):
        unit, _ = standardized(x[here].astype(F32))
        norm[here] = (unit * gain + shift).astype(BF16)

    step(pl.ds(0, rows))
    for block in range(3):
        wait_all(loads[block])
        done = contract(norm[...], full[:, block * width : (block + 1) * width], 1, 0)
        if block != 1:
            bias = QUERY if block == 0 else VALUE
            done = done + vec[bias : bias + 1]
        packed[:, block * width : (block + 1) * width] = done.astype(BF16)
    lane = lax.broadcasted_iota(jnp.int32, (space, pair), 1)
    left = lane < head
    live = lax.broadcasted_iota(jnp.int32, (space, pair), 0) < length
    key_live = lax.broadcasted_iota(jnp.int32, (space, space), 1) < length
    columns[...] = jnp.zeros_like(columns)

    def heads(index, carry):
        for image in range(count):
            span = pl.ds(image * space, space)

            def part(block):
                offset = pl.multiple_of(block * width + index * pair, pair)
                return packed[span, pl.ds(offset, pair)]

            query, key, value = part(0).astype(F32) * scale, part(1), part(2).astype(F32)
            found = []
            tops = []
            for side in range(2):
                mine = left if side == 0 else ~left
                asked = jnp.where(mine, query, 0.0).astype(BF16)
                held = jnp.where(live, jnp.where(mine, value, 1.0), 0.0).astype(BF16)
                scores = jnp.where(key_live, contract(asked, key, 1, 1), NEGATIVE)
                top = jnp.max(scores, axis=-1, keepdims=True)
                raised = jnp.exp(scores - top).astype(BF16)
                found.append(contract(raised, held, 1, 0))
                tops.append(top)
            inside = jnp.where(left, found[0], found[1])
            total = jnp.where(left, found[1], found[0])
            turned = pltpu.roll(total, head, 1)
            offset = pl.multiple_of(index * pair, pair)
            mixed[span, pl.ds(offset, pair)] = (inside / turned).astype(BF16)
            if logs is None:
                continue
            logged = jnp.where(left, tops[0], tops[1]) + jnp.log(turned)
            columns[image] = jnp.where((lane & (head - 1)) == index, logged, columns[image])
        return carry

    lax.fori_loop(0, HEADS // 2, heads, 0, unroll=2)
    if logs is not None:
        for image in range(count):
            rows_of = columns[image].T
            logs[image, 0 : HEADS // 2] = rows_of[0 : HEADS // 2]
            logs[image, HEADS // 2 : HEADS] = rows_of[head : head + HEADS // 2]


def hidden_stage(x, vec, mixed, middle, active, second, slope, full_out, full, first_load, loads):
    rows, width = x.shape
    wait_all(first_load)
    gain, shift, bias = vec[GAIN1 : GAIN1 + 1], vec[SHIFT1 : SHIFT1 + 1], vec[OUT : OUT + 1]
    middle[...] = contract(mixed[...], full_out[...], 1, 0)

    def step(here):
        total = middle[here] + x[here].astype(F32) + bias
        middle[here] = total
        unit, _ = standardized(total)
        second[here] = (unit * gain + shift).astype(BF16)

    step(pl.ds(0, rows))
    for block, load in enumerate(loads):
        wait_all(load)
        part = slice(block * width, (block + 1) * width)
        value = contract(second[...], full[:, part], 1, 0) + vec[EXPAND + block : EXPAND + block + 1]
        share = 0.5 + 0.5 * lax.erf(value * ROOT_HALF)
        active[:, part] = (value * share).astype(BF16)
        if slope is not None:
            density = ROOT_TAU * jnp.exp(-0.5 * value * value)
            slope[:, part] = (share + value * density).astype(BF16)


def forward(
    lower, upper, mixed_in, qkv, wide, params, meta, count, length, weight=LIGHT
):
    rows, width = lower.shape
    space = rows // count
    pair = 2 * width // HEADS
    attend, feed = qkv is not None, wide is not None
    both = attend and feed
    parts = len(qkv if attend else wide)
    many = len(flat(qkv if attend else wide))
    spots = parts + 1 + count
    inner = wide[0][0].shape[1] - width if feed else 0
    share = width // parts
    blocks = inner // width
    same = lower is upper

    def body(*refs):
        refs = list(refs)
        low = refs.pop(0)
        up = low if same else refs.pop(0)
        if not attend:
            arrived = refs.pop(0)
        lists = [[refs.pop(0) for _ in range(many)] for _ in range(attend + 2 * feed)]
        vec, info = refs.pop(0), refs.pop(0)
        if both:
            left, packed, logs, middle, slope = (refs.pop(0) for _ in range(5))
            active, second, mixed, norm = (
                left.at[:, pl.ds(start, size)]
                for start, size in ((0, inner), *((inner + width * i, width) for i in range(3)))
            )
        elif attend:
            mixed = refs.pop(0)
        else:
            middle, active = refs.pop(0), refs.pop(0)
        x, x_sem = refs.pop(0), refs.pop(0)
        section = info[parts]
        take = start_chosen(section, low, up, x, x_sem.at[0])
        if attend:
            columns, full, a_sem = (refs.pop(0) for _ in range(3))
            if not both:
                norm, packed, logs = refs.pop(0), refs.pop(0), None
            weight = lists.pop(0)
            loads = [
                start_pieces(weight, info, spots, full, a_sem, block, (block * width, width), share)
                for block in range(3)
            ]
        if feed:
            full_out, full_in, o_sem, w_sem = (refs.pop(0) for _ in range(4))
            if not attend:
                mixed, second, slope = refs.pop(0), refs.pop(0), None
                extra = pltpu.make_async_copy(arrived, mixed, x_sem.at[1])
                extra.start()
            first_load = start_pieces(lists[0], info, spots, full_out, o_sem, 0, (0, width), share)
            inner_loads = [
                start_pieces(lists[1], info, spots, full_in, w_sem, block, (block * width, width), share, width)
                for block in range(blocks)
            ]
        take.wait()
        if attend:
            attention_stage(
                x, vec, norm, packed, mixed, logs, columns, full, loads, count, length
            )
        if feed:
            if not attend:
                extra.wait()
            hidden_stage(
                x, vec, mixed, middle, active, second, slope, full_out, full_in, first_load,
                inner_loads,
            )

    outs, inputs = [], [lower] if same else [lower, upper]
    scratch = [pltpu.VMEM((rows, width), BF16), pltpu.SemaphoreType.DMA((2,))]
    flops = 0
    if attend:
        outs += [
            ((rows, width), BF16),
            ((rows, 3 * width), BF16),
            ((rows, width), BF16),
            ((count, HEADS, space), F32),
        ]
        scratch += [
            pltpu.VMEM((count, space, pair), F32),
            pltpu.VMEM((width, 3 * width), BF16),
            pltpu.SemaphoreType.DMA((3, many)),
        ]
        if not feed:
            scratch += [pltpu.VMEM((rows, width), BF16), pltpu.VMEM((rows, 3 * width), BF16)]
        flops += 2 * rows * width * (3 * width + 2 * space)
    else:
        inputs += [mixed_in]
    if feed:
        outs += [
            ((rows, width), F32),
            ((rows, inner), BF16),
            ((rows, width), BF16),
            ((rows, inner), BF16),
        ]
        scratch += [
            pltpu.VMEM((width, width), BF16),
            pltpu.VMEM((width, inner), BF16),
            pltpu.SemaphoreType.DMA((1, many)),
            pltpu.SemaphoreType.DMA((blocks, many)),
        ]
        if not attend:
            scratch += [pltpu.VMEM((rows, width), BF16), pltpu.VMEM((rows, width), BF16)]
        flops += 2 * rows * width * (width + inner)
    if both:
        outs = [((rows, inner + 3 * width), BF16), outs[1], outs[3], outs[4], outs[7]]
    else:
        outs = [outs[2]] if attend else outs[:2]
    weights = (flat(qkv) if attend else []) + (2 * flat(wide) if feed else [])
    return call(
        body,
        "forward" + "_attend" * attend + "_feed" * feed,
        inputs + weights + [params, meta],
        [ANY] * (len(inputs) + len(weights)) + [VMEM, SMEM],
        outs,
        scratch,
        flops,
        weight,
    )


def output_forward(middle, active, pieces, params, meta, count, weight=LIGHT):
    rows, width = middle.shape
    inner = sum(piece.shape[0] for piece in flat(pieces))
    space = rows // count
    parts, many = len(pieces), len(flat(pieces))
    spots = parts + 1 + count
    deep = inner // parts

    def body(*refs):
        refs = list(refs)
        mid_in, act_in = refs.pop(0), refs.pop(0)
        reduce = [refs.pop(0) for _ in range(many)]
        vec, info, result, mid, act, full, total, x_sem, w_sem = refs
        every = start_pieces(reduce[:1], info, spots + many, full, w_sem, 0, (0, width), deep)
        columns = [pl.ds(pl.multiple_of(info[index] * deep, deep), deep) for index in range(parts)]
        takes = []
        for index in range(parts):
            takes.append(
                pltpu.make_async_copy(act_in.at[:, columns[index]], act.at[index], x_sem.at[index])
            )
            takes[-1].start()
            if index == 0:
                every += start_pieces(
                    reduce[1:], info, spots + many + 1, full, w_sem.at[:, pl.ds(1, many - 1)], 0,
                    (0, width), deep,
                )
        last = pltpu.make_async_copy(mid_in, mid, x_sem.at[parts])
        last.start()
        for index, group in enumerate(pieces):
            takes[index].wait()
            wait_all([every.pop(0) for _ in group])
            value = contract(act[index], full[columns[index]], 1, 0)
            if index:
                value = value + total[...]
            if index < parts - 1:
                total[...] = value
        last.wait()
        value = value + mid[...] + vec[FEED : FEED + 1]
        for image in range(count):
            alive = jnp.where(info[parts + 1 + image] > 0, 1.0, 0.0)
            here = slice(image * space, (image + 1) * space)
            result[here] = (value[here] * alive).astype(BF16)

    return call(
        body,
        "output_forward",
        [middle, active] + flat(pieces) + [params, meta],
        [ANY] * (2 + many) + [VMEM, SMEM],
        [((rows, width), BF16)],
        [
            pltpu.VMEM((rows, width), F32),
            pltpu.VMEM((parts, rows, deep), BF16),
            pltpu.VMEM((inner, width), BF16),
            pltpu.VMEM((rows, width), F32),
            pltpu.SemaphoreType.DMA((parts + 1,)),
            pltpu.SemaphoreType.DMA((1, many)),
        ],
        2 * rows * width * inner,
        weight,
    )[0]


def hidden_back_stage(
    grad, vec, info, feed, slope, middle, hidden, second, mid_grad, branch, sums, inner_sums, full_out,
    full, deep, first_load, load, for_slope, for_middle, tallies, count, parts,
):
    rows, width = grad.shape
    space = rows // count
    half = width // 2
    for image in range(count):
        alive = jnp.where(info[parts + 1 + image] > 0, 1.0, 0.0)
        here = slice(image * space, (image + 1) * space)
        feed[here] = (grad[here].astype(F32) * alive).astype(BF16)
    for_slope.wait()
    for index in range(parts):
        wait_all(first_load[index])
        where = pl.multiple_of(info[index] * deep, deep)
        value = contract(feed[...], full_out[pl.ds(where, deep)], 1, 1)
        value = (value * slope[:, pl.ds(where, deep)].astype(F32)).astype(BF16)
        hidden[:, pl.ds(where, deep)] = value
        inner_sums[:, pl.ds(where, deep)] = jnp.sum(value.astype(F32), axis=0, keepdims=True)
    wait_all(load)
    for block in range(2):
        second[:, block * half : (block + 1) * half] = contract(
            hidden[...], full[block * half : (block + 1) * half], 1, 1
        )
    for_middle.wait()
    gain = vec[GAIN1 : GAIN1 + 1]
    tallies[...] = jnp.zeros_like(tallies)

    def step(here):
        unit, scale = standardized(middle[here])
        down = second[here]
        top = feed[here].astype(F32)
        total = top + norm_pull(down, gain, unit, scale)
        low = total.astype(BF16)
        mid_grad[here] = total
        branch[here] = low
        tallies[0] += eights(down * unit)
        tallies[1] += eights(down)
        tallies[2] += eights(low.astype(F32))
        tallies[3] += eights(top)

    step(pl.ds(0, rows))
    for index in range(4):
        sums[index : index + 1] = jnp.sum(tallies[index], axis=0, keepdims=True)


def attention_back_stage(
    x, vec, branch, mid_grad, packed, mixed, logs, grads, result, sums, down, normal, stage, full_out,
    full, first_load, load, takes, tallies, count, length,
):
    rows, width = x.shape
    space = rows // count
    head = width // HEADS
    pair = 2 * head
    scale = head**-0.5
    half = width // 2
    wait_all(first_load)
    down[...] = contract(branch[...], full_out[...], 1, 1).astype(BF16)
    wait_all(takes)
    owner = lax.shift_right_logical(
        lax.broadcasted_iota(jnp.int32, (HEADS, width), 1), head.bit_length() - 1
    )
    chosen = jnp.where(
        owner == lax.broadcasted_iota(jnp.int32, (HEADS, width), 0), 1.0, 0.0
    ).astype(BF16)
    left = lax.broadcasted_iota(jnp.int32, (space, pair), 1) < head
    live = lax.broadcasted_iota(jnp.int32, (space, pair), 0) < length
    key_live = lax.broadcasted_iota(jnp.int32, (space, space), 0) < length
    for image in range(count):
        span = pl.ds(image * space, space)
        product = down[span].astype(F32) * mixed[span].astype(F32)
        coarse = product.astype(BF16)
        fine = (product - coarse.astype(F32)).astype(BF16)
        stage[image, :, 0:space] = contract(chosen, coarse, 1, 1) + contract(chosen, fine, 1, 1)

    def heads(index, carry):
        for image in range(count):
            span = pl.ds(image * space, space)

            def part(block):
                offset = pl.multiple_of(block * width + index * pair, pair)
                return packed[span, pl.ds(offset, pair)]

            query, key, value = part(0), part(1), part(2)
            wide = key.astype(F32) * scale
            value = value.astype(F32)
            arrived = down[span, pl.ds(pl.multiple_of(index * pair, pair), pair)]
            found = []
            for side in range(2):
                mine = left if side == 0 else ~left
                log = logs[image, pl.ds(side * (HEADS // 2) + index, 1), :]
                dot = stage[image, pl.ds(2 * index + side, 1), 0:space]
                scores = contract(jnp.where(mine, wide, 0.0).astype(BF16), query, 1, 1)
                chance = jnp.exp(jnp.where(key_live, scores - log, NEGATIVE))
                back = contract(jnp.where(mine, value, 0.0).astype(BF16), arrived, 1, 1)
                change = (chance * (back - dot)).astype(BF16)
                found.append(
                    (
                        contract(change, key, 0, 0),
                        contract(change, query, 1, 0),
                        contract(chance.astype(BF16), arrived, 1, 0),
                    )
                )
            for block, factor in enumerate((scale, scale, 1.0)):
                total = jnp.where(left, found[0][block], found[1][block]) * factor
                offset = pl.multiple_of(block * width + index * pair, pair)
                grads[span, pl.ds(offset, pair)] = jnp.where(live, total, 0.0).astype(BF16)
        return carry

    lax.fori_loop(0, HEADS // 2, heads, 0, unroll=4)
    wait_all(load)
    for block in range(2):
        normal[:, block * half : (block + 1) * half] = contract(
            grads[...], full[block * half : (block + 1) * half], 1, 1
        )
    gain = vec[GAIN0 : GAIN0 + 1]
    tallies[...] = jnp.zeros_like(tallies)

    def step(here):
        unit, rate = standardized(x[here].astype(F32))
        grad = normal[here]
        tallies[0] += eights(grad * unit)
        tallies[1] += eights(grad)
        result[here] = (mid_grad[here] + norm_pull(grad, gain, unit, rate)).astype(BF16)

    step(pl.ds(0, rows))
    for index in range(2):
        sums[index : index + 1] = jnp.sum(tallies[index], axis=0, keepdims=True)
    sums[2:3] = jnp.sum(grads[:, 0:width].astype(F32), axis=0, keepdims=True)
    sums[3:4] = jnp.sum(grads[:, 2 * width : 3 * width].astype(F32), axis=0, keepdims=True)


def backward(
    start, lower, upper, kept_low, kept_up, reduce, wide, qkv, params, meta, count, length,
    mixed_at, weight=LIGHT,
):
    feed, attend = reduce is not None, qkv is not None
    rows, width = start[0].shape
    space = rows // count
    pair = 2 * width // HEADS
    parts = len(reduce if feed else qkv)
    many = len(flat(reduce if feed else qkv))
    spots = parts + 1 + count
    inner = wide[0][0].shape[1] - width if feed else 0
    deep, share = inner // parts, width // parts
    both = feed and attend
    choices = []
    if feed:
        choices += [(kept_low[0], kept_up[0]), (kept_low[1], kept_up[1])]
        if start[0] is not start[1]:
            choices += [start]
    if attend:
        choices += [(kept_low[index], kept_up[index]) for index in (2, 3, 4)]
        choices += [(lower, upper)]
    plain = [start[0]] if feed and start[0] is start[1] else [] if feed else list(start)
    operands = []
    for low, up in choices:
        operands += [low] if low is up else [low, up]

    def body(*refs):
        refs = list(refs)
        firsts = [refs.pop(0) for _ in plain]
        pairs = []
        for low, up in choices:
            one = refs.pop(0)
            pairs.append((one, one if low is up else refs.pop(0)))
        lists = [[refs.pop(0) for _ in range(many)] for _ in range(2 * feed + 2 * attend)]
        vec, info = refs.pop(0), refs.pop(0)
        section = info[parts]
        if feed:
            if both:
                right = refs.pop(0)
                hidden, branch = right.at[:, pl.ds(0, inner)], right.at[:, pl.ds(inner, width)]
            else:
                hidden, branch = refs.pop(0), refs.pop(0)
            feed_sums, inner_sums = refs.pop(0), refs.pop(0)
            mid_grad = None if both else refs.pop(0)
        if attend:
            grads, result, sums = (refs.pop(0) for _ in range(3)) if not both else (None, refs.pop(0), refs.pop(0))
        if both:
            feed_grad = right.at[:, pl.ds(inner + width, width)]
            grads = right.at[:, pl.ds(inner + 2 * width, 3 * width)]
        tallies, x_sem = refs.pop(0), refs.pop(0)
        if feed:
            grad, slope, middle, second, full_out, full, o_sem, w_sem = (
                refs.pop(0) for _ in range(8)
            )
            if both:
                mid_grad, keep = refs.pop(0), feed_grad
            else:
                keep = refs.pop(0)
            begin = pairs.pop(2) if start[0] is not start[1] else (firsts[0], firsts[0])
            take = start_chosen(section, *begin, grad, x_sem.at[0])
            for_slope = start_chosen(section, *pairs.pop(0), slope, x_sem.at[1])
            every = start_pieces(lists.pop(0), info, spots + many, full_out, o_sem, 0, (0, width), deep)
            first_load = [[every.pop(0) for _ in group] for group in reduce]
            for_middle = start_chosen(section, *pairs.pop(0), middle, x_sem.at[2])
            load = start_pieces(lists.pop(0), info, spots, full, w_sem, 0, (0, inner), share, width)
        if attend:
            x, packed, mixed, logs, down, normal, stage, full_o, full_q, p_sem, q_sem = (
                refs.pop(0) for _ in range(11)
            )
            if not feed:
                branch, mid_grad = refs.pop(0), refs.pop(0)
                givens = [
                    pltpu.make_async_copy(source, target, x_sem.at[index])
                    for index, (source, target) in enumerate(zip(firsts, (branch, mid_grad)))
                ]
                for given in givens:
                    given.start()
            project_load = start_pieces(lists.pop(0), info, spots, full_o, p_sem, 0, (0, width), share)
            sames = [one is two for one, two in pairs]
            pairs[1] = tuple(one.at[:, pl.ds(mixed_at, width)] for one in pairs[1])
            takes = [
                start_chosen(section, *pairs[index], target, x_sem.at[3 + index], sames[index])
                for index, target in ((1, mixed), (0, packed), (2, logs), (3, x))
            ]
            last_load = start_pieces(lists.pop(0), info, spots, full_q, q_sem, 0, (0, 3 * width), share)
            if not feed:
                wait_all(givens)
        if feed:
            take.wait()
            hidden_back_stage(
                grad, vec, info, keep, slope, middle, hidden, second, mid_grad, branch, feed_sums,
                inner_sums, full_out, full, deep, first_load, load, for_slope, for_middle, tallies,
                count, parts,
            )
        if attend:
            attention_back_stage(
                x, vec, branch, mid_grad, packed, mixed, logs, grads, result, sums, down, normal,
                stage, full_o, full_q, project_load, last_load, takes, tallies, count, length,
            )

    outs = []
    scratch = [pltpu.VMEM((4, 8, width), F32), pltpu.SemaphoreType.DMA((7,))]
    flops = 0
    if feed:
        outs += [((rows, inner + 5 * width), BF16)] if both else [((rows, inner), BF16), ((rows, width), BF16)]
        outs += [
            ((8, width), F32),
            ((1, inner), F32),
        ]
        if not both:
            outs += [((rows, width), F32)]
        scratch += [
            pltpu.VMEM((rows, width), BF16),
            pltpu.VMEM((rows, inner), BF16),
            pltpu.VMEM((rows, width), F32),
            pltpu.VMEM((rows, width), F32),
            pltpu.VMEM((inner, width), BF16),
            pltpu.VMEM((width, inner), BF16),
            pltpu.SemaphoreType.DMA((1, many)),
            pltpu.SemaphoreType.DMA((1, many)),
        ]
        scratch += [pltpu.VMEM((rows, width), F32 if both else BF16)]
        flops += 4 * rows * width * inner
    if attend:
        outs += [] if both else [((rows, 3 * width), BF16)]
        outs += [((rows, width), BF16), ((8, width), F32)]
        scratch += [
            pltpu.VMEM((rows, width), BF16),
            pltpu.VMEM((rows, 3 * width), BF16),
            pltpu.VMEM((rows, width), BF16),
            pltpu.VMEM((count, HEADS, space), F32),
            pltpu.VMEM((rows, width), BF16),
            pltpu.VMEM((rows, width), F32),
            pltpu.VMEM((count, HEADS, 2 * pair), F32),
            pltpu.VMEM((width, width), BF16),
            pltpu.VMEM((width, 3 * width), BF16),
            pltpu.SemaphoreType.DMA((1, many)),
            pltpu.SemaphoreType.DMA((1, many)),
        ]
        if not feed:
            scratch += [pltpu.VMEM((rows, width), BF16), pltpu.VMEM((rows, width), F32)]
        flops += 2 * rows * width * (4 * width + 5 * space)
    weights = (flat(reduce) + flat(wide) if feed else []) + (
        flat(wide) + flat(qkv) if attend else []
    )
    return call(
        body,
        "backward" + "_feed" * feed + "_attend" * attend,
        plain + operands + weights + [params, meta],
        [ANY] * (len(plain) + len(operands) + len(weights)) + [VMEM, SMEM],
        outs,
        scratch,
        flops,
        weight,
    )


def weight_gradient(
    lefts, rights, meta, parts, blocks, quarter, rows_of, columns_of, name, weight=LIGHT
):
    terms = len(lefts)
    first_row, height = rows_of
    first_column, breadth = columns_of
    step = breadth // 2
    rows = lefts[0].shape[0]
    operands = list(lefts)
    places = []
    for pair in rights:
        found = []
        for array, _ in pair:
            if not any(array is other for other in operands):
                operands.append(array)
            found.append(next(i for i, other in enumerate(operands) if other is array))
        places.append(found)

    def body(*refs):
        sources, info = refs[: len(operands)], refs[len(operands)]
        results = refs[len(operands) + 1 : len(operands) + 1 + len(blocks)]
        left_full, right_full, l_sem, r_sem = refs[len(operands) + 1 + len(blocks) :]
        section = info[parts]

        def start_lefts():
            loads = [[] for _ in blocks]
            for index, block in reversed(list(enumerate(blocks))):
                start = pl.multiple_of(info[block] * quarter + first_row, 128)
                for term in range(terms):
                    copy = pltpu.make_async_copy(
                        sources[term].at[:, pl.ds(start, height)],
                        left_full.at[index, pl.ds(term * rows, rows)],
                        l_sem.at[index, term],
                    )
                    copy.start()
                    loads[index].append(copy)
            return loads

        waits = [[], []]
        for cut in range(2):
            for term in range(terms):
                sides = [
                    sources[place].at[:, pl.ds(column + first_column + cut * step, step)]
                    for place, (_, column) in zip(places[term], rights[term])
                ]
                same = rights[term][0] is rights[term][1]
                target = right_full.at[cut, pl.ds(term * rows, rows)]
                waits[cut].append(start_chosen(section, *sides, target, r_sem.at[cut, term], same))
            if cut == 0:
                loads = start_lefts()
        for cut in range(2):
            wait_all(waits[cut])
            for index in reversed(range(len(blocks))):
                if cut == 0:
                    wait_all(loads[index])
                done = contract(left_full[index], right_full[cut], 0, 0)
                results[index][:, cut * step : (cut + 1) * step] = done.astype(BF16)

    return call(
        body,
        name,
        operands + [meta],
        [ANY] * len(operands) + [SMEM],
        [((height, breadth), BF16)] * len(blocks),
        [
            pltpu.VMEM((len(blocks), terms * rows, height), BF16),
            pltpu.VMEM((2, terms * rows, step), BF16),
            pltpu.SemaphoreType.DMA((len(blocks), terms)),
            pltpu.SemaphoreType.DMA((2, terms)),
        ],
        2 * len(blocks) * terms * rows * height * breadth,
        weight,
    )


def after(value, *earlier):
    return lax.optimization_barrier((value,) + earlier)[0]


def added(*values):
    total = values[0].astype(F32)
    for value in values[1:]:
        total = total + value.astype(F32)
    return total.astype(values[0].dtype)


class FourByFour:
    parts = 4
    blocks = (0, 2)

    def __init__(self):
        self.group = lax.axis_index("group")
        self.place = lax.axis_index("replica")
        self.order = [self.group ^ part for part in range(4)]
        odd = self.place % 2
        near = [4 * self.order[part] for part in (0, 1)]
        far = [4 * self.order[part] for part in (2, 3)]
        self.spots = near + [block + place for block in far for place in (2 * odd, 2 - 2 * odd)]
        self.last_spots = near + [block + place for block in far for place in (odd, 3 - 3 * odd)]

    def core(self, block):
        return lax.ppermute(block, "group", [(i, i ^ 1) for i in range(4)])

    def across(self, block):
        return lax.ppermute(block, "group", [(i, i ^ 2) for i in range(4)])

    def beside(self, block):
        return lax.ppermute(block, "replica", [(i, i ^ 1) for i in range(4)])

    def gather_small(self, block):
        near, far = self.core(block), self.across(block)
        return [block, near, far, self.core(far)]

    def gather(self, blocks, prepare):
        odd = self.place % 2
        quarters = [block.shape[0] // 4 for block in blocks]
        asked = [
            lax.dynamic_slice_in_dim(block, 2 * odd * rows, 2 * rows)
            for block, rows in zip(blocks[:-1], quarters)
        ]
        asked.append(lax.dynamic_slice_in_dim(blocks[-1], odd * quarters[-1], 3 * quarters[-1]))
        halves, sibling = [], []
        for index, block in enumerate(blocks):
            halves.append(self.across(after(asked[index], *halves[: max(index - 1, 0)])))
            sibling.append(self.core(after(block, sibling[-1]) if index else block))
        others = []
        tokens = prepare(halves[0]) + asked[2:]
        swaps = halves[:-1] + [
            lax.dynamic_slice_in_dim(halves[-1], 2 * odd * quarters[-1], quarters[-1])
        ]
        for index, half in enumerate(swaps):
            earlier = others[-1:] if index == 1 else []
            others.append(self.beside(after(half, *earlier, *(tokens if index == 1 else []))))
        self.swapped = others[-1]

        def pieces(index, before_one=(), before_two=()):
            one, two = after(halves[index], *before_one), after(others[index], *before_two)
            return [
                [blocks[index]],
                [sibling[index]],
                [halves[index], others[index]],
                [self.core(one), self.core(two)],
            ]

        return [partial(pieces, index) for index in range(len(blocks))]

    def shared(self, block):
        return [block, self.core(block)]

    def total(self, blocks):
        passed = self.across(blocks[1])
        token = yield
        mine = added(after(blocks[0], token), passed)
        inward = lax.ppermute(mine, "replica", [(0, 1), (3, 2)])
        token = yield mine
        joined = added(after(mine, token), inward)
        crossing = lax.ppermute(joined, "replica", [(1, 2), (2, 1)])
        token = yield joined
        summed = added(after(joined, token), crossing)
        outward = lax.ppermute(summed, "replica", [(1, 0), (2, 3)])
        token = yield summed
        inner = (self.place == 1) | (self.place == 2)
        yield jnp.where(inner, after(summed, token), outward)


class General:
    def __init__(self):
        self.parts = lax.axis_size("group")
        self.blocks = tuple(range(self.parts))
        self.order = [jnp.int32(part) for part in range(self.parts)]
        self.spots = self.last_spots = [4 * part for part in self.order]

    def gather_small(self, block):
        whole = lax.all_gather(block, "group", axis=0)
        return [whole[part] for part in range(self.parts)]

    def gather(self, blocks, prepare):
        prepare(blocks[0])
        self.swapped = blocks[0]
        found = [[[piece] for piece in self.gather_small(block)] for block in blocks]
        return [lambda *tokens, groups=groups: groups for groups in found]

    def shared(self, block):
        return [block]

    def total(self, blocks):
        yield
        mine = lax.psum_scatter(jnp.stack(blocks), "group", scatter_dimension=0)
        yield mine
        yield lax.psum(mine, "replica")


def shifted(block, distance):
    devices = range(lax.axis_size("section"))
    route = [(i - distance, i) for i in devices if i - distance in devices]
    return lax.ppermute(block, "section", route)


def in_order(pieces, order):
    place = jnp.stack(order)
    stacked = []
    for block in range(len(pieces)):
        chosen = pieces[0]
        for part in range(1, len(pieces)):
            chosen = jnp.where(place[part] == block, pieces[part], chosen)
        stacked.append(chosen)
    return jnp.stack(stacked)


class Sequence:
    def __init__(self, net, token):
        self.net, self.sums, self.results, self.token = net, {}, {}, token

    def now(self, value):
        return after(value, self.token)

    def ran(self, value):
        self.token = value

    def add(self, name, blocks):
        self.sums[name] = self.net.total(blocks)
        next(self.sums[name])

    def step(self, *names):
        for name in names:
            try:
                self.results[name] = self.token = self.sums[name].send(self.token)
            except StopIteration:
                continue

    def finish(self, name):
        while True:
            try:
                self.results[name] = self.sums[name].send(self.token)
            except StopIteration:
                return self.results[name]


def per_device(
    images,
    cotangent,
    counts,
    qkv_weight,
    out_weight,
    expand_weight,
    reduce_weight,
    norm_gains,
    biases,
    expand_bias,
):
    micro, slots, length, width = images.shape
    space = padded(length)
    section = lax.axis_index("section")
    first = section == 0
    sizes = (lax.axis_size("group"), lax.axis_size("replica"))
    net = FourByFour() if sizes == (4, 4) else General()
    parts = net.parts
    share = width // parts
    batches = tuple(range(micro))

    def rows_of(array):
        fulls = [jnp.pad(array[batch], ((0, 0), (0, space - length), (0, 0))) for batch in batches]
        return [full.reshape(slots * space, width) for full in fulls]

    def images_of(array):
        return array.reshape(slots, space, width)[:, :length]

    small = jnp.concatenate([norm_gains[0], biases[0], expand_bias[0].reshape(-1, share)])
    slot = jnp.arange(slots, dtype=jnp.int32)
    alive = [(slot < counts[batch, 0]).astype(jnp.int32) for batch in batches]
    head = jnp.stack(net.order + [section]).astype(jnp.int32)

    spots = jnp.stack(net.spots + net.last_spots).astype(jnp.int32)

    def meta(living):
        return jnp.concatenate([head, living, spots])

    infos = [meta(alive[batch]) for batch in batches]
    pieces = net.gather_small(small)
    vectors = in_order(pieces, net.order)
    top = vectors[:, :8].transpose(1, 0, 2).reshape(8, width)
    bottom = vectors[:, 8:].reshape(-1, width)
    params = jnp.concatenate([top, bottom]).astype(F32)
    slot = jnp.arange(slots, dtype=jnp.int32)
    alive = [(slot < counts[batch, 0]).astype(jnp.int32) for batch in batches]
    head = jnp.stack(net.order + [section]).astype(jnp.int32)
    spots = jnp.stack(net.spots + net.last_spots).astype(jnp.int32)

    def meta(living):
        return jnp.concatenate([head, living, spots])

    infos = [meta(alive[batch]) for batch in batches]
    inputs, targets = [], []

    def prepare(token):
        inputs.extend(rows_of(after(images, token)))
        targets.extend(rows_of(after(cotangent, token)))
        return [params, *inputs, *targets, *infos]

    qkv, wide, reduce = net.gather(
        [qkv_weight[0], jnp.concatenate([out_weight[0], expand_weight[0]], axis=1), reduce_weight[0]],
        prepare,
    )

    qkv = qkv()
    attended = []
    for batch in batches:
        start = inputs[batch] if batch == 0 else after(inputs[batch], attended[-1][0])
        attended.append(
            forward(start, start, None, qkv, None, params, infos[batch], slots, length)
        )
    wide = wide(attended[0], attended[-1])
    fed = []
    for batch in batches:
        start = inputs[batch] if batch == 0 else after(inputs[batch], fed[-1][0], net.swapped)
        fed.append(
            forward(start, start, attended[batch][0], None, wide, params, infos[batch], slots, length)
        )
    reduce = reduce(attended[-1], fed[0][:1])
    early, incoming = [], []
    for batch in batches:
        middle, active = fed[batch]
        if batch:
            active = after(active, early[-1])
        early.append(output_forward(middle, active, reduce, params, infos[batch], slots))
        incoming.append(shifted(early[batch], 1))

    inner = wide[0][0].shape[1] - width
    mixed_at = inner + width
    kept, lefts, rights, results = [], [], [], []
    sums_a, sums_b, sums_c, returning = [], [], [], []
    token = early[-1]
    for batch in batches:
        start = after(incoming[batch], token)
        left, packed, logs, middle, slope = forward(
            inputs[batch], start, None, qkv, wide, params, infos[batch], slots, length, 8.0
        )
        kept.append((slope, middle, packed, left, logs))
        lefts.append(net.shared(left))
        if batch == 0:
            pair, sides = (targets[0], targets[0]), (kept[0], kept[0])
            lower, chosen = incoming[0], infos[0]
        else:
            pair = (returning[batch - 1], targets[batch])
            sides = (kept[batch - 1], kept[batch])
            lower = inputs[batch - 1]
            chosen = meta(jnp.where(first, alive[batch - 1], alive[batch]))
        right, some, more, result, rest = backward(
            pair, lower, incoming[batch], sides[0], sides[1], reduce, wide, qkv, params, chosen,
            slots, length, mixed_at, 8.0,
        )
        token = result
        rights.append(net.shared(right))
        results.append(result)
        sums_a.append(some)
        sums_b.append(more)
        sums_c.append(rest)
        returning.append(shifted(result, -1))
    late = []
    for batch in batches:
        ready = lefts[batch][1:] + (rights[batch][1:] if batch < micro - 1 else [])
        active = after(kept[batch][3], token, *ready)
        late.append(output_forward(kept[batch][1], active, reduce, params, infos[batch], slots, 8.0))
        token = late[-1]

    last = micro - 1
    run = Sequence(net, token)
    arrived = run.now(returning[last])
    living = jnp.repeat(alive[last] > 0, space)[:, None]
    masked = net.shared(jnp.where(living, arrived, jnp.zeros_like(arrived)))
    many = len(masked)

    def gradient(name, left_at, final, final_at, right_at, quarter, rows, columns, weight=LIGHT):
        left = [lefts[batch][side] for batch in batches for side in range(many)]
        right = []
        for batch in batches:
            for side in range(many):
                upper = (rights[batch][side], right_at)
                lower = (final[side], final_at) if batch == last else (rights[batch + 1][side], right_at)
                right.append((lower, upper))
        blocks = weight_gradient(
            left, right, run.now(head), parts, net.blocks, quarter, (left_at + rows[0], rows[1]), columns,
            name, weight,
        )
        run.ran(blocks[0])
        return blocks

    half, at = inner // 2, inner + 2 * width
    deep = inner // parts
    state = {"mid": None, "rows": None}

    def feed_back(weight):
        start = run.now(arrived)
        hidden, branch, some, more, mid = backward(
            (start, start), None, None, kept[last], kept[last], reduce, wide, None, params, infos[last],
            slots, length, mixed_at, weight,
        )
        run.ran(hidden)
        state.update(mid=mid, branch=branch, hidden=net.shared(hidden), branches=net.shared(branch))
        sums_a.append(some)
        sums_b.append(more)

    def attend_back(weight):
        start = run.now(after(state["branch"], *state["branches"][1:], *state["hidden"][1:]))
        grads, result, rest = backward(
            (start, state["mid"]), inputs[last], inputs[last], kept[last], kept[last], None, wide, qkv,
            params, infos[last], slots, length, mixed_at, weight,
        )
        run.ran(result)
        state["grads"] = net.shared(grads)
        results.append(result)
        sums_c.append(rest)

    def reduce_part(index, weight):
        step = deep // 2
        return gradient(
            "reduce", 0, masked, 0, inner + width, deep, (index * step, step), (0, width), weight
        )

    def expand_part(begin, size, weight):
        return gradient("expand", inner, state["hidden"], 0, 0, share, (0, share), (begin, size), weight)

    def project_part(weight):
        return gradient(
            "project", mixed_at, state["branches"], 0, inner, share, (0, share), (0, width), weight
        )

    def qkv_part(begin, size, weight):
        return gradient("qkv", at, state["grads"], 0, at, share, (0, share), (begin, size), weight)

    def over_batches(values):
        return sum(jnp.where(first, values[batch + 1], values[batch]) for batch in batches)

    def small_sums():
        some, more, rest = over_batches(sums_a), over_batches(sums_b), over_batches(sums_c)
        rows = jnp.concatenate([rest[0:1], some[0:1], rest[1:2], some[1:2], rest[2:4], some[2:4]])
        rows = rows.reshape(8, parts, share).transpose(1, 0, 2)
        rows = jnp.concatenate([rows, more.reshape(parts, -1, share)], axis=1)
        rows = sum(net.shared(run.now(rows)))
        rows = jnp.stack(
            [lax.dynamic_index_in_dim(rows, net.order[block], 0, keepdims=False) for block in net.blocks]
        )
        state["count"] = rows.shape[1]
        state["rows"] = rows.reshape(len(net.blocks), -1).astype(BF16)

    def with_small(blocks):
        step, rows = blocks[0].shape[1], state["rows"]
        rows = jnp.pad(rows, ((0, 0), (0, -rows.shape[1] % (16 * step)))).reshape(len(blocks), -1, step)
        return [jnp.concatenate([block, row]) for block, row in zip(blocks, rows)]

    outputs = []

    def assemble():
        index = len(outputs)
        low, up = (early + results[1:])[index], (late + results[:-1])[index]
        outputs.append(images_of(jnp.where(first, run.now(low), up)))

    def joined(axis, *names):
        found = [run.finish(name) for name in names]
        found = [value[:share] if name == LAST.lower() else value for name, value in zip(names, found)]
        return jnp.concatenate(found, axis=axis).astype(F32)[None]

    shapes = {"q": (1, "q0", "q1"), "p": (1, "p0"), "e": (1, "e0", "e1"), "r": (0, "r0", "r1")}
    gradients = {}

    third = 3 * width // 2
    kernels = {
        "R0": lambda weight: reduce_part(0, weight),
        "R1": lambda weight: reduce_part(1, weight),
        "E0": lambda weight: expand_part(0, half, weight),
        "E1": lambda weight: expand_part(half, half, weight),
        "Q0": lambda weight: qkv_part(0, third, weight),
        "Q1": lambda weight: qkv_part(third, third, weight),
        "P0": lambda weight: project_part(weight),
    }
    for entry in " ".join(PLAN).split():
        name, _, factor = entry.partition("*")
        weight = float(factor or HEAVY) if "*" in entry else LIGHT
        if name in kernels:
            blocks = kernels[name](weight)
            if name == LAST:
                blocks = with_small(blocks)
            run.add(name.lower(), blocks)
        elif name == "BF":
            feed_back(weight)
        elif name == "BA":
            attend_back(weight)
        elif name == "V":
            small_sums()
        elif name == "O":
            assemble()
        elif name[0] == "C":
            gradients[name[1]] = joined(*shapes[name[1]])
        else:
            run.step(name)
    while len(outputs) < 2 * micro:
        assemble()
    for name in shapes:
        if name not in gradients:
            gradients[name] = joined(*shapes[name])
    count = state["count"]
    vector = run.finish(LAST.lower())[share:].reshape(-1)[: count * share].reshape(count, share).astype(F32)
    return (
        jnp.stack(outputs[:micro])[None],
        jnp.stack(outputs[micro:])[None],
        gradients["q"],
        gradients["p"],
        gradients["e"],
        gradients["r"],
        vector[None, 0:2],
        vector[None, 2:8],
        vector[8:].reshape(1, -1),
    )


def solution(mesh):
    placed = (
        P(None, ("group", "replica"), None, None),
        P(None, ("group", "replica"), None, None),
        P(None, ("group", "replica")),
        P("section", "group", None),
        P("section", "group", None),
        P("section", "group", None),
        P("section", "group", None),
        P("section", None, "group"),
        P("section", None, "group"),
        P("section", "group"),
    )
    return jax.shard_map(
        per_device,
        mesh=mesh,
        in_specs=placed,
        out_specs=(
            P("section", None, ("group", "replica"), None, None),
            P("section", None, ("group", "replica"), None, None),
            P("section", "group", None),
            P("section", "group", None),
            P("section", "group", None),
            P("section", "group", None),
            P("section", None, "group"),
            P("section", None, "group"),
            P("section", "group"),
        ),
        check_vma=False,
    )
```

```python
from functools import partial

import jax
import jax.numpy as jnp
from jax import lax
from jax.experimental import pallas as pl
from jax.experimental.pallas import tpu as pltpu
from jax.sharding import PartitionSpec as P

HEADS = 16
EPSILON = 1e-06
NEGATIVE = -1e30
F32 = jnp.float32
BF16 = jnp.bfloat16
LIGHT, HEAVY = 1.0 / 64, 16.0
PLAN = (
    "R0 BF r0 R1*",
    "BA r0 r1 E0*",
    "r1 Q0 r0 e0",
    "E1 q0 r1 e0",
    "r0 Q1 e1 q0",
    "r1 e0 V P0",
    "e1 q1 O q0",
    "e0 p0 q1 O",
    "e1 q0 p0 O",
    "O q1 e1 p0",
    "q1 p0",
)
LAST = "P0"
VMEM_LIMIT = 58 * 2**20
ROOT_HALF = 0.7071067811865476
ROOT_TAU = 0.3989422804014327
ANY = pl.BlockSpec(memory_space=pl.ANY)
VMEM = pl.BlockSpec(memory_space=pltpu.VMEM)
SMEM = pl.BlockSpec(memory_space=pltpu.SMEM)
GAIN0, GAIN1, SHIFT0, SHIFT1, QUERY, VALUE, OUT, FEED, EXPAND = range(9)


def padded(length):
    return -(-length // 16) * 16


def contract(left, right, left_dim, right_dim):
    return lax.dot_general(
        left, right, (((left_dim,), (right_dim,)), ((), ())), preferred_element_type=F32
    )


def standardized(values):
    center = values - jnp.mean(values, axis=-1, keepdims=True)
    spread = jnp.mean(center * center, axis=-1, keepdims=True)
    scale = lax.rsqrt(spread + EPSILON)
    return center * scale, scale


def norm_pull(grad, gain, unit, scale):
    scaled = grad * gain
    mean = jnp.mean(scaled, axis=-1, keepdims=True)
    along = jnp.mean(scaled * unit, axis=-1, keepdims=True)
    return scale * (scaled - mean - unit * along)


def call(body, name, operands, specs, outs, scratch, flops, weight=LIGHT):
    moved = sum(o.size * o.dtype.itemsize for o in operands)
    out_shape = [jax.ShapeDtypeStruct(shape, dtype) for shape, dtype in outs]
    moved += sum(o.size * o.dtype.itemsize for o in out_shape)
    return pl.pallas_call(
        body,
        out_shape=out_shape,
        in_specs=specs,
        out_specs=[VMEM] * len(outs),
        scratch_shapes=scratch,
        compiler_params=pltpu.CompilerParams(vmem_limit_bytes=VMEM_LIMIT),
        cost_estimate=pl.CostEstimate(flops=int(flops * weight), bytes_accessed=int(moved * weight), transcendentals=0),
        name=name,
    )(*operands)


def flat(groups):
    return [piece for group in groups for piece in group]


def start_pieces(pieces, info, first, target, sems, slot, columns, block, shift=0):
    begin, size = columns
    columns = pl.ds(begin, size)
    copies = []
    for index, piece in enumerate(pieces):
        rows = piece.shape[0]
        where = pl.multiple_of(info[first + index] * (block // 4), block // 4)
        copy = pltpu.make_async_copy(
            piece.at[:, pl.ds(begin + shift, size)],
            target.at[pl.ds(where, rows), columns],
            sems.at[slot, index],
        )
        copy.start()
        copies.append(copy)
    return copies


def wait_all(copies):
    for copy in copies:
        copy.wait()


def start_chosen(section, lower, upper, target, sem, same=False):
    if lower is upper or same:
        copy = pltpu.make_async_copy(lower, target, sem)
        copy.start()
        return copy

    @pl.when(section == 0)
    def _():
        pltpu.make_async_copy(lower, target, sem).start()

    @pl.when(section != 0)
    def _():
        pltpu.make_async_copy(upper, target, sem).start()

    return pltpu.make_async_copy(lower, target, sem)


def eights(values):
    return jnp.sum(values.reshape(-1, 8, values.shape[-1]), axis=0)


def attention_stage(x, vec, norm, packed, mixed, logs, columns, full, loads, count, length):
    rows, width = x.shape
    space = rows // count
    head = width // HEADS
    pair = 2 * head
    scale = head**-0.5
    gain, shift = vec[GAIN0 : GAIN0 + 1], vec[SHIFT0 : SHIFT0 + 1]

    def step(here):
        unit, _ = standardized(x[here].astype(F32))
        norm[here] = (unit * gain + shift).astype(BF16)

    step(pl.ds(0, rows))
    for block in range(3):
        wait_all(loads[block])
        done = contract(norm[...], full[:, block * width : (block + 1) * width], 1, 0)
        if block != 1:
            bias = QUERY if block == 0 else VALUE
            done = done + vec[bias : bias + 1]
        packed[:, block * width : (block + 1) * width] = done.astype(BF16)
    lane = lax.broadcasted_iota(jnp.int32, (space, pair), 1)
    left = lane < head
    live = lax.broadcasted_iota(jnp.int32, (space, pair), 0) < length
    key_live = lax.broadcasted_iota(jnp.int32, (space, space), 1) < length
    columns[...] = jnp.zeros_like(columns)

    def heads(index, carry):
        for image in range(count):
            span = pl.ds(image * space, space)

            def part(block):
                offset = pl.multiple_of(block * width + index * pair, pair)
                return packed[span, pl.ds(offset, pair)]

            query, key, value = part(0).astype(F32) * scale, part(1), part(2).astype(F32)
            found = []
            tops = []
            for side in range(2):
                mine = left if side == 0 else ~left
                asked = jnp.where(mine, query, 0.0).astype(BF16)
                held = jnp.where(live, jnp.where(mine, value, 1.0), 0.0).astype(BF16)
                scores = jnp.where(key_live, contract(asked, key, 1, 1), NEGATIVE)
                top = jnp.max(scores, axis=-1, keepdims=True)
                raised = jnp.exp(scores - top).astype(BF16)
                found.append(contract(raised, held, 1, 0))
                tops.append(top)
            inside = jnp.where(left, found[0], found[1])
            total = jnp.where(left, found[1], found[0])
            turned = pltpu.roll(total, head, 1)
            offset = pl.multiple_of(index * pair, pair)
            mixed[span, pl.ds(offset, pair)] = (inside / turned).astype(BF16)
            if logs is None:
                continue
            logged = jnp.where(left, tops[0], tops[1]) + jnp.log(turned)
            columns[image] = jnp.where((lane & (head - 1)) == index, logged, columns[image])
        return carry

    lax.fori_loop(0, HEADS // 2, heads, 0, unroll=4)
    if logs is not None:
        for image in range(count):
            rows_of = columns[image].T
            logs[image, 0 : HEADS // 2] = rows_of[0 : HEADS // 2]
            logs[image, HEADS // 2 : HEADS] = rows_of[head : head + HEADS // 2]


def hidden_stage(x, vec, mixed, middle, active, second, slope, full_out, full, first_load, loads):
    rows, width = x.shape
    wait_all(first_load)
    gain, shift, bias = vec[GAIN1 : GAIN1 + 1], vec[SHIFT1 : SHIFT1 + 1], vec[OUT : OUT + 1]
    middle[...] = contract(mixed[...], full_out[...], 1, 0)

    def step(here):
        total = middle[here] + x[here].astype(F32) + bias
        middle[here] = total
        unit, _ = standardized(total)
        second[here] = (unit * gain + shift).astype(BF16)

    step(pl.ds(0, rows))
    for block, load in enumerate(loads):
        wait_all(load)
        part = slice(block * width, (block + 1) * width)
        value = contract(second[...], full[:, part], 1, 0) + vec[EXPAND + block : EXPAND + block + 1]
        share = 0.5 + 0.5 * lax.erf(value * ROOT_HALF)
        active[:, part] = (value * share).astype(BF16)
        if slope is not None:
            density = ROOT_TAU * jnp.exp(-0.5 * value * value)
            slope[:, part] = (share + value * density).astype(BF16)


def forward(
    lower, upper, mixed_in, qkv, wide, params, meta, count, length, weight=LIGHT
):
    rows, width = lower.shape
    space = rows // count
    pair = 2 * width // HEADS
    attend, feed = qkv is not None, wide is not None
    both = attend and feed
    parts = len(qkv if attend else wide)
    many = len(flat(qkv if attend else wide))
    spots = parts + 1 + count
    inner = wide[0][0].shape[1] - width if feed else 0
    share = width // parts
    blocks = inner // width
    same = lower is upper

    def body(*refs):
        refs = list(refs)
        low = refs.pop(0)
        up = low if same else refs.pop(0)
        if not attend:
            arrived = refs.pop(0)
        lists = [[refs.pop(0) for _ in range(many)] for _ in range(attend + 2 * feed)]
        vec, info = refs.pop(0), refs.pop(0)
        if both:
            left, packed, logs, middle, slope = (refs.pop(0) for _ in range(5))
            active, second, mixed, norm = (
                left.at[:, pl.ds(start, size)]
                for start, size in ((0, inner), *((inner + width * i, width) for i in range(3)))
            )
        elif attend:
            mixed = refs.pop(0)
        else:
            middle, active = refs.pop(0), refs.pop(0)
        x, x_sem = refs.pop(0), refs.pop(0)
        section = info[parts]
        take = start_chosen(section, low, up, x, x_sem.at[0])
        if attend:
            columns, full, a_sem = (refs.pop(0) for _ in range(3))
            if not both:
                norm, packed, logs = refs.pop(0), refs.pop(0), None
            weight = lists.pop(0)
            loads = [
                start_pieces(weight, info, spots, full, a_sem, block, (block * width, width), share)
                for block in range(3)
            ]
        if feed:
            full_out, full_in, o_sem, w_sem = (refs.pop(0) for _ in range(4))
            if not attend:
                mixed, second, slope = refs.pop(0), refs.pop(0), None
                extra = pltpu.make_async_copy(arrived, mixed, x_sem.at[1])
                extra.start()
            first_load = start_pieces(lists[0], info, spots, full_out, o_sem, 0, (0, width), share)
            inner_loads = [
                start_pieces(lists[1], info, spots, full_in, w_sem, block, (block * width, width), share, width)
                for block in range(blocks)
            ]
        take.wait()
        if attend:
            attention_stage(
                x, vec, norm, packed, mixed, logs, columns, full, loads, count, length
            )
        if feed:
            if not attend:
                extra.wait()
            hidden_stage(
                x, vec, mixed, middle, active, second, slope, full_out, full_in, first_load,
                inner_loads,
            )

    outs, inputs = [], [lower] if same else [lower, upper]
    scratch = [pltpu.VMEM((rows, width), BF16), pltpu.SemaphoreType.DMA((2,))]
    flops = 0
    if attend:
        outs += [
            ((rows, width), BF16),
            ((rows, 3 * width), BF16),
            ((rows, width), BF16),
            ((count, HEADS, space), F32),
        ]
        scratch += [
            pltpu.VMEM((count, space, pair), F32),
            pltpu.VMEM((width, 3 * width), BF16),
            pltpu.SemaphoreType.DMA((3, many)),
        ]
        if not feed:
            scratch += [pltpu.VMEM((rows, width), BF16), pltpu.VMEM((rows, 3 * width), BF16)]
        flops += 2 * rows * width * (3 * width + 2 * space)
    else:
        inputs += [mixed_in]
    if feed:
        outs += [
            ((rows, width), F32),
            ((rows, inner), BF16),
            ((rows, width), BF16),
            ((rows, inner), BF16),
        ]
        scratch += [
            pltpu.VMEM((width, width), BF16),
            pltpu.VMEM((width, inner), BF16),
            pltpu.SemaphoreType.DMA((1, many)),
            pltpu.SemaphoreType.DMA((blocks, many)),
        ]
        if not attend:
            scratch += [pltpu.VMEM((rows, width), BF16), pltpu.VMEM((rows, width), BF16)]
        flops += 2 * rows * width * (width + inner)
    if both:
        outs = [((rows, inner + 3 * width), BF16), outs[1], outs[3], outs[4], outs[7]]
    else:
        outs = [outs[2]] if attend else outs[:2]
    weights = (flat(qkv) if attend else []) + (2 * flat(wide) if feed else [])
    return call(
        body,
        "forward" + "_attend" * attend + "_feed" * feed,
        inputs + weights + [params, meta],
        [ANY] * (len(inputs) + len(weights)) + [VMEM, SMEM],
        outs,
        scratch,
        flops,
        weight,
    )


def output_forward(middle, active, pieces, params, meta, count, weight=LIGHT):
    rows, width = middle.shape
    inner = sum(piece.shape[0] for piece in flat(pieces))
    space = rows // count
    parts, many = len(pieces), len(flat(pieces))
    spots = parts + 1 + count
    deep = inner // parts

    def body(*refs):
        refs = list(refs)
        mid_in, act_in = refs.pop(0), refs.pop(0)
        reduce = [refs.pop(0) for _ in range(many)]
        vec, info, result, mid, act, full, total, x_sem, w_sem = refs
        every = start_pieces(reduce[:1], info, spots + many, full, w_sem, 0, (0, width), deep)
        columns = [pl.ds(pl.multiple_of(info[index] * deep, deep), deep) for index in range(parts)]
        takes = []
        for index in range(parts):
            takes.append(
                pltpu.make_async_copy(act_in.at[:, columns[index]], act.at[index], x_sem.at[index])
            )
            takes[-1].start()
            if index == 0:
                every += start_pieces(
                    reduce[1:], info, spots + many + 1, full, w_sem.at[:, pl.ds(1, many - 1)], 0,
                    (0, width), deep,
                )
        last = pltpu.make_async_copy(mid_in, mid, x_sem.at[parts])
        last.start()
        for index, group in enumerate(pieces):
            takes[index].wait()
            wait_all([every.pop(0) for _ in group])
            value = contract(act[index], full[columns[index]], 1, 0)
            if index:
                value = value + total[...]
            if index < parts - 1:
                total[...] = value
        last.wait()
        value = value + mid[...] + vec[FEED : FEED + 1]
        for image in range(count):
            alive = jnp.where(info[parts + 1 + image] > 0, 1.0, 0.0)
            here = slice(image * space, (image + 1) * space)
            result[here] = (value[here] * alive).astype(BF16)

    return call(
        body,
        "output_forward",
        [middle, active] + flat(pieces) + [params, meta],
        [ANY] * (2 + many) + [VMEM, SMEM],
        [((rows, width), BF16)],
        [
            pltpu.VMEM((rows, width), F32),
            pltpu.VMEM((parts, rows, deep), BF16),
            pltpu.VMEM((inner, width), BF16),
            pltpu.VMEM((rows, width), F32),
            pltpu.SemaphoreType.DMA((parts + 1,)),
            pltpu.SemaphoreType.DMA((1, many)),
        ],
        2 * rows * width * inner,
        weight,
    )[0]


def hidden_back_stage(
    grad, vec, info, feed, slope, middle, hidden, second, mid_grad, branch, sums, inner_sums, full_out,
    full, deep, first_load, load, for_slope, for_middle, tallies, count, parts,
):
    rows, width = grad.shape
    space = rows // count
    half = width // 2
    for image in range(count):
        alive = jnp.where(info[parts + 1 + image] > 0, 1.0, 0.0)
        here = slice(image * space, (image + 1) * space)
        feed[here] = (grad[here].astype(F32) * alive).astype(BF16)
    for_slope.wait()
    for index in range(parts):
        wait_all(first_load[index])
        where = pl.multiple_of(info[index] * deep, deep)
        value = contract(feed[...], full_out[pl.ds(where, deep)], 1, 1)
        value = (value * slope[:, pl.ds(where, deep)].astype(F32)).astype(BF16)
        hidden[:, pl.ds(where, deep)] = value
        inner_sums[:, pl.ds(where, deep)] = jnp.sum(value.astype(F32), axis=0, keepdims=True)
    wait_all(load)
    for block in range(2):
        second[:, block * half : (block + 1) * half] = contract(
            hidden[...], full[block * half : (block + 1) * half], 1, 1
        )
    for_middle.wait()
    gain = vec[GAIN1 : GAIN1 + 1]
    tallies[...] = jnp.zeros_like(tallies)

    def step(here):
        unit, scale = standardized(middle[here])
        down = second[here]
        top = feed[here].astype(F32)
        total = top + norm_pull(down, gain, unit, scale)
        low = total.astype(BF16)
        mid_grad[here] = total
        branch[here] = low
        tallies[0] += eights(down * unit)
        tallies[1] += eights(down)
        tallies[2] += eights(low.astype(F32))
        tallies[3] += eights(top)

    step(pl.ds(0, rows))
    for index in range(4):
        sums[index : index + 1] = jnp.sum(tallies[index], axis=0, keepdims=True)


def attention_back_stage(
    x, vec, branch, mid_grad, packed, mixed, logs, grads, result, sums, down, normal, stage, full_out,
    full, first_load, load, takes, tallies, count, length,
):
    rows, width = x.shape
    space = rows // count
    head = width // HEADS
    pair = 2 * head
    scale = head**-0.5
    half = width // 2
    wait_all(first_load)
    down[...] = contract(branch[...], full_out[...], 1, 1).astype(BF16)
    wait_all(takes)
    owner = lax.shift_right_logical(
        lax.broadcasted_iota(jnp.int32, (HEADS, width), 1), head.bit_length() - 1
    )
    chosen = jnp.where(
        owner == lax.broadcasted_iota(jnp.int32, (HEADS, width), 0), 1.0, 0.0
    ).astype(BF16)
    left = lax.broadcasted_iota(jnp.int32, (space, pair), 1) < head
    live = lax.broadcasted_iota(jnp.int32, (space, pair), 0) < length
    key_live = lax.broadcasted_iota(jnp.int32, (space, space), 0) < length
    for image in range(count):
        span = pl.ds(image * space, space)
        product = down[span].astype(F32) * mixed[span].astype(F32)
        coarse = product.astype(BF16)
        fine = (product - coarse.astype(F32)).astype(BF16)
        stage[image, :, 0:space] = contract(chosen, coarse, 1, 1) + contract(chosen, fine, 1, 1)

    def heads(index, carry):
        for image in range(count):
            span = pl.ds(image * space, space)

            def part(block):
                offset = pl.multiple_of(block * width + index * pair, pair)
                return packed[span, pl.ds(offset, pair)]

            query, key, value = part(0), part(1), part(2)
            wide = key.astype(F32) * scale
            value = value.astype(F32)
            arrived = down[span, pl.ds(pl.multiple_of(index * pair, pair), pair)]
            found = []
            for side in range(2):
                mine = left if side == 0 else ~left
                log = logs[image, pl.ds(side * (HEADS // 2) + index, 1), :]
                dot = stage[image, pl.ds(2 * index + side, 1), 0:space]
                scores = contract(jnp.where(mine, wide, 0.0).astype(BF16), query, 1, 1)
                chance = jnp.exp(jnp.where(key_live, scores - log, NEGATIVE))
                back = contract(jnp.where(mine, value, 0.0).astype(BF16), arrived, 1, 1)
                change = (chance * (back - dot)).astype(BF16)
                found.append(
                    (
                        contract(change, key, 0, 0),
                        contract(change, query, 1, 0),
                        contract(chance.astype(BF16), arrived, 1, 0),
                    )
                )
            for block, factor in enumerate((scale, scale, 1.0)):
                total = jnp.where(left, found[0][block], found[1][block]) * factor
                offset = pl.multiple_of(block * width + index * pair, pair)
                grads[span, pl.ds(offset, pair)] = jnp.where(live, total, 0.0).astype(BF16)
        return carry

    lax.fori_loop(0, HEADS // 2, heads, 0, unroll=8)
    wait_all(load)
    for block in range(2):
        normal[:, block * half : (block + 1) * half] = contract(
            grads[...], full[block * half : (block + 1) * half], 1, 1
        )
    gain = vec[GAIN0 : GAIN0 + 1]
    tallies[...] = jnp.zeros_like(tallies)

    def step(here):
        unit, rate = standardized(x[here].astype(F32))
        grad = normal[here]
        tallies[0] += eights(grad * unit)
        tallies[1] += eights(grad)
        result[here] = (mid_grad[here] + norm_pull(grad, gain, unit, rate)).astype(BF16)

    step(pl.ds(0, rows))
    for index in range(2):
        sums[index : index + 1] = jnp.sum(tallies[index], axis=0, keepdims=True)
    sums[2:3] = jnp.sum(grads[:, 0:width].astype(F32), axis=0, keepdims=True)
    sums[3:4] = jnp.sum(grads[:, 2 * width : 3 * width].astype(F32), axis=0, keepdims=True)


def backward(
    start, lower, upper, kept_low, kept_up, reduce, wide, qkv, params, meta, count, length,
    mixed_at, weight=LIGHT,
):
    feed, attend = reduce is not None, qkv is not None
    rows, width = start[0].shape
    space = rows // count
    pair = 2 * width // HEADS
    parts = len(reduce if feed else qkv)
    many = len(flat(reduce if feed else qkv))
    spots = parts + 1 + count
    inner = wide[0][0].shape[1] - width if feed else 0
    deep, share = inner // parts, width // parts
    both = feed and attend
    choices = []
    if feed:
        choices += [(kept_low[0], kept_up[0]), (kept_low[1], kept_up[1])]
        if start[0] is not start[1]:
            choices += [start]
    if attend:
        choices += [(kept_low[index], kept_up[index]) for index in (2, 3, 4)]
        choices += [(lower, upper)]
    plain = [start[0]] if feed and start[0] is start[1] else [] if feed else list(start)
    operands = []
    for low, up in choices:
        operands += [low] if low is up else [low, up]

    def body(*refs):
        refs = list(refs)
        firsts = [refs.pop(0) for _ in plain]
        pairs = []
        for low, up in choices:
            one = refs.pop(0)
            pairs.append((one, one if low is up else refs.pop(0)))
        lists = [[refs.pop(0) for _ in range(many)] for _ in range(2 * feed + 2 * attend)]
        vec, info = refs.pop(0), refs.pop(0)
        section = info[parts]
        if feed:
            if both:
                right = refs.pop(0)
                hidden, branch = right.at[:, pl.ds(0, inner)], right.at[:, pl.ds(inner, width)]
            else:
                hidden, branch = refs.pop(0), refs.pop(0)
            feed_sums, inner_sums = refs.pop(0), refs.pop(0)
            mid_grad = None if both else refs.pop(0)
        if attend:
            grads, result, sums = (refs.pop(0) for _ in range(3)) if not both else (None, refs.pop(0), refs.pop(0))
        if both:
            feed_grad = right.at[:, pl.ds(inner + width, width)]
            grads = right.at[:, pl.ds(inner + 2 * width, 3 * width)]
        tallies, x_sem = refs.pop(0), refs.pop(0)
        if feed:
            grad, slope, middle, second, full_out, full, o_sem, w_sem = (
                refs.pop(0) for _ in range(8)
            )
            if both:
                mid_grad, keep = refs.pop(0), feed_grad
            else:
                keep = refs.pop(0)
            begin = pairs.pop(2) if start[0] is not start[1] else (firsts[0], firsts[0])
            take = start_chosen(section, *begin, grad, x_sem.at[0])
            for_slope = start_chosen(section, *pairs.pop(0), slope, x_sem.at[1])
            every = start_pieces(lists.pop(0), info, spots + many, full_out, o_sem, 0, (0, width), deep)
            first_load = [[every.pop(0) for _ in group] for group in reduce]
            for_middle = start_chosen(section, *pairs.pop(0), middle, x_sem.at[2])
            load = start_pieces(lists.pop(0), info, spots, full, w_sem, 0, (0, inner), share, width)
        if attend:
            x, packed, mixed, logs, down, normal, stage, full_o, full_q, p_sem, q_sem = (
                refs.pop(0) for _ in range(11)
            )
            if not feed:
                branch, mid_grad = refs.pop(0), refs.pop(0)
                givens = [
                    pltpu.make_async_copy(source, target, x_sem.at[index])
                    for index, (source, target) in enumerate(zip(firsts, (branch, mid_grad)))
                ]
                for given in givens:
                    given.start()
            project_load = start_pieces(lists.pop(0), info, spots, full_o, p_sem, 0, (0, width), share)
            sames = [one is two for one, two in pairs]
            pairs[1] = tuple(one.at[:, pl.ds(mixed_at, width)] for one in pairs[1])
            takes = [
                start_chosen(section, *pairs[index], target, x_sem.at[3 + index], sames[index])
                for index, target in ((1, mixed), (0, packed), (2, logs), (3, x))
            ]
            last_load = start_pieces(lists.pop(0), info, spots, full_q, q_sem, 0, (0, 3 * width), share)
            if not feed:
                wait_all(givens)
        if feed:
            take.wait()
            hidden_back_stage(
                grad, vec, info, keep, slope, middle, hidden, second, mid_grad, branch, feed_sums,
                inner_sums, full_out, full, deep, first_load, load, for_slope, for_middle, tallies,
                count, parts,
            )
        if attend:
            attention_back_stage(
                x, vec, branch, mid_grad, packed, mixed, logs, grads, result, sums, down, normal,
                stage, full_o, full_q, project_load, last_load, takes, tallies, count, length,
            )

    outs = []
    scratch = [pltpu.VMEM((4, 8, width), F32), pltpu.SemaphoreType.DMA((7,))]
    flops = 0
    if feed:
        outs += [((rows, inner + 5 * width), BF16)] if both else [((rows, inner), BF16), ((rows, width), BF16)]
        outs += [
            ((8, width), F32),
            ((1, inner), F32),
        ]
        if not both:
            outs += [((rows, width), F32)]
        scratch += [
            pltpu.VMEM((rows, width), BF16),
            pltpu.VMEM((rows, inner), BF16),
            pltpu.VMEM((rows, width), F32),
            pltpu.VMEM((rows, width), F32),
            pltpu.VMEM((inner, width), BF16),
            pltpu.VMEM((width, inner), BF16),
            pltpu.SemaphoreType.DMA((1, many)),
            pltpu.SemaphoreType.DMA((1, many)),
        ]
        scratch += [pltpu.VMEM((rows, width), F32 if both else BF16)]
        flops += 4 * rows * width * inner
    if attend:
        outs += [] if both else [((rows, 3 * width), BF16)]
        outs += [((rows, width), BF16), ((8, width), F32)]
        scratch += [
            pltpu.VMEM((rows, width), BF16),
            pltpu.VMEM((rows, 3 * width), BF16),
            pltpu.VMEM((rows, width), BF16),
            pltpu.VMEM((count, HEADS, space), F32),
            pltpu.VMEM((rows, width), BF16),
            pltpu.VMEM((rows, width), F32),
            pltpu.VMEM((count, HEADS, 2 * pair), F32),
            pltpu.VMEM((width, width), BF16),
            pltpu.VMEM((width, 3 * width), BF16),
            pltpu.SemaphoreType.DMA((1, many)),
            pltpu.SemaphoreType.DMA((1, many)),
        ]
        if not feed:
            scratch += [pltpu.VMEM((rows, width), BF16), pltpu.VMEM((rows, width), F32)]
        flops += 2 * rows * width * (4 * width + 5 * space)
    weights = (flat(reduce) + flat(wide) if feed else []) + (
        flat(wide) + flat(qkv) if attend else []
    )
    return call(
        body,
        "backward" + "_feed" * feed + "_attend" * attend,
        plain + operands + weights + [params, meta],
        [ANY] * (len(plain) + len(operands) + len(weights)) + [VMEM, SMEM],
        outs,
        scratch,
        flops,
        weight,
    )


def weight_gradient(
    lefts, rights, meta, parts, blocks, quarter, rows_of, columns_of, name, weight=LIGHT
):
    terms = len(lefts)
    first_row, height = rows_of
    first_column, breadth = columns_of
    step = breadth // 2
    rows = lefts[0].shape[0]
    operands = list(lefts)
    places = []
    for pair in rights:
        found = []
        for array, _ in pair:
            if not any(array is other for other in operands):
                operands.append(array)
            found.append(next(i for i, other in enumerate(operands) if other is array))
        places.append(found)

    def body(*refs):
        sources, info = refs[: len(operands)], refs[len(operands)]
        results = refs[len(operands) + 1 : len(operands) + 1 + len(blocks)]
        left_full, right_full, l_sem, r_sem = refs[len(operands) + 1 + len(blocks) :]
        section = info[parts]

        def start_lefts():
            loads = [[] for _ in blocks]
            for index, block in reversed(list(enumerate(blocks))):
                start = pl.multiple_of(info[block] * quarter + first_row, 128)
                for term in range(terms):
                    copy = pltpu.make_async_copy(
                        sources[term].at[:, pl.ds(start, height)],
                        left_full.at[index, pl.ds(term * rows, rows)],
                        l_sem.at[index, term],
                    )
                    copy.start()
                    loads[index].append(copy)
            return loads

        waits = [[], []]
        for cut in range(2):
            for term in range(terms):
                sides = [
                    sources[place].at[:, pl.ds(column + first_column + cut * step, step)]
                    for place, (_, column) in zip(places[term], rights[term])
                ]
                same = rights[term][0] is rights[term][1]
                target = right_full.at[cut, pl.ds(term * rows, rows)]
                waits[cut].append(start_chosen(section, *sides, target, r_sem.at[cut, term], same))
            if cut == 0:
                loads = start_lefts()
        for cut in range(2):
            wait_all(waits[cut])
            for index in reversed(range(len(blocks))):
                if cut == 0:
                    wait_all(loads[index])
                done = contract(left_full[index], right_full[cut], 0, 0)
                results[index][:, cut * step : (cut + 1) * step] = done.astype(BF16)

    return call(
        body,
        name,
        operands + [meta],
        [ANY] * len(operands) + [SMEM],
        [((height, breadth), BF16)] * len(blocks),
        [
            pltpu.VMEM((len(blocks), terms * rows, height), BF16),
            pltpu.VMEM((2, terms * rows, step), BF16),
            pltpu.SemaphoreType.DMA((len(blocks), terms)),
            pltpu.SemaphoreType.DMA((2, terms)),
        ],
        2 * len(blocks) * terms * rows * height * breadth,
        weight,
    )


def after(value, *earlier):
    return lax.optimization_barrier((value,) + earlier)[0]


def added(*values):
    total = values[0].astype(F32)
    for value in values[1:]:
        total = total + value.astype(F32)
    return total.astype(values[0].dtype)


class FourByFour:
    parts = 4
    blocks = (0, 2)

    def __init__(self):
        self.group = lax.axis_index("group")
        self.place = lax.axis_index("replica")
        self.order = [self.group ^ part for part in range(4)]
        odd = self.place % 2
        near = [4 * self.order[part] for part in (0, 1)]
        far = [4 * self.order[part] for part in (2, 3)]
        self.spots = near + [block + place for block in far for place in (2 * odd, 2 - 2 * odd)]
        self.last_spots = near + [block + place for block in far for place in (odd, 3 - 3 * odd)]

    def core(self, block):
        return lax.ppermute(block, "group", [(i, i ^ 1) for i in range(4)])

    def across(self, block):
        return lax.ppermute(block, "group", [(i, i ^ 2) for i in range(4)])

    def beside(self, block):
        return lax.ppermute(block, "replica", [(i, i ^ 1) for i in range(4)])

    def gather_small(self, block):
        near, far = self.core(block), self.across(block)
        return [block, near, far, self.core(far)]

    def gather(self, blocks, prepare):
        odd = self.place % 2
        quarters = [block.shape[0] // 4 for block in blocks]
        asked = [
            lax.dynamic_slice_in_dim(block, 2 * odd * rows, 2 * rows)
            for block, rows in zip(blocks[:-1], quarters)
        ]
        asked.append(lax.dynamic_slice_in_dim(blocks[-1], odd * quarters[-1], 3 * quarters[-1]))
        halves, sibling = [], []
        for index, block in enumerate(blocks):
            halves.append(self.across(after(asked[index], *halves[: max(index - 1, 0)])))
            sibling.append(self.core(after(block, sibling[-1]) if index else block))
        others = []
        tokens = prepare(halves[0]) + asked[2:]
        swaps = halves[:-1] + [
            lax.dynamic_slice_in_dim(halves[-1], 2 * odd * quarters[-1], quarters[-1])
        ]
        for index, half in enumerate(swaps):
            earlier = others[-1:] if index == 1 else []
            others.append(self.beside(after(half, *earlier, *(tokens if index == 1 else []))))
        self.swapped = others[-1]

        def pieces(index, before_one=(), before_two=()):
            one, two = after(halves[index], *before_one), after(others[index], *before_two)
            return [
                [blocks[index]],
                [sibling[index]],
                [halves[index], others[index]],
                [self.core(one), self.core(two)],
            ]

        return [partial(pieces, index) for index in range(len(blocks))]

    def shared(self, block):
        return [block, self.core(block)]

    def total(self, blocks):
        passed = self.across(blocks[1])
        token = yield
        mine = added(after(blocks[0], token), passed)
        inward = lax.ppermute(mine, "replica", [(0, 1), (3, 2)])
        token = yield mine
        joined = added(after(mine, token), inward)
        crossing = lax.ppermute(joined, "replica", [(1, 2), (2, 1)])
        token = yield joined
        summed = added(after(joined, token), crossing)
        outward = lax.ppermute(summed, "replica", [(1, 0), (2, 3)])
        token = yield summed
        inner = (self.place == 1) | (self.place == 2)
        yield jnp.where(inner, after(summed, token), outward)


class General:
    def __init__(self):
        self.parts = lax.axis_size("group")
        self.blocks = tuple(range(self.parts))
        self.order = [jnp.int32(part) for part in range(self.parts)]
        self.spots = self.last_spots = [4 * part for part in self.order]

    def gather_small(self, block):
        whole = lax.all_gather(block, "group", axis=0)
        return [whole[part] for part in range(self.parts)]

    def gather(self, blocks, prepare):
        prepare(blocks[0])
        self.swapped = blocks[0]
        found = [[[piece] for piece in self.gather_small(block)] for block in blocks]
        return [lambda *tokens, groups=groups: groups for groups in found]

    def shared(self, block):
        return [block]

    def total(self, blocks):
        yield
        mine = lax.psum_scatter(jnp.stack(blocks), "group", scatter_dimension=0)
        yield mine
        yield lax.psum(mine, "replica")


def shifted(block, distance):
    devices = range(lax.axis_size("section"))
    route = [(i - distance, i) for i in devices if i - distance in devices]
    return lax.ppermute(block, "section", route)


def in_order(pieces, order):
    place = jnp.stack(order)
    stacked = []
    for block in range(len(pieces)):
        chosen = pieces[0]
        for part in range(1, len(pieces)):
            chosen = jnp.where(place[part] == block, pieces[part], chosen)
        stacked.append(chosen)
    return jnp.stack(stacked)


class Sequence:
    def __init__(self, net, token):
        self.net, self.sums, self.results, self.token = net, {}, {}, token

    def now(self, value):
        return after(value, self.token)

    def ran(self, value):
        self.token = value

    def add(self, name, blocks):
        self.sums[name] = self.net.total(blocks)
        next(self.sums[name])

    def step(self, *names):
        for name in names:
            try:
                self.results[name] = self.token = self.sums[name].send(self.token)
            except StopIteration:
                continue

    def finish(self, name):
        while True:
            try:
                self.results[name] = self.sums[name].send(self.token)
            except StopIteration:
                return self.results[name]


def per_device(
    images,
    cotangent,
    counts,
    qkv_weight,
    out_weight,
    expand_weight,
    reduce_weight,
    norm_gains,
    biases,
    expand_bias,
):
    micro, slots, length, width = images.shape
    space = padded(length)
    section = lax.axis_index("section")
    first = section == 0
    sizes = (lax.axis_size("group"), lax.axis_size("replica"))
    net = FourByFour() if sizes == (4, 4) else General()
    parts = net.parts
    share = width // parts
    batches = tuple(range(micro))

    def rows_of(array):
        fulls = [jnp.pad(array[batch], ((0, 0), (0, space - length), (0, 0))) for batch in batches]
        return [full.reshape(slots * space, width) for full in fulls]

    def images_of(array):
        return array.reshape(slots, space, width)[:, :length]

    small = jnp.concatenate([norm_gains[0], biases[0], expand_bias[0].reshape(-1, share)])
    slot = jnp.arange(slots, dtype=jnp.int32)
    alive = [(slot < counts[batch, 0]).astype(jnp.int32) for batch in batches]
    head = jnp.stack(net.order + [section]).astype(jnp.int32)

    spots = jnp.stack(net.spots + net.last_spots).astype(jnp.int32)

    def meta(living):
        return jnp.concatenate([head, living, spots])

    infos = [meta(alive[batch]) for batch in batches]
    pieces = net.gather_small(small)
    vectors = in_order(pieces, net.order)
    top = vectors[:, :8].transpose(1, 0, 2).reshape(8, width)
    bottom = vectors[:, 8:].reshape(-1, width)
    params = jnp.concatenate([top, bottom]).astype(F32)
    slot = jnp.arange(slots, dtype=jnp.int32)
    alive = [(slot < counts[batch, 0]).astype(jnp.int32) for batch in batches]
    head = jnp.stack(net.order + [section]).astype(jnp.int32)
    spots = jnp.stack(net.spots + net.last_spots).astype(jnp.int32)

    def meta(living):
        return jnp.concatenate([head, living, spots])

    infos = [meta(alive[batch]) for batch in batches]
    inputs, targets = [], []

    def prepare(token):
        inputs.extend(rows_of(after(images, token)))
        targets.extend(rows_of(after(cotangent, token)))
        return [params, *inputs, *targets, *infos]

    qkv, wide, reduce = net.gather(
        [qkv_weight[0], jnp.concatenate([out_weight[0], expand_weight[0]], axis=1), reduce_weight[0]],
        prepare,
    )

    qkv = qkv()
    attended = []
    for batch in batches:
        start = inputs[batch] if batch == 0 else after(inputs[batch], attended[-1][0])
        attended.append(
            forward(start, start, None, qkv, None, params, infos[batch], slots, length)
        )
    wide = wide(attended[0], attended[-1])
    fed = []
    for batch in batches:
        start = inputs[batch] if batch == 0 else after(inputs[batch], fed[-1][0], net.swapped)
        fed.append(
            forward(start, start, attended[batch][0], None, wide, params, infos[batch], slots, length)
        )
    reduce = reduce(attended[-1], fed[0][:1])
    early, incoming = [], []
    for batch in batches:
        middle, active = fed[batch]
        if batch:
            active = after(active, early[-1])
        early.append(output_forward(middle, active, reduce, params, infos[batch], slots))
        incoming.append(shifted(early[batch], 1))

    inner = wide[0][0].shape[1] - width
    mixed_at = inner + width
    kept, lefts, rights, results = [], [], [], []
    sums_a, sums_b, sums_c, returning = [], [], [], []
    token = early[-1]
    for batch in batches:
        start = after(incoming[batch], token)
        left, packed, logs, middle, slope = forward(
            inputs[batch], start, None, qkv, wide, params, infos[batch], slots, length, 8.0
        )
        kept.append((slope, middle, packed, left, logs))
        lefts.append(net.shared(left))
        if batch == 0:
            pair, sides = (targets[0], targets[0]), (kept[0], kept[0])
            lower, chosen = incoming[0], infos[0]
        else:
            pair = (returning[batch - 1], targets[batch])
            sides = (kept[batch - 1], kept[batch])
            lower = inputs[batch - 1]
            chosen = meta(jnp.where(first, alive[batch - 1], alive[batch]))
        right, some, more, result, rest = backward(
            pair, lower, incoming[batch], sides[0], sides[1], reduce, wide, qkv, params, chosen,
            slots, length, mixed_at, 8.0,
        )
        token = result
        rights.append(net.shared(right))
        results.append(result)
        sums_a.append(some)
        sums_b.append(more)
        sums_c.append(rest)
        returning.append(shifted(result, -1))
    late = []
    for batch in batches:
        ready = lefts[batch][1:] + (rights[batch][1:] if batch < micro - 1 else [])
        active = after(kept[batch][3], token, *ready)
        late.append(output_forward(kept[batch][1], active, reduce, params, infos[batch], slots, 8.0))
        token = late[-1]

    last = micro - 1
    run = Sequence(net, token)
    arrived = run.now(returning[last])
    living = jnp.repeat(alive[last] > 0, space)[:, None]
    masked = net.shared(jnp.where(living, arrived, jnp.zeros_like(arrived)))
    many = len(masked)

    def gradient(name, left_at, final, final_at, right_at, quarter, rows, columns, weight=LIGHT):
        left = [lefts[batch][side] for batch in batches for side in range(many)]
        right = []
        for batch in batches:
            for side in range(many):
                upper = (rights[batch][side], right_at)
                lower = (final[side], final_at) if batch == last else (rights[batch + 1][side], right_at)
                right.append((lower, upper))
        blocks = weight_gradient(
            left, right, run.now(head), parts, net.blocks, quarter, (left_at + rows[0], rows[1]), columns,
            name, weight,
        )
        run.ran(blocks[0])
        return blocks

    half, at = inner // 2, inner + 2 * width
    deep = inner // parts
    state = {"mid": None, "rows": None}

    def feed_back(weight):
        start = run.now(arrived)
        hidden, branch, some, more, mid = backward(
            (start, start), None, None, kept[last], kept[last], reduce, wide, None, params, infos[last],
            slots, length, mixed_at, weight,
        )
        run.ran(hidden)
        state.update(mid=mid, branch=branch, hidden=net.shared(hidden), branches=net.shared(branch))
        sums_a.append(some)
        sums_b.append(more)

    def attend_back(weight):
        start = run.now(after(state["branch"], *state["branches"][1:], *state["hidden"][1:]))
        grads, result, rest = backward(
            (start, state["mid"]), inputs[last], inputs[last], kept[last], kept[last], None, wide, qkv,
            params, infos[last], slots, length, mixed_at, weight,
        )
        run.ran(result)
        state["grads"] = net.shared(grads)
        results.append(result)
        sums_c.append(rest)

    def reduce_part(index, weight):
        step = deep // 2
        return gradient(
            "reduce", 0, masked, 0, inner + width, deep, (index * step, step), (0, width), weight
        )

    def expand_part(begin, size, weight):
        return gradient("expand", inner, state["hidden"], 0, 0, share, (0, share), (begin, size), weight)

    def project_part(weight):
        return gradient(
            "project", mixed_at, state["branches"], 0, inner, share, (0, share), (0, width), weight
        )

    def qkv_part(begin, size, weight):
        return gradient("qkv", at, state["grads"], 0, at, share, (0, share), (begin, size), weight)

    def over_batches(values):
        return sum(jnp.where(first, values[batch + 1], values[batch]) for batch in batches)

    def small_sums():
        some, more, rest = over_batches(sums_a), over_batches(sums_b), over_batches(sums_c)
        rows = jnp.concatenate([rest[0:1], some[0:1], rest[1:2], some[1:2], rest[2:4], some[2:4]])
        rows = rows.reshape(8, parts, share).transpose(1, 0, 2)
        rows = jnp.concatenate([rows, more.reshape(parts, -1, share)], axis=1)
        rows = sum(net.shared(run.now(rows)))
        rows = jnp.stack(
            [lax.dynamic_index_in_dim(rows, net.order[block], 0, keepdims=False) for block in net.blocks]
        )
        state["count"] = rows.shape[1]
        state["rows"] = rows.reshape(len(net.blocks), -1).astype(BF16)

    def with_small(blocks):
        step, rows = blocks[0].shape[1], state["rows"]
        rows = jnp.pad(rows, ((0, 0), (0, -rows.shape[1] % (16 * step)))).reshape(len(blocks), -1, step)
        return [jnp.concatenate([block, row]) for block, row in zip(blocks, rows)]

    outputs = []

    def assemble():
        index = len(outputs)
        low, up = (early + results[1:])[index], (late + results[:-1])[index]
        outputs.append(images_of(jnp.where(first, run.now(low), up)))

    def joined(axis, *names):
        found = [run.finish(name) for name in names]
        found = [value[:share] if name == LAST.lower() else value for name, value in zip(names, found)]
        return jnp.concatenate(found, axis=axis).astype(F32)[None]

    shapes = {"q": (1, "q0", "q1"), "p": (1, "p0"), "e": (1, "e0", "e1"), "r": (0, "r0", "r1")}
    gradients = {}

    third = 3 * width // 2
    kernels = {
        "R0": lambda weight: reduce_part(0, weight),
        "R1": lambda weight: reduce_part(1, weight),
        "E0": lambda weight: expand_part(0, half, weight),
        "E1": lambda weight: expand_part(half, half, weight),
        "Q0": lambda weight: qkv_part(0, third, weight),
        "Q1": lambda weight: qkv_part(third, third, weight),
        "P0": lambda weight: project_part(weight),
    }
    for entry in " ".join(PLAN).split():
        name, _, factor = entry.partition("*")
        weight = float(factor or HEAVY) if "*" in entry else LIGHT
        if name in kernels:
            blocks = kernels[name](weight)
            if name == LAST:
                blocks = with_small(blocks)
            run.add(name.lower(), blocks)
        elif name == "BF":
            feed_back(weight)
        elif name == "BA":
            attend_back(weight)
        elif name == "V":
            small_sums()
        elif name == "O":
            assemble()
        elif name[0] == "C":
            gradients[name[1]] = joined(*shapes[name[1]])
        else:
            run.step(name)
    while len(outputs) < 2 * micro:
        assemble()
    for name in shapes:
        if name not in gradients:
            gradients[name] = joined(*shapes[name])
    count = state["count"]
    vector = run.finish(LAST.lower())[share:].reshape(-1)[: count * share].reshape(count, share).astype(F32)
    return (
        jnp.stack(outputs[:micro])[None],
        jnp.stack(outputs[micro:])[None],
        gradients["q"],
        gradients["p"],
        gradients["e"],
        gradients["r"],
        vector[None, 0:2],
        vector[None, 2:8],
        vector[8:].reshape(1, -1),
    )


def solution(mesh):
    placed = (
        P(None, ("group", "replica"), None, None),
        P(None, ("group", "replica"), None, None),
        P(None, ("group", "replica")),
        P("section", "group", None),
        P("section", "group", None),
        P("section", "group", None),
        P("section", "group", None),
        P("section", None, "group"),
        P("section", None, "group"),
        P("section", "group"),
    )
    return jax.shard_map(
        per_device,
        mesh=mesh,
        in_specs=placed,
        out_specs=(
            P("section", None, ("group", "replica"), None, None),
            P("section", None, ("group", "replica"), None, None),
            P("section", "group", None),
            P("section", "group", None),
            P("section", "group", None),
            P("section", "group", None),
            P("section", None, "group"),
            P("section", None, "group"),
            P("section", "group"),
        ),
        check_vma=False,
    )
```
